32 devices in a mesh: member: 2 (over x), dp: 16 (over z, y, core).
Axes of the slice: x: 2, y: 2, z: 4, core: 2. Of those that a mesh axis runs over, the one named last changes fastest.
Arguments:
- features: bfloat16 [64, 256, 1024], P(('dp', 'member')), may hold values from -10 to 10
- teacher_logits: bfloat16 [4, 64, 256, 256], P('member', 'dp'), may hold values from -320 to 320
- lengths: int32 [64], P(('dp', 'member')), may hold values from 16 to 256
- gain_conv: float32 [1024], replicated, may hold values from 0.5 to 1.5
- weight_in: bfloat16 [1024, 2048], replicated, may hold values from -0.1875 to 0.1875
- weight_depth: float32 [31, 1024], replicated, may hold values from -1 to 1
- weight_out: bfloat16 [1024, 1024], replicated, may hold values from -0.1875 to 0.1875
- gain_out: float32 [1024], replicated, may hold values from 0.5 to 1.5
- head_weight: bfloat16 [1024, 256], replicated, may hold values from -1 to 1
Outputs:
- grad_gain_conv: float32 [1024], replicated
- grad_weight_in: float32 [1024, 2048], replicated
- grad_weight_depth: float32 [31, 1024], replicated
- grad_weight_out: float32 [1024, 1024], replicated
- grad_gain_out: float32 [1024], replicated
- grad_head: float32 [1024, 256], replicated
- utt_loss: float32 [64], P(('dp', 'member'))
The draws below stay inside these ranges and needn't reach their ends.
All inputs are finite; a program needn't handle non-finite values.
Results may differ from the reference program's by a relative error of at most 0.015.
Values may be sent and summed in bfloat16 or wider, within the bound.
No kernel may reach another device: no remote copies, remote signals or barrier semaphores. Data moves between devices by JAX's collectives and lax.ppermute only.
A program may use at most 128 MiB of HBM per device.

```python
import math
import jax
import jax.numpy as jnp
from jax import lax

D = 1024
V = 256
KERNEL = 31
TEACHERS = 4
LEN = 256
U_DEV = 2
UTTS = 64


def draw_features(key, part):
    values = jnp.clip(jax.random.normal(jax.random.fold_in(key, 1), (UTTS, LEN, D), jnp.float32), -6.0, 6.0)
    return values.astype(jnp.bfloat16)


def draw_head_weight(key, part):
    values = jax.random.normal(jax.random.fold_in(key, 2), (D, V), jnp.float32) * (1.0 / math.sqrt(D))
    return jnp.clip(values, -1.0, 1.0).astype(jnp.bfloat16)


def draw_teacher_logits(key, part):
    first_key = jax.random.fold_in(key, 0)
    base = 3.0 * jax.random.normal(first_key, (TEACHERS, UTTS, LEN, V), jnp.float32)
    return jnp.clip(base, -18.0, 18.0).astype(jnp.bfloat16)


def draw_lengths(key, part):
    utterance_index = jnp.arange(UTTS, dtype=jnp.int32)
    lowest = LEN // 16 + 3 * LEN // 4 * utterance_index // UTTS
    drawn = jax.random.randint(key, (UTTS,), 0, LEN // 4 + 1, dtype=jnp.int32) + lowest
    drawn = jnp.minimum(drawn, LEN)
    drawn = drawn.at[0].set(LEN // 16)
    return drawn.at[UTTS - 1].set(LEN)


def noise(own_key, extent, scale, limit, kind=jnp.bfloat16):
    return jnp.clip(scale * jax.random.normal(own_key, extent, jnp.float32), -limit, limit).astype(kind)


def setup_inputs(seed: int = 0) -> dict:
    splits = jax.random.split(jax.random.key(seed), 10)
    return {
        "features": draw_features(jax.random.fold_in(splits[9], 71), 0),
        "teacher_logits": draw_teacher_logits(jax.random.fold_in(splits[9], 71), 0),
        "lengths": draw_lengths(jax.random.fold_in(splits[9], 71), 0),
        "gain_conv": jnp.clip(1.0 + 0.1 * jax.random.normal(splits[3], (D,), jnp.float32), 0.5, 1.5),
        "weight_in": noise(splits[4], (D, 2 * D), D ** -0.5, 0.1875),
        "weight_depth": noise(splits[5], (KERNEL, D), KERNEL ** -0.5, 1.0, jnp.float32),
        "weight_out": noise(splits[6], (D, D), D ** -0.5, 0.1875),
        "gain_out": jnp.clip(1.0 + 0.1 * jax.random.normal(splits[7], (D,), jnp.float32), 0.5, 1.5),
        "head_weight": draw_head_weight(jax.random.fold_in(splits[9], 71), 0),
    }


def normalize(values, gain):
    average = lax.optimization_barrier(jnp.mean(values, axis=-1, keepdims=True))
    centred = values - average
    spread = lax.optimization_barrier(jnp.mean(centred * centred, axis=-1, keepdims=True))
    return centred * lax.rsqrt(spread + 1e-05) * gain

def live_frames(lengths, frames):
    return (jnp.arange(frames, dtype=jnp.int32)[None, :] < lengths[:, None]).astype(jnp.float32)

def depthwise(gated, weight_depth):
    frames = gated.shape[1]
    taps = weight_depth.shape[0]
    half_width = taps // 2
    padded = jnp.pad(gated, ((0, 0), (half_width, half_width), (0, 0)))
    total = jnp.zeros(gated.shape, gated.dtype)
    for offset in range(taps):
        total = total + weight_depth[offset][None, None, :] * padded[:, offset:offset + frames, :]
    return total

def lower_part(conv_weights, features, lengths):
    gain_conv, weight_in, weight_depth, weight_out = conv_weights
    utterances, frames, model_width = features.shape
    widened = features.astype(jnp.float32)
    normed = normalize(widened, gain_conv).astype(jnp.bfloat16).reshape(utterances * frames, model_width)
    projected = jnp.dot(normed, weight_in, preferred_element_type=jnp.float32)
    live_mask = live_frames(lengths, frames)
    gated = (projected[:, :model_width] * jax.nn.sigmoid(projected[:, model_width:])).reshape(utterances, frames, model_width) * live_mask[:, :, None]
    convolved = depthwise(gated, weight_depth)
    activated = (convolved * jax.nn.sigmoid(convolved)).astype(jnp.bfloat16).reshape(utterances * frames, model_width)
    update = jnp.dot(activated, weight_out, preferred_element_type=jnp.float32)
    return widened + update.reshape(utterances, frames, model_width)

def upper_part(top_weights, residual_sum, target, lengths, mean_frames):
    gain_out, head_weight = top_weights
    utterances, frames, model_width = residual_sum.shape
    final_norm = normalize(residual_sum, gain_out).astype(jnp.bfloat16).reshape(utterances * frames, model_width)
    student_logits = jnp.dot(final_norm, head_weight, preferred_element_type=jnp.float32)
    student_logp = jax.nn.log_softmax(student_logits, axis=-1).reshape(utterances, frames, -1)
    cross_entropy = -lax.optimization_barrier(jnp.sum(target * student_logp, axis=-1))
    return lax.optimization_barrier(jnp.sum(cross_entropy * live_frames(lengths, frames), axis=-1)) / mean_frames

def student_losses(weights, features, target, lengths, mean_frames):
    residual_sum = lower_part(weights[:4], features, lengths)
    return upper_part(weights[4:], residual_sum, target, lengths, mean_frames)

def teacher_target(summed):
    return jnp.exp(jax.nn.log_softmax(summed / TEACHERS, axis=-1))

def reference(features, teacher_logits, lengths, gain_conv, weight_in, weight_depth, weight_out, gain_out, head_weight):
    mean_frames = jnp.sum(lengths.astype(jnp.float32)) / UTTS
    weights = (gain_conv, weight_in, weight_depth, weight_out, gain_out, head_weight)

    def one_block(running, block_index):
        start = block_index * U_DEV
        block_features = lax.dynamic_slice_in_dim(features, start, U_DEV, 0)
        block_logits = lax.dynamic_slice_in_dim(teacher_logits, start, U_DEV, 1)
        block_lengths = lax.dynamic_slice_in_dim(lengths, start, U_DEV, 0)
        summed = lax.optimization_barrier(jnp.sum(jax.nn.log_softmax(block_logits.astype(jnp.float32), axis=-1), axis=0))
        target = teacher_target(summed)

        def local_loss(trainable):
            return student_losses(trainable, block_features, target, block_lengths, mean_frames)
        losses, pullback = jax.vjp(local_loss, weights)
        gradients = pullback(jnp.ones_like(losses))[0]
        updated = tuple((running_sum + piece_grad.astype(jnp.float32) for running_sum, piece_grad in zip(running, gradients)))
        return (updated, losses)
    initial = tuple((jnp.zeros(weight.shape, jnp.float32) for weight in weights))
    totals, losses = lax.scan(one_block, initial, jnp.arange(UTTS // U_DEV, dtype=jnp.int32))
    return (totals[0], totals[1], totals[2], totals[3], totals[4], totals[5], losses.reshape(UTTS))
```

```python
import functools

import jax
import jax.numpy as jnp
from jax import lax
from jax.experimental import pallas as pl
from jax.experimental.pallas import tpu as pltpu
from jax.sharding import PartitionSpec as P

TEACHERS = 4
AXES = ("member", "dp")
SPLIT_BITS = 5
SHARDS = 1 << SPLIT_BITS


def normalize(values, gain):
    average = jnp.mean(values, axis=-1, keepdims=True)
    centred = values - average
    spread = jnp.mean(centred * centred, axis=-1, keepdims=True)
    return centred * lax.rsqrt(spread + 1e-05) * gain


def live_frames(lengths, frames):
    return (jnp.arange(frames, dtype=jnp.int32)[None, :] < lengths[:, None]).astype(jnp.float32)


def lower_part(conv_weights, features, lengths):
    gain_conv, weight_in, weight_depth, weight_out = conv_weights
    utterances, frames, model_width = features.shape
    widened = features.astype(jnp.float32)
    normed = (
        normalize(widened, gain_conv).astype(jnp.bfloat16).reshape(utterances * frames, model_width)
    )
    projected = jnp.dot(normed, weight_in, preferred_element_type=jnp.float32)
    live_mask = live_frames(lengths, frames)
    gated = (projected[:, :model_width] * jax.nn.sigmoid(projected[:, model_width:])).reshape(
        utterances, frames, model_width
    ) * live_mask[:, :, None]
    half_width = weight_depth.shape[0] // 2
    convolved = lax.conv_general_dilated(
        gated,
        weight_depth[:, None, :],
        (1,),
        [(half_width, half_width)],
        dimension_numbers=("NWC", "WIO", "NWC"),
        feature_group_count=model_width,
        precision=lax.Precision.HIGHEST,
    )
    activated = (
        (convolved * jax.nn.sigmoid(convolved))
        .astype(jnp.bfloat16)
        .reshape(utterances * frames, model_width)
    )
    update = jnp.dot(activated, weight_out, preferred_element_type=jnp.float32)
    return widened + update.reshape(utterances, frames, model_width)


def upper_part(top_weights, residual_sum, target, lengths):
    gain_out, head_weight = top_weights
    utterances, frames, model_width = residual_sum.shape
    final_norm = (
        normalize(residual_sum, gain_out)
        .astype(jnp.bfloat16)
        .reshape(utterances * frames, model_width)
    )
    student_logits = jnp.dot(final_norm, head_weight, preferred_element_type=jnp.float32)
    student_logp = jax.nn.log_softmax(student_logits, axis=-1).reshape(utterances, frames, -1)
    cross_entropy = -jnp.sum(target * student_logp, axis=-1)
    return jnp.sum(cross_entropy * live_frames(lengths, frames), axis=-1)


def teacher_target(summed):
    return jnp.exp(jax.nn.log_softmax(summed / TEACHERS, axis=-1))


def bit_orders(count):
    bits = count.bit_length() - 1
    top = bits - 1
    middle = list(range(2, top))
    return [0, top, 1] + middle, [0, 1, top] + middle


def shard_of(device, order):
    own = jnp.int32(0)
    for place, bit in enumerate(order[:SPLIT_BITS]):
        own = own | (((device >> bit) & 1) << (SPLIT_BITS - 1 - place))
    return own


def swap(values, bit, count):
    return lax.ppermute(values, AXES, [(i, i ^ (1 << bit)) for i in range(count)])


def add_pair(own, other):
    return (own.astype(jnp.float32) + other.astype(jnp.float32)).astype(own.dtype)


def reduce_scatter(parts, orders, count):
    parts = list(parts)
    for place in range(len(orders[0])):
        received = []
        for part, order in zip(parts, orders):
            half = part.shape[0] // 2 if place < SPLIT_BITS else 0
            received.append(swap(part[half:], order[place], count))
        for group, other in enumerate(received):
            half = other.shape[0]
            parts[group] = add_pair(parts[group][:half], other)
    return parts


def all_gather(parts, orders, count):
    parts = list(parts)
    for place in reversed(range(SPLIT_BITS)):
        received = [swap(part, order[place], count) for part, order in zip(parts, orders)]
        parts = [jnp.concatenate([part, other], axis=0) for part, other in zip(parts, received)]
    return parts


def all_sum(values, count):
    for bit in range(count.bit_length() - 1):
        values = values + swap(values, bit, count)
    return values


def pack_kernel(own_ref, *refs):
    half = len(refs) // 2
    for source, target in zip(refs[:half], refs[half:]):
        rows = target.shape[1]
        group = 0 if source is refs[0] else 1

        def one(piece, carry, source=source, target=target, rows=rows, group=group):
            start = pl.multiple_of((piece ^ own_ref[group]) * rows, rows)
            target[piece] = source[pl.ds(start, rows), :]
            return carry

        lax.fori_loop(0, target.shape[0], one, 0)


def pack(own, first, second):
    rows, width = first.shape
    shape = jax.ShapeDtypeStruct((SHARDS, rows // SHARDS, width), jnp.bfloat16)
    whole = pl.BlockSpec(memory_space=pltpu.VMEM)
    return pl.pallas_call(
        pack_kernel,
        out_shape=(shape, shape),
        in_specs=[pl.BlockSpec(memory_space=pltpu.SMEM), whole, whole],
        out_specs=(whole, whole),
        compiler_params=pltpu.CompilerParams(vmem_limit_bytes=40 << 20),
        name="pack",
    )(own, first, second)


def unpack_kernel(steps, own_ref, scale_ref, top_a, top_b, in_a, in_b, win_ref, wout_ref, head_ref):
    scale = scale_ref[0:1, 0:1]
    per_step = in_a.shape[0]
    rows = in_a.shape[1]
    width_out = wout_ref.shape[1] // 2
    width_head = head_ref.shape[1] // 2
    width_in = win_ref.shape[1] // 2
    for index in range(per_step):
        here = slice(index * rows, (index + 1) * rows)
        for group, top, inner in ((0, top_a, in_a), (1, top_b, in_b)):
            piece = index ^ (own_ref[group] & (per_step - 1))
            wide = top[piece].astype(jnp.float32) * scale
            wout_ref[here, group * width_out : (group + 1) * width_out] = wide[:, :width_out]
            head_ref[here, group * width_head : (group + 1) * width_head] = wide[:, width_out:]
            win_ref[here, group * width_in : (group + 1) * width_in] = (
                inner[piece].astype(jnp.float32) * scale
            )


def unpack(own, scale, tops, inners, width_out, width_head):
    steps = 8
    per_step = SHARDS // steps
    rows = inners[0].shape[1]
    width_in = inners[0].shape[2]
    model = SHARDS * rows

    def piece_spec(array, group):
        return pl.BlockSpec(
            (per_step,) + array.shape[1:],
            lambda i, own_ref: (i ^ (own_ref[group] // per_step), 0, 0),
        )

    def out_spec(width):
        return pl.BlockSpec((per_step * rows, width), lambda i, own_ref: (i, 0))

    widths = (2 * width_in, width_out, width_head)
    return pl.pallas_call(
        functools.partial(unpack_kernel, steps),
        out_shape=tuple(jax.ShapeDtypeStruct((model, width), jnp.float32) for width in widths),
        grid_spec=pltpu.PrefetchScalarGridSpec(
            num_scalar_prefetch=1,
            grid=(steps,),
            in_specs=[pl.BlockSpec((8, 128), lambda i, own_ref: (0, 0))]
            + [piece_spec(array, group) for group, array in enumerate(tops)]
            + [piece_spec(array, group) for group, array in enumerate(inners)],
            out_specs=tuple(out_spec(width) for width in widths),
        ),
        compiler_params=pltpu.CompilerParams(vmem_limit_bytes=40 << 20),
        name="unpack",
    )(own, scale, *tops, *inners)


def on_device(
    features,
    teacher_logits,
    lengths,
    gain_conv,
    weight_in,
    weight_depth,
    weight_out,
    gain_out,
    head_weight,
):
    count = lax.axis_size("member") * lax.axis_size("dp")
    device = lax.axis_index("member") * lax.axis_size("dp") + lax.axis_index("dp")
    orders = bit_orders(count)
    own = jnp.stack([shard_of(device, order) for order in orders]).astype(jnp.int32)
    member = lax.axis_index("member")
    taps, model = weight_depth.shape

    local_sum = jnp.sum(jax.nn.log_softmax(teacher_logits.astype(jnp.float32), axis=-1), axis=0)
    own_count = lengths.shape[0]
    give = lax.dynamic_slice_in_dim(local_sum, (1 - member) * own_count, own_count, 0)
    keep = lax.dynamic_slice_in_dim(local_sum, member * own_count, own_count, 0)
    own_sum = keep + swap(give, count.bit_length() - 2, count)
    target = teacher_target(own_sum)
    weights = (gain_conv, weight_in, weight_depth, weight_out, gain_out, head_weight)

    def local_loss(trainable):
        residual_sum = lower_part(trainable[:4], features, lengths)
        return upper_part(trainable[4:], residual_sum, target, lengths)

    losses, pullback = jax.vjp(local_loss, weights)
    gradients = pullback(jnp.ones_like(losses))[0]

    small = jnp.concatenate(
        [
            gradients[2],
            gradients[0][None],
            gradients[4][None],
            jnp.broadcast_to(jnp.sum(lengths.astype(jnp.float32)), (1, model)),
        ],
        axis=0,
    )
    small = all_sum(small, count)
    scale = own_count * count / small[taps + 2, 0]

    half_out = weight_out.shape[1] // 2
    half_head = head_weight.shape[1] // 2
    top_a = jnp.concatenate([gradients[3][:, :half_out], gradients[5][:, :half_head]], axis=1)
    top_b = jnp.concatenate([gradients[3][:, half_out:], gradients[5][:, half_head:]], axis=1)
    tops = pack(own, top_a, top_b)
    tops = all_gather(reduce_scatter(tops, orders, count), orders, count)
    half_in = weight_in.shape[1] // 2
    inners = pack(own, gradients[1][:, :half_in], gradients[1][:, half_in:])
    inners = all_gather(reduce_scatter(inners, orders, count), orders, count)
    grad_in, grad_out, grad_head = unpack(
        own,
        jnp.broadcast_to(scale, (8, 128)),
        tops,
        inners,
        weight_out.shape[1],
        head_weight.shape[1],
    )
    small = small * scale
    return (small[taps], grad_in, small[:taps], grad_out, small[taps + 1], grad_head, losses * scale)


def solution(mesh):
    in_specs = (
        P(("dp", "member"), None, None),
        P("member", "dp", None, None),
        P(("dp", "member")),
        P(),
        P(),
        P(),
        P(),
        P(),
        P(),
    )
    out_specs = (P(), P(), P(), P(), P(), P(), P(("dp", "member")))
    return jax.shard_map(
        on_device, mesh=mesh, in_specs=in_specs, out_specs=out_specs, check_vma=False
    )
```

```python
import functools

import jax
import jax.numpy as jnp
from jax import lax
from jax.experimental import pallas as pl
from jax.experimental.pallas import tpu as pltpu
from jax.sharding import PartitionSpec as P

TEACHERS = 4
AXES = ("member", "dp")
PLACE_BITS = 4
PLACES = 1 << PLACE_BITS
WIDE = 256
LANES = 128
TILE = 128
MARGIN = 16
CHUNKS = 2
VMEM = 56 << 20
SMEM_SPEC = pl.BlockSpec(memory_space=pltpu.SMEM)
F32 = jnp.float32
BF16 = jnp.bfloat16


def params():
    return pltpu.CompilerParams(vmem_limit_bytes=VMEM)


def dot(left, right, left_axis=1, right_axis=0):
    return lax.dot_general(
        left, right, (((left_axis,), (right_axis,)), ((), ())), preferred_element_type=F32
    )


def fixed(*shape):
    return pl.BlockSpec(shape, lambda i, *_: (0,) * len(shape))


def bit_orders(count):
    top = count.bit_length() - 2
    middle = list(range(2, top))
    return [top, 1] + middle, [1, top] + middle


def place_of(device, order):
    own = jnp.int32(0)
    for index, bit in enumerate(order[:PLACE_BITS]):
        own = own | (((device >> bit) & 1) << (PLACE_BITS - 1 - index))
    return own


def swap(values, bit, count):
    return lax.ppermute(values, AXES, [(i, i ^ (1 << bit)) for i in range(count)])


def add_pair(own, other):
    return (own.astype(F32) + other.astype(F32)).astype(own.dtype)


def sum_pieces(send, keep, orders, count):
    both = add_pair(keep, swap(send, 0, count))
    parts = [both[0], both[1]]
    for index in range(len(orders[0])):
        received = []
        for part, order in zip(parts, orders):
            half = part.shape[0] // 2 if index < PLACE_BITS else 0
            received.append(swap(part[half:], order[index], count))
        for group, other in enumerate(received):
            parts[group] = add_pair(parts[group][: other.shape[0]], other)
    for index in reversed(range(PLACE_BITS)):
        received = [swap(part, order[index], count) for part, order in zip(parts, orders)]
        parts = [jnp.concatenate([part, other], axis=0) for part, other in zip(parts, received)]
    own = jnp.stack(parts)
    return own, swap(own, 0, count)


def all_sum(values, count):
    for bit in range(count.bit_length() - 1):
        values = values + swap(values, bit, count)
    return values


def write_pieces(place, core, product, send_ref, keep_ref, lead, columns):
    rows = keep_ref.shape[-2]

    def one(piece, carry):
        base = (piece ^ place) * (2 * rows)
        kept = pl.multiple_of(base + core * rows, rows)
        sent = pl.multiple_of(base + (1 - core) * rows, rows)
        keep_ref[lead, piece, :, columns] = product[pl.ds(kept, rows), :].astype(BF16)
        send_ref[lead, piece, :, columns] = product[pl.ds(sent, rows), :].astype(BF16)
        return carry

    lax.fori_loop(0, PLACES, one, 0)


def teacher_kernel(member_ref, logits_ref, give_ref, keep_ref, *, own_count):
    step = pl.program_id(0)
    total = None
    for teacher in range(logits_ref.shape[0]):
        logits = logits_ref[teacher, 0].astype(F32)
        shifted = logits - jnp.max(logits, axis=-1, keepdims=True)
        logp = shifted - jnp.log(jnp.sum(jnp.exp(shifted), axis=-1, keepdims=True))
        total = logp if total is None else total + logp

    @pl.when(step < own_count)
    def _():
        give_ref[0] = total

    @pl.when(step >= own_count)
    def _():
        keep_ref[0] = total


def teacher_sums(member, logits, own_count):
    teachers, utterances, frames, symbols = logits.shape
    shape = jax.ShapeDtypeStruct((own_count, frames, symbols), F32)

    def source(i, member_ref):
        mine = member_ref[0] * own_count
        theirs = (1 - member_ref[0]) * own_count
        return (0, jnp.where(i < own_count, theirs + i, mine + i - own_count), 0, 0)

    return pl.pallas_call(
        functools.partial(teacher_kernel, own_count=own_count),
        out_shape=(shape, shape),
        grid_spec=pltpu.PrefetchScalarGridSpec(
            num_scalar_prefetch=1,
            grid=(2 * own_count,),
            in_specs=[pl.BlockSpec((teachers, 1, frames, symbols), source)],
            out_specs=(
                pl.BlockSpec(
                    (1, frames, symbols), lambda i, _: (jnp.minimum(i, own_count - 1), 0, 0)
                ),
                pl.BlockSpec(
                    (1, frames, symbols), lambda i, _: (jnp.maximum(i - own_count, 0), 0, 0)
                ),
            ),
        ),
        compiler_params=params(),
        name="teachers",
    )(member, logits)


def live_column(lengths_ref, utterance, frames):
    position = lax.broadcasted_iota(jnp.int32, (frames, 1), 0)
    return (position < lengths_ref[utterance]).astype(F32)


def clear_margins(pad_ref):
    frames = pad_ref.shape[2] - 2 * MARGIN
    zeros = jnp.zeros(pad_ref.shape[:2] + (MARGIN, LANES), F32)
    pad_ref[:, :, :MARGIN, :] = zeros
    pad_ref[:, :, MARGIN + frames :, :] = zeros


def shifted_views(pad_ref, lane, utterance, start, taps):
    first = MARGIN - taps // 2
    for phase in range(8):
        offsets = [offset for offset in range(first, first + taps) if offset % 8 == phase]
        if not offsets:
            continue
        low = offsets[0]
        span = offsets[-1] - low + TILE
        view = pad_ref[lane, utterance, start + low : start + low + span, :]
        for offset in offsets:
            yield offset - first, view[offset - low : offset - low + TILE]


def convolve(pad_ref, lane, utterance, start, depth_ref, flipped):
    taps = depth_ref.shape[0]
    columns = slice(lane * LANES, (lane + 1) * LANES)
    total = jnp.zeros((TILE, LANES), F32)
    for tap, view in shifted_views(pad_ref, lane, utterance, start, taps):
        row = taps - 1 - tap if flipped else tap
        total = total + view * depth_ref[row : row + 1, columns]
    return total


def forward_kernel(
    lengths_ref,
    features_ref,
    gain_ref,
    value_weight_ref,
    gate_weight_ref,
    depth_ref,
    out_weight_ref,
    normed_ref,
    gated_ref,
    gate_ref,
    slope_ref,
    active_ref,
    residual_ref,
    pad_ref,
):
    utterances = pad_ref.shape[1]
    frames = pad_ref.shape[2] - 2 * MARGIN

    @pl.when(pl.program_id(0) == 0)
    def _():
        values = features_ref[...].astype(F32)
        centred = values - jnp.mean(values, axis=-1, keepdims=True)
        spread = jnp.mean(centred * centred, axis=-1, keepdims=True)
        normed_ref[...] = (centred * lax.rsqrt(spread + 1e-05) * gain_ref[...]).astype(BF16)
        residual_ref[...] = values
        clear_margins(pad_ref)

    for utterance in range(utterances):
        rows = slice(utterance * frames, (utterance + 1) * frames)
        normed = normed_ref[rows, :]
        gate = jax.nn.sigmoid(dot(normed, gate_weight_ref[...]))
        gated = dot(normed, value_weight_ref[...]) * gate
        gated = gated * live_column(lengths_ref, utterance, frames)
        gate_ref[rows, :] = gate
        gated_ref[rows, :] = gated
        for lane in range(WIDE // LANES):
            pad_ref[lane, utterance, MARGIN : MARGIN + frames, :] = gated[
                :, lane * LANES : (lane + 1) * LANES
            ]

    for lane in range(WIDE // LANES):
        columns = slice(lane * LANES, (lane + 1) * LANES)

        def one(utterance, carry, lane=lane, columns=columns):
            for start in range(0, frames, TILE):
                rows = pl.ds(pl.multiple_of(utterance * frames + start, TILE), TILE)
                convolved = convolve(pad_ref, lane, utterance, start, depth_ref, False)
                squash = jax.nn.sigmoid(convolved)
                active_ref[rows, columns] = (convolved * squash).astype(BF16)
                slope_ref[rows, columns] = squash * (1.0 + convolved * (1.0 - squash))
            return carry

        lax.fori_loop(0, utterances, one, 0)

    residual_ref[...] += dot(active_ref[...], out_weight_ref[...])


def forward(lengths, features, gain, weight_in, depth, weight_out, utterances):
    rows, model = features.shape
    frames = rows // utterances
    steps = model // WIDE
    column = pl.BlockSpec((rows, WIDE), lambda i: (0, i))
    wide = jax.ShapeDtypeStruct((rows, model), F32)
    narrow = jax.ShapeDtypeStruct((rows, model), BF16)
    return pl.pallas_call(
        forward_kernel,
        grid=(steps,),
        out_shape=(narrow, wide, wide, wide, narrow, wide),
        in_specs=[
            SMEM_SPEC,
            fixed(rows, model),
            fixed(1, model),
            pl.BlockSpec((model, WIDE), lambda i: (0, i)),
            pl.BlockSpec((model, WIDE), lambda i: (0, steps + i)),
            pl.BlockSpec((depth.shape[0], WIDE), lambda i: (0, i)),
            pl.BlockSpec((WIDE, model), lambda i: (i, 0)),
        ],
        out_specs=(fixed(rows, model), column, column, column, column, fixed(rows, model)),
        scratch_shapes=[pltpu.VMEM((WIDE // LANES, utterances, frames + 2 * MARGIN, LANES), F32)],
        compiler_params=params(),
        name="forward",
    )(lengths, features, gain, weight_in, weight_in, depth, weight_out)


def top_kernel(
    lengths_ref,
    residual_ref,
    gain_ref,
    head_ref,
    kept_ref,
    got_ref,
    loss_ref,
    final_ref,
    dlogits_ref,
    dresidual_ref,
):
    frames = residual_ref.shape[0]
    live = live_column(lengths_ref, pl.program_id(0), frames)
    values = residual_ref[...]
    centred = values - jnp.mean(values, axis=-1, keepdims=True)
    spread = jnp.mean(centred * centred, axis=-1, keepdims=True)
    inverse = lax.rsqrt(spread + 1e-05)
    unit = centred * inverse
    final = (unit * gain_ref[...]).astype(BF16)
    final_ref[...] = final

    def log_softmax(logits):
        shifted = logits - jnp.max(logits, axis=-1, keepdims=True)
        return shifted - jnp.log(jnp.sum(jnp.exp(shifted), axis=-1, keepdims=True))

    target = jnp.exp(log_softmax((kept_ref[0] + got_ref[0]) * (1.0 / TEACHERS)))
    logp = log_softmax(dot(final, head_ref[...]))
    cross = -jnp.sum(target * logp, axis=-1, keepdims=True)
    loss_ref[...] = jnp.broadcast_to(jnp.sum(cross * live, axis=0, keepdims=True), (1, 1, LANES))
    weight = jnp.sum(target, axis=-1, keepdims=True)
    dlogits = ((jnp.exp(logp) * weight - target) * live).astype(BF16)
    dlogits_ref[...] = dlogits
    dunit = dot(dlogits, head_ref[...], 1, 1) * gain_ref[...]
    average = jnp.mean(dunit, axis=-1, keepdims=True)
    along = jnp.mean(dunit * unit, axis=-1, keepdims=True)
    dresidual_ref[...] = (inverse * (dunit - average - unit * along)).astype(BF16)


def top(lengths, residual, gain, head, kept, got):
    rows, model = residual.shape
    utterances, frames, symbols = kept.shape
    per_row = pl.BlockSpec((frames, model), lambda i: (i, 0))
    sums = pl.BlockSpec((1, frames, symbols), lambda i: (i, 0, 0))
    return pl.pallas_call(
        top_kernel,
        grid=(utterances,),
        out_shape=(
            jax.ShapeDtypeStruct((utterances, 1, LANES), F32),
            jax.ShapeDtypeStruct((rows, model), BF16),
            jax.ShapeDtypeStruct((rows, symbols), BF16),
            jax.ShapeDtypeStruct((rows, model), BF16),
        ),
        in_specs=[SMEM_SPEC, per_row, fixed(1, model), fixed(model, symbols), sums, sums],
        out_specs=(
            pl.BlockSpec((1, 1, LANES), lambda i: (i, 0, 0)),
            per_row,
            pl.BlockSpec((frames, symbols), lambda i: (i, 0)),
            per_row,
        ),
        compiler_params=params(),
        name="top",
    )(lengths, residual, gain, head, kept, got)


def outer_kernel(
    own_ref, active_ref, dresidual_ref, final_ref, dlogits_ref, send_ref, keep_ref, product_ref
):
    group = pl.program_id(0)
    width = dresidual_ref.shape[1]
    product_ref[:, :width] = dot(active_ref[...], dresidual_ref[...], 0, 0)
    product_ref[:, width:] = dot(final_ref[...], dlogits_ref[...], 0, 0)
    write_pieces(own_ref[group], own_ref[2], product_ref, send_ref, keep_ref, 0, slice(None))


def outer(own, active, dresidual, final, dlogits):
    rows, model = active.shape
    half_out = dresidual.shape[1] // 2
    half_head = dlogits.shape[1] // 2
    width = half_out + half_head
    piece = (PLACES, model // (2 * PLACES), width)
    shape = jax.ShapeDtypeStruct((2,) + piece, BF16)
    out = pl.BlockSpec((1,) + piece, lambda i: (i, 0, 0, 0))
    return pl.pallas_call(
        outer_kernel,
        grid=(2,),
        out_shape=(shape, shape),
        in_specs=[
            SMEM_SPEC,
            fixed(rows, model),
            pl.BlockSpec((rows, half_out), lambda i: (0, i)),
            fixed(rows, model),
            pl.BlockSpec((rows, half_head), lambda i: (0, i)),
        ],
        out_specs=(out, out),
        scratch_shapes=[pltpu.VMEM((model, width), F32)],
        compiler_params=params(),
        name="outer",
    )(own, active, dresidual, final, dlogits)


def inner_kernel(
    own_ref,
    lengths_ref,
    dresidual_ref,
    out_weight_ref,
    slope_ref,
    gated_ref,
    gate_ref,
    normed_ref,
    depth_ref,
    send_ref,
    keep_ref,
    dconv_ref,
    pad_ref,
    dvalue_ref,
    dgate_ref,
    product_ref,
):
    utterances = pad_ref.shape[1]
    frames = pad_ref.shape[2] - 2 * MARGIN

    @pl.when(pl.program_id(0) == 0)
    def _():
        clear_margins(pad_ref)

    for utterance in range(utterances):
        rows = slice(utterance * frames, (utterance + 1) * frames)
        dconv = dot(dresidual_ref[rows, :], out_weight_ref[...], 1, 1) * slope_ref[rows, :]
        dconv_ref[rows, :] = dconv
        for lane in range(WIDE // LANES):
            pad_ref[lane, utterance, MARGIN : MARGIN + frames, :] = dconv[
                :, lane * LANES : (lane + 1) * LANES
            ]

    for lane in range(WIDE // LANES):
        columns = slice(lane * LANES, (lane + 1) * LANES)

        def one(utterance, carry, lane=lane, columns=columns):
            for start in range(0, frames, TILE):
                rows = pl.ds(pl.multiple_of(utterance * frames + start, TILE), TILE)
                position = lax.broadcasted_iota(jnp.int32, (TILE, 1), 0) + start
                live = (position < lengths_ref[utterance]).astype(F32)
                dgated = convolve(pad_ref, lane, utterance, start, depth_ref, True) * live
                gate = gate_ref[rows, columns]
                dvalue_ref[rows, columns] = (dgated * gate).astype(BF16)
                dgate_ref[rows, columns] = (dgated * gated_ref[rows, columns] * (1.0 - gate)).astype(
                    BF16
                )
            return carry

        lax.fori_loop(0, utterances, one, 0)

    for group, source in ((0, dvalue_ref), (1, dgate_ref)):
        product_ref[...] = dot(normed_ref[...], source[...], 0, 0)
        write_pieces(own_ref[group], own_ref[2], product_ref, send_ref, keep_ref, group, slice(None))


def inner(own, lengths, dresidual, weight_out, slope, gated, gate, normed, depth, chunk, utterances):
    rows, model = normed.shape
    frames = rows // utterances
    steps = model // WIDE // CHUNKS
    first = chunk * steps
    column = pl.BlockSpec((rows, WIDE), lambda i: (0, first + i))
    piece = (2, PLACES, model // (2 * PLACES))
    shape = jax.ShapeDtypeStruct(piece + (steps * WIDE,), BF16)
    out = pl.BlockSpec(piece + (WIDE,), lambda i: (0, 0, 0, i))
    return pl.pallas_call(
        inner_kernel,
        grid=(steps,),
        out_shape=(shape, shape, jax.ShapeDtypeStruct((rows, steps * WIDE), F32)),
        in_specs=[
            SMEM_SPEC,
            SMEM_SPEC,
            fixed(rows, model),
            pl.BlockSpec((WIDE, model), lambda i: (first + i, 0)),
            column,
            column,
            column,
            fixed(rows, model),
            pl.BlockSpec((depth.shape[0], WIDE), lambda i: (0, first + i)),
        ],
        out_specs=(out, out, pl.BlockSpec((rows, WIDE), lambda i: (0, i))),
        scratch_shapes=[
            pltpu.VMEM((WIDE // LANES, utterances, frames + 2 * MARGIN, LANES), F32),
            pltpu.VMEM((rows, WIDE), BF16),
            pltpu.VMEM((rows, WIDE), BF16),
            pltpu.VMEM((model, WIDE), F32),
        ],
        compiler_params=params(),
        name="inner",
    )(own, lengths, dresidual, weight_out, slope, gated, gate, normed, depth)


def taps_kernel(lengths_ref, gated_ref, dconv_ref, out_ref, pad_ref, sums_ref):
    utterances = pad_ref.shape[1]
    frames = pad_ref.shape[2] - 2 * MARGIN
    taps = out_ref.shape[0] - 1
    valid = lengths_ref[0]
    for utterance in range(1, utterances):
        valid = valid + lengths_ref[utterance]

    @pl.when(pl.program_id(0) == 0)
    def _():
        clear_margins(pad_ref)

    for lane in range(WIDE // LANES):
        columns = slice(lane * LANES, (lane + 1) * LANES)
        for utterance in range(utterances):
            rows = slice(utterance * frames, (utterance + 1) * frames)
            pad_ref[lane, utterance, MARGIN : MARGIN + frames, :] = gated_ref[rows, columns]
        sums_ref[...] = jnp.zeros_like(sums_ref)

        def one(utterance, carry, lane=lane, columns=columns):
            for start in range(0, frames, TILE):
                rows = pl.ds(pl.multiple_of(utterance * frames + start, TILE), TILE)
                dconv = dconv_ref[rows, columns]
                for tap, view in shifted_views(pad_ref, lane, utterance, start, taps):
                    sums_ref[tap] += jnp.sum((view * dconv).reshape(TILE // 8, 8, LANES), axis=0)
            return carry

        lax.fori_loop(0, utterances, one, 0)
        out_ref[:taps, columns] = jnp.sum(sums_ref[...], axis=1)
    out_ref[taps:, :] = jnp.zeros((1, WIDE), F32) + valid.astype(F32)


def tap_sums(lengths, gated, dconv, taps, chunk, utterances):
    rows, width = dconv.shape
    steps = width // WIDE
    first = chunk * steps
    return pl.pallas_call(
        taps_kernel,
        grid=(steps,),
        out_shape=jax.ShapeDtypeStruct((taps + 1, width), F32),
        in_specs=[
            SMEM_SPEC,
            pl.BlockSpec((rows, WIDE), lambda i: (0, first + i)),
            pl.BlockSpec((rows, WIDE), lambda i: (0, i)),
        ],
        out_specs=pl.BlockSpec((taps + 1, WIDE), lambda i: (0, i)),
        scratch_shapes=[
            pltpu.VMEM((WIDE // LANES, utterances, rows // utterances + 2 * MARGIN, LANES), F32),
            pltpu.VMEM((taps, 8, LANES), F32),
        ],
        compiler_params=params(),
        name="taps",
    )(lengths, gated, dconv)


def unpack_kernel(utts, per_step, own_ref, small_ref, weight_ref, head_ref, *refs):
    arrays = (len(refs) - 5) // 4
    pieces, (win_ref, wout_ref, dhead_ref, gain_in_ref, gain_out_ref) = refs[:-5], refs[-5:]
    scale = utts / small_ref[small_ref.shape[0] - 1 :, 0:1]
    core = own_ref[2]
    rows = pieces[0].shape[2]
    half_out = wout_ref.shape[1] // 2
    half_in = win_ref.shape[1] // 2
    half_head = dhead_ref.shape[1] // 2
    for index in range(per_step):
        for group in range(2):
            piece = index ^ (own_ref[group] & (per_step - 1))
            for whose in range(2):
                side = core if whose == 0 else 1 - core
                here = pl.ds(pl.multiple_of(index * 2 * rows + side * rows, rows), rows)
                for array in range(arrays):
                    source = pieces[(array * 2 + whose) * 2 + group]
                    wide = source[0, piece].astype(F32) * scale
                    if array == 0:
                        wout_ref[here, group * half_out : (group + 1) * half_out] = wide[:, :half_out]
                        dhead_ref[here, group * half_head : (group + 1) * half_head] = wide[
                            :, half_out:
                        ]
                    else:
                        width = wide.shape[1]
                        first = group * half_in + (array - 1) * width
                        win_ref[here, first : first + width] = wide
    gain_in_ref[...] = jnp.sum(weight_ref[...].astype(F32) * win_ref[...], axis=1, keepdims=True)
    gain_out_ref[...] = jnp.sum(head_ref[...].astype(F32) * dhead_ref[...], axis=1, keepdims=True)


def unpack(utts, own, small, weight_in, head, sums, width_out):
    steps = 4
    per_step = PLACES // steps
    model = head.shape[0]
    rows = model // steps
    widths = (weight_in.shape[1], width_out, head.shape[1], 1, 1)
    operands = []
    specs = []
    for pair in sums:
        for array in pair:
            for group in range(2):
                operands.append(array)
                specs.append(
                    pl.BlockSpec(
                        (1, per_step) + array.shape[2:],
                        lambda i, own_ref, group=group: (
                            group,
                            i ^ (own_ref[group] // per_step),
                            0,
                            0,
                        ),
                    )
                )

    def block(width):
        return pl.BlockSpec((rows, width), lambda i, own_ref: (i, 0))

    return pl.pallas_call(
        functools.partial(unpack_kernel, utts, per_step),
        out_shape=tuple(jax.ShapeDtypeStruct((model, width), F32) for width in widths),
        grid_spec=pltpu.PrefetchScalarGridSpec(
            num_scalar_prefetch=1,
            grid=(steps,),
            in_specs=[fixed(*small.shape), block(weight_in.shape[1]), block(head.shape[1])] + specs,
            out_specs=tuple(block(width) for width in widths),
        ),
        compiler_params=params(),
        name="unpack",
    )(own, small, weight_in, head, *operands)


def on_device(
    features,
    teacher_logits,
    lengths,
    gain_conv,
    weight_in,
    weight_depth,
    weight_out,
    gain_out,
    head_weight,
):
    count = lax.axis_size("member") * lax.axis_size("dp")
    member = lax.axis_index("member").astype(jnp.int32)
    device = member * lax.axis_size("dp") + lax.axis_index("dp")
    orders = bit_orders(count)
    own = jnp.stack([place_of(device, order) for order in orders] + [device & 1]).astype(jnp.int32)
    taps, model = weight_depth.shape
    utterances, frames, _ = features.shape
    utts = float(utterances * count)

    give, kept = teacher_sums(member[None], teacher_logits, utterances)
    got = swap(give, count.bit_length() - 2, count)
    flat = features.reshape(utterances * frames, model)
    normed, gated, gate, slope, active, residual = forward(
        lengths, flat, gain_conv[None], weight_in, weight_depth, weight_out, utterances
    )
    losses, final, dlogits, dresidual = top(
        lengths, residual, gain_out[None], head_weight, kept, got
    )
    sums = [sum_pieces(*outer(own, active, dresidual, final, dlogits), orders, count)]
    dconvs = []
    for chunk in range(CHUNKS):
        send, keep, dconv = inner(
            own,
            lengths,
            dresidual,
            weight_out,
            slope,
            gated,
            gate,
            normed,
            weight_depth,
            chunk,
            utterances,
        )
        dconvs.append(dconv)
        sums.append(sum_pieces(send, keep, orders, count))
    small = jnp.concatenate(
        [
            tap_sums(lengths, gated, dconv, taps, chunk, utterances)
            for chunk, dconv in enumerate(dconvs)
        ],
        axis=1,
    )
    small = all_sum(small, count)
    grad_in, grad_out, grad_head, by_in, by_head = unpack(
        utts, own, small, weight_in, head_weight, sums, weight_out.shape[1]
    )
    scale = utts / small[taps, 0]
    return (
        by_in.reshape(model) / gain_conv,
        grad_in,
        small[:taps] * scale,
        grad_out,
        by_head.reshape(model) / gain_out,
        grad_head,
        losses[:, 0, 0] * scale,
    )


def solution(mesh):
    in_specs = (
        P(("dp", "member"), None, None),
        P("member", "dp", None, None),
        P(("dp", "member")),
        P(),
        P(),
        P(),
        P(),
        P(),
        P(),
    )
    out_specs = (P(), P(), P(), P(), P(), P(), P(("dp", "member")))
    return jax.shard_map(
        on_device, mesh=mesh, in_specs=in_specs, out_specs=out_specs, check_vma=False
    )
```

```python
import functools

import jax
import jax.numpy as jnp
from jax import lax
from jax.experimental import pallas as pl
from jax.experimental.pallas import tpu as pltpu
from jax.sharding import PartitionSpec as P

TEACHERS = 4
PLACES = 16
WIDE = 256
LANES = 128
TILE = 128
MARGIN = 16
CHUNKS = 2
VMEM = 56 << 20
SMEM_SPEC = pl.BlockSpec(memory_space=pltpu.SMEM)
F32 = jnp.float32
BF16 = jnp.bfloat16


def params():
    return pltpu.CompilerParams(vmem_limit_bytes=VMEM)


def dot(left, right, left_axis=1, right_axis=0):
    return lax.dot_general(
        left, right, (((left_axis,), (right_axis,)), ((), ())), preferred_element_type=F32
    )


def fixed(*shape):
    return pl.BlockSpec(shape, lambda i, *_: (0,) * len(shape))


NEAR = ("member", "near")
FAR = "far"
REST = "rest"
CORE = "core"


def other_core(values):
    return lax.ppermute(values, CORE, [(0, 1), (1, 0)])


def sum_core(send, keep):
    return (keep.astype(F32) + other_core(send).astype(F32)).astype(BF16)


def sum_over(values, axis):
    got = lax.all_to_all(values, axis, 0, 0)
    return jnp.sum(got.astype(F32), axis=0).astype(values.dtype)


def gather_over(values, axis):
    return lax.all_to_all(
        jnp.broadcast_to(values[None], (lax.axis_size(axis),) + values.shape), axis, 0, 0
    )


def sum_near(pieces):
    near = lax.axis_size(NEAR)
    return sum_over(pieces.reshape((near, pieces.shape[0] // near) + pieces.shape[1:]), NEAR)


def sum_far(pieces):
    own = sum_over(pieces, FAR)
    return lax.psum(own, REST) if lax.axis_size(REST) > 1 else own


def gather_near(pieces):
    got = gather_over(pieces, NEAR)
    return got.reshape((got.shape[0] * got.shape[1],) + got.shape[2:])


def all_sum(values):
    for axis in (NEAR, FAR):
        values = jnp.sum(gather_over(values, axis), axis=0)
    if lax.axis_size(REST) > 1:
        values = lax.psum(values, REST)
    return values + other_core(values)


def write_pieces(core, product, send_ref, keep_ref, columns):
    rows = keep_ref.shape[-2]

    def one(piece, carry):
        base = piece * (2 * rows)
        kept = pl.multiple_of(base + core * rows, rows)
        sent = pl.multiple_of(base + (1 - core) * rows, rows)
        keep_ref[piece, :, columns] = product[pl.ds(kept, rows), :].astype(BF16)
        send_ref[piece, :, columns] = product[pl.ds(sent, rows), :].astype(BF16)
        return carry

    lax.fori_loop(0, keep_ref.shape[0], one, 0)


def teacher_kernel(member_ref, logits_ref, give_ref, keep_ref, *, own_count):
    step = pl.program_id(0)
    total = None
    for teacher in range(logits_ref.shape[0]):
        logits = logits_ref[teacher, 0].astype(F32)
        shifted = logits - jnp.max(logits, axis=-1, keepdims=True)
        logp = shifted - jnp.log(jnp.sum(jnp.exp(shifted), axis=-1, keepdims=True))
        total = logp if total is None else total + logp

    @pl.when(step < own_count)
    def _():
        give_ref[0] = total

    @pl.when(step >= own_count)
    def _():
        keep_ref[0] = total


def teacher_sums(member, logits, own_count):
    teachers, utterances, frames, symbols = logits.shape
    shape = jax.ShapeDtypeStruct((own_count, frames, symbols), F32)

    def source(i, member_ref):
        mine = member_ref[0] * own_count
        theirs = (1 - member_ref[0]) * own_count
        return (0, jnp.where(i < own_count, theirs + i, mine + i - own_count), 0, 0)

    return pl.pallas_call(
        functools.partial(teacher_kernel, own_count=own_count),
        out_shape=(shape, shape),
        grid_spec=pltpu.PrefetchScalarGridSpec(
            num_scalar_prefetch=1,
            grid=(2 * own_count,),
            in_specs=[pl.BlockSpec((teachers, 1, frames, symbols), source)],
            out_specs=(
                pl.BlockSpec(
                    (1, frames, symbols), lambda i, _: (jnp.minimum(i, own_count - 1), 0, 0)
                ),
                pl.BlockSpec(
                    (1, frames, symbols), lambda i, _: (jnp.maximum(i - own_count, 0), 0, 0)
                ),
            ),
        ),
        compiler_params=params(),
        name="teachers",
    )(member, logits)


def live_column(lengths_ref, utterance, frames):
    position = lax.broadcasted_iota(jnp.int32, (frames, 1), 0)
    return (position < lengths_ref[utterance]).astype(F32)


def clear_margins(pad_ref):
    frames = pad_ref.shape[2] - 2 * MARGIN
    zeros = jnp.zeros(pad_ref.shape[:2] + (MARGIN, LANES), F32)
    pad_ref[:, :, :MARGIN, :] = zeros
    pad_ref[:, :, MARGIN + frames :, :] = zeros


def shifted_views(pad_ref, lane, utterance, start, taps):
    first = MARGIN - taps // 2
    for phase in range(8):
        offsets = [offset for offset in range(first, first + taps) if offset % 8 == phase]
        if not offsets:
            continue
        low = offsets[0]
        span = offsets[-1] - low + TILE
        view = pad_ref[lane, utterance, start + low : start + low + span, :]
        for offset in offsets:
            yield offset - first, view[offset - low : offset - low + TILE]


def convolve(pad_ref, lane, utterance, start, depth_ref, flipped):
    taps = depth_ref.shape[0]
    columns = slice(lane * LANES, (lane + 1) * LANES)
    total = jnp.zeros((TILE, LANES), F32)
    for tap, view in shifted_views(pad_ref, lane, utterance, start, taps):
        row = taps - 1 - tap if flipped else tap
        total = total + view * depth_ref[row : row + 1, columns]
    return total


def forward_kernel(
    lengths_ref,
    features_ref,
    gain_ref,
    value_weight_ref,
    gate_weight_ref,
    depth_ref,
    out_weight_ref,
    normed_ref,
    gated_ref,
    gate_ref,
    slope_ref,
    active_ref,
    residual_ref,
    pad_ref,
):
    utterances = pad_ref.shape[1]
    frames = pad_ref.shape[2] - 2 * MARGIN

    @pl.when(pl.program_id(0) == 0)
    def _():
        values = features_ref[...].astype(F32)
        centred = values - jnp.mean(values, axis=-1, keepdims=True)
        spread = jnp.mean(centred * centred, axis=-1, keepdims=True)
        normed_ref[...] = (centred * lax.rsqrt(spread + 1e-05) * gain_ref[...]).astype(BF16)
        residual_ref[...] = values
        clear_margins(pad_ref)

    for utterance in range(utterances):
        rows = slice(utterance * frames, (utterance + 1) * frames)
        normed = normed_ref[rows, :]
        gate = jax.nn.sigmoid(dot(normed, gate_weight_ref[...]))
        gated = dot(normed, value_weight_ref[...]) * gate
        gated = gated * live_column(lengths_ref, utterance, frames)
        gate_ref[rows, :] = gate
        gated_ref[rows, :] = gated
        for lane in range(WIDE // LANES):
            pad_ref[lane, utterance, MARGIN : MARGIN + frames, :] = gated[
                :, lane * LANES : (lane + 1) * LANES
            ]

    for lane in range(WIDE // LANES):
        columns = slice(lane * LANES, (lane + 1) * LANES)

        def one(utterance, carry, lane=lane, columns=columns):
            for start in range(0, frames, TILE):
                rows = pl.ds(pl.multiple_of(utterance * frames + start, TILE), TILE)
                convolved = convolve(pad_ref, lane, utterance, start, depth_ref, False)
                squash = jax.nn.sigmoid(convolved)
                active_ref[rows, columns] = (convolved * squash).astype(BF16)
                slope_ref[rows, columns] = squash * (1.0 + convolved * (1.0 - squash))
            return carry

        lax.fori_loop(0, utterances, one, 0)

    residual_ref[...] += dot(active_ref[...], out_weight_ref[...])


def forward(lengths, features, gain, weight_in, depth, weight_out, utterances):
    rows, model = features.shape
    frames = rows // utterances
    steps = model // WIDE
    column = pl.BlockSpec((rows, WIDE), lambda i: (0, i))
    wide = jax.ShapeDtypeStruct((rows, model), F32)
    narrow = jax.ShapeDtypeStruct((rows, model), BF16)
    return pl.pallas_call(
        forward_kernel,
        grid=(steps,),
        out_shape=(narrow, wide, wide, wide, narrow, wide),
        in_specs=[
            SMEM_SPEC,
            fixed(rows, model),
            fixed(1, model),
            pl.BlockSpec((model, WIDE), lambda i: (0, i)),
            pl.BlockSpec((model, WIDE), lambda i: (0, steps + i)),
            pl.BlockSpec((depth.shape[0], WIDE), lambda i: (0, i)),
            pl.BlockSpec((WIDE, model), lambda i: (i, 0)),
        ],
        out_specs=(fixed(rows, model), column, column, column, column, fixed(rows, model)),
        scratch_shapes=[pltpu.VMEM((WIDE // LANES, utterances, frames + 2 * MARGIN, LANES), F32)],
        compiler_params=params(),
        name="forward",
    )(lengths, features, gain, weight_in, weight_in, depth, weight_out)


def top_kernel(
    lengths_ref,
    residual_ref,
    gain_ref,
    head_ref,
    kept_ref,
    got_ref,
    loss_ref,
    final_ref,
    dlogits_ref,
    dresidual_ref,
):
    frames = residual_ref.shape[0]
    live = live_column(lengths_ref, pl.program_id(0), frames)
    values = residual_ref[...]
    centred = values - jnp.mean(values, axis=-1, keepdims=True)
    spread = jnp.mean(centred * centred, axis=-1, keepdims=True)
    inverse = lax.rsqrt(spread + 1e-05)
    unit = centred * inverse
    final = (unit * gain_ref[...]).astype(BF16)
    final_ref[...] = final

    def log_softmax(logits):
        shifted = logits - jnp.max(logits, axis=-1, keepdims=True)
        return shifted - jnp.log(jnp.sum(jnp.exp(shifted), axis=-1, keepdims=True))

    target = jnp.exp(log_softmax((kept_ref[0] + got_ref[0]) * (1.0 / TEACHERS)))
    logp = log_softmax(dot(final, head_ref[...]))
    cross = -jnp.sum(target * logp, axis=-1, keepdims=True)
    loss_ref[...] = jnp.broadcast_to(jnp.sum(cross * live, axis=0, keepdims=True), (1, 1, LANES))
    weight = jnp.sum(target, axis=-1, keepdims=True)
    dlogits = ((jnp.exp(logp) * weight - target) * live).astype(BF16)
    dlogits_ref[...] = dlogits
    dunit = dot(dlogits, head_ref[...], 1, 1) * gain_ref[...]
    average = jnp.mean(dunit, axis=-1, keepdims=True)
    along = jnp.mean(dunit * unit, axis=-1, keepdims=True)
    dresidual_ref[...] = (inverse * (dunit - average - unit * along)).astype(BF16)


def top(lengths, residual, gain, head, kept, got):
    rows, model = residual.shape
    utterances, frames, symbols = kept.shape
    per_row = pl.BlockSpec((frames, model), lambda i: (i, 0))
    sums = pl.BlockSpec((1, frames, symbols), lambda i: (i, 0, 0))
    return pl.pallas_call(
        top_kernel,
        grid=(utterances,),
        out_shape=(
            jax.ShapeDtypeStruct((utterances, 1, LANES), F32),
            jax.ShapeDtypeStruct((rows, model), BF16),
            jax.ShapeDtypeStruct((rows, symbols), BF16),
            jax.ShapeDtypeStruct((rows, model), BF16),
        ),
        in_specs=[SMEM_SPEC, per_row, fixed(1, model), fixed(model, symbols), sums, sums],
        out_specs=(
            pl.BlockSpec((1, 1, LANES), lambda i: (i, 0, 0)),
            per_row,
            pl.BlockSpec((frames, symbols), lambda i: (i, 0)),
            per_row,
        ),
        compiler_params=params(),
        name="top",
    )(lengths, residual, gain, head, kept, got)


def outer_kernel(
    core_ref, active_ref, dresidual_ref, final_ref, dlogits_ref, send_ref, keep_ref, product_ref
):
    width = dresidual_ref.shape[1]
    product_ref[:, :width] = dot(active_ref[...], dresidual_ref[...], 0, 0)
    product_ref[:, width:] = dot(final_ref[...], dlogits_ref[...], 0, 0)
    write_pieces(core_ref[0], product_ref, send_ref, keep_ref, slice(None))


def outer(core, active, dresidual, final, dlogits):
    rows, model = active.shape
    half_out = dresidual.shape[1] // 2
    half_head = dlogits.shape[1] // 2
    width = half_out + half_head
    piece = (PLACES, model // (2 * PLACES))
    shape = jax.ShapeDtypeStruct(piece + (2 * width,), BF16)
    out = pl.BlockSpec(piece + (width,), lambda i: (0, 0, i))
    return pl.pallas_call(
        outer_kernel,
        grid=(2,),
        out_shape=(shape, shape),
        in_specs=[
            SMEM_SPEC,
            fixed(rows, model),
            pl.BlockSpec((rows, half_out), lambda i: (0, i)),
            fixed(rows, model),
            pl.BlockSpec((rows, half_head), lambda i: (0, i)),
        ],
        out_specs=(out, out),
        scratch_shapes=[pltpu.VMEM((model, width), F32)],
        compiler_params=params(),
        name="outer",
    )(core, active, dresidual, final, dlogits)


def inner_kernel(
    core_ref,
    lengths_ref,
    dresidual_ref,
    out_weight_ref,
    slope_ref,
    gated_ref,
    gate_ref,
    normed_ref,
    depth_ref,
    send_ref,
    keep_ref,
    dconv_ref,
    pad_ref,
    dvalue_ref,
    dgate_ref,
    product_ref,
):
    utterances = pad_ref.shape[1]
    frames = pad_ref.shape[2] - 2 * MARGIN

    @pl.when(pl.program_id(0) == 0)
    def _():
        clear_margins(pad_ref)

    for utterance in range(utterances):
        rows = slice(utterance * frames, (utterance + 1) * frames)
        dconv = dot(dresidual_ref[rows, :], out_weight_ref[...], 1, 1) * slope_ref[rows, :]
        dconv_ref[rows, :] = dconv
        for lane in range(WIDE // LANES):
            pad_ref[lane, utterance, MARGIN : MARGIN + frames, :] = dconv[
                :, lane * LANES : (lane + 1) * LANES
            ]

    for lane in range(WIDE // LANES):
        columns = slice(lane * LANES, (lane + 1) * LANES)

        def one(utterance, carry, lane=lane, columns=columns):
            for start in range(0, frames, TILE):
                rows = pl.ds(pl.multiple_of(utterance * frames + start, TILE), TILE)
                position = lax.broadcasted_iota(jnp.int32, (TILE, 1), 0) + start
                live = (position < lengths_ref[utterance]).astype(F32)
                dgated = convolve(pad_ref, lane, utterance, start, depth_ref, True) * live
                gate = gate_ref[rows, columns]
                dvalue_ref[rows, columns] = (dgated * gate).astype(BF16)
                dgate_ref[rows, columns] = (dgated * gated_ref[rows, columns] * (1.0 - gate)).astype(
                    BF16
                )
            return carry

        lax.fori_loop(0, utterances, one, 0)

    for group, source in ((0, dvalue_ref), (1, dgate_ref)):
        product_ref[...] = dot(normed_ref[...], source[...], 0, 0)
        columns = slice(group * WIDE, (group + 1) * WIDE)
        write_pieces(core_ref[0], product_ref, send_ref, keep_ref, columns)


def inner(core, lengths, dresidual, weight_out, slope, gated, gate, normed, depth, chunk, utterances):
    rows, model = normed.shape
    frames = rows // utterances
    steps = model // WIDE // CHUNKS
    first = chunk * steps
    column = pl.BlockSpec((rows, WIDE), lambda i: (0, first + i))
    piece = (PLACES, model // (2 * PLACES))
    shape = jax.ShapeDtypeStruct(piece + (steps * 2 * WIDE,), BF16)
    out = pl.BlockSpec(piece + (2 * WIDE,), lambda i: (0, 0, i))
    return pl.pallas_call(
        inner_kernel,
        grid=(steps,),
        out_shape=(shape, shape, jax.ShapeDtypeStruct((rows, steps * WIDE), F32)),
        in_specs=[
            SMEM_SPEC,
            SMEM_SPEC,
            fixed(rows, model),
            pl.BlockSpec((WIDE, model), lambda i: (first + i, 0)),
            column,
            column,
            column,
            fixed(rows, model),
            pl.BlockSpec((depth.shape[0], WIDE), lambda i: (0, first + i)),
        ],
        out_specs=(out, out, pl.BlockSpec((rows, WIDE), lambda i: (0, i))),
        scratch_shapes=[
            pltpu.VMEM((WIDE // LANES, utterances, frames + 2 * MARGIN, LANES), F32),
            pltpu.VMEM((rows, WIDE), BF16),
            pltpu.VMEM((rows, WIDE), BF16),
            pltpu.VMEM((model, WIDE), F32),
        ],
        compiler_params=params(),
        name="inner",
    )(core, lengths, dresidual, weight_out, slope, gated, gate, normed, depth)


def taps_kernel(lengths_ref, gated_ref, dconv_ref, out_ref, pad_ref, sums_ref):
    utterances = pad_ref.shape[1]
    frames = pad_ref.shape[2] - 2 * MARGIN
    taps = out_ref.shape[0] - 1
    valid = lengths_ref[0]
    for utterance in range(1, utterances):
        valid = valid + lengths_ref[utterance]

    @pl.when(pl.program_id(0) == 0)
    def _():
        clear_margins(pad_ref)

    for lane in range(WIDE // LANES):
        columns = slice(lane * LANES, (lane + 1) * LANES)
        for utterance in range(utterances):
            rows = slice(utterance * frames, (utterance + 1) * frames)
            pad_ref[lane, utterance, MARGIN : MARGIN + frames, :] = gated_ref[rows, columns]
        sums_ref[...] = jnp.zeros_like(sums_ref)

        def one(utterance, carry, lane=lane, columns=columns):
            for start in range(0, frames, TILE):
                rows = pl.ds(pl.multiple_of(utterance * frames + start, TILE), TILE)
                dconv = dconv_ref[rows, columns]
                for tap, view in shifted_views(pad_ref, lane, utterance, start, taps):
                    sums_ref[tap] += jnp.sum((view * dconv).reshape(TILE // 8, 8, LANES), axis=0)
            return carry

        lax.fori_loop(0, utterances, one, 0)
        out_ref[:taps, columns] = jnp.sum(sums_ref[...], axis=1)
    out_ref[taps:, :] = jnp.zeros((1, WIDE), F32) + valid.astype(F32)


def tap_sums(lengths, gated, dconv, taps, chunk, utterances):
    rows, width = dconv.shape
    steps = width // WIDE
    first = chunk * steps
    return pl.pallas_call(
        taps_kernel,
        grid=(steps,),
        out_shape=jax.ShapeDtypeStruct((taps + 1, width), F32),
        in_specs=[
            SMEM_SPEC,
            pl.BlockSpec((rows, WIDE), lambda i: (0, first + i)),
            pl.BlockSpec((rows, WIDE), lambda i: (0, i)),
        ],
        out_specs=pl.BlockSpec((taps + 1, WIDE), lambda i: (0, i)),
        scratch_shapes=[
            pltpu.VMEM((WIDE // LANES, utterances, rows // utterances + 2 * MARGIN, LANES), F32),
            pltpu.VMEM((taps, 8, LANES), F32),
        ],
        compiler_params=params(),
        name="taps",
    )(lengths, gated, dconv)


def gain_row(weight, grad, gain):
    along = jnp.sum(weight.astype(F32) * grad, axis=1, keepdims=True)
    return jnp.broadcast_to(along, (along.shape[0], LANES)).T[0:1, :] / gain


def write_rows(core, pieces, other, scale, targets):
    rows = pieces.shape[1]
    for index in range(pieces.shape[0]):
        for side, source in ((core, pieces), (1 - core, other)):
            here = pl.ds(pl.multiple_of(index * 2 * rows + side * rows, rows), rows)
            for target, there, first, width in targets:
                target[here, there : there + width] = (
                    source[index, :, first : first + width].astype(F32) * scale
                )


def unpack_top_kernel(
    utts,
    core_ref,
    small_ref,
    own_ref,
    other_ref,
    head_ref,
    gain_ref,
    losses_ref,
    wout_ref,
    dhead_ref,
    dgain_ref,
    depth_ref,
    loss_ref,
):
    taps = depth_ref.shape[0]
    scale = utts / small_ref[taps:, 0:1]
    half_out = wout_ref.shape[1] // 2
    half_head = dhead_ref.shape[1] // 2
    targets = []
    for half in range(2):
        first = half * (half_out + half_head)
        targets.append((wout_ref, half * half_out, first, half_out))
        targets.append((dhead_ref, half * half_head, first + half_out, half_head))
    write_rows(core_ref[0], own_ref, other_ref, scale, targets)
    dgain_ref[...] = gain_row(head_ref[...], dhead_ref[...], gain_ref[...])
    depth_ref[...] = small_ref[:taps, :] * scale
    loss_ref[...] = losses_ref[...] * scale[None]


def unpack_inner_kernel(utts, core_ref, small_ref, weight_ref, gain_ref, *refs):
    pieces, (win_ref, dgain_ref) = refs[:-2], refs[-2:]
    scale = utts / small_ref[small_ref.shape[0] - 1 :, 0:1]
    half_in = win_ref.shape[1] // 2
    column = 0
    for chunk in range(len(pieces) // 2):
        own_ref, other_ref = pieces[2 * chunk : 2 * chunk + 2]
        targets = []
        for first in range(0, own_ref.shape[2], 2 * WIDE):
            targets.append((win_ref, column, first, WIDE))
            targets.append((win_ref, half_in + column, first + WIDE, WIDE))
            column += WIDE
        write_rows(core_ref[0], own_ref, other_ref, scale, targets)
    dgain_ref[...] = gain_row(weight_ref[...], win_ref[...], gain_ref[...])


def piece_spec(array, steps):
    return pl.BlockSpec((array.shape[0] // steps,) + array.shape[1:], lambda i: (i, 0, 0))


def unpack_top(utts, core, small, own, other, head, gain, losses, width_out):
    steps = 4
    model, symbols = head.shape
    rows = model // steps
    taps = small.shape[0] - 1
    row = pl.BlockSpec((1, rows), lambda i: (0, i))

    def block(width):
        return pl.BlockSpec((rows, width), lambda i: (i, 0))

    return pl.pallas_call(
        functools.partial(unpack_top_kernel, utts),
        grid=(steps,),
        out_shape=(
            jax.ShapeDtypeStruct((model, width_out), F32),
            jax.ShapeDtypeStruct((model, symbols), F32),
            jax.ShapeDtypeStruct((1, model), F32),
            jax.ShapeDtypeStruct((taps, model), F32),
            jax.ShapeDtypeStruct(losses.shape, F32),
        ),
        in_specs=[
            SMEM_SPEC,
            fixed(*small.shape),
            piece_spec(own, steps),
            piece_spec(other, steps),
            block(symbols),
            row,
            fixed(*losses.shape),
        ],
        out_specs=(
            block(width_out),
            block(symbols),
            row,
            fixed(taps, model),
            fixed(*losses.shape),
        ),
        compiler_params=params(),
        name="unpack_top",
    )(core, small, own, other, head, gain, losses)


def unpack_inner(utts, core, small, sums, weight, gain):
    steps = 8
    model, width = weight.shape
    rows = model // steps
    row = pl.BlockSpec((1, rows), lambda i: (0, i))
    block = pl.BlockSpec((rows, width), lambda i: (i, 0))
    pieces = [array for pair in sums for array in pair]
    return pl.pallas_call(
        functools.partial(unpack_inner_kernel, utts),
        grid=(steps,),
        out_shape=(
            jax.ShapeDtypeStruct((model, width), F32),
            jax.ShapeDtypeStruct((1, model), F32),
        ),
        in_specs=[SMEM_SPEC, fixed(*small.shape), block, row]
        + [piece_spec(array, steps) for array in pieces],
        out_specs=(block, row),
        compiler_params=params(),
        name="unpack_inner",
    )(core, small, weight, gain, *pieces)


def on_device(
    features,
    teacher_logits,
    lengths,
    gain_conv,
    weight_in,
    weight_depth,
    weight_out,
    gain_out,
    head_weight,
):
    count = lax.axis_size(NEAR) * lax.axis_size(FAR) * lax.axis_size(REST) * lax.axis_size(CORE)
    member = lax.axis_index("member").astype(jnp.int32)[None]
    core = lax.axis_index(CORE).astype(jnp.int32)[None]
    taps, model = weight_depth.shape
    utterances, frames, _ = features.shape
    utts = float(utterances * count)
    tie = lax.optimization_barrier

    give, kept = teacher_sums(member, teacher_logits, utterances)
    got = lax.ppermute(give, "member", [(0, 1), (1, 0)])
    flat = features.reshape(utterances * frames, model)
    normed, gated, gate, slope, active, residual = forward(
        lengths, flat, gain_conv[None], weight_in, weight_depth, weight_out, utterances
    )
    losses, final, dlogits, dresidual = top(
        lengths, residual, gain_out[None], head_weight, kept, got
    )

    def weight_in_chunk(chunk, dresidual):
        return inner(
            core,
            lengths,
            dresidual,
            weight_out,
            slope,
            gated,
            gate,
            normed,
            weight_depth,
            chunk,
            utterances,
        )

    send, keep = outer(core, active, dresidual, final, dlogits)
    send, keep, dresidual = tie((send, keep, dresidual))
    top_sum = sum_core(send, keep)
    inner_sums = []
    dconvs = []
    for chunk in range(CHUNKS):
        send, keep, dconv = weight_in_chunk(chunk, dresidual)
        inner_sums.append(sum_core(send, keep))
        dconvs.append(dconv)
        if chunk == 0:
            top_sum, dresidual = tie((top_sum, dresidual))
    dconvs[0], inner_sums[0] = tie((dconvs[0], inner_sums[0]))
    small = jnp.concatenate(
        [
            tap_sums(lengths, gated, dconv, taps, chunk, utterances)
            for chunk, dconv in enumerate(dconvs)
        ],
        axis=1,
    )
    top_all = gather_near(gather_over(sum_far(sum_near(top_sum)), FAR))
    top_other = other_core(top_all)
    small = all_sum(small)
    pairs = []
    for values in inner_sums:
        every = gather_near(gather_over(sum_far(sum_near(values)), FAR))
        pairs.append((every, other_core(every)))
    grad_out, grad_head, by_head, grad_depth, losses = unpack_top(
        utts,
        core,
        small,
        top_all,
        top_other,
        head_weight,
        gain_out[None],
        losses,
        weight_out.shape[1],
    )
    grad_in, by_in = unpack_inner(utts, core, small, pairs, weight_in, gain_conv[None])
    return (
        by_in.reshape(model),
        grad_in,
        grad_depth,
        grad_out,
        by_head.reshape(model),
        grad_head,
        losses[:, 0, 0],
    )


def solution(mesh):
    members, others = mesh.devices.shape
    near, cores = 2, 2
    far = PLACES // (members * near)
    rest = others // (far * near * cores)
    split = jax.sharding.Mesh(
        mesh.devices.reshape(members, rest, far, near, cores),
        ("member", REST, FAR, "near", CORE),
    )
    dp = (REST, FAR, "near", CORE)
    in_specs = (
        P(dp + ("member",), None, None),
        P("member", dp, None, None),
        P(dp + ("member",)),
        P(),
        P(),
        P(),
        P(),
        P(),
        P(),
    )
    out_specs = (P(), P(), P(), P(), P(), P(), P(dp + ("member",)))
    return jax.shard_map(
        on_device, mesh=split, in_specs=in_specs, out_specs=out_specs, check_vma=False
    )
```

```python
import functools

import jax
import jax.numpy as jnp
from jax import lax
from jax.experimental import pallas as pl
from jax.experimental.pallas import tpu as pltpu
from jax.sharding import PartitionSpec as P

TEACHERS = 4
PLACES = 16
WIDE = 256
LANES = 128
TILE = 128
MARGIN = 16
CHUNKS = 2
VMEM = 56 << 20
SMEM_SPEC = pl.BlockSpec(memory_space=pltpu.SMEM)
F32 = jnp.float32
BF16 = jnp.bfloat16


def params():
    return pltpu.CompilerParams(vmem_limit_bytes=VMEM)


def cost(microseconds):
    return pl.CostEstimate(flops=int(microseconds * 1.15e9), bytes_accessed=1 << 20, transcendentals=0)


def dot(left, right, left_axis=1, right_axis=0):
    return lax.dot_general(
        left, right, (((left_axis,), (right_axis,)), ((), ())), preferred_element_type=F32
    )


def fixed(*shape):
    return pl.BlockSpec(shape, lambda i, *_: (0,) * len(shape))


XY = ("member", "near")
YX = ("near", "member")
FAR = "far"
REST = "rest"
CORE = "core"


def other_core(values):
    return lax.ppermute(values, CORE, [(0, 1), (1, 0)])


def sum_core(send, keep):
    return (keep.astype(F32) + other_core(send).astype(F32)).astype(BF16)


def halve(pieces, dim, axis, bit):
    size = lax.axis_size(axis)
    got = lax.ppermute(
        lax.index_in_dim(pieces, 1, dim, keepdims=False), axis, [(i, i ^ bit) for i in range(size)]
    )
    kept = lax.index_in_dim(pieces, 0, dim, keepdims=False)
    return (kept.astype(F32) + got.astype(F32)).astype(pieces.dtype)


def sum_chips(pieces, order):
    pieces = pieces.reshape((2, 2, 2, 2) + pieces.shape[1:])
    pieces = halve(pieces, 0, order[0], 1)
    pieces = halve(pieces, 0, order[1], 1)
    pieces = halve(pieces, 1, FAR, 1)
    pieces = halve(pieces, 0, FAR, 2)
    return over_rest(pieces)


def over_rest(values):
    return lax.psum(values, REST) if lax.axis_size(REST) > 1 else values


def gather(shard, order):
    return lax.all_gather(shard, order + (FAR,), axis=0, tiled=False)


def own_place(order):
    place = lax.axis_index(order[0]) * 8 + lax.axis_index(order[1]) * 4 + lax.axis_index(FAR)
    return place.astype(jnp.int32)


def all_sum(values):
    for axis, bit in (("member", 1), ("near", 1), (FAR, 1), (FAR, 2)):
        size = lax.axis_size(axis)
        values = values + lax.ppermute(values, axis, [(i, i ^ bit) for i in range(size)])
    values = over_rest(values)
    return values + other_core(values)


def write_pieces(own_ref, product, send_ref, keep_ref, columns):
    rows = keep_ref.shape[-2]
    core, place = own_ref[0], own_ref[1]

    def one(piece, carry):
        base = (piece ^ place) * (2 * rows)
        kept = pl.multiple_of(base + core * rows, rows)
        sent = pl.multiple_of(base + (1 - core) * rows, rows)
        keep_ref[piece, :, columns] = product[pl.ds(kept, rows), :].astype(BF16)
        send_ref[piece, :, columns] = product[pl.ds(sent, rows), :].astype(BF16)
        return carry

    lax.fori_loop(0, keep_ref.shape[0], one, 0)


def teacher_kernel(member_ref, logits_ref, give_ref, keep_ref, *, own_count):
    step = pl.program_id(0)
    total = None
    for teacher in range(logits_ref.shape[0]):
        logits = logits_ref[teacher, 0].astype(F32)
        shifted = logits - jnp.max(logits, axis=-1, keepdims=True)
        logp = shifted - jnp.log(jnp.sum(jnp.exp(shifted), axis=-1, keepdims=True))
        total = logp if total is None else total + logp

    @pl.when(step < own_count)
    def _():
        give_ref[0] = total

    @pl.when(step >= own_count)
    def _():
        keep_ref[0] = total


def teacher_sums(member, logits, own_count):
    teachers, utterances, frames, symbols = logits.shape
    shape = jax.ShapeDtypeStruct((own_count, frames, symbols), F32)

    def source(i, member_ref):
        mine = member_ref[0] * own_count
        theirs = (1 - member_ref[0]) * own_count
        return (0, jnp.where(i < own_count, theirs + i, mine + i - own_count), 0, 0)

    return pl.pallas_call(
        functools.partial(teacher_kernel, own_count=own_count),
        out_shape=(shape, shape),
        grid_spec=pltpu.PrefetchScalarGridSpec(
            num_scalar_prefetch=1,
            grid=(2 * own_count,),
            in_specs=[pl.BlockSpec((teachers, 1, frames, symbols), source)],
            out_specs=(
                pl.BlockSpec(
                    (1, frames, symbols), lambda i, _: (jnp.minimum(i, own_count - 1), 0, 0)
                ),
                pl.BlockSpec(
                    (1, frames, symbols), lambda i, _: (jnp.maximum(i - own_count, 0), 0, 0)
                ),
            ),
        ),
        compiler_params=params(),
        cost_estimate=cost(4),
        name="teachers",
    )(member, logits)


def live_column(lengths_ref, utterance, frames):
    position = lax.broadcasted_iota(jnp.int32, (frames, 1), 0)
    return (position < lengths_ref[utterance]).astype(F32)


def clear_margins(pad_ref):
    frames = pad_ref.shape[2] - 2 * MARGIN
    zeros = jnp.zeros(pad_ref.shape[:2] + (MARGIN, LANES), F32)
    pad_ref[:, :, :MARGIN, :] = zeros
    pad_ref[:, :, MARGIN + frames :, :] = zeros


def shifted_views(pad_ref, lane, utterance, start, taps):
    first = MARGIN - taps // 2
    for phase in range(8):
        offsets = [offset for offset in range(first, first + taps) if offset % 8 == phase]
        if not offsets:
            continue
        low = offsets[0]
        span = offsets[-1] - low + TILE
        view = pad_ref[lane, utterance, start + low : start + low + span, :]
        for offset in offsets:
            yield offset - first, view[offset - low : offset - low + TILE]


def convolve(pad_ref, lane, utterance, start, depth_ref, flipped):
    taps = depth_ref.shape[0]
    columns = slice(lane * LANES, (lane + 1) * LANES)
    total = jnp.zeros((TILE, LANES), F32)
    for tap, view in shifted_views(pad_ref, lane, utterance, start, taps):
        row = taps - 1 - tap if flipped else tap
        total = total + view * depth_ref[row : row + 1, columns]
    return total


def forward_kernel(
    lengths_ref,
    features_ref,
    gain_ref,
    value_weight_ref,
    gate_weight_ref,
    depth_ref,
    out_weight_ref,
    normed_ref,
    gated_ref,
    gate_ref,
    slope_ref,
    active_ref,
    residual_ref,
    pad_ref,
):
    utterances = pad_ref.shape[1]
    frames = pad_ref.shape[2] - 2 * MARGIN

    @pl.when(pl.program_id(0) == 0)
    def _():
        values = features_ref[...].astype(F32)
        centred = values - jnp.mean(values, axis=-1, keepdims=True)
        spread = jnp.mean(centred * centred, axis=-1, keepdims=True)
        normed_ref[...] = (centred * lax.rsqrt(spread + 1e-05) * gain_ref[...]).astype(BF16)
        residual_ref[...] = values
        clear_margins(pad_ref)

    for utterance in range(utterances):
        rows = slice(utterance * frames, (utterance + 1) * frames)
        normed = normed_ref[rows, :]
        gate = jax.nn.sigmoid(dot(normed, gate_weight_ref[...]))
        gated = dot(normed, value_weight_ref[...]) * gate
        gated = gated * live_column(lengths_ref, utterance, frames)
        gate_ref[rows, :] = gate
        gated_ref[rows, :] = gated
        for lane in range(WIDE // LANES):
            pad_ref[lane, utterance, MARGIN : MARGIN + frames, :] = gated[
                :, lane * LANES : (lane + 1) * LANES
            ]

    for lane in range(WIDE // LANES):
        columns = slice(lane * LANES, (lane + 1) * LANES)

        def one(utterance, carry, lane=lane, columns=columns):
            for start in range(0, frames, TILE):
                rows = pl.ds(pl.multiple_of(utterance * frames + start, TILE), TILE)
                convolved = convolve(pad_ref, lane, utterance, start, depth_ref, False)
                squash = jax.nn.sigmoid(convolved)
                active_ref[rows, columns] = (convolved * squash).astype(BF16)
                slope_ref[rows, columns] = squash * (1.0 + convolved * (1.0 - squash))
            return carry

        lax.fori_loop(0, utterances, one, 0)

    residual_ref[...] += dot(active_ref[...], out_weight_ref[...])


def forward(lengths, features, gain, weight_in, depth, weight_out, utterances):
    rows, model = features.shape
    frames = rows // utterances
    steps = model // WIDE
    column = pl.BlockSpec((rows, WIDE), lambda i: (0, i))
    wide = jax.ShapeDtypeStruct((rows, model), F32)
    narrow = jax.ShapeDtypeStruct((rows, model), BF16)
    return pl.pallas_call(
        forward_kernel,
        grid=(steps,),
        out_shape=(narrow, wide, wide, wide, narrow, wide),
        in_specs=[
            SMEM_SPEC,
            fixed(rows, model),
            fixed(1, model),
            pl.BlockSpec((model, WIDE), lambda i: (0, i)),
            pl.BlockSpec((model, WIDE), lambda i: (0, steps + i)),
            pl.BlockSpec((depth.shape[0], WIDE), lambda i: (0, i)),
            pl.BlockSpec((WIDE, model), lambda i: (i, 0)),
        ],
        out_specs=(fixed(rows, model), column, column, column, column, fixed(rows, model)),
        scratch_shapes=[pltpu.VMEM((WIDE // LANES, utterances, frames + 2 * MARGIN, LANES), F32)],
        compiler_params=params(),
        cost_estimate=cost(15),
        name="forward",
    )(lengths, features, gain, weight_in, weight_in, depth, weight_out)


def top_kernel(
    lengths_ref,
    residual_ref,
    gain_ref,
    head_ref,
    kept_ref,
    got_ref,
    loss_ref,
    final_ref,
    dlogits_ref,
    dresidual_ref,
):
    frames = residual_ref.shape[0]
    live = live_column(lengths_ref, pl.program_id(0), frames)
    values = residual_ref[...]
    centred = values - jnp.mean(values, axis=-1, keepdims=True)
    spread = jnp.mean(centred * centred, axis=-1, keepdims=True)
    inverse = lax.rsqrt(spread + 1e-05)
    unit = centred * inverse
    final = (unit * gain_ref[...]).astype(BF16)
    final_ref[...] = final

    def log_softmax(logits):
        shifted = logits - jnp.max(logits, axis=-1, keepdims=True)
        return shifted - jnp.log(jnp.sum(jnp.exp(shifted), axis=-1, keepdims=True))

    target = jnp.exp(log_softmax((kept_ref[0] + got_ref[0]) * (1.0 / TEACHERS)))
    logp = log_softmax(dot(final, head_ref[...]))
    cross = -jnp.sum(target * logp, axis=-1, keepdims=True)
    loss_ref[...] = jnp.broadcast_to(jnp.sum(cross * live, axis=0, keepdims=True), (1, 1, LANES))
    weight = jnp.sum(target, axis=-1, keepdims=True)
    dlogits = ((jnp.exp(logp) * weight - target) * live).astype(BF16)
    dlogits_ref[...] = dlogits
    dunit = dot(dlogits, head_ref[...], 1, 1) * gain_ref[...]
    average = jnp.mean(dunit, axis=-1, keepdims=True)
    along = jnp.mean(dunit * unit, axis=-1, keepdims=True)
    dresidual_ref[...] = (inverse * (dunit - average - unit * along)).astype(BF16)


def top(lengths, residual, gain, head, kept, got):
    rows, model = residual.shape
    utterances, frames, symbols = kept.shape
    per_row = pl.BlockSpec((frames, model), lambda i: (i, 0))
    sums = pl.BlockSpec((1, frames, symbols), lambda i: (i, 0, 0))
    return pl.pallas_call(
        top_kernel,
        grid=(utterances,),
        out_shape=(
            jax.ShapeDtypeStruct((utterances, 1, LANES), F32),
            jax.ShapeDtypeStruct((rows, model), BF16),
            jax.ShapeDtypeStruct((rows, symbols), BF16),
            jax.ShapeDtypeStruct((rows, model), BF16),
        ),
        in_specs=[SMEM_SPEC, per_row, fixed(1, model), fixed(model, symbols), sums, sums],
        out_specs=(
            pl.BlockSpec((1, 1, LANES), lambda i: (i, 0, 0)),
            per_row,
            pl.BlockSpec((frames, symbols), lambda i: (i, 0)),
            per_row,
        ),
        compiler_params=params(),
        cost_estimate=cost(5),
        name="top",
    )(lengths, residual, gain, head, kept, got)


def outer_kernel(
    own_ref, active_ref, dresidual_ref, final_ref, dlogits_ref, send_ref, keep_ref, product_ref
):
    width = dresidual_ref.shape[1]
    product_ref[:, :width] = dot(active_ref[...], dresidual_ref[...], 0, 0)
    product_ref[:, width:] = dot(final_ref[...], dlogits_ref[...], 0, 0)
    write_pieces(own_ref, product_ref, send_ref, keep_ref, slice(None))


def outer(own, active, dresidual, final, dlogits):
    rows, model = active.shape
    half_out = dresidual.shape[1] // 2
    half_head = dlogits.shape[1] // 2
    width = half_out + half_head
    piece = (PLACES, model // (2 * PLACES))
    shape = jax.ShapeDtypeStruct(piece + (2 * width,), BF16)
    out = pl.BlockSpec(piece + (width,), lambda i: (0, 0, i))
    return pl.pallas_call(
        outer_kernel,
        grid=(2,),
        out_shape=(shape, shape),
        in_specs=[
            SMEM_SPEC,
            fixed(rows, model),
            pl.BlockSpec((rows, half_out), lambda i: (0, i)),
            fixed(rows, model),
            pl.BlockSpec((rows, half_head), lambda i: (0, i)),
        ],
        out_specs=(out, out),
        scratch_shapes=[pltpu.VMEM((model, width), F32)],
        compiler_params=params(),
        cost_estimate=cost(5),
        name="outer",
    )(own, active, dresidual, final, dlogits)


def inner_kernel(
    own_ref,
    lengths_ref,
    dresidual_ref,
    out_weight_ref,
    slope_ref,
    gated_ref,
    gate_ref,
    normed_ref,
    depth_ref,
    send_ref,
    keep_ref,
    dconv_ref,
    pad_ref,
    dvalue_ref,
    dgate_ref,
    product_ref,
):
    utterances = pad_ref.shape[1]
    frames = pad_ref.shape[2] - 2 * MARGIN

    @pl.when(pl.program_id(0) == 0)
    def _():
        clear_margins(pad_ref)

    for utterance in range(utterances):
        rows = slice(utterance * frames, (utterance + 1) * frames)
        dconv = dot(dresidual_ref[rows, :], out_weight_ref[...], 1, 1) * slope_ref[rows, :]
        dconv_ref[rows, :] = dconv
        for lane in range(WIDE // LANES):
            pad_ref[lane, utterance, MARGIN : MARGIN + frames, :] = dconv[
                :, lane * LANES : (lane + 1) * LANES
            ]

    for lane in range(WIDE // LANES):
        columns = slice(lane * LANES, (lane + 1) * LANES)

        def one(utterance, carry, lane=lane, columns=columns):
            for start in range(0, frames, TILE):
                rows = pl.ds(pl.multiple_of(utterance * frames + start, TILE), TILE)
                position = lax.broadcasted_iota(jnp.int32, (TILE, 1), 0) + start
                live = (position < lengths_ref[utterance]).astype(F32)
                dgated = convolve(pad_ref, lane, utterance, start, depth_ref, True) * live
                gate = gate_ref[rows, columns]
                dvalue_ref[rows, columns] = (dgated * gate).astype(BF16)
                dgate_ref[rows, columns] = (dgated * gated_ref[rows, columns] * (1.0 - gate)).astype(
                    BF16
                )
            return carry

        lax.fori_loop(0, utterances, one, 0)

    for group, source in ((0, dvalue_ref), (1, dgate_ref)):
        product_ref[...] = dot(normed_ref[...], source[...], 0, 0)
        columns = slice(group * WIDE, (group + 1) * WIDE)
        write_pieces(own_ref, product_ref, send_ref, keep_ref, columns)


def inner(own, lengths, dresidual, weight_out, slope, gated, gate, normed, depth, chunk, utterances):
    rows, model = normed.shape
    frames = rows // utterances
    steps = model // WIDE // CHUNKS
    first = chunk * steps
    column = pl.BlockSpec((rows, WIDE), lambda i: (0, first + i))
    piece = (PLACES, model // (2 * PLACES))
    shape = jax.ShapeDtypeStruct(piece + (steps * 2 * WIDE,), BF16)
    out = pl.BlockSpec(piece + (2 * WIDE,), lambda i: (0, 0, i))
    return pl.pallas_call(
        inner_kernel,
        grid=(steps,),
        out_shape=(shape, shape, jax.ShapeDtypeStruct((rows, steps * WIDE), F32)),
        in_specs=[
            SMEM_SPEC,
            SMEM_SPEC,
            fixed(rows, model),
            pl.BlockSpec((WIDE, model), lambda i: (first + i, 0)),
            column,
            column,
            column,
            fixed(rows, model),
            pl.BlockSpec((depth.shape[0], WIDE), lambda i: (0, first + i)),
        ],
        out_specs=(out, out, pl.BlockSpec((rows, WIDE), lambda i: (0, i))),
        scratch_shapes=[
            pltpu.VMEM((WIDE // LANES, utterances, frames + 2 * MARGIN, LANES), F32),
            pltpu.VMEM((rows, WIDE), BF16),
            pltpu.VMEM((rows, WIDE), BF16),
            pltpu.VMEM((model, WIDE), F32),
        ],
        compiler_params=params(),
        cost_estimate=cost(11),
        name="inner",
    )(own, lengths, dresidual, weight_out, slope, gated, gate, normed, depth)


def taps_kernel(lengths_ref, gated_ref, dconv_ref, out_ref, pad_ref, sums_ref):
    utterances = pad_ref.shape[1]
    frames = pad_ref.shape[2] - 2 * MARGIN
    taps = out_ref.shape[0] - 1
    valid = lengths_ref[0]
    for utterance in range(1, utterances):
        valid = valid + lengths_ref[utterance]

    @pl.when(pl.program_id(0) == 0)
    def _():
        clear_margins(pad_ref)

    for lane in range(WIDE // LANES):
        columns = slice(lane * LANES, (lane + 1) * LANES)
        for utterance in range(utterances):
            rows = slice(utterance * frames, (utterance + 1) * frames)
            pad_ref[lane, utterance, MARGIN : MARGIN + frames, :] = gated_ref[rows, columns]
        sums_ref[...] = jnp.zeros_like(sums_ref)

        def one(utterance, carry, lane=lane, columns=columns):
            for start in range(0, frames, TILE):
                rows = pl.ds(pl.multiple_of(utterance * frames + start, TILE), TILE)
                dconv = dconv_ref[rows, columns]
                for tap, view in shifted_views(pad_ref, lane, utterance, start, taps):
                    sums_ref[tap] += jnp.sum((view * dconv).reshape(TILE // 8, 8, LANES), axis=0)
            return carry

        lax.fori_loop(0, utterances, one, 0)
        out_ref[:taps, columns] = jnp.sum(sums_ref[...], axis=1)
    out_ref[taps:, :] = jnp.zeros((1, WIDE), F32) + valid.astype(F32)


def tap_sums(lengths, gated, dconv, taps, chunk, utterances):
    rows, width = dconv.shape
    steps = width // WIDE
    first = chunk * steps
    return pl.pallas_call(
        taps_kernel,
        grid=(steps,),
        out_shape=jax.ShapeDtypeStruct((taps + 1, width), F32),
        in_specs=[
            SMEM_SPEC,
            pl.BlockSpec((rows, WIDE), lambda i: (0, first + i)),
            pl.BlockSpec((rows, WIDE), lambda i: (0, i)),
        ],
        out_specs=pl.BlockSpec((taps + 1, WIDE), lambda i: (0, i)),
        scratch_shapes=[
            pltpu.VMEM((WIDE // LANES, utterances, rows // utterances + 2 * MARGIN, LANES), F32),
            pltpu.VMEM((taps, 8, LANES), F32),
        ],
        compiler_params=params(),
        cost_estimate=cost(4),
        name="taps",
    )(lengths, gated, dconv)


def gain_row(weight, grad, gain):
    along = jnp.sum(weight.astype(F32) * grad, axis=1, keepdims=True)
    return jnp.broadcast_to(along, (along.shape[0], LANES)).T[0:1, :] / gain


def write_rows(core, pieces, other, scale, targets):
    rows = pieces.shape[1]
    for index in range(pieces.shape[0]):
        for side, source in ((core, pieces), (1 - core, other)):
            here = pl.ds(pl.multiple_of(index * 2 * rows + side * rows, rows), rows)
            for target, there, first, width in targets:
                target[here, there : there + width] = (
                    source[index, :, first : first + width].astype(F32) * scale
                )


def unpack_top_kernel(
    utts,
    core_ref,
    small_ref,
    own_ref,
    other_ref,
    head_ref,
    gain_ref,
    losses_ref,
    wout_ref,
    dhead_ref,
    dgain_ref,
    depth_ref,
    loss_ref,
):
    taps = depth_ref.shape[0]
    scale = utts / small_ref[taps:, 0:1]
    half_out = wout_ref.shape[1] // 2
    half_head = dhead_ref.shape[1] // 2
    targets = []
    for half in range(2):
        first = half * (half_out + half_head)
        targets.append((wout_ref, half * half_out, first, half_out))
        targets.append((dhead_ref, half * half_head, first + half_out, half_head))
    write_rows(core_ref[0], own_ref, other_ref, scale, targets)
    dgain_ref[...] = gain_row(head_ref[...], dhead_ref[...], gain_ref[...])
    depth_ref[...] = small_ref[:taps, :] * scale
    loss_ref[...] = losses_ref[...] * scale[None]


def unpack_inner_kernel(utts, core_ref, small_ref, weight_ref, gain_ref, *refs):
    pieces, (win_ref, dgain_ref) = refs[:-2], refs[-2:]
    scale = utts / small_ref[small_ref.shape[0] - 1 :, 0:1]
    half_in = win_ref.shape[1] // 2
    column = 0
    for chunk in range(len(pieces) // 2):
        own_ref, other_ref = pieces[2 * chunk : 2 * chunk + 2]
        targets = []
        for first in range(0, own_ref.shape[2], 2 * WIDE):
            targets.append((win_ref, column, first, WIDE))
            targets.append((win_ref, half_in + column, first + WIDE, WIDE))
            column += WIDE
        write_rows(core_ref[0], own_ref, other_ref, scale, targets)
    dgain_ref[...] = gain_row(weight_ref[...], win_ref[...], gain_ref[...])


def piece_spec(array, steps):
    return pl.BlockSpec((array.shape[0] // steps,) + array.shape[1:], lambda i: (i, 0, 0))


def unpack_top(utts, core, small, own, other, head, gain, losses, width_out):
    steps = 4
    model, symbols = head.shape
    rows = model // steps
    taps = small.shape[0] - 1
    row = pl.BlockSpec((1, rows), lambda i: (0, i))

    def block(width):
        return pl.BlockSpec((rows, width), lambda i: (i, 0))

    return pl.pallas_call(
        functools.partial(unpack_top_kernel, utts),
        grid=(steps,),
        out_shape=(
            jax.ShapeDtypeStruct((model, width_out), F32),
            jax.ShapeDtypeStruct((model, symbols), F32),
            jax.ShapeDtypeStruct((1, model), F32),
            jax.ShapeDtypeStruct((taps, model), F32),
            jax.ShapeDtypeStruct(losses.shape, F32),
        ),
        in_specs=[
            SMEM_SPEC,
            fixed(*small.shape),
            piece_spec(own, steps),
            piece_spec(other, steps),
            block(symbols),
            row,
            fixed(*losses.shape),
        ],
        out_specs=(
            block(width_out),
            block(symbols),
            row,
            fixed(taps, model),
            fixed(*losses.shape),
        ),
        compiler_params=params(),
        cost_estimate=cost(5),
        name="unpack_top",
    )(core, small, own, other, head, gain, losses)


def unpack_inner(utts, core, small, sums, weight, gain):
    steps = 8
    model, width = weight.shape
    rows = model // steps
    row = pl.BlockSpec((1, rows), lambda i: (0, i))
    block = pl.BlockSpec((rows, width), lambda i: (i, 0))
    pieces = [array for pair in sums for array in pair]
    return pl.pallas_call(
        functools.partial(unpack_inner_kernel, utts),
        grid=(steps,),
        out_shape=(
            jax.ShapeDtypeStruct((model, width), F32),
            jax.ShapeDtypeStruct((1, model), F32),
        ),
        in_specs=[SMEM_SPEC, fixed(*small.shape), block, row]
        + [piece_spec(array, steps) for array in pieces],
        out_specs=(block, row),
        compiler_params=params(),
        cost_estimate=cost(9),
        name="unpack_inner",
    )(core, small, weight, gain, *pieces)


def on_device(
    features,
    teacher_logits,
    lengths,
    gain_conv,
    weight_in,
    weight_depth,
    weight_out,
    gain_out,
    head_weight,
):
    count = lax.axis_size(XY) * lax.axis_size(FAR) * lax.axis_size(REST) * lax.axis_size(CORE)
    member = lax.axis_index("member").astype(jnp.int32)[None]
    core = lax.axis_index(CORE).astype(jnp.int32)[None]
    taps, model = weight_depth.shape
    utterances, frames, _ = features.shape
    utts = float(utterances * count)
    tie = lax.optimization_barrier

    give, kept = teacher_sums(member, teacher_logits, utterances)
    got = lax.ppermute(give, "member", [(0, 1), (1, 0)])
    flat = features.reshape(utterances * frames, model)
    normed, gated, gate, slope, active, residual = forward(
        lengths, flat, gain_conv[None], weight_in, weight_depth, weight_out, utterances
    )
    losses, final, dlogits, dresidual = top(
        lengths, residual, gain_out[None], head_weight, kept, got
    )

    def weight_in_chunk(chunk, order, dresidual):
        return inner(
            jnp.stack([core[0], own_place(order)]),
            lengths,
            dresidual,
            weight_out,
            slope,
            gated,
            gate,
            normed,
            weight_depth,
            chunk,
            utterances,
        )

    unordered = jnp.stack([core[0], jnp.int32(0)])
    send, keep = outer(unordered, active, dresidual, final, dlogits)
    send, keep, dresidual = tie((send, keep, dresidual))
    top_sum = sum_core(send, keep)
    inner_sums = []
    dconvs = []
    for chunk in range(CHUNKS):
        order = XY if chunk % 2 else YX
        send, keep, dconv = weight_in_chunk(chunk, order, dresidual)
        inner_sums.append(sum_core(send, keep))
        dconvs.append(dconv)
        if chunk == 0:
            top_sum, dresidual = tie((top_sum, dresidual))
    dconvs[0], inner_sums[0] = tie((dconvs[0], inner_sums[0]))
    small = jnp.concatenate(
        [
            tap_sums(lengths, gated, dconv, taps, chunk, utterances)
            for chunk, dconv in enumerate(dconvs)
        ],
        axis=1,
    )
    top_own = over_rest(lax.psum_scatter(top_sum, XY + (FAR,), scatter_dimension=0, tiled=False))
    top_all = gather(top_own, XY)
    top_other = other_core(top_all)
    small = all_sum(small)
    pairs = []
    for chunk, values in enumerate(inner_sums):
        order = XY if chunk % 2 else YX
        every = gather(sum_chips(values, order), order)
        pairs.append((every, other_core(every)))
    grad_out, grad_head, by_head, grad_depth, losses = unpack_top(
        utts,
        core,
        small,
        top_all,
        top_other,
        head_weight,
        gain_out[None],
        losses,
        weight_out.shape[1],
    )
    grad_in, by_in = unpack_inner(utts, core, small, pairs, weight_in, gain_conv[None])
    return (
        by_in.reshape(model),
        grad_in,
        grad_depth,
        grad_out,
        by_head.reshape(model),
        grad_head,
        losses[:, 0, 0],
    )


def solution(mesh):
    members, others = mesh.devices.shape
    near, cores = 2, 2
    far = PLACES // (members * near)
    rest = others // (far * near * cores)
    split = jax.sharding.Mesh(
        mesh.devices.reshape(members, rest, far, near, cores),
        ("member", REST, FAR, "near", CORE),
    )
    dp = (REST, FAR, "near", CORE)
    in_specs = (
        P(dp + ("member",), None, None),
        P("member", dp, None, None),
        P(dp + ("member",)),
        P(),
        P(),
        P(),
        P(),
        P(),
        P(),
    )
    out_specs = (P(), P(), P(), P(), P(), P(), P(dp + ("member",)))
    return jax.shard_map(
        on_device, mesh=split, in_specs=in_specs, out_specs=out_specs, check_vma=False
    )
```

```python
import functools

import jax
import jax.numpy as jnp
from jax import lax
from jax.experimental import pallas as pl
from jax.experimental.pallas import tpu as pltpu
from jax.sharding import PartitionSpec as P

TEACHERS = 4
PLACES = 8
WIDE = 256
LANES = 128
TILE = 128
MARGIN = 16
CHUNKS = 2
VMEM = 56 << 20
SMEM_SPEC = pl.BlockSpec(memory_space=pltpu.SMEM)
F32 = jnp.float32
BF16 = jnp.bfloat16


def params():
    return pltpu.CompilerParams(vmem_limit_bytes=VMEM)


def cost(microseconds):
    return pl.CostEstimate(flops=int(microseconds * 1.15e9), bytes_accessed=1 << 20, transcendentals=0)


def dot(left, right, left_axis=1, right_axis=0):
    return lax.dot_general(
        left, right, (((left_axis,), (right_axis,)), ((), ())), preferred_element_type=F32
    )


def fixed(*shape):
    return pl.BlockSpec(shape, lambda i, *_: (0,) * len(shape))


FAR = "far"
REST = "rest"
CORE = "core"


def exchange(values, axis, bit=1):
    size = lax.axis_size(axis)
    return lax.ppermute(values, axis, [(i, i ^ bit) for i in range(size)])


def add(own, other):
    return (own.astype(F32) + other.astype(F32)).astype(own.dtype)


def halve(pieces, axis):
    half = pieces.shape[1] // 2
    return add(pieces[:, :half], exchange(pieces[:, half:], axis))


def double(pieces):
    pieces = add(pieces, exchange(pieces, FAR, 2))
    return lax.psum(pieces, REST) if lax.axis_size(REST) > 1 else pieces


def gather(pieces, axis):
    return jnp.concatenate([pieces, exchange(pieces, axis)], axis=1)


def own_place(order):
    place = lax.axis_index(order[0]) * 4 + lax.axis_index(order[1]) * 2 + (lax.axis_index(FAR) & 1)
    return place.astype(jnp.int32)


def all_sum(values):
    for axis, bit in ((CORE, 1), ("member", 1), ("near", 1), (FAR, 1), (FAR, 2)):
        values = values + exchange(values, axis, bit)
    return lax.psum(values, REST) if lax.axis_size(REST) > 1 else values


def write_pieces(own_ref, product, send_ref, keep_ref, group):
    rows = keep_ref.shape[-2]
    core, place = own_ref[0], own_ref[1]

    def one(piece, carry):
        base = (piece ^ place) * (2 * rows)
        kept = pl.multiple_of(base + core * rows, rows)
        sent = pl.multiple_of(base + (1 - core) * rows, rows)
        keep_ref[group, piece] = product[pl.ds(kept, rows), :].astype(BF16)
        send_ref[group, piece] = product[pl.ds(sent, rows), :].astype(BF16)
        return carry

    lax.fori_loop(0, keep_ref.shape[1], one, 0)


def teacher_kernel(member_ref, logits_ref, give_ref, keep_ref, *, own_count):
    step = pl.program_id(0)
    total = None
    for teacher in range(logits_ref.shape[0]):
        logits = logits_ref[teacher, 0].astype(F32)
        shifted = logits - jnp.max(logits, axis=-1, keepdims=True)
        logp = shifted - jnp.log(jnp.sum(jnp.exp(shifted), axis=-1, keepdims=True))
        total = logp if total is None else total + logp

    @pl.when(step < own_count)
    def _():
        give_ref[0] = total

    @pl.when(step >= own_count)
    def _():
        keep_ref[0] = total


def teacher_sums(member, logits, own_count):
    teachers, utterances, frames, symbols = logits.shape
    shape = jax.ShapeDtypeStruct((own_count, frames, symbols), F32)

    def source(i, member_ref):
        mine = member_ref[0] * own_count
        theirs = (1 - member_ref[0]) * own_count
        return (0, jnp.where(i < own_count, theirs + i, mine + i - own_count), 0, 0)

    return pl.pallas_call(
        functools.partial(teacher_kernel, own_count=own_count),
        out_shape=(shape, shape),
        grid_spec=pltpu.PrefetchScalarGridSpec(
            num_scalar_prefetch=1,
            grid=(2 * own_count,),
            in_specs=[pl.BlockSpec((teachers, 1, frames, symbols), source)],
            out_specs=(
                pl.BlockSpec(
                    (1, frames, symbols), lambda i, _: (jnp.minimum(i, own_count - 1), 0, 0)
                ),
                pl.BlockSpec(
                    (1, frames, symbols), lambda i, _: (jnp.maximum(i - own_count, 0), 0, 0)
                ),
            ),
        ),
        compiler_params=params(),
        cost_estimate=cost(4),
        name="teachers",
    )(member, logits)


def live_column(lengths_ref, utterance, frames):
    position = lax.broadcasted_iota(jnp.int32, (frames, 1), 0)
    return (position < lengths_ref[utterance]).astype(F32)


def clear_margins(pad_ref):
    frames = pad_ref.shape[2] - 2 * MARGIN
    zeros = jnp.zeros(pad_ref.shape[:2] + (MARGIN, LANES), F32)
    pad_ref[:, :, :MARGIN, :] = zeros
    pad_ref[:, :, MARGIN + frames :, :] = zeros


def shifted_views(pad_ref, lane, utterance, start, taps):
    first = MARGIN - taps // 2
    for phase in range(8):
        offsets = [offset for offset in range(first, first + taps) if offset % 8 == phase]
        if not offsets:
            continue
        low = offsets[0]
        span = offsets[-1] - low + TILE
        view = pad_ref[lane, utterance, start + low : start + low + span, :]
        for offset in offsets:
            yield offset - first, view[offset - low : offset - low + TILE]


def convolve(pad_ref, lane, utterance, start, depth_ref, flipped):
    taps = depth_ref.shape[0]
    columns = slice(lane * LANES, (lane + 1) * LANES)
    total = jnp.zeros((TILE, LANES), F32)
    for tap, view in shifted_views(pad_ref, lane, utterance, start, taps):
        row = taps - 1 - tap if flipped else tap
        total = total + view * depth_ref[row : row + 1, columns]
    return total


def forward_kernel(
    lengths_ref,
    features_ref,
    gain_ref,
    value_weight_ref,
    gate_weight_ref,
    depth_ref,
    out_weight_ref,
    normed_ref,
    gated_ref,
    gate_ref,
    slope_ref,
    active_ref,
    residual_ref,
    pad_ref,
):
    utterances = pad_ref.shape[1]
    frames = pad_ref.shape[2] - 2 * MARGIN

    @pl.when(pl.program_id(0) == 0)
    def _():
        values = features_ref[...].astype(F32)
        centred = values - jnp.mean(values, axis=-1, keepdims=True)
        spread = jnp.mean(centred * centred, axis=-1, keepdims=True)
        normed_ref[...] = (centred * lax.rsqrt(spread + 1e-05) * gain_ref[...]).astype(BF16)
        residual_ref[...] = values
        clear_margins(pad_ref)

    for utterance in range(utterances):
        rows = slice(utterance * frames, (utterance + 1) * frames)
        normed = normed_ref[rows, :]
        gate = jax.nn.sigmoid(dot(normed, gate_weight_ref[...]))
        gated = dot(normed, value_weight_ref[...]) * gate
        gated = gated * live_column(lengths_ref, utterance, frames)
        gate_ref[rows, :] = gate
        gated_ref[rows, :] = gated
        for lane in range(WIDE // LANES):
            pad_ref[lane, utterance, MARGIN : MARGIN + frames, :] = gated[
                :, lane * LANES : (lane + 1) * LANES
            ]

    for lane in range(WIDE // LANES):
        columns = slice(lane * LANES, (lane + 1) * LANES)

        def one(utterance, carry, lane=lane, columns=columns):
            for start in range(0, frames, TILE):
                rows = pl.ds(pl.multiple_of(utterance * frames + start, TILE), TILE)
                convolved = convolve(pad_ref, lane, utterance, start, depth_ref, False)
                squash = jax.nn.sigmoid(convolved)
                active_ref[rows, columns] = (convolved * squash).astype(BF16)
                slope_ref[rows, columns] = squash * (1.0 + convolved * (1.0 - squash))
            return carry

        lax.fori_loop(0, utterances, one, 0)

    residual_ref[...] += dot(active_ref[...], out_weight_ref[...])


def forward(lengths, features, gain, weight_in, depth, weight_out, utterances):
    rows, model = features.shape
    frames = rows // utterances
    steps = model // WIDE
    column = pl.BlockSpec((rows, WIDE), lambda i: (0, i))
    wide = jax.ShapeDtypeStruct((rows, model), F32)
    narrow = jax.ShapeDtypeStruct((rows, model), BF16)
    return pl.pallas_call(
        forward_kernel,
        grid=(steps,),
        out_shape=(narrow, wide, wide, wide, narrow, wide),
        in_specs=[
            SMEM_SPEC,
            fixed(rows, model),
            fixed(1, model),
            pl.BlockSpec((model, WIDE), lambda i: (0, i)),
            pl.BlockSpec((model, WIDE), lambda i: (0, steps + i)),
            pl.BlockSpec((depth.shape[0], WIDE), lambda i: (0, i)),
            pl.BlockSpec((WIDE, model), lambda i: (i, 0)),
        ],
        out_specs=(fixed(rows, model), column, column, column, column, fixed(rows, model)),
        scratch_shapes=[pltpu.VMEM((WIDE // LANES, utterances, frames + 2 * MARGIN, LANES), F32)],
        compiler_params=params(),
        cost_estimate=cost(15),
        name="forward",
    )(lengths, features, gain, weight_in, weight_in, depth, weight_out)


def top_kernel(
    lengths_ref,
    residual_ref,
    gain_ref,
    head_ref,
    kept_ref,
    got_ref,
    loss_ref,
    final_ref,
    dlogits_ref,
    dresidual_ref,
):
    frames = residual_ref.shape[0]
    live = live_column(lengths_ref, pl.program_id(0), frames)
    values = residual_ref[...]
    centred = values - jnp.mean(values, axis=-1, keepdims=True)
    spread = jnp.mean(centred * centred, axis=-1, keepdims=True)
    inverse = lax.rsqrt(spread + 1e-05)
    unit = centred * inverse
    final = (unit * gain_ref[...]).astype(BF16)
    final_ref[...] = final

    def log_softmax(logits):
        shifted = logits - jnp.max(logits, axis=-1, keepdims=True)
        return shifted - jnp.log(jnp.sum(jnp.exp(shifted), axis=-1, keepdims=True))

    target = jnp.exp(log_softmax((kept_ref[0] + got_ref[0]) * (1.0 / TEACHERS)))
    logp = log_softmax(dot(final, head_ref[...]))
    cross = -jnp.sum(target * logp, axis=-1, keepdims=True)
    loss_ref[...] = jnp.broadcast_to(jnp.sum(cross * live, axis=0, keepdims=True), (1, 1, LANES))
    weight = jnp.sum(target, axis=-1, keepdims=True)
    dlogits = ((jnp.exp(logp) * weight - target) * live).astype(BF16)
    dlogits_ref[...] = dlogits
    dunit = dot(dlogits, head_ref[...], 1, 1) * gain_ref[...]
    average = jnp.mean(dunit, axis=-1, keepdims=True)
    along = jnp.mean(dunit * unit, axis=-1, keepdims=True)
    dresidual_ref[...] = (inverse * (dunit - average - unit * along)).astype(BF16)


def top(lengths, residual, gain, head, kept, got):
    rows, model = residual.shape
    utterances, frames, symbols = kept.shape
    per_row = pl.BlockSpec((frames, model), lambda i: (i, 0))
    sums = pl.BlockSpec((1, frames, symbols), lambda i: (i, 0, 0))
    return pl.pallas_call(
        top_kernel,
        grid=(utterances,),
        out_shape=(
            jax.ShapeDtypeStruct((utterances, 1, LANES), F32),
            jax.ShapeDtypeStruct((rows, model), BF16),
            jax.ShapeDtypeStruct((rows, symbols), BF16),
            jax.ShapeDtypeStruct((rows, model), BF16),
        ),
        in_specs=[SMEM_SPEC, per_row, fixed(1, model), fixed(model, symbols), sums, sums],
        out_specs=(
            pl.BlockSpec((1, 1, LANES), lambda i: (i, 0, 0)),
            per_row,
            pl.BlockSpec((frames, symbols), lambda i: (i, 0)),
            per_row,
        ),
        compiler_params=params(),
        cost_estimate=cost(5),
        name="top",
    )(lengths, residual, gain, head, kept, got)


def outer_kernel(
    own_ref, active_ref, dresidual_ref, final_ref, dlogits_ref, send_ref, keep_ref, product_ref
):
    width = dresidual_ref.shape[1]
    product_ref[:, :width] = dot(active_ref[...], dresidual_ref[...], 0, 0)
    product_ref[:, width:] = dot(final_ref[...], dlogits_ref[...], 0, 0)
    write_pieces(own_ref, product_ref, send_ref, keep_ref, 0)


def outer(own, active, dresidual, final, dlogits):
    rows, model = active.shape
    half_out = dresidual.shape[1] // 2
    half_head = dlogits.shape[1] // 2
    width = half_out + half_head
    piece = (PLACES, model // (2 * PLACES), width)
    shape = jax.ShapeDtypeStruct((2,) + piece, BF16)
    out = pl.BlockSpec((1,) + piece, lambda i: (i, 0, 0, 0))
    return pl.pallas_call(
        outer_kernel,
        grid=(2,),
        out_shape=(shape, shape),
        in_specs=[
            SMEM_SPEC,
            fixed(rows, model),
            pl.BlockSpec((rows, half_out), lambda i: (0, i)),
            fixed(rows, model),
            pl.BlockSpec((rows, half_head), lambda i: (0, i)),
        ],
        out_specs=(out, out),
        scratch_shapes=[pltpu.VMEM((model, width), F32)],
        compiler_params=params(),
        cost_estimate=cost(5),
        name="outer",
    )(own, active, dresidual, final, dlogits)


def inner_kernel(
    own_ref,
    lengths_ref,
    dresidual_ref,
    out_weight_ref,
    slope_ref,
    gated_ref,
    gate_ref,
    normed_ref,
    depth_ref,
    send_ref,
    keep_ref,
    dconv_ref,
    pad_ref,
    dvalue_ref,
    dgate_ref,
    product_ref,
):
    utterances = pad_ref.shape[1]
    frames = pad_ref.shape[2] - 2 * MARGIN

    @pl.when(pl.program_id(0) == 0)
    def _():
        clear_margins(pad_ref)

    for utterance in range(utterances):
        rows = slice(utterance * frames, (utterance + 1) * frames)
        dconv = dot(dresidual_ref[rows, :], out_weight_ref[...], 1, 1) * slope_ref[rows, :]
        dconv_ref[rows, :] = dconv
        for lane in range(WIDE // LANES):
            pad_ref[lane, utterance, MARGIN : MARGIN + frames, :] = dconv[
                :, lane * LANES : (lane + 1) * LANES
            ]

    for lane in range(WIDE // LANES):
        columns = slice(lane * LANES, (lane + 1) * LANES)

        def one(utterance, carry, lane=lane, columns=columns):
            for start in range(0, frames, TILE):
                rows = pl.ds(pl.multiple_of(utterance * frames + start, TILE), TILE)
                position = lax.broadcasted_iota(jnp.int32, (TILE, 1), 0) + start
                live = (position < lengths_ref[utterance]).astype(F32)
                dgated = convolve(pad_ref, lane, utterance, start, depth_ref, True) * live
                gate = gate_ref[rows, columns]
                dvalue_ref[rows, columns] = (dgated * gate).astype(BF16)
                dgate_ref[rows, columns] = (dgated * gated_ref[rows, columns] * (1.0 - gate)).astype(
                    BF16
                )
            return carry

        lax.fori_loop(0, utterances, one, 0)

    for group, source in ((0, dvalue_ref), (1, dgate_ref)):
        product_ref[...] = dot(normed_ref[...], source[...], 0, 0)
        write_pieces(own_ref, product_ref, send_ref, keep_ref, group)


def inner(own, lengths, dresidual, weight_out, slope, gated, gate, normed, depth, chunk, utterances):
    rows, model = normed.shape
    frames = rows // utterances
    steps = model // WIDE // CHUNKS
    first = chunk * steps
    column = pl.BlockSpec((rows, WIDE), lambda i: (0, first + i))
    piece = (2, PLACES, model // (2 * PLACES))
    shape = jax.ShapeDtypeStruct(piece + (steps * WIDE,), BF16)
    out = pl.BlockSpec(piece + (WIDE,), lambda i: (0, 0, 0, i))
    return pl.pallas_call(
        inner_kernel,
        grid=(steps,),
        out_shape=(shape, shape, jax.ShapeDtypeStruct((rows, steps * WIDE), F32)),
        in_specs=[
            SMEM_SPEC,
            SMEM_SPEC,
            fixed(rows, model),
            pl.BlockSpec((WIDE, model), lambda i: (first + i, 0)),
            column,
            column,
            column,
            fixed(rows, model),
            pl.BlockSpec((depth.shape[0], WIDE), lambda i: (0, first + i)),
        ],
        out_specs=(out, out, pl.BlockSpec((rows, WIDE), lambda i: (0, i))),
        scratch_shapes=[
            pltpu.VMEM((WIDE // LANES, utterances, frames + 2 * MARGIN, LANES), F32),
            pltpu.VMEM((rows, WIDE), BF16),
            pltpu.VMEM((rows, WIDE), BF16),
            pltpu.VMEM((model, WIDE), F32),
        ],
        compiler_params=params(),
        cost_estimate=cost(11),
        name="inner",
    )(own, lengths, dresidual, weight_out, slope, gated, gate, normed, depth)


def taps_kernel(lengths_ref, gated_ref, dconv_ref, out_ref, pad_ref, sums_ref):
    utterances = pad_ref.shape[1]
    frames = pad_ref.shape[2] - 2 * MARGIN
    taps = out_ref.shape[0] - 1
    valid = lengths_ref[0]
    for utterance in range(1, utterances):
        valid = valid + lengths_ref[utterance]

    @pl.when(pl.program_id(0) == 0)
    def _():
        clear_margins(pad_ref)

    for lane in range(WIDE // LANES):
        columns = slice(lane * LANES, (lane + 1) * LANES)
        for utterance in range(utterances):
            rows = slice(utterance * frames, (utterance + 1) * frames)
            pad_ref[lane, utterance, MARGIN : MARGIN + frames, :] = gated_ref[rows, columns]
        sums_ref[...] = jnp.zeros_like(sums_ref)

        def one(utterance, carry, lane=lane, columns=columns):
            for start in range(0, frames, TILE):
                rows = pl.ds(pl.multiple_of(utterance * frames + start, TILE), TILE)
                dconv = dconv_ref[rows, columns]
                for tap, view in shifted_views(pad_ref, lane, utterance, start, taps):
                    sums_ref[tap] += jnp.sum((view * dconv).reshape(TILE // 8, 8, LANES), axis=0)
            return carry

        lax.fori_loop(0, utterances, one, 0)
        out_ref[:taps, columns] = jnp.sum(sums_ref[...], axis=1)
    out_ref[taps:, :] = jnp.zeros((1, WIDE), F32) + valid.astype(F32)


def tap_sums(lengths, gated, dconv, taps, chunk, utterances):
    rows, width = dconv.shape
    steps = width // WIDE
    first = chunk * steps
    return pl.pallas_call(
        taps_kernel,
        grid=(steps,),
        out_shape=jax.ShapeDtypeStruct((taps + 1, width), F32),
        in_specs=[
            SMEM_SPEC,
            pl.BlockSpec((rows, WIDE), lambda i: (0, first + i)),
            pl.BlockSpec((rows, WIDE), lambda i: (0, i)),
        ],
        out_specs=pl.BlockSpec((taps + 1, WIDE), lambda i: (0, i)),
        scratch_shapes=[
            pltpu.VMEM((WIDE // LANES, utterances, rows // utterances + 2 * MARGIN, LANES), F32),
            pltpu.VMEM((taps, 8, LANES), F32),
        ],
        compiler_params=params(),
        cost_estimate=cost(4),
        name="taps",
    )(lengths, gated, dconv)


def gain_row(weight, grad):
    along = jnp.sum(weight.astype(F32) * grad, axis=1, keepdims=True)
    return jnp.broadcast_to(along, (along.shape[0], LANES)).T[0:1, :]


def write_rows(own_ref, step, piece_refs, group, scale, targets):
    mine_ref, other_ref = piece_refs
    places, rows = mine_ref.shape[1:3]
    core, place = own_ref[0], own_ref[1]
    for index in range(places):
        piece = index ^ (place & (places - 1))
        for side, source in ((core, mine_ref), (1 - core, other_ref)):
            here = pl.ds(pl.multiple_of(index * 2 * rows + side * rows, rows), rows)
            for target, there, first, width in targets:
                target[here, there : there + width] = (
                    source[group, piece, :, first : first + width].astype(F32) * scale
                )


def unpack_top_kernel(
    utts,
    own_ref,
    small_ref,
    mine_ref,
    other_ref,
    head_ref,
    gain_ref,
    losses_ref,
    wout_ref,
    dhead_ref,
    dgain_ref,
    depth_ref,
    loss_ref,
):
    taps = depth_ref.shape[0]
    scale = utts / small_ref[taps:, 0:1]
    half_out = wout_ref.shape[1] // 2
    half_head = dhead_ref.shape[1] // 2
    for group in range(2):
        targets = (
            (wout_ref, group * half_out, 0, half_out),
            (dhead_ref, group * half_head, half_out, half_head),
        )
        write_rows(own_ref, pl.program_id(0), (mine_ref, other_ref), group, scale, targets)
    dgain_ref[...] = gain_row(head_ref[...], dhead_ref[...]) / gain_ref[...]
    depth_ref[...] = small_ref[:taps, :] * scale
    loss_ref[...] = losses_ref[...] * scale[None]


def unpack_top(utts, own, small, mine, other, head, gain, losses, width_out):
    steps = 4
    model, symbols = head.shape
    rows = model // steps
    taps = small.shape[0] - 1
    places = PLACES // steps
    row = pl.BlockSpec((1, rows), lambda i, own_ref: (0, i))
    piece = pl.BlockSpec(
        (2, places) + mine.shape[2:], lambda i, own_ref: (0, i ^ (own_ref[1] // places), 0, 0)
    )

    def block(width):
        return pl.BlockSpec((rows, width), lambda i, own_ref: (i, 0))

    return pl.pallas_call(
        functools.partial(unpack_top_kernel, utts),
        out_shape=(
            jax.ShapeDtypeStruct((model, width_out), F32),
            jax.ShapeDtypeStruct((model, symbols), F32),
            jax.ShapeDtypeStruct((1, model), F32),
            jax.ShapeDtypeStruct((taps, model), F32),
            jax.ShapeDtypeStruct(losses.shape, F32),
        ),
        grid_spec=pltpu.PrefetchScalarGridSpec(
            num_scalar_prefetch=1,
            grid=(steps,),
            in_specs=[
                fixed(*small.shape),
                piece,
                piece,
                block(symbols),
                row,
                fixed(*losses.shape),
            ],
            out_specs=(
                block(width_out),
                block(symbols),
                row,
                fixed(taps, model),
                fixed(*losses.shape),
            ),
        ),
        compiler_params=params(),
        cost_estimate=cost(5),
        name="unpack_top",
    )(own, small, mine, other, head, gain, losses)


def unpack_inner_kernel(
    utts, last, own_ref, small_ref, mine_ref, other_ref, weight_ref, gain_ref, *refs
):
    win_ref, dgain_ref = refs[-2:]
    scale = utts / small_ref[small_ref.shape[0] - 1 :, 0:1]
    targets = ((win_ref, 0, 0, win_ref.shape[1]),)
    write_rows(own_ref, pl.program_id(0), (mine_ref, other_ref), 0, scale, targets)
    row = gain_row(weight_ref[...], win_ref[...])

    @pl.when(pl.program_id(1) == 0)
    def _():
        dgain_ref[...] = row + refs[1][...] if len(refs) > 2 else row

    @pl.when(pl.program_id(1) == 1)
    def _():
        total = dgain_ref[...] + row
        dgain_ref[...] = total / gain_ref[...] if last else total


def unpack_inner(utts, own, small, mine, other, weight, gain, chunk, before):
    steps = 2
    model, width = weight.shape
    rows = model // steps
    wide = mine.shape[3]
    places = PLACES // steps
    row = pl.BlockSpec((1, rows), lambda i, j, own_ref: (0, i))
    block = pl.BlockSpec((rows, wide), lambda i, j, own_ref: (i, j * CHUNKS + chunk))
    piece = pl.BlockSpec(
        (1, places) + mine.shape[2:], lambda i, j, own_ref: (j, i ^ (own_ref[1] // places), 0, 0)
    )
    return pl.pallas_call(
        functools.partial(unpack_inner_kernel, utts, chunk == CHUNKS - 1),
        out_shape=(
            jax.ShapeDtypeStruct((model, width), F32),
            jax.ShapeDtypeStruct((1, model), F32),
        ),
        grid_spec=pltpu.PrefetchScalarGridSpec(
            num_scalar_prefetch=1,
            grid=(steps, 2),
            in_specs=[
                pl.BlockSpec(small.shape, lambda i, j, own_ref: (0, 0)),
                piece,
                piece,
                block,
                row,
            ]
            + ([pl.BlockSpec(memory_space=pl.ANY), row] if before else []),
            out_specs=(block, row),
        ),
        input_output_aliases={6: 0} if before else {},
        compiler_params=params(),
        cost_estimate=cost(4),
        name="unpack_inner",
    )(own, small, mine, other, weight, gain, *before)


def on_device(
    features,
    teacher_logits,
    lengths,
    gain_conv,
    weight_in,
    weight_depth,
    weight_out,
    gain_out,
    head_weight,
):
    count = 1
    for axis in ("member", "near", FAR, REST, CORE):
        count *= lax.axis_size(axis)
    member = lax.axis_index("member").astype(jnp.int32)[None]
    core = lax.axis_index(CORE).astype(jnp.int32)
    orders = (("near", "member"), ("member", "near"))
    owns = [jnp.stack([core, own_place(order)]) for order in orders]
    taps, model = weight_depth.shape
    utterances, frames, _ = features.shape
    utts = float(utterances * count)
    tie = lax.optimization_barrier

    give, kept = teacher_sums(member, teacher_logits, utterances)
    got = exchange(give, "member")
    flat = features.reshape(utterances * frames, model)
    normed, gated, gate, slope, active, residual = forward(
        lengths, flat, gain_conv[None], weight_in, weight_depth, weight_out, utterances
    )
    losses, final, dlogits, dresidual = top(
        lengths, residual, gain_out[None], head_weight, kept, got
    )

    def weight_in_chunk(chunk, dresidual):
        send, keep, dconv = inner(
            owns[chunk],
            lengths,
            dresidual,
            weight_out,
            slope,
            gated,
            gate,
            normed,
            weight_depth,
            chunk,
            utterances,
        )
        return add(keep, exchange(send, CORE)), dconv

    def chip_sums(pieces, order):
        pieces = double(halve(halve(pieces, order[1]), FAR))
        return gather(gather(gather(pieces, FAR), order[1]), order[0])

    send, keep = outer(owns[1], active, dresidual, final, dlogits)
    send, keep, dresidual = tie((send, keep, dresidual))
    top_sum = add(keep, exchange(send, CORE))
    first_sum, first_dconv = weight_in_chunk(0, dresidual)
    top_sum, dresidual = tie((top_sum, dresidual))
    top_sum = halve(top_sum, orders[1][0])
    second_sum, second_dconv = weight_in_chunk(1, dresidual)
    top_sum, first_sum, first_dconv = tie((top_sum, first_sum, first_dconv))
    first_sum = halve(first_sum, orders[0][0])
    first_taps = tap_sums(lengths, gated, first_dconv, taps, 0, utterances)
    second_sum, second_dconv = tie((second_sum, second_dconv))
    second_sum = halve(second_sum, orders[1][0])
    second_taps = tap_sums(lengths, gated, second_dconv, taps, 1, utterances)
    small = all_sum(jnp.concatenate([first_taps, second_taps], axis=1))

    top_all = chip_sums(top_sum, orders[1])
    grad_out, grad_head, by_head, grad_depth, losses = unpack_top(
        utts,
        owns[1],
        small,
        top_all,
        exchange(top_all, CORE),
        head_weight,
        gain_out[None],
        losses,
        weight_out.shape[1],
    )
    unpacked = ()
    for chunk, values in enumerate((first_sum, second_sum)):
        every = chip_sums(values, orders[chunk])
        unpacked = unpack_inner(
            utts,
            owns[chunk],
            small,
            every,
            exchange(every, CORE),
            weight_in,
            gain_conv[None],
            chunk,
            unpacked,
        )
    grad_in, by_in = unpacked
    return (
        by_in.reshape(model),
        grad_in,
        grad_depth,
        grad_out,
        by_head.reshape(model),
        grad_head,
        losses[:, 0, 0],
    )


def solution(mesh):
    members, others = mesh.devices.shape
    near, cores = 2, 2
    far = 2 * PLACES // (members * near)
    rest = others // (far * near * cores)
    split = jax.sharding.Mesh(
        mesh.devices.reshape(members, rest, far, near, cores),
        ("member", REST, FAR, "near", CORE),
    )
    dp = (REST, FAR, "near", CORE)
    in_specs = (
        P(dp + ("member",), None, None),
        P("member", dp, None, None),
        P(dp + ("member",)),
        P(),
        P(),
        P(),
        P(),
        P(),
        P(),
    )
    out_specs = (P(), P(), P(), P(), P(), P(), P(dp + ("member",)))
    return jax.shard_map(
        on_device, mesh=split, in_specs=in_specs, out_specs=out_specs, check_vma=False
    )
```

```python
import functools

import jax
import jax.numpy as jnp
from jax import lax
from jax.experimental import pallas as pl
from jax.experimental.pallas import tpu as pltpu
from jax.sharding import PartitionSpec as P

TEACHERS = 4
PLACES = 8
WIDE = 256
LANES = 128
TILE = 128
MARGIN = 16
CHUNKS = 2
VMEM = 56 << 20
ORDER = (
    "in0", "in1", "top", "small", "in0", "top", "in1", "small", "in0", "top", "in1", "small",
    "in0", "top", "in1", "small", "in0", "top", "in1", "small", "top", "in0", "in1", "top",
    "write_top", "in0", "in0", "write0", "in1", "in1", "write1",
)
SMEM_SPEC = pl.BlockSpec(memory_space=pltpu.SMEM)
F32 = jnp.float32
BF16 = jnp.bfloat16


def params():
    return pltpu.CompilerParams(vmem_limit_bytes=VMEM)


def cost(microseconds):
    return pl.CostEstimate(flops=int(microseconds * 1.15e9), bytes_accessed=1 << 20, transcendentals=0)


def dot(left, right, left_axis=1, right_axis=0):
    return lax.dot_general(
        left, right, (((left_axis,), (right_axis,)), ((), ())), preferred_element_type=F32
    )


def fixed(*shape):
    return pl.BlockSpec(shape, lambda i, *_: (0,) * len(shape))


FAR = "far"
REST = "rest"
CORE = "core"
SMALL_STEPS = ((CORE, 1), ("member", 1), ("near", 1), (FAR, 1), (FAR, 2))


def exchange(values, axis, bit=1):
    size = lax.axis_size(axis)
    return lax.ppermute(values, axis, [(i, i ^ bit) for i in range(size)])


def add(own, other):
    return (own.astype(F32) + other.astype(F32)).astype(own.dtype)


def own_place(order):
    place = lax.axis_index(order[0]) * 4 + lax.axis_index(order[1]) * 2 + (lax.axis_index(FAR) & 1)
    return place.astype(jnp.int32)


def over_rest(values):
    return lax.psum(values, REST) if lax.axis_size(REST) > 1 else values


class Line:
    def __init__(self):
        self.values = {}
        self.pending = {}
        self.steps = {}
        self.last = None

    def after_last(self, value):
        if self.last is not None:
            value, self.values[self.last] = lax.optimization_barrier(
                (value, self.values[self.last])
            )
        return value

    def before_kernel(self, value):
        value = self.after_last(value)
        if self.last in self.steps and self.last not in self.pending:
            self.start(self.last)
        return value

    def put(self, name, value):
        self.values[name] = value
        self.last = name

    def begin(self, name, send, keep, order):
        self.values[name] = keep
        self.pending[name] = exchange(send, CORE)
        halve, gather = [("halve", axis) for axis in order], [("gather", axis) for axis in order]
        self.steps[name] = (
            [("add", CORE)]
            + halve
            + [("halve", FAR), ("double", FAR), ("gather", FAR)]
            + gather[::-1]
            + [("done", CORE)]
        )

    def begin_small(self, name, value):
        self.values[name] = value
        self.steps[name] = [("sum", step) for step in SMALL_STEPS]
        self.start(name)

    def start(self, name):
        if not self.steps[name]:
            return
        kind, axis = self.steps[name][0]
        values = self.values[name]
        if kind == "halve":
            self.pending[name] = exchange(values[:, values.shape[1] // 2 :], axis)
        elif kind == "double":
            self.pending[name] = exchange(values, axis, 2)
        elif kind == "sum":
            self.pending[name] = exchange(values, *axis)
        else:
            self.pending[name] = exchange(values, axis)

    def step(self, name, start=True):
        kind, _ = self.steps[name].pop(0)
        got = self.after_last(self.pending.pop(name))
        own = self.values[name]
        if kind == "halve":
            own = own[:, : got.shape[1]]
        if kind == "gather":
            result = jnp.concatenate([own, got], axis=1)
        elif kind == "done":
            result = (own, got)
        else:
            result = add(own, got)
        if kind == "double" or (kind == "sum" and not self.steps[name]):
            result = over_rest(result)
        self.put(name, result)
        if start:
            self.start(name)


def write_pieces(own_ref, product, send_ref, keep_ref, group):
    rows = keep_ref.shape[-2]
    core, place = own_ref[0], own_ref[1]

    def one(piece, carry):
        base = (piece ^ place) * (2 * rows)
        kept = pl.multiple_of(base + core * rows, rows)
        sent = pl.multiple_of(base + (1 - core) * rows, rows)
        keep_ref[group, piece] = product[pl.ds(kept, rows), :].astype(BF16)
        send_ref[group, piece] = product[pl.ds(sent, rows), :].astype(BF16)
        return carry

    lax.fori_loop(0, keep_ref.shape[1], one, 0)


def teacher_kernel(member_ref, logits_ref, give_ref, keep_ref, *, own_count):
    step = pl.program_id(0)
    total = None
    for teacher in range(logits_ref.shape[0]):
        logits = logits_ref[teacher, 0].astype(F32)
        shifted = logits - jnp.max(logits, axis=-1, keepdims=True)
        logp = shifted - jnp.log(jnp.sum(jnp.exp(shifted), axis=-1, keepdims=True))
        total = logp if total is None else total + logp

    @pl.when(step < own_count)
    def _():
        give_ref[0] = total

    @pl.when(step >= own_count)
    def _():
        keep_ref[0] = total


def teacher_sums(member, logits, own_count):
    teachers, utterances, frames, symbols = logits.shape
    shape = jax.ShapeDtypeStruct((own_count, frames, symbols), F32)

    def source(i, member_ref):
        mine = member_ref[0] * own_count
        theirs = (1 - member_ref[0]) * own_count
        return (0, jnp.where(i < own_count, theirs + i, mine + i - own_count), 0, 0)

    return pl.pallas_call(
        functools.partial(teacher_kernel, own_count=own_count),
        out_shape=(shape, shape),
        grid_spec=pltpu.PrefetchScalarGridSpec(
            num_scalar_prefetch=1,
            grid=(2 * own_count,),
            in_specs=[pl.BlockSpec((teachers, 1, frames, symbols), source)],
            out_specs=(
                pl.BlockSpec(
                    (1, frames, symbols), lambda i, _: (jnp.minimum(i, own_count - 1), 0, 0)
                ),
                pl.BlockSpec(
                    (1, frames, symbols), lambda i, _: (jnp.maximum(i - own_count, 0), 0, 0)
                ),
            ),
        ),
        compiler_params=params(),
        cost_estimate=cost(4),
        name="teachers",
    )(member, logits)


def live_column(lengths_ref, utterance, frames):
    position = lax.broadcasted_iota(jnp.int32, (frames, 1), 0)
    return (position < lengths_ref[utterance]).astype(F32)


def clear_margins(pad_ref):
    frames = pad_ref.shape[2] - 2 * MARGIN
    zeros = jnp.zeros(pad_ref.shape[:2] + (MARGIN, LANES), F32)
    pad_ref[:, :, :MARGIN, :] = zeros
    pad_ref[:, :, MARGIN + frames :, :] = zeros


def shifted_views(pad_ref, lane, utterance, start, taps):
    first = MARGIN - taps // 2
    for phase in range(8):
        offsets = [offset for offset in range(first, first + taps) if offset % 8 == phase]
        if not offsets:
            continue
        low = offsets[0]
        span = offsets[-1] - low + TILE
        view = pad_ref[lane, utterance, start + low : start + low + span, :]
        for offset in offsets:
            yield offset - first, view[offset - low : offset - low + TILE]


def convolve(pad_ref, lane, utterance, start, depth_ref, flipped):
    taps = depth_ref.shape[0]
    columns = slice(lane * LANES, (lane + 1) * LANES)
    total = jnp.zeros((TILE, LANES), F32)
    for tap, view in shifted_views(pad_ref, lane, utterance, start, taps):
        row = taps - 1 - tap if flipped else tap
        total = total + view * depth_ref[row : row + 1, columns]
    return total


def forward_kernel(
    lengths_ref,
    features_ref,
    gain_ref,
    value_weight_ref,
    gate_weight_ref,
    depth_ref,
    out_weight_ref,
    turned_ref,
    gated_ref,
    gate_ref,
    slope_ref,
    active_ref,
    residual_ref,
    normed_ref,
    pad_ref,
):
    utterances = pad_ref.shape[1]
    frames = pad_ref.shape[2] - 2 * MARGIN

    @pl.when(pl.program_id(0) == 0)
    def _():
        values = features_ref[...].astype(F32)
        centred = values - jnp.mean(values, axis=-1, keepdims=True)
        spread = jnp.mean(centred * centred, axis=-1, keepdims=True)
        normed = centred * lax.rsqrt(spread + 1e-05) * gain_ref[...]
        normed_ref[...] = normed.astype(BF16)
        turned_ref[...] = normed.T.astype(BF16)
        residual_ref[...] = values
        clear_margins(pad_ref)

    for utterance in range(utterances):
        rows = slice(utterance * frames, (utterance + 1) * frames)
        normed = normed_ref[rows, :]
        gate = jax.nn.sigmoid(dot(normed, gate_weight_ref[...]))
        gated = dot(normed, value_weight_ref[...]) * gate
        gated = gated * live_column(lengths_ref, utterance, frames)
        gate_ref[rows, :] = gate
        gated_ref[rows, :] = gated
        for lane in range(WIDE // LANES):
            pad_ref[lane, utterance, MARGIN : MARGIN + frames, :] = gated[
                :, lane * LANES : (lane + 1) * LANES
            ]

    for lane in range(WIDE // LANES):
        columns = slice(lane * LANES, (lane + 1) * LANES)

        def one(utterance, carry, lane=lane, columns=columns):
            for start in range(0, frames, TILE):
                rows = pl.ds(pl.multiple_of(utterance * frames + start, TILE), TILE)
                convolved = convolve(pad_ref, lane, utterance, start, depth_ref, False)
                squash = jax.nn.sigmoid(convolved)
                active_ref[rows, columns] = (convolved * squash).astype(BF16)
                slope_ref[rows, columns] = squash * (1.0 + convolved * (1.0 - squash))
            return carry

        lax.fori_loop(0, utterances, one, 0)

    residual_ref[...] += dot(active_ref[...], out_weight_ref[...])


def forward(lengths, features, gain, weight_in, depth, weight_out, utterances):
    rows, model = features.shape
    frames = rows // utterances
    steps = model // WIDE
    column = pl.BlockSpec((rows, WIDE), lambda i: (0, i))
    wide = jax.ShapeDtypeStruct((rows, model), F32)
    narrow = jax.ShapeDtypeStruct((rows, model), BF16)
    return pl.pallas_call(
        forward_kernel,
        grid=(steps,),
        out_shape=(jax.ShapeDtypeStruct((model, rows), BF16), wide, wide, wide, narrow, wide),
        in_specs=[
            SMEM_SPEC,
            fixed(rows, model),
            fixed(1, model),
            pl.BlockSpec((model, WIDE), lambda i: (0, i)),
            pl.BlockSpec((model, WIDE), lambda i: (0, steps + i)),
            pl.BlockSpec((depth.shape[0], WIDE), lambda i: (0, i)),
            pl.BlockSpec((WIDE, model), lambda i: (i, 0)),
        ],
        out_specs=(fixed(model, rows), column, column, column, column, fixed(rows, model)),
        scratch_shapes=[
            pltpu.VMEM((rows, model), BF16),
            pltpu.VMEM((WIDE // LANES, utterances, frames + 2 * MARGIN, LANES), F32),
        ],
        compiler_params=params(),
        cost_estimate=cost(15),
        name="forward",
    )(lengths, features, gain, weight_in, weight_in, depth, weight_out)


def top_kernel(
    lengths_ref,
    residual_ref,
    gain_ref,
    head_ref,
    kept_ref,
    got_ref,
    loss_ref,
    final_ref,
    dlogits_ref,
    dresidual_ref,
):
    frames = residual_ref.shape[0]
    live = live_column(lengths_ref, pl.program_id(0), frames)
    values = residual_ref[...]
    centred = values - jnp.mean(values, axis=-1, keepdims=True)
    spread = jnp.mean(centred * centred, axis=-1, keepdims=True)
    inverse = lax.rsqrt(spread + 1e-05)
    unit = centred * inverse
    final = (unit * gain_ref[...]).astype(BF16)
    final_ref[...] = final

    def log_softmax(logits):
        shifted = logits - jnp.max(logits, axis=-1, keepdims=True)
        return shifted - jnp.log(jnp.sum(jnp.exp(shifted), axis=-1, keepdims=True))

    target = jnp.exp(log_softmax((kept_ref[0] + got_ref[0]) * (1.0 / TEACHERS)))
    logp = log_softmax(dot(final, head_ref[...]))
    cross = -jnp.sum(target * logp, axis=-1, keepdims=True)
    loss_ref[...] = jnp.broadcast_to(jnp.sum(cross * live, axis=0, keepdims=True), (1, 1, LANES))
    weight = jnp.sum(target, axis=-1, keepdims=True)
    dlogits = ((jnp.exp(logp) * weight - target) * live).astype(BF16)
    dlogits_ref[...] = dlogits
    dunit = dot(dlogits, head_ref[...], 1, 1) * gain_ref[...]
    average = jnp.mean(dunit, axis=-1, keepdims=True)
    along = jnp.mean(dunit * unit, axis=-1, keepdims=True)
    dresidual_ref[...] = (inverse * (dunit - average - unit * along)).astype(BF16)


def top(lengths, residual, gain, head, kept, got):
    rows, model = residual.shape
    utterances, frames, symbols = kept.shape
    per_row = pl.BlockSpec((frames, model), lambda i: (i, 0))
    sums = pl.BlockSpec((1, frames, symbols), lambda i: (i, 0, 0))
    return pl.pallas_call(
        top_kernel,
        grid=(utterances,),
        out_shape=(
            jax.ShapeDtypeStruct((utterances, 1, LANES), F32),
            jax.ShapeDtypeStruct((rows, model), BF16),
            jax.ShapeDtypeStruct((rows, symbols), BF16),
            jax.ShapeDtypeStruct((rows, model), BF16),
        ),
        in_specs=[SMEM_SPEC, per_row, fixed(1, model), fixed(model, symbols), sums, sums],
        out_specs=(
            pl.BlockSpec((1, 1, LANES), lambda i: (i, 0, 0)),
            per_row,
            pl.BlockSpec((frames, symbols), lambda i: (i, 0)),
            per_row,
        ),
        compiler_params=params(),
        cost_estimate=cost(5),
        name="top",
    )(lengths, residual, gain, head, kept, got)


def outer_kernel(
    own_ref,
    active_ref,
    dresidual_ref,
    final_ref,
    dlogits_ref,
    send_ref,
    keep_ref,
    update_ref,
    head_ref,
):
    core, place = own_ref[0], own_ref[1]
    _, places, rows, _ = keep_ref.shape
    half_out = update_ref.shape[1] // 2
    half_head = head_ref.shape[1] // 2
    update_ref[...] = dot(active_ref[...], dresidual_ref[...], 0, 0)
    head_ref[...] = dot(final_ref[...], dlogits_ref[...], 0, 0)
    for index in range(places):
        piece = index ^ (place & (places - 1))
        for side, target in ((core, keep_ref), (1 - core, send_ref)):
            here = pl.ds(pl.multiple_of(index * 2 * rows + side * rows, rows), rows)
            for group in range(2):
                target[group, piece, :, :half_out] = update_ref[
                    here, group * half_out : (group + 1) * half_out
                ].astype(BF16)
                target[group, piece, :, half_out:] = head_ref[
                    here, group * half_head : (group + 1) * half_head
                ].astype(BF16)


def outer(own, active, dresidual, final, dlogits):
    steps = 4
    rows, model = active.shape
    symbols = dlogits.shape[1]
    places = PLACES // steps
    block = model // steps
    piece = (model // (2 * PLACES), (model + symbols) // 2)
    shape = jax.ShapeDtypeStruct((2, PLACES) + piece, BF16)
    out = pl.BlockSpec(
        (2, places) + piece, lambda i, own_ref: (0, i ^ (own_ref[1] // places), 0, 0)
    )
    column = pl.BlockSpec((rows, block), lambda i, own_ref: (0, i))
    return pl.pallas_call(
        outer_kernel,
        out_shape=(shape, shape),
        grid_spec=pltpu.PrefetchScalarGridSpec(
            num_scalar_prefetch=1,
            grid=(steps,),
            in_specs=[column, fixed(rows, model), column, fixed(rows, symbols)],
            out_specs=(out, out),
            scratch_shapes=[pltpu.VMEM((block, model), F32), pltpu.VMEM((block, symbols), F32)],
        ),
        compiler_params=params(),
        cost_estimate=cost(5),
        name="outer",
    )(own, active, dresidual, final, dlogits)


def inner_kernel(
    own_ref,
    lengths_ref,
    dresidual_ref,
    out_weight_ref,
    slope_ref,
    gated_ref,
    gate_ref,
    turned_ref,
    depth_ref,
    send_ref,
    keep_ref,
    dconv_ref,
    pad_ref,
    dvalue_ref,
    dgate_ref,
    product_ref,
):
    utterances = pad_ref.shape[1]
    frames = pad_ref.shape[2] - 2 * MARGIN

    @pl.when(pl.program_id(0) == 0)
    def _():
        clear_margins(pad_ref)

    for utterance in range(utterances):
        rows = slice(utterance * frames, (utterance + 1) * frames)
        dconv = dot(dresidual_ref[rows, :], out_weight_ref[...], 1, 1) * slope_ref[rows, :]
        dconv_ref[rows, :] = dconv
        for lane in range(WIDE // LANES):
            pad_ref[lane, utterance, MARGIN : MARGIN + frames, :] = dconv[
                :, lane * LANES : (lane + 1) * LANES
            ]

    for lane in range(WIDE // LANES):
        columns = slice(lane * LANES, (lane + 1) * LANES)

        def one(utterance, carry, lane=lane, columns=columns):
            for start in range(0, frames, TILE):
                rows = pl.ds(pl.multiple_of(utterance * frames + start, TILE), TILE)
                position = lax.broadcasted_iota(jnp.int32, (TILE, 1), 0) + start
                live = (position < lengths_ref[utterance]).astype(F32)
                dgated = convolve(pad_ref, lane, utterance, start, depth_ref, True) * live
                gate = gate_ref[rows, columns]
                dvalue_ref[rows, columns] = (dgated * gate).astype(BF16)
                dgate_ref[rows, columns] = (dgated * gated_ref[rows, columns] * (1.0 - gate)).astype(
                    BF16
                )
            return carry

        lax.fori_loop(0, utterances, one, 0)

    for group, source in ((0, dvalue_ref), (1, dgate_ref)):
        product_ref[...] = dot(turned_ref[...], source[...])
        write_pieces(own_ref, product_ref, send_ref, keep_ref, group)


def inner(own, lengths, dresidual, weight_out, slope, gated, gate, turned, depth, chunk, utterances):
    model, rows = turned.shape
    frames = rows // utterances
    steps = model // WIDE // CHUNKS
    first = chunk * steps
    column = pl.BlockSpec((rows, WIDE), lambda i: (0, first + i))
    piece = (2, PLACES, model // (2 * PLACES))
    shape = jax.ShapeDtypeStruct(piece + (steps * WIDE,), BF16)
    out = pl.BlockSpec(piece + (WIDE,), lambda i: (0, 0, 0, i))
    return pl.pallas_call(
        inner_kernel,
        grid=(steps,),
        out_shape=(shape, shape, jax.ShapeDtypeStruct((rows, steps * WIDE), F32)),
        in_specs=[
            SMEM_SPEC,
            SMEM_SPEC,
            fixed(rows, model),
            pl.BlockSpec((WIDE, model), lambda i: (first + i, 0)),
            column,
            column,
            column,
            fixed(model, rows),
            pl.BlockSpec((depth.shape[0], WIDE), lambda i: (0, first + i)),
        ],
        out_specs=(out, out, pl.BlockSpec((rows, WIDE), lambda i: (0, i))),
        scratch_shapes=[
            pltpu.VMEM((WIDE // LANES, utterances, frames + 2 * MARGIN, LANES), F32),
            pltpu.VMEM((rows, WIDE), BF16),
            pltpu.VMEM((rows, WIDE), BF16),
            pltpu.VMEM((model, WIDE), F32),
        ],
        compiler_params=params(),
        cost_estimate=cost(11),
        name="inner",
    )(own, lengths, dresidual, weight_out, slope, gated, gate, turned, depth)


def taps_kernel(lengths_ref, gated_ref, dconv_ref, out_ref, pad_ref, sums_ref):
    utterances = pad_ref.shape[1]
    frames = pad_ref.shape[2] - 2 * MARGIN
    taps = out_ref.shape[0] - 1
    valid = lengths_ref[0]
    for utterance in range(1, utterances):
        valid = valid + lengths_ref[utterance]

    @pl.when(pl.program_id(0) == 0)
    def _():
        clear_margins(pad_ref)

    for lane in range(WIDE // LANES):
        columns = slice(lane * LANES, (lane + 1) * LANES)
        for utterance in range(utterances):
            rows = slice(utterance * frames, (utterance + 1) * frames)
            pad_ref[lane, utterance, MARGIN : MARGIN + frames, :] = gated_ref[rows, columns]
        sums_ref[...] = jnp.zeros_like(sums_ref)

        def one(utterance, carry, lane=lane, columns=columns):
            for start in range(0, frames, TILE):
                rows = pl.ds(pl.multiple_of(utterance * frames + start, TILE), TILE)
                dconv = dconv_ref[rows, columns]
                for tap, view in shifted_views(pad_ref, lane, utterance, start, taps):
                    sums_ref[tap] += jnp.sum((view * dconv).reshape(TILE // 8, 8, LANES), axis=0)
            return carry

        lax.fori_loop(0, utterances, one, 0)
        out_ref[:taps, columns] = jnp.sum(sums_ref[...], axis=1)
    out_ref[taps:, :] = jnp.zeros((1, WIDE), F32) + valid.astype(F32)


def tap_sums(lengths, gated, dconv, taps, chunk, utterances):
    rows, width = dconv.shape
    steps = width // WIDE
    first = chunk * steps
    return pl.pallas_call(
        taps_kernel,
        grid=(steps,),
        out_shape=jax.ShapeDtypeStruct((taps + 1, width), F32),
        in_specs=[
            SMEM_SPEC,
            pl.BlockSpec((rows, WIDE), lambda i: (0, first + i)),
            pl.BlockSpec((rows, WIDE), lambda i: (0, i)),
        ],
        out_specs=pl.BlockSpec((taps + 1, WIDE), lambda i: (0, i)),
        scratch_shapes=[
            pltpu.VMEM((WIDE // LANES, utterances, rows // utterances + 2 * MARGIN, LANES), F32),
            pltpu.VMEM((taps, 8, LANES), F32),
        ],
        compiler_params=params(),
        cost_estimate=cost(1),
        name="taps",
    )(lengths, gated, dconv)


def gain_row(weight, grad):
    terms = weight.astype(F32) * grad
    high = terms.astype(BF16)
    low = (terms - high.astype(F32)).astype(BF16)
    ones = jnp.ones((8, terms.shape[1]), BF16)
    return (dot(ones, high, 1, 1) + dot(ones, low, 1, 1))[0:1, :]


def write_rows(own_ref, step, piece_refs, group, scale, targets):
    mine_ref, other_ref = piece_refs
    places, rows = mine_ref.shape[1:3]
    core, place = own_ref[0], own_ref[1]
    for index in range(places):
        piece = index ^ (place & (places - 1))
        for side, source in ((core, mine_ref), (1 - core, other_ref)):
            here = pl.ds(pl.multiple_of(index * 2 * rows + side * rows, rows), rows)
            for target, there, first, width in targets:
                target[here, there : there + width] = (
                    source[group, piece, :, first : first + width].astype(F32) * scale
                )


def unpack_top_kernel(
    utts,
    own_ref,
    small_ref,
    mine_ref,
    other_ref,
    head_ref,
    gain_ref,
    losses_ref,
    wout_ref,
    dhead_ref,
    dgain_ref,
    depth_ref,
    loss_ref,
):
    taps = depth_ref.shape[0]
    scale = utts / small_ref[taps:, 0:1]
    half_out = wout_ref.shape[1] // 2
    half_head = dhead_ref.shape[1] // 2
    for group in range(2):
        targets = (
            (wout_ref, group * half_out, 0, half_out),
            (dhead_ref, group * half_head, half_out, half_head),
        )
        write_rows(own_ref, pl.program_id(0), (mine_ref, other_ref), group, scale, targets)
    dgain_ref[...] = gain_row(head_ref[...], dhead_ref[...]) / gain_ref[...]
    depth_ref[...] = small_ref[:taps, :] * scale
    loss_ref[...] = losses_ref[...] * scale[None]


def unpack_top(utts, own, small, mine, other, head, gain, losses, width_out):
    steps = 4
    model, symbols = head.shape
    rows = model // steps
    taps = small.shape[0] - 1
    places = PLACES // steps
    row = pl.BlockSpec((1, rows), lambda i, own_ref: (0, i))
    piece = pl.BlockSpec(
        (2, places) + mine.shape[2:], lambda i, own_ref: (0, i ^ (own_ref[1] // places), 0, 0)
    )

    def block(width):
        return pl.BlockSpec((rows, width), lambda i, own_ref: (i, 0))

    return pl.pallas_call(
        functools.partial(unpack_top_kernel, utts),
        out_shape=(
            jax.ShapeDtypeStruct((model, width_out), F32),
            jax.ShapeDtypeStruct((model, symbols), F32),
            jax.ShapeDtypeStruct((1, model), F32),
            jax.ShapeDtypeStruct((taps, model), F32),
            jax.ShapeDtypeStruct(losses.shape, F32),
        ),
        grid_spec=pltpu.PrefetchScalarGridSpec(
            num_scalar_prefetch=1,
            grid=(steps,),
            in_specs=[
                fixed(*small.shape),
                piece,
                piece,
                block(symbols),
                row,
                fixed(*losses.shape),
            ],
            out_specs=(
                block(width_out),
                block(symbols),
                row,
                fixed(taps, model),
                fixed(*losses.shape),
            ),
        ),
        compiler_params=params(),
        cost_estimate=cost(5),
        name="unpack_top",
    )(own, small, mine, other, head, gain, losses)


def unpack_inner_kernel(
    utts, last, own_ref, small_ref, mine_ref, other_ref, weight_ref, gain_ref, *refs
):
    win_ref, dgain_ref = refs[-2:]
    scale = utts / small_ref[small_ref.shape[0] - 1 :, 0:1]
    targets = ((win_ref, 0, 0, win_ref.shape[1]),)
    write_rows(own_ref, pl.program_id(0), (mine_ref, other_ref), 0, scale, targets)
    row = gain_row(weight_ref[...], win_ref[...])

    @pl.when(pl.program_id(1) == 0)
    def _():
        dgain_ref[...] = row + refs[1][...] if len(refs) > 2 else row

    @pl.when(pl.program_id(1) == 1)
    def _():
        total = dgain_ref[...] + row
        dgain_ref[...] = total / gain_ref[...] if last else total


def unpack_inner(utts, own, small, mine, other, weight, gain, chunk, before):
    steps = 2
    model, width = weight.shape
    rows = model // steps
    wide = mine.shape[3]
    places = PLACES // steps
    row = pl.BlockSpec((1, rows), lambda i, j, own_ref: (0, i))
    block = pl.BlockSpec((rows, wide), lambda i, j, own_ref: (i, j * CHUNKS + chunk))
    piece = pl.BlockSpec(
        (1, places) + mine.shape[2:], lambda i, j, own_ref: (j, i ^ (own_ref[1] // places), 0, 0)
    )
    return pl.pallas_call(
        functools.partial(unpack_inner_kernel, utts, chunk == CHUNKS - 1),
        out_shape=(
            jax.ShapeDtypeStruct((model, width), F32),
            jax.ShapeDtypeStruct((1, model), F32),
        ),
        grid_spec=pltpu.PrefetchScalarGridSpec(
            num_scalar_prefetch=1,
            grid=(steps, 2),
            in_specs=[
                pl.BlockSpec(small.shape, lambda i, j, own_ref: (0, 0)),
                piece,
                piece,
                block,
                row,
            ]
            + ([pl.BlockSpec(memory_space=pl.ANY), row] if before else []),
            out_specs=(block, row),
        ),
        input_output_aliases={6: 0} if before else {},
        compiler_params=params(),
        cost_estimate=cost(4),
        name="unpack_inner",
    )(own, small, mine, other, weight, gain, *before)


def on_device(
    features,
    teacher_logits,
    lengths,
    gain_conv,
    weight_in,
    weight_depth,
    weight_out,
    gain_out,
    head_weight,
):
    count = 1
    for axis in ("member", "near", FAR, REST, CORE):
        count *= lax.axis_size(axis)
    member = lax.axis_index("member").astype(jnp.int32)[None]
    core = lax.axis_index(CORE).astype(jnp.int32)
    orders = (("near", "member"), ("member", "near"))
    owns = [jnp.stack([core, own_place(order)]) for order in orders]
    taps, model = weight_depth.shape
    utterances, frames, _ = features.shape
    utts = float(utterances * count)
    tie = lax.optimization_barrier

    give, kept = teacher_sums(member, teacher_logits, utterances)
    got = exchange(give, "member")
    flat = features.reshape(utterances * frames, model)
    turned, gated, gate, slope, active, residual = forward(
        lengths, flat, gain_conv[None], weight_in, weight_depth, weight_out, utterances
    )
    losses, final, dlogits, dresidual = top(
        lengths, residual, gain_out[None], head_weight, kept, got
    )

    line = Line()

    def products(name, chunk):
        nonlocal dresidual
        dresidual = line.before_kernel(dresidual)
        send, keep, dconv = inner(
            owns[chunk],
            lengths,
            dresidual,
            weight_out,
            slope,
            gated,
            gate,
            turned,
            weight_depth,
            chunk,
            utterances,
        )
        line.begin(name, send, keep, orders[chunk])
        line.put(name + "_conv", dconv)

    def tap_rows(name, chunk):
        dconv = line.before_kernel(line.values[name + "_conv"])
        line.put(name + "_taps", tap_sums(lengths, gated, dconv, taps, chunk, utterances))

    send, keep = outer(owns[1], active, dresidual, final, dlogits)
    send, keep, dresidual = tie((send, keep, dresidual))
    line.begin("top", send, keep, orders[1])
    products("in0", 0)
    line.step("top", False)
    products("in1", 1)
    line.step("top")
    line.step("in0")
    line.step("in1")
    tap_rows("in0", 0)
    tap_rows("in1", 1)
    small = jnp.concatenate([line.values["in0_taps"], line.values["in1_taps"]], axis=1)
    line.begin_small("small", small)
    written = {}

    def write_top():
        mine, other = line.values["top"]
        *rest, written["losses"] = unpack_top(
            utts,
            owns[1],
            line.values["small"],
            line.after_last(mine),
            other,
            head_weight,
            gain_out[None],
            losses,
            weight_out.shape[1],
        )
        written["out"], written["head"], by_head, written["depth"] = rest
        line.put("by_head", by_head)

    def write_in(chunk, name):
        mine, other = line.values[name]
        before = (written["in"], line.values["by_in"]) if chunk else ()
        written["in"], by_in = unpack_inner(
            utts,
            owns[chunk],
            line.values["small"],
            line.after_last(mine),
            other,
            weight_in,
            gain_conv[None],
            chunk,
            before,
        )
        line.put("by_in", by_in)

    writes = {
        "write_top": write_top,
        "write0": functools.partial(write_in, 0, "in0"),
        "write1": functools.partial(write_in, 1, "in1"),
    }
    for name in ORDER:
        if name in writes:
            writes[name]()
        else:
            line.step(name)
    return (
        line.values["by_in"].reshape(model),
        written["in"],
        written["depth"],
        written["out"],
        line.values["by_head"].reshape(model),
        written["head"],
        written["losses"][:, 0, 0],
    )


def solution(mesh):
    members, others = mesh.devices.shape
    near, cores = 2, 2
    far = 2 * PLACES // (members * near)
    rest = others // (far * near * cores)
    split = jax.sharding.Mesh(
        mesh.devices.reshape(members, rest, far, near, cores),
        ("member", REST, FAR, "near", CORE),
    )
    dp = (REST, FAR, "near", CORE)
    in_specs = (
        P(dp + ("member",), None, None),
        P("member", dp, None, None),
        P(dp + ("member",)),
        P(),
        P(),
        P(),
        P(),
        P(),
        P(),
    )
    out_specs = (P(), P(), P(), P(), P(), P(), P(dp + ("member",)))
    return jax.shard_map(
        on_device, mesh=split, in_specs=in_specs, out_specs=out_specs, check_vma=False
    )
```

```python
import functools

import jax
import jax.numpy as jnp
from jax import lax
from jax.experimental import pallas as pl
from jax.experimental.pallas import tpu as pltpu
from jax.sharding import PartitionSpec as P

TEACHERS = 4
PLACES = 8
WIDE = 256
LANES = 128
TILE = 128
MARGIN = 16
CHUNKS = 2
VMEM = 56 << 20
SMEM_SPEC = pl.BlockSpec(memory_space=pltpu.SMEM)
F32 = jnp.float32
BF16 = jnp.bfloat16


def params():
    return pltpu.CompilerParams(vmem_limit_bytes=VMEM)


def cost(microseconds):
    return pl.CostEstimate(flops=int(microseconds * 1.15e9), bytes_accessed=1 << 20, transcendentals=0)


def dot(left, right, left_axis=1, right_axis=0):
    return lax.dot_general(
        left, right, (((left_axis,), (right_axis,)), ((), ())), preferred_element_type=F32
    )


def fixed(*shape):
    return pl.BlockSpec(shape, lambda i, *_: (0,) * len(shape))


FAR = "far"
REST = "rest"
CORE = "core"
SMALL_STEPS = ((CORE, 1), ("member", 1), ("near", 1), (FAR, 1), (FAR, 2))


def exchange(values, axis, bit=1):
    size = lax.axis_size(axis)
    return lax.ppermute(values, axis, [(i, i ^ bit) for i in range(size)])


def add(own, other):
    return (own.astype(F32) + other.astype(F32)).astype(own.dtype)


def own_place(order):
    place = lax.axis_index(order[0]) * 4 + lax.axis_index(order[1]) * 2 + (lax.axis_index(FAR) & 1)
    return place.astype(jnp.int32)


def over_rest(values):
    return lax.psum(values, REST) if lax.axis_size(REST) > 1 else values


class Line:
    def __init__(self):
        self.values = {}
        self.pending = {}
        self.steps = {}
        self.last = None

    def after_last(self, value):
        if self.last is not None:
            value, self.values[self.last] = lax.optimization_barrier(
                (value, self.values[self.last])
            )
        return value

    def before_kernel(self, value):
        value = self.after_last(value)
        if self.last in self.steps and self.last not in self.pending:
            self.start(self.last)
        return value

    def put(self, name, value):
        self.values[name] = value
        self.last = name

    def begin(self, name, send, keep, order):
        self.values[name] = keep
        self.pending[name] = exchange(send, CORE)
        halve, gather = [("halve", axis) for axis in order], [("gather", axis) for axis in order]
        self.steps[name] = (
            [("add", CORE)]
            + halve
            + [("halve", FAR), ("double", FAR), ("gather", FAR)]
            + gather[::-1]
            + [("done", CORE)]
        )

    def begin_small(self, name, value):
        self.values[name] = value
        self.steps[name] = [("sum", step) for step in SMALL_STEPS]
        self.start(name)

    def start(self, name):
        if not self.steps[name]:
            return
        kind, axis = self.steps[name][0]
        values = self.values[name]
        if kind == "halve":
            self.pending[name] = exchange(values[:, values.shape[1] // 2 :], axis)
        elif kind == "double":
            self.pending[name] = exchange(values, axis, 2)
        elif kind == "sum":
            self.pending[name] = exchange(values, *axis)
        else:
            self.pending[name] = exchange(values, axis)

    def meet(self, *names):
        met = lax.optimization_barrier(tuple(self.values[name] for name in names))
        self.values.update(zip(names, met))
        for name in names:
            if name in self.steps and name not in self.pending:
                self.start(name)

    def step(self, name, start=True, tied=False):
        kind, _ = self.steps[name].pop(0)
        got = self.pending.pop(name)
        if tied:
            got = self.after_last(got)
        own = self.values[name]
        if kind == "halve":
            own = own[:, : got.shape[1]]
        if kind == "gather":
            result = jnp.concatenate([own, got], axis=1)
        elif kind == "done":
            result = (own, got)
        else:
            result = add(own, got)
        if kind == "double" or (kind == "sum" and not self.steps[name]):
            result = over_rest(result)
        self.put(name, result)
        if start:
            self.start(name)


def write_pieces(own_ref, product, send_ref, keep_ref, group):
    rows = keep_ref.shape[-2]
    core, place = own_ref[0], own_ref[1]

    def one(piece, carry):
        base = (piece ^ place) * (2 * rows)
        kept = pl.multiple_of(base + core * rows, rows)
        sent = pl.multiple_of(base + (1 - core) * rows, rows)
        keep_ref[group, piece] = product[pl.ds(kept, rows), :].astype(BF16)
        send_ref[group, piece] = product[pl.ds(sent, rows), :].astype(BF16)
        return carry

    lax.fori_loop(0, keep_ref.shape[1], one, 0)


def teacher_kernel(member_ref, logits_ref, give_ref, keep_ref, *, own_count):
    step = pl.program_id(0)
    total = None
    for teacher in range(logits_ref.shape[0]):
        logits = logits_ref[teacher, 0].astype(F32)
        shifted = logits - jnp.max(logits, axis=-1, keepdims=True)
        logp = shifted - jnp.log(jnp.sum(jnp.exp(shifted), axis=-1, keepdims=True))
        total = logp if total is None else total + logp

    @pl.when(step < own_count)
    def _():
        give_ref[0] = total

    @pl.when(step >= own_count)
    def _():
        keep_ref[0] = total


def teacher_sums(member, logits, own_count):
    teachers, utterances, frames, symbols = logits.shape
    shape = jax.ShapeDtypeStruct((own_count, frames, symbols), F32)

    def source(i, member_ref):
        mine = member_ref[0] * own_count
        theirs = (1 - member_ref[0]) * own_count
        return (0, jnp.where(i < own_count, theirs + i, mine + i - own_count), 0, 0)

    return pl.pallas_call(
        functools.partial(teacher_kernel, own_count=own_count),
        out_shape=(shape, shape),
        grid_spec=pltpu.PrefetchScalarGridSpec(
            num_scalar_prefetch=1,
            grid=(2 * own_count,),
            in_specs=[pl.BlockSpec((teachers, 1, frames, symbols), source)],
            out_specs=(
                pl.BlockSpec(
                    (1, frames, symbols), lambda i, _: (jnp.minimum(i, own_count - 1), 0, 0)
                ),
                pl.BlockSpec(
                    (1, frames, symbols), lambda i, _: (jnp.maximum(i - own_count, 0), 0, 0)
                ),
            ),
        ),
        compiler_params=params(),
        cost_estimate=cost(4),
        name="teachers",
    )(member, logits)


def live_column(lengths_ref, utterance, frames):
    position = lax.broadcasted_iota(jnp.int32, (frames, 1), 0)
    return (position < lengths_ref[utterance]).astype(F32)


def clear_margins(pad_ref):
    frames = pad_ref.shape[2] - 2 * MARGIN
    zeros = jnp.zeros(pad_ref.shape[:2] + (MARGIN, LANES), F32)
    pad_ref[:, :, :MARGIN, :] = zeros
    pad_ref[:, :, MARGIN + frames :, :] = zeros


def shifted_views(pad_ref, lane, utterance, start, taps):
    first = MARGIN - taps // 2
    for phase in range(8):
        offsets = [offset for offset in range(first, first + taps) if offset % 8 == phase]
        if not offsets:
            continue
        low = offsets[0]
        span = offsets[-1] - low + TILE
        view = pad_ref[lane, utterance, start + low : start + low + span, :]
        for offset in offsets:
            yield offset - first, view[offset - low : offset - low + TILE]


def convolve(pad_ref, lane, utterance, start, depth_ref, flipped):
    taps = depth_ref.shape[0]
    columns = slice(lane * LANES, (lane + 1) * LANES)
    total = jnp.zeros((TILE, LANES), F32)
    for tap, view in shifted_views(pad_ref, lane, utterance, start, taps):
        row = taps - 1 - tap if flipped else tap
        total = total + view * depth_ref[row : row + 1, columns]
    return total


def forward_kernel(
    lengths_ref,
    features_ref,
    gain_ref,
    value_weight_ref,
    gate_weight_ref,
    depth_ref,
    out_weight_ref,
    turned_ref,
    gated_ref,
    gate_ref,
    slope_ref,
    active_ref,
    residual_ref,
    normed_ref,
    pad_ref,
):
    utterances = pad_ref.shape[1]
    frames = pad_ref.shape[2] - 2 * MARGIN

    @pl.when(pl.program_id(0) == 0)
    def _():
        values = features_ref[...].astype(F32)
        centred = values - jnp.mean(values, axis=-1, keepdims=True)
        spread = jnp.mean(centred * centred, axis=-1, keepdims=True)
        normed = centred * lax.rsqrt(spread + 1e-05) * gain_ref[...]
        normed_ref[...] = normed.astype(BF16)
        turned_ref[...] = normed.T.astype(BF16)
        residual_ref[...] = values
        clear_margins(pad_ref)

    for utterance in range(utterances):
        rows = slice(utterance * frames, (utterance + 1) * frames)
        normed = normed_ref[rows, :]
        gate = jax.nn.sigmoid(dot(normed, gate_weight_ref[...]))
        gated = dot(normed, value_weight_ref[...]) * gate
        gated = gated * live_column(lengths_ref, utterance, frames)
        gate_ref[rows, :] = gate
        gated_ref[rows, :] = gated
        for lane in range(WIDE // LANES):
            pad_ref[lane, utterance, MARGIN : MARGIN + frames, :] = gated[
                :, lane * LANES : (lane + 1) * LANES
            ]

    for lane in range(WIDE // LANES):
        columns = slice(lane * LANES, (lane + 1) * LANES)

        def one(utterance, carry, lane=lane, columns=columns):
            for start in range(0, frames, TILE):
                rows = pl.ds(pl.multiple_of(utterance * frames + start, TILE), TILE)
                convolved = convolve(pad_ref, lane, utterance, start, depth_ref, False)
                squash = jax.nn.sigmoid(convolved)
                active_ref[rows, columns] = (convolved * squash).astype(BF16)
                slope_ref[rows, columns] = squash * (1.0 + convolved * (1.0 - squash))
            return carry

        lax.fori_loop(0, utterances, one, 0)

    residual_ref[...] += dot(active_ref[...], out_weight_ref[...])


def forward(lengths, features, gain, weight_in, depth, weight_out, utterances):
    rows, model = features.shape
    frames = rows // utterances
    steps = model // WIDE
    column = pl.BlockSpec((rows, WIDE), lambda i: (0, i))
    wide = jax.ShapeDtypeStruct((rows, model), F32)
    narrow = jax.ShapeDtypeStruct((rows, model), BF16)
    return pl.pallas_call(
        forward_kernel,
        grid=(steps,),
        out_shape=(jax.ShapeDtypeStruct((model, rows), BF16), wide, wide, wide, narrow, wide),
        in_specs=[
            SMEM_SPEC,
            fixed(rows, model),
            fixed(1, model),
            pl.BlockSpec((model, WIDE), lambda i: (0, i)),
            pl.BlockSpec((model, WIDE), lambda i: (0, steps + i)),
            pl.BlockSpec((depth.shape[0], WIDE), lambda i: (0, i)),
            pl.BlockSpec((WIDE, model), lambda i: (i, 0)),
        ],
        out_specs=(fixed(model, rows), column, column, column, column, fixed(rows, model)),
        scratch_shapes=[
            pltpu.VMEM((rows, model), BF16),
            pltpu.VMEM((WIDE // LANES, utterances, frames + 2 * MARGIN, LANES), F32),
        ],
        compiler_params=params(),
        cost_estimate=cost(15),
        name="forward",
    )(lengths, features, gain, weight_in, weight_in, depth, weight_out)


def top_kernel(
    lengths_ref,
    residual_ref,
    gain_ref,
    head_ref,
    kept_ref,
    got_ref,
    loss_ref,
    final_ref,
    dlogits_ref,
    dresidual_ref,
):
    frames = residual_ref.shape[0]
    live = live_column(lengths_ref, pl.program_id(0), frames)
    values = residual_ref[...]
    centred = values - jnp.mean(values, axis=-1, keepdims=True)
    spread = jnp.mean(centred * centred, axis=-1, keepdims=True)
    inverse = lax.rsqrt(spread + 1e-05)
    unit = centred * inverse
    final = (unit * gain_ref[...]).astype(BF16)
    final_ref[...] = final

    def log_softmax(logits):
        shifted = logits - jnp.max(logits, axis=-1, keepdims=True)
        return shifted - jnp.log(jnp.sum(jnp.exp(shifted), axis=-1, keepdims=True))

    target = jnp.exp(log_softmax((kept_ref[0] + got_ref[0]) * (1.0 / TEACHERS)))
    logp = log_softmax(dot(final, head_ref[...]))
    cross = -jnp.sum(target * logp, axis=-1, keepdims=True)
    loss_ref[...] = jnp.broadcast_to(jnp.sum(cross * live, axis=0, keepdims=True), (1, 1, LANES))
    weight = jnp.sum(target, axis=-1, keepdims=True)
    dlogits = ((jnp.exp(logp) * weight - target) * live).astype(BF16)
    dlogits_ref[...] = dlogits
    dunit = dot(dlogits, head_ref[...], 1, 1) * gain_ref[...]
    average = jnp.mean(dunit, axis=-1, keepdims=True)
    along = jnp.mean(dunit * unit, axis=-1, keepdims=True)
    dresidual_ref[...] = (inverse * (dunit - average - unit * along)).astype(BF16)


def top(lengths, residual, gain, head, kept, got):
    rows, model = residual.shape
    utterances, frames, symbols = kept.shape
    per_row = pl.BlockSpec((frames, model), lambda i: (i, 0))
    sums = pl.BlockSpec((1, frames, symbols), lambda i: (i, 0, 0))
    return pl.pallas_call(
        top_kernel,
        grid=(utterances,),
        out_shape=(
            jax.ShapeDtypeStruct((utterances, 1, LANES), F32),
            jax.ShapeDtypeStruct((rows, model), BF16),
            jax.ShapeDtypeStruct((rows, symbols), BF16),
            jax.ShapeDtypeStruct((rows, model), BF16),
        ),
        in_specs=[SMEM_SPEC, per_row, fixed(1, model), fixed(model, symbols), sums, sums],
        out_specs=(
            pl.BlockSpec((1, 1, LANES), lambda i: (i, 0, 0)),
            per_row,
            pl.BlockSpec((frames, symbols), lambda i: (i, 0)),
            per_row,
        ),
        compiler_params=params(),
        cost_estimate=cost(5),
        name="top",
    )(lengths, residual, gain, head, kept, got)


def outer_kernel(
    own_ref, active_ref, dresidual_ref, final_ref, dlogits_ref, send_ref, keep_ref, product_ref
):
    width = dresidual_ref.shape[1]
    product_ref[:, :width] = dot(active_ref[...], dresidual_ref[...], 0, 0)
    product_ref[:, width:] = dot(final_ref[...], dlogits_ref[...], 0, 0)
    write_pieces(own_ref, product_ref, send_ref, keep_ref, 0)


def outer(own, active, dresidual, final, dlogits):
    rows, model = active.shape
    half_out = dresidual.shape[1] // 2
    half_head = dlogits.shape[1] // 2
    width = half_out + half_head
    piece = (PLACES, model // (2 * PLACES), width)
    shape = jax.ShapeDtypeStruct((2,) + piece, BF16)
    out = pl.BlockSpec((1,) + piece, lambda i: (i, 0, 0, 0))
    return pl.pallas_call(
        outer_kernel,
        grid=(2,),
        out_shape=(shape, shape),
        in_specs=[
            SMEM_SPEC,
            fixed(rows, model),
            pl.BlockSpec((rows, half_out), lambda i: (0, i)),
            fixed(rows, model),
            pl.BlockSpec((rows, half_head), lambda i: (0, i)),
        ],
        out_specs=(out, out),
        scratch_shapes=[pltpu.VMEM((model, width), F32)],
        compiler_params=params(),
        cost_estimate=cost(5),
        name="outer",
    )(own, active, dresidual, final, dlogits)


def inner_kernel(
    own_ref,
    lengths_ref,
    dresidual_ref,
    out_weight_ref,
    slope_ref,
    gated_ref,
    gate_ref,
    turned_ref,
    depth_ref,
    send_ref,
    keep_ref,
    dconv_ref,
    pad_ref,
    dvalue_ref,
    dgate_ref,
    product_ref,
):
    utterances = pad_ref.shape[1]
    frames = pad_ref.shape[2] - 2 * MARGIN

    @pl.when(pl.program_id(0) == 0)
    def _():
        clear_margins(pad_ref)

    for utterance in range(utterances):
        rows = slice(utterance * frames, (utterance + 1) * frames)
        dconv = dot(dresidual_ref[rows, :], out_weight_ref[...], 1, 1) * slope_ref[rows, :]
        dconv_ref[rows, :] = dconv
        for lane in range(WIDE // LANES):
            pad_ref[lane, utterance, MARGIN : MARGIN + frames, :] = dconv[
                :, lane * LANES : (lane + 1) * LANES
            ]

    for lane in range(WIDE // LANES):
        columns = slice(lane * LANES, (lane + 1) * LANES)

        def one(utterance, carry, lane=lane, columns=columns):
            for start in range(0, frames, TILE):
                rows = pl.ds(pl.multiple_of(utterance * frames + start, TILE), TILE)
                position = lax.broadcasted_iota(jnp.int32, (TILE, 1), 0) + start
                live = (position < lengths_ref[utterance]).astype(F32)
                dgated = convolve(pad_ref, lane, utterance, start, depth_ref, True) * live
                gate = gate_ref[rows, columns]
                dvalue_ref[rows, columns] = (dgated * gate).astype(BF16)
                dgate_ref[rows, columns] = (dgated * gated_ref[rows, columns] * (1.0 - gate)).astype(
                    BF16
                )
            return carry

        lax.fori_loop(0, utterances, one, 0)

    for group, source in ((0, dvalue_ref), (1, dgate_ref)):
        product_ref[...] = dot(turned_ref[...], source[...])
        write_pieces(own_ref, product_ref, send_ref, keep_ref, group)


def inner(own, lengths, dresidual, weight_out, slope, gated, gate, turned, depth, chunk, utterances):
    model, rows = turned.shape
    frames = rows // utterances
    steps = model // WIDE // CHUNKS
    first = chunk * steps
    column = pl.BlockSpec((rows, WIDE), lambda i: (0, first + i))
    piece = (2, PLACES, model // (2 * PLACES))
    shape = jax.ShapeDtypeStruct(piece + (steps * WIDE,), BF16)
    out = pl.BlockSpec(piece + (WIDE,), lambda i: (0, 0, 0, i))
    return pl.pallas_call(
        inner_kernel,
        grid=(steps,),
        out_shape=(shape, shape, jax.ShapeDtypeStruct((rows, steps * WIDE), F32)),
        in_specs=[
            SMEM_SPEC,
            SMEM_SPEC,
            fixed(rows, model),
            pl.BlockSpec((WIDE, model), lambda i: (first + i, 0)),
            column,
            column,
            column,
            fixed(model, rows),
            pl.BlockSpec((depth.shape[0], WIDE), lambda i: (0, first + i)),
        ],
        out_specs=(out, out, pl.BlockSpec((rows, WIDE), lambda i: (0, i))),
        scratch_shapes=[
            pltpu.VMEM((WIDE // LANES, utterances, frames + 2 * MARGIN, LANES), F32),
            pltpu.VMEM((rows, WIDE), BF16),
            pltpu.VMEM((rows, WIDE), BF16),
            pltpu.VMEM((model, WIDE), F32),
        ],
        compiler_params=params(),
        cost_estimate=cost(11),
        name="inner",
    )(own, lengths, dresidual, weight_out, slope, gated, gate, turned, depth)


def taps_kernel(lengths_ref, gated_ref, *refs):
    *dconv_refs, out_ref, pad_ref, sums_ref = refs
    utterances = pad_ref.shape[1]
    frames = pad_ref.shape[2] - 2 * MARGIN
    taps = out_ref.shape[0] - 1
    step = pl.program_id(0)
    per_chunk = pl.num_programs(0) // len(dconv_refs)
    valid = lengths_ref[0]
    for utterance in range(1, utterances):
        valid = valid + lengths_ref[utterance]

    @pl.when(step == 0)
    def _():
        clear_margins(pad_ref)

    for lane in range(WIDE // LANES):
        columns = slice(lane * LANES, (lane + 1) * LANES)
        for utterance in range(utterances):
            rows = slice(utterance * frames, (utterance + 1) * frames)
            pad_ref[lane, utterance, MARGIN : MARGIN + frames, :] = gated_ref[rows, columns]

    for chunk, dconv_ref in enumerate(dconv_refs):

        @pl.when(step // per_chunk == chunk)
        def _(dconv_ref=dconv_ref):
            for lane in range(WIDE // LANES):
                columns = slice(lane * LANES, (lane + 1) * LANES)
                sums_ref[...] = jnp.zeros_like(sums_ref)

                def one(utterance, carry, lane=lane, columns=columns):
                    for start in range(0, frames, TILE):
                        rows = pl.ds(pl.multiple_of(utterance * frames + start, TILE), TILE)
                        dconv = dconv_ref[rows, columns]
                        for tap, view in shifted_views(pad_ref, lane, utterance, start, taps):
                            sums_ref[tap] += jnp.sum(
                                (view * dconv).reshape(TILE // 8, 8, LANES), axis=0
                            )
                    return carry

                lax.fori_loop(0, utterances, one, 0)
                out_ref[:taps, columns] = jnp.sum(sums_ref[...], axis=1)

    out_ref[taps:, :] = jnp.zeros((1, WIDE), F32) + valid.astype(F32)


def tap_sums(lengths, gated, dconvs, taps, utterances):
    rows, model = gated.shape
    steps = model // WIDE
    per_chunk = steps // len(dconvs)

    def part(chunk):
        low = chunk * per_chunk
        return pl.BlockSpec((rows, WIDE), lambda i: (0, jnp.clip(i - low, 0, per_chunk - 1)))

    return pl.pallas_call(
        taps_kernel,
        grid=(steps,),
        out_shape=jax.ShapeDtypeStruct((taps + 1, model), F32),
        in_specs=[SMEM_SPEC, pl.BlockSpec((rows, WIDE), lambda i: (0, i))]
        + [part(chunk) for chunk in range(len(dconvs))],
        out_specs=pl.BlockSpec((taps + 1, WIDE), lambda i: (0, i)),
        scratch_shapes=[
            pltpu.VMEM((WIDE // LANES, utterances, rows // utterances + 2 * MARGIN, LANES), F32),
            pltpu.VMEM((taps, 8, LANES), F32),
        ],
        compiler_params=params(),
        cost_estimate=cost(9),
        name="taps",
    )(lengths, gated, *dconvs)


def gain_row(weight, grad):
    terms = weight.astype(F32) * grad
    high = terms.astype(BF16)
    low = (terms - high.astype(F32)).astype(BF16)
    ones = jnp.ones((8, terms.shape[1]), BF16)
    return (dot(ones, high, 1, 1) + dot(ones, low, 1, 1))[0:1, :]


def write_rows(own_ref, step, piece_refs, group, scale, targets):
    mine_ref, other_ref = piece_refs
    places, rows = mine_ref.shape[1:3]
    core, place = own_ref[0], own_ref[1]
    for index in range(places):
        piece = index ^ (place & (places - 1))
        for side, source in ((core, mine_ref), (1 - core, other_ref)):
            here = pl.ds(pl.multiple_of(index * 2 * rows + side * rows, rows), rows)
            for target, there, first, width in targets:
                target[here, there : there + width] = (
                    source[group, piece, :, first : first + width].astype(F32) * scale
                )


def unpack_top_kernel(
    utts,
    own_ref,
    small_ref,
    mine_ref,
    other_ref,
    head_ref,
    gain_ref,
    losses_ref,
    wout_ref,
    dhead_ref,
    dgain_ref,
    depth_ref,
    loss_ref,
):
    taps = depth_ref.shape[0]
    scale = utts / small_ref[taps:, 0:1]
    half_out = wout_ref.shape[1] // 2
    half_head = dhead_ref.shape[1] // 2
    for group in range(2):
        targets = (
            (wout_ref, group * half_out, 0, half_out),
            (dhead_ref, group * half_head, half_out, half_head),
        )
        write_rows(own_ref, pl.program_id(0), (mine_ref, other_ref), group, scale, targets)
    dgain_ref[...] = gain_row(head_ref[...], dhead_ref[...]) / gain_ref[...]
    depth_ref[...] = small_ref[:taps, :] * scale
    loss_ref[...] = losses_ref[...] * scale[None]


def unpack_top(utts, own, small, mine, other, head, gain, losses, width_out):
    steps = 4
    model, symbols = head.shape
    rows = model // steps
    taps = small.shape[0] - 1
    places = PLACES // steps
    row = pl.BlockSpec((1, rows), lambda i, own_ref: (0, i))
    piece = pl.BlockSpec(
        (2, places) + mine.shape[2:], lambda i, own_ref: (0, i ^ (own_ref[1] // places), 0, 0)
    )

    def block(width):
        return pl.BlockSpec((rows, width), lambda i, own_ref: (i, 0))

    return pl.pallas_call(
        functools.partial(unpack_top_kernel, utts),
        out_shape=(
            jax.ShapeDtypeStruct((model, width_out), F32),
            jax.ShapeDtypeStruct((model, symbols), F32),
            jax.ShapeDtypeStruct((1, model), F32),
            jax.ShapeDtypeStruct((taps, model), F32),
            jax.ShapeDtypeStruct(losses.shape, F32),
        ),
        grid_spec=pltpu.PrefetchScalarGridSpec(
            num_scalar_prefetch=1,
            grid=(steps,),
            in_specs=[
                fixed(*small.shape),
                piece,
                piece,
                block(symbols),
                row,
                fixed(*losses.shape),
            ],
            out_specs=(
                block(width_out),
                block(symbols),
                row,
                fixed(taps, model),
                fixed(*losses.shape),
            ),
        ),
        compiler_params=params(),
        cost_estimate=cost(5),
        name="unpack_top",
    )(own, small, mine, other, head, gain, losses)


def unpack_inner_kernel(
    utts, last, own_ref, small_ref, mine_ref, other_ref, weight_ref, gain_ref, *refs
):
    win_ref, dgain_ref = refs[-2:]
    scale = utts / small_ref[small_ref.shape[0] - 1 :, 0:1]
    targets = ((win_ref, 0, 0, win_ref.shape[1]),)
    write_rows(own_ref, pl.program_id(0), (mine_ref, other_ref), 0, scale, targets)
    row = gain_row(weight_ref[...], win_ref[...])

    @pl.when(pl.program_id(1) == 0)
    def _():
        dgain_ref[...] = row + refs[1][...] if len(refs) > 2 else row

    @pl.when(pl.program_id(1) == 1)
    def _():
        total = dgain_ref[...] + row
        dgain_ref[...] = total / gain_ref[...] if last else total


def unpack_inner(utts, own, small, mine, other, weight, gain, chunk, before):
    steps = 2
    model, width = weight.shape
    rows = model // steps
    wide = mine.shape[3]
    places = PLACES // steps
    row = pl.BlockSpec((1, rows), lambda i, j, own_ref: (0, i))
    block = pl.BlockSpec((rows, wide), lambda i, j, own_ref: (i, j * CHUNKS + chunk))
    piece = pl.BlockSpec(
        (1, places) + mine.shape[2:], lambda i, j, own_ref: (j, i ^ (own_ref[1] // places), 0, 0)
    )
    return pl.pallas_call(
        functools.partial(unpack_inner_kernel, utts, chunk == CHUNKS - 1),
        out_shape=(
            jax.ShapeDtypeStruct((model, width), F32),
            jax.ShapeDtypeStruct((1, model), F32),
        ),
        grid_spec=pltpu.PrefetchScalarGridSpec(
            num_scalar_prefetch=1,
            grid=(steps, 2),
            in_specs=[
                pl.BlockSpec(small.shape, lambda i, j, own_ref: (0, 0)),
                piece,
                piece,
                block,
                row,
            ]
            + ([pl.BlockSpec(memory_space=pl.ANY), row] if before else []),
            out_specs=(block, row),
        ),
        input_output_aliases={6: 0} if before else {},
        compiler_params=params(),
        cost_estimate=cost(4),
        name="unpack_inner",
    )(own, small, mine, other, weight, gain, *before)


def on_device(
    features,
    teacher_logits,
    lengths,
    gain_conv,
    weight_in,
    weight_depth,
    weight_out,
    gain_out,
    head_weight,
):
    count = 1
    for axis in ("member", "near", FAR, REST, CORE):
        count *= lax.axis_size(axis)
    member = lax.axis_index("member").astype(jnp.int32)[None]
    core = lax.axis_index(CORE).astype(jnp.int32)
    orders = (("near", "member"), ("member", "near"))
    owns = [jnp.stack([core, own_place(order)]) for order in orders]
    taps, model = weight_depth.shape
    utterances, frames, _ = features.shape
    utts = float(utterances * count)
    tie = lax.optimization_barrier

    give, kept = teacher_sums(member, teacher_logits, utterances)
    got = exchange(give, "member")
    flat = features.reshape(utterances * frames, model)
    turned, gated, gate, slope, active, residual = forward(
        lengths, flat, gain_conv[None], weight_in, weight_depth, weight_out, utterances
    )
    losses, final, dlogits, dresidual = top(
        lengths, residual, gain_out[None], head_weight, kept, got
    )

    line = Line()

    def products(name, chunk):
        nonlocal dresidual
        dresidual = line.before_kernel(dresidual)
        send, keep, dconv = inner(
            owns[chunk],
            lengths,
            dresidual,
            weight_out,
            slope,
            gated,
            gate,
            turned,
            weight_depth,
            chunk,
            utterances,
        )
        line.begin(name, send, keep, orders[chunk])
        line.put(name + "_conv", dconv)

    send, keep = outer(owns[1], active, dresidual, final, dlogits)
    send, keep, dresidual = tie((send, keep, dresidual))
    line.begin("top", send, keep, orders[1])
    products("in0", 0)
    line.step("top", start=False)
    products("in1", 1)
    line.last = None
    line.step("top", start=False)
    line.step("in0", start=False, tied=True)
    line.step("in1", start=False, tied=True)
    line.meet("top", "in0", "in1", "in0_conv", "in1_conv")
    dconvs = (line.values["in0_conv"], line.values["in1_conv"])
    line.put("taps", tap_sums(lengths, gated, dconvs, taps, utterances))
    line.begin_small("small", line.values["taps"])
    line.step("in0", tied=True)
    line.step("in1", tied=True, start=False)
    line.step("top", tied=True)
    written = {}

    def write_top():
        mine, other = line.values["top"]
        *rest, written["losses"] = unpack_top(
            utts,
            owns[1],
            line.values["small"],
            mine,
            other,
            head_weight,
            gain_out[None],
            losses,
            weight_out.shape[1],
        )
        written["out"], written["head"], by_head, written["depth"] = rest
        line.put("by_head", by_head)

    def write_in(chunk, name):
        mine, other = line.values[name]
        before = (written["in"], line.values["by_in"]) if chunk else ()
        written["in"], by_in = unpack_inner(
            utts,
            owns[chunk],
            line.values["small"],
            mine,
            other,
            weight_in,
            gain_conv[None],
            chunk,
            before,
        )
        line.put("by_in", by_in)

    line.step("small")
    line.meet("in1", "small")
    line.step("small")
    line.step("in1", start=False)
    line.meet("in1", "small")
    line.step("small")
    line.step("small")
    line.step("in1", start=False)
    line.meet("in1", "small")
    line.step("small")
    line.step("in1", start=False)
    line.meet("in1", "small")
    for _ in range(4):
        line.step("top")
    line.step("in1", tied=True)
    line.step("top")
    line.step("top")
    write_top()
    while line.steps["in0"]:
        line.step("in0")
    line.step("in1")
    line.last = "by_head"
    line.step("in1", tied=True)
    write_in(0, "in0")
    line.step("in1")
    write_in(1, "in1")
    return (
        line.values["by_in"].reshape(model),
        written["in"],
        written["depth"],
        written["out"],
        line.values["by_head"].reshape(model),
        written["head"],
        written["losses"][:, 0, 0],
    )


def solution(mesh):
    members, others = mesh.devices.shape
    near, cores = 2, 2
    far = 2 * PLACES // (members * near)
    rest = others // (far * near * cores)
    split = jax.sharding.Mesh(
        mesh.devices.reshape(members, rest, far, near, cores),
        ("member", REST, FAR, "near", CORE),
    )
    dp = (REST, FAR, "near", CORE)
    in_specs = (
        P(dp + ("member",), None, None),
        P("member", dp, None, None),
        P(dp + ("member",)),
        P(),
        P(),
        P(),
        P(),
        P(),
        P(),
    )
    out_specs = (P(), P(), P(), P(), P(), P(), P(dp + ("member",)))
    return jax.shard_map(
        on_device, mesh=split, in_specs=in_specs, out_specs=out_specs, check_vma=False
    )
```

```python
import functools

import jax
import jax.numpy as jnp
from jax import lax
from jax.experimental import pallas as pl
from jax.experimental.pallas import tpu as pltpu
from jax.sharding import PartitionSpec as P

TEACHERS = 4
PLACES = 8
WIDE = 256
LANES = 128
TILE = 128
MARGIN = 16
CHUNKS = 2
VMEM = 56 << 20
ORDER = (
    "top", "in0", "in1", "taps", "in0", "small", "in1", "top", "in0", "small", "top", "in1",
    "in0", "small", "in1", "top", "small", "in0", "top", "in1", "in0", "small", "in1", "top",
    "in0", "in1", "top", "in0", "top", "in0", "write_top", "in1", "write0", "in1", "write1",
)
SMEM_SPEC = pl.BlockSpec(memory_space=pltpu.SMEM)
F32 = jnp.float32
BF16 = jnp.bfloat16


def params():
    return pltpu.CompilerParams(vmem_limit_bytes=VMEM)


def cost(microseconds):
    return pl.CostEstimate(flops=int(microseconds * 1.15e9), bytes_accessed=1 << 20, transcendentals=0)


def dot(left, right, left_axis=1, right_axis=0):
    return lax.dot_general(
        left, right, (((left_axis,), (right_axis,)), ((), ())), preferred_element_type=F32
    )


def fixed(*shape):
    return pl.BlockSpec(shape, lambda i, *_: (0,) * len(shape))


FAR = "far"
REST = "rest"
CORE = "core"
SMALL_STEPS = ((CORE, 1), ("member", 1), ("near", 1), (FAR, 1), (FAR, 2))


def exchange(values, axis, bit=1):
    size = lax.axis_size(axis)
    return lax.ppermute(values, axis, [(i, i ^ bit) for i in range(size)])


def add(own, other):
    return (own.astype(F32) + other.astype(F32)).astype(own.dtype)


def own_place(order):
    place = lax.axis_index(order[0]) * 4 + lax.axis_index(order[1]) * 2 + (lax.axis_index(FAR) & 1)
    return place.astype(jnp.int32)


def over_rest(values):
    return lax.psum(values, REST) if lax.axis_size(REST) > 1 else values


class Line:
    def __init__(self):
        self.values = {}
        self.pending = {}
        self.steps = {}
        self.last = None

    def after_last(self, value):
        if self.last is not None:
            value, self.values[self.last] = lax.optimization_barrier(
                (value, self.values[self.last])
            )
        return value

    def before_kernel(self, value):
        value = self.after_last(value)
        if self.last in self.steps and self.last not in self.pending:
            self.start(self.last)
        return value

    def put(self, name, value):
        self.values[name] = value
        self.last = name

    def begin(self, name, send, keep, order):
        self.values[name] = keep
        self.pending[name] = exchange(send, CORE)
        halve, gather = [("halve", axis) for axis in order], [("gather", axis) for axis in order]
        self.steps[name] = (
            [("add", CORE)]
            + halve
            + [("halve", FAR), ("double", FAR), ("gather", FAR)]
            + gather[::-1]
            + [("done", CORE)]
        )

    def begin_small(self, name, value):
        self.values[name] = value
        self.steps[name] = [("sum", step) for step in SMALL_STEPS]
        self.start(name)

    def start(self, name):
        if not self.steps[name]:
            return
        kind, axis = self.steps[name][0]
        values = self.values[name]
        if kind == "halve":
            self.pending[name] = exchange(values[:, values.shape[1] // 2 :], axis)
        elif kind == "double":
            self.pending[name] = exchange(values, axis, 2)
        elif kind == "sum":
            self.pending[name] = exchange(values, *axis)
        else:
            self.pending[name] = exchange(values, axis)

    def step(self, name, start=True):
        kind, _ = self.steps[name].pop(0)
        got = self.after_last(self.pending.pop(name))
        own = self.values[name]
        if kind == "halve":
            own = own[:, : got.shape[1]]
        if kind == "gather":
            result = jnp.concatenate([own, got], axis=1)
        elif kind == "done":
            result = (own, got)
        else:
            result = add(own, got)
        if kind == "double" or (kind == "sum" and not self.steps[name]):
            result = over_rest(result)
        self.put(name, result)
        if start:
            self.start(name)


def write_pieces(own_ref, product, send_ref, keep_ref, group):
    rows = keep_ref.shape[-2]
    core, place = own_ref[0], own_ref[1]

    def one(piece, carry):
        base = (piece ^ place) * (2 * rows)
        kept = pl.multiple_of(base + core * rows, rows)
        sent = pl.multiple_of(base + (1 - core) * rows, rows)
        keep_ref[group, piece] = product[pl.ds(kept, rows), :].astype(BF16)
        send_ref[group, piece] = product[pl.ds(sent, rows), :].astype(BF16)
        return carry

    lax.fori_loop(0, keep_ref.shape[1], one, 0)


def teacher_kernel(member_ref, logits_ref, give_ref, keep_ref, *, own_count):
    step = pl.program_id(0)
    total = None
    for teacher in range(logits_ref.shape[0]):
        logits = logits_ref[teacher, 0].astype(F32)
        shifted = logits - jnp.max(logits, axis=-1, keepdims=True)
        logp = shifted - jnp.log(jnp.sum(jnp.exp(shifted), axis=-1, keepdims=True))
        total = logp if total is None else total + logp

    @pl.when(step < own_count)
    def _():
        give_ref[0] = total

    @pl.when(step >= own_count)
    def _():
        keep_ref[0] = total


def teacher_sums(member, logits, own_count):
    teachers, utterances, frames, symbols = logits.shape
    shape = jax.ShapeDtypeStruct((own_count, frames, symbols), F32)

    def source(i, member_ref):
        mine = member_ref[0] * own_count
        theirs = (1 - member_ref[0]) * own_count
        return (0, jnp.where(i < own_count, theirs + i, mine + i - own_count), 0, 0)

    return pl.pallas_call(
        functools.partial(teacher_kernel, own_count=own_count),
        out_shape=(shape, shape),
        grid_spec=pltpu.PrefetchScalarGridSpec(
            num_scalar_prefetch=1,
            grid=(2 * own_count,),
            in_specs=[pl.BlockSpec((teachers, 1, frames, symbols), source)],
            out_specs=(
                pl.BlockSpec(
                    (1, frames, symbols), lambda i, _: (jnp.minimum(i, own_count - 1), 0, 0)
                ),
                pl.BlockSpec(
                    (1, frames, symbols), lambda i, _: (jnp.maximum(i - own_count, 0), 0, 0)
                ),
            ),
        ),
        compiler_params=params(),
        cost_estimate=cost(4),
        name="teachers",
    )(member, logits)


def live_column(lengths_ref, utterance, frames):
    position = lax.broadcasted_iota(jnp.int32, (frames, 1), 0)
    return (position < lengths_ref[utterance]).astype(F32)


def clear_margins(pad_ref):
    frames = pad_ref.shape[2] - 2 * MARGIN
    zeros = jnp.zeros(pad_ref.shape[:2] + (MARGIN, LANES), F32)
    pad_ref[:, :, :MARGIN, :] = zeros
    pad_ref[:, :, MARGIN + frames :, :] = zeros


def shifted_views(pad_ref, lane, utterance, start, taps):
    first = MARGIN - taps // 2
    for phase in range(8):
        offsets = [offset for offset in range(first, first + taps) if offset % 8 == phase]
        if not offsets:
            continue
        low = offsets[0]
        span = offsets[-1] - low + TILE
        view = pad_ref[lane, utterance, start + low : start + low + span, :]
        for offset in offsets:
            yield offset - first, view[offset - low : offset - low + TILE]


def convolve(pad_ref, lane, utterance, start, depth_ref, flipped):
    taps = depth_ref.shape[0]
    columns = slice(lane * LANES, (lane + 1) * LANES)
    total = jnp.zeros((TILE, LANES), F32)
    for tap, view in shifted_views(pad_ref, lane, utterance, start, taps):
        row = taps - 1 - tap if flipped else tap
        total = total + view * depth_ref[row : row + 1, columns]
    return total


def forward_kernel(
    lengths_ref,
    features_ref,
    gain_ref,
    value_weight_ref,
    gate_weight_ref,
    depth_ref,
    out_weight_ref,
    turned_ref,
    gated_ref,
    gate_ref,
    slope_ref,
    active_ref,
    residual_ref,
    normed_ref,
    pad_ref,
):
    utterances = pad_ref.shape[1]
    frames = pad_ref.shape[2] - 2 * MARGIN

    @pl.when(pl.program_id(0) == 0)
    def _():
        values = features_ref[...].astype(F32)
        centred = values - jnp.mean(values, axis=-1, keepdims=True)
        spread = jnp.mean(centred * centred, axis=-1, keepdims=True)
        normed = centred * lax.rsqrt(spread + 1e-05) * gain_ref[...]
        normed_ref[...] = normed.astype(BF16)
        turned_ref[...] = normed.T.astype(BF16)
        residual_ref[...] = values
        clear_margins(pad_ref)

    for utterance in range(utterances):
        rows = slice(utterance * frames, (utterance + 1) * frames)
        normed = normed_ref[rows, :]
        gate = jax.nn.sigmoid(dot(normed, gate_weight_ref[...]))
        gated = dot(normed, value_weight_ref[...]) * gate
        gated = gated * live_column(lengths_ref, utterance, frames)
        gate_ref[rows, :] = gate
        gated_ref[rows, :] = gated
        for lane in range(WIDE // LANES):
            pad_ref[lane, utterance, MARGIN : MARGIN + frames, :] = gated[
                :, lane * LANES : (lane + 1) * LANES
            ]

    for lane in range(WIDE // LANES):
        columns = slice(lane * LANES, (lane + 1) * LANES)

        def one(utterance, carry, lane=lane, columns=columns):
            for start in range(0, frames, TILE):
                rows = pl.ds(pl.multiple_of(utterance * frames + start, TILE), TILE)
                convolved = convolve(pad_ref, lane, utterance, start, depth_ref, False)
                squash = jax.nn.sigmoid(convolved)
                active_ref[rows, columns] = (convolved * squash).astype(BF16)
                slope_ref[rows, columns] = squash * (1.0 + convolved * (1.0 - squash))
            return carry

        lax.fori_loop(0, utterances, one, 0)

    residual_ref[...] += dot(active_ref[...], out_weight_ref[...])


def forward(lengths, features, gain, weight_in, depth, weight_out, utterances):
    rows, model = features.shape
    frames = rows // utterances
    steps = model // WIDE
    column = pl.BlockSpec((rows, WIDE), lambda i: (0, i))
    wide = jax.ShapeDtypeStruct((rows, model), F32)
    narrow = jax.ShapeDtypeStruct((rows, model), BF16)
    return pl.pallas_call(
        forward_kernel,
        grid=(steps,),
        out_shape=(jax.ShapeDtypeStruct((model, rows), BF16), wide, wide, wide, narrow, wide),
        in_specs=[
            SMEM_SPEC,
            fixed(rows, model),
            fixed(1, model),
            pl.BlockSpec((model, WIDE), lambda i: (0, i)),
            pl.BlockSpec((model, WIDE), lambda i: (0, steps + i)),
            pl.BlockSpec((depth.shape[0], WIDE), lambda i: (0, i)),
            pl.BlockSpec((WIDE, model), lambda i: (i, 0)),
        ],
        out_specs=(fixed(model, rows), column, column, column, column, fixed(rows, model)),
        scratch_shapes=[
            pltpu.VMEM((rows, model), BF16),
            pltpu.VMEM((WIDE // LANES, utterances, frames + 2 * MARGIN, LANES), F32),
        ],
        compiler_params=params(),
        cost_estimate=cost(15),
        name="forward",
    )(lengths, features, gain, weight_in, weight_in, depth, weight_out)


def top_kernel(
    lengths_ref,
    residual_ref,
    gain_ref,
    head_ref,
    kept_ref,
    got_ref,
    loss_ref,
    final_ref,
    dlogits_ref,
    dresidual_ref,
):
    frames = residual_ref.shape[0]
    live = live_column(lengths_ref, pl.program_id(0), frames)
    values = residual_ref[...]
    centred = values - jnp.mean(values, axis=-1, keepdims=True)
    spread = jnp.mean(centred * centred, axis=-1, keepdims=True)
    inverse = lax.rsqrt(spread + 1e-05)
    unit = centred * inverse
    final = (unit * gain_ref[...]).astype(BF16)
    final_ref[...] = final

    def log_softmax(logits):
        shifted = logits - jnp.max(logits, axis=-1, keepdims=True)
        return shifted - jnp.log(jnp.sum(jnp.exp(shifted), axis=-1, keepdims=True))

    target = jnp.exp(log_softmax((kept_ref[0] + got_ref[0]) * (1.0 / TEACHERS)))
    logp = log_softmax(dot(final, head_ref[...]))
    cross = -jnp.sum(target * logp, axis=-1, keepdims=True)
    loss_ref[...] = jnp.broadcast_to(jnp.sum(cross * live, axis=0, keepdims=True), (1, 1, LANES))
    weight = jnp.sum(target, axis=-1, keepdims=True)
    dlogits = ((jnp.exp(logp) * weight - target) * live).astype(BF16)
    dlogits_ref[...] = dlogits
    dunit = dot(dlogits, head_ref[...], 1, 1) * gain_ref[...]
    average = jnp.mean(dunit, axis=-1, keepdims=True)
    along = jnp.mean(dunit * unit, axis=-1, keepdims=True)
    dresidual_ref[...] = (inverse * (dunit - average - unit * along)).astype(BF16)


def top(lengths, residual, gain, head, kept, got):
    rows, model = residual.shape
    utterances, frames, symbols = kept.shape
    per_row = pl.BlockSpec((frames, model), lambda i: (i, 0))
    sums = pl.BlockSpec((1, frames, symbols), lambda i: (i, 0, 0))
    return pl.pallas_call(
        top_kernel,
        grid=(utterances,),
        out_shape=(
            jax.ShapeDtypeStruct((utterances, 1, LANES), F32),
            jax.ShapeDtypeStruct((rows, model), BF16),
            jax.ShapeDtypeStruct((rows, symbols), BF16),
            jax.ShapeDtypeStruct((rows, model), BF16),
        ),
        in_specs=[SMEM_SPEC, per_row, fixed(1, model), fixed(model, symbols), sums, sums],
        out_specs=(
            pl.BlockSpec((1, 1, LANES), lambda i: (i, 0, 0)),
            per_row,
            pl.BlockSpec((frames, symbols), lambda i: (i, 0)),
            per_row,
        ),
        compiler_params=params(),
        cost_estimate=cost(5),
        name="top",
    )(lengths, residual, gain, head, kept, got)


def outer_kernel(
    own_ref, active_ref, dresidual_ref, final_ref, dlogits_ref, send_ref, keep_ref, product_ref
):
    width = dresidual_ref.shape[1]
    product_ref[:, :width] = dot(active_ref[...], dresidual_ref[...], 0, 0)
    product_ref[:, width:] = dot(final_ref[...], dlogits_ref[...], 0, 0)
    write_pieces(own_ref, product_ref, send_ref, keep_ref, 0)


def outer(own, active, dresidual, final, dlogits):
    rows, model = active.shape
    half_out = dresidual.shape[1] // 2
    half_head = dlogits.shape[1] // 2
    width = half_out + half_head
    piece = (PLACES, model // (2 * PLACES), width)
    shape = jax.ShapeDtypeStruct((2,) + piece, BF16)
    out = pl.BlockSpec((1,) + piece, lambda i: (i, 0, 0, 0))
    return pl.pallas_call(
        outer_kernel,
        grid=(2,),
        out_shape=(shape, shape),
        in_specs=[
            SMEM_SPEC,
            fixed(rows, model),
            pl.BlockSpec((rows, half_out), lambda i: (0, i)),
            fixed(rows, model),
            pl.BlockSpec((rows, half_head), lambda i: (0, i)),
        ],
        out_specs=(out, out),
        scratch_shapes=[pltpu.VMEM((model, width), F32)],
        compiler_params=params(),
        cost_estimate=cost(5),
        name="outer",
    )(own, active, dresidual, final, dlogits)


def inner_kernel(
    own_ref,
    lengths_ref,
    dresidual_ref,
    out_weight_ref,
    slope_ref,
    gated_ref,
    gate_ref,
    turned_ref,
    depth_ref,
    send_ref,
    keep_ref,
    dconv_ref,
    pad_ref,
    dvalue_ref,
    dgate_ref,
    product_ref,
):
    utterances = pad_ref.shape[1]
    frames = pad_ref.shape[2] - 2 * MARGIN

    @pl.when(pl.program_id(0) == 0)
    def _():
        clear_margins(pad_ref)

    for utterance in range(utterances):
        rows = slice(utterance * frames, (utterance + 1) * frames)
        dconv = dot(dresidual_ref[rows, :], out_weight_ref[...], 1, 1) * slope_ref[rows, :]
        dconv_ref[rows, :] = dconv
        for lane in range(WIDE // LANES):
            pad_ref[lane, utterance, MARGIN : MARGIN + frames, :] = dconv[
                :, lane * LANES : (lane + 1) * LANES
            ]

    for lane in range(WIDE // LANES):
        columns = slice(lane * LANES, (lane + 1) * LANES)

        def one(utterance, carry, lane=lane, columns=columns):
            for start in range(0, frames, TILE):
                rows = pl.ds(pl.multiple_of(utterance * frames + start, TILE), TILE)
                position = lax.broadcasted_iota(jnp.int32, (TILE, 1), 0) + start
                live = (position < lengths_ref[utterance]).astype(F32)
                dgated = convolve(pad_ref, lane, utterance, start, depth_ref, True) * live
                gate = gate_ref[rows, columns]
                dvalue_ref[rows, columns] = (dgated * gate).astype(BF16)
                dgate_ref[rows, columns] = (dgated * gated_ref[rows, columns] * (1.0 - gate)).astype(
                    BF16
                )
            return carry

        lax.fori_loop(0, utterances, one, 0)

    for group, source in ((0, dvalue_ref), (1, dgate_ref)):
        product_ref[...] = dot(turned_ref[...], source[...])
        write_pieces(own_ref, product_ref, send_ref, keep_ref, group)


def inner(own, lengths, dresidual, weight_out, slope, gated, gate, turned, depth, chunk, utterances):
    model, rows = turned.shape
    frames = rows // utterances
    steps = model // WIDE // CHUNKS
    first = chunk * steps
    column = pl.BlockSpec((rows, WIDE), lambda i: (0, first + i))
    piece = (2, PLACES, model // (2 * PLACES))
    shape = jax.ShapeDtypeStruct(piece + (steps * WIDE,), BF16)
    out = pl.BlockSpec(piece + (WIDE,), lambda i: (0, 0, 0, i))
    return pl.pallas_call(
        inner_kernel,
        grid=(steps,),
        out_shape=(shape, shape, jax.ShapeDtypeStruct((rows, steps * WIDE), F32)),
        in_specs=[
            SMEM_SPEC,
            SMEM_SPEC,
            fixed(rows, model),
            pl.BlockSpec((WIDE, model), lambda i: (first + i, 0)),
            column,
            column,
            column,
            fixed(model, rows),
            pl.BlockSpec((depth.shape[0], WIDE), lambda i: (0, first + i)),
        ],
        out_specs=(out, out, pl.BlockSpec((rows, WIDE), lambda i: (0, i))),
        scratch_shapes=[
            pltpu.VMEM((WIDE // LANES, utterances, frames + 2 * MARGIN, LANES), F32),
            pltpu.VMEM((rows, WIDE), BF16),
            pltpu.VMEM((rows, WIDE), BF16),
            pltpu.VMEM((model, WIDE), F32),
        ],
        compiler_params=params(),
        cost_estimate=cost(11),
        name="inner",
    )(own, lengths, dresidual, weight_out, slope, gated, gate, turned, depth)


def taps_kernel(lengths_ref, gated_ref, *refs):
    *dconv_refs, out_ref, pad_ref, sums_ref = refs
    utterances = pad_ref.shape[1]
    frames = pad_ref.shape[2] - 2 * MARGIN
    taps = out_ref.shape[0] - 1
    step = pl.program_id(0)
    per_chunk = pl.num_programs(0) // len(dconv_refs)
    valid = lengths_ref[0]
    for utterance in range(1, utterances):
        valid = valid + lengths_ref[utterance]

    @pl.when(step == 0)
    def _():
        clear_margins(pad_ref)

    for lane in range(WIDE // LANES):
        columns = slice(lane * LANES, (lane + 1) * LANES)
        for utterance in range(utterances):
            rows = slice(utterance * frames, (utterance + 1) * frames)
            pad_ref[lane, utterance, MARGIN : MARGIN + frames, :] = gated_ref[rows, columns]

    for chunk, dconv_ref in enumerate(dconv_refs):

        @pl.when(step // per_chunk == chunk)
        def _(dconv_ref=dconv_ref):
            for lane in range(WIDE // LANES):
                columns = slice(lane * LANES, (lane + 1) * LANES)
                sums_ref[...] = jnp.zeros_like(sums_ref)

                def one(utterance, carry, lane=lane, columns=columns):
                    for start in range(0, frames, TILE):
                        rows = pl.ds(pl.multiple_of(utterance * frames + start, TILE), TILE)
                        dconv = dconv_ref[rows, columns]
                        for tap, view in shifted_views(pad_ref, lane, utterance, start, taps):
                            sums_ref[tap] += jnp.sum(
                                (view * dconv).reshape(TILE // 8, 8, LANES), axis=0
                            )
                    return carry

                lax.fori_loop(0, utterances, one, 0)
                out_ref[:taps, columns] = jnp.sum(sums_ref[...], axis=1)

    out_ref[taps:, :] = jnp.zeros((1, WIDE), F32) + valid.astype(F32)


def tap_sums(lengths, gated, dconvs, taps, utterances):
    rows, model = gated.shape
    steps = model // WIDE
    per_chunk = steps // len(dconvs)

    def part(chunk):
        low = chunk * per_chunk
        return pl.BlockSpec((rows, WIDE), lambda i: (0, jnp.clip(i - low, 0, per_chunk - 1)))

    return pl.pallas_call(
        taps_kernel,
        grid=(steps,),
        out_shape=jax.ShapeDtypeStruct((taps + 1, model), F32),
        in_specs=[SMEM_SPEC, pl.BlockSpec((rows, WIDE), lambda i: (0, i))]
        + [part(chunk) for chunk in range(len(dconvs))],
        out_specs=pl.BlockSpec((taps + 1, WIDE), lambda i: (0, i)),
        scratch_shapes=[
            pltpu.VMEM((WIDE // LANES, utterances, rows // utterances + 2 * MARGIN, LANES), F32),
            pltpu.VMEM((taps, 8, LANES), F32),
        ],
        compiler_params=params(),
        cost_estimate=cost(9),
        name="taps",
    )(lengths, gated, *dconvs)


def gain_terms(weight, grad):
    terms = weight.astype(F32) * grad
    total = terms[:, :LANES]
    for first in range(LANES, terms.shape[1], LANES):
        total = total + terms[:, first : first + LANES]
    return total


def gain_row(terms):
    high = terms.astype(BF16)
    low = (terms - high.astype(F32)).astype(BF16)
    ones = jnp.ones((8, LANES), BF16)
    return (dot(ones, high, 1, 1) + dot(ones, low, 1, 1))[0:1, :]


def write_rows(own_ref, step, piece_refs, group, scale, targets):
    mine_ref, other_ref = piece_refs
    places, rows = mine_ref.shape[1:3]
    core, place = own_ref[0], own_ref[1]
    for index in range(places):
        piece = index ^ (place & (places - 1))
        for side, source in ((core, mine_ref), (1 - core, other_ref)):
            here = pl.ds(pl.multiple_of(index * 2 * rows + side * rows, rows), rows)
            for target, there, first, width in targets:
                target[here, there : there + width] = (
                    source[group, piece, :, first : first + width].astype(F32) * scale
                )


def unpack_top_kernel(
    utts,
    own_ref,
    small_ref,
    mine_ref,
    other_ref,
    head_ref,
    gain_ref,
    losses_ref,
    wout_ref,
    dhead_ref,
    dgain_ref,
    depth_ref,
    loss_ref,
):
    taps = depth_ref.shape[0]
    scale = utts / small_ref[taps:, 0:1]
    half_out = wout_ref.shape[1] // 2
    half_head = dhead_ref.shape[1] // 2
    for group in range(2):
        targets = (
            (wout_ref, group * half_out, 0, half_out),
            (dhead_ref, group * half_head, half_out, half_head),
        )
        write_rows(own_ref, pl.program_id(0), (mine_ref, other_ref), group, scale, targets)
    dgain_ref[...] = gain_row(gain_terms(head_ref[...], dhead_ref[...])) / gain_ref[...]
    depth_ref[...] = small_ref[:taps, :] * scale
    loss_ref[...] = losses_ref[...] * scale[None]


def unpack_top(utts, own, small, mine, other, head, gain, losses, width_out):
    steps = 4
    model, symbols = head.shape
    rows = model // steps
    taps = small.shape[0] - 1
    places = PLACES // steps
    row = pl.BlockSpec((1, rows), lambda i, own_ref: (0, i))
    piece = pl.BlockSpec(
        (2, places) + mine.shape[2:], lambda i, own_ref: (0, i ^ (own_ref[1] // places), 0, 0)
    )

    def block(width):
        return pl.BlockSpec((rows, width), lambda i, own_ref: (i, 0))

    return pl.pallas_call(
        functools.partial(unpack_top_kernel, utts),
        out_shape=(
            jax.ShapeDtypeStruct((model, width_out), F32),
            jax.ShapeDtypeStruct((model, symbols), F32),
            jax.ShapeDtypeStruct((1, model), F32),
            jax.ShapeDtypeStruct((taps, model), F32),
            jax.ShapeDtypeStruct(losses.shape, F32),
        ),
        grid_spec=pltpu.PrefetchScalarGridSpec(
            num_scalar_prefetch=1,
            grid=(steps,),
            in_specs=[
                fixed(*small.shape),
                piece,
                piece,
                block(symbols),
                row,
                fixed(*losses.shape),
            ],
            out_specs=(
                block(width_out),
                block(symbols),
                row,
                fixed(taps, model),
                fixed(*losses.shape),
            ),
        ),
        compiler_params=params(),
        cost_estimate=cost(5),
        name="unpack_top",
    )(own, small, mine, other, head, gain, losses)


def unpack_inner_kernel(
    utts, last, own_ref, small_ref, mine_ref, other_ref, weight_ref, gain_ref, *refs
):
    win_ref, dgain_ref, sums_ref = refs[-3:]
    scale = utts / small_ref[small_ref.shape[0] - 1 :, 0:1]
    targets = ((win_ref, 0, 0, win_ref.shape[1]),)
    write_rows(own_ref, pl.program_id(0), (mine_ref, other_ref), 0, scale, targets)
    terms = gain_terms(weight_ref[...], win_ref[...])

    @pl.when(pl.program_id(1) == 0)
    def _():
        sums_ref[...] = terms

    @pl.when(pl.program_id(1) == 1)
    def _():
        total = gain_row(sums_ref[...] + terms)
        if len(refs) > 3:
            total = total + refs[1][...]
        dgain_ref[...] = total / gain_ref[...] if last else total


def unpack_inner(utts, own, small, mine, other, weight, gain, chunk, before):
    steps = 2
    model, width = weight.shape
    rows = model // steps
    wide = mine.shape[3]
    places = PLACES // steps
    row = pl.BlockSpec((1, rows), lambda i, j, own_ref: (0, i))
    block = pl.BlockSpec((rows, wide), lambda i, j, own_ref: (i, j * CHUNKS + chunk))
    piece = pl.BlockSpec(
        (1, places) + mine.shape[2:], lambda i, j, own_ref: (j, i ^ (own_ref[1] // places), 0, 0)
    )
    return pl.pallas_call(
        functools.partial(unpack_inner_kernel, utts, chunk == CHUNKS - 1),
        out_shape=(
            jax.ShapeDtypeStruct((model, width), F32),
            jax.ShapeDtypeStruct((1, model), F32),
        ),
        grid_spec=pltpu.PrefetchScalarGridSpec(
            num_scalar_prefetch=1,
            grid=(steps, 2),
            in_specs=[
                pl.BlockSpec(small.shape, lambda i, j, own_ref: (0, 0)),
                piece,
                piece,
                block,
                row,
            ]
            + ([pl.BlockSpec(memory_space=pl.ANY), row] if before else []),
            out_specs=(block, row),
            scratch_shapes=[pltpu.VMEM((rows, LANES), F32)],
        ),
        input_output_aliases={6: 0} if before else {},
        compiler_params=params(),
        cost_estimate=cost(4),
        name="unpack_inner",
    )(own, small, mine, other, weight, gain, *before)


def on_device(
    features,
    teacher_logits,
    lengths,
    gain_conv,
    weight_in,
    weight_depth,
    weight_out,
    gain_out,
    head_weight,
):
    count = 1
    for axis in ("member", "near", FAR, REST, CORE):
        count *= lax.axis_size(axis)
    member = lax.axis_index("member").astype(jnp.int32)[None]
    core = lax.axis_index(CORE).astype(jnp.int32)
    orders = (("near", "member"), ("member", "near"))
    owns = [jnp.stack([core, own_place(order)]) for order in orders]
    taps, model = weight_depth.shape
    utterances, frames, _ = features.shape
    utts = float(utterances * count)
    tie = lax.optimization_barrier

    give, kept = teacher_sums(member, teacher_logits, utterances)
    got = exchange(give, "member")
    flat = features.reshape(utterances * frames, model)
    turned, gated, gate, slope, active, residual = forward(
        lengths, flat, gain_conv[None], weight_in, weight_depth, weight_out, utterances
    )
    losses, final, dlogits, dresidual = top(
        lengths, residual, gain_out[None], head_weight, kept, got
    )

    line = Line()

    def products(name, chunk):
        nonlocal dresidual
        dresidual = line.before_kernel(dresidual)
        send, keep, dconv = inner(
            owns[chunk],
            lengths,
            dresidual,
            weight_out,
            slope,
            gated,
            gate,
            turned,
            weight_depth,
            chunk,
            utterances,
        )
        line.begin(name, send, keep, orders[chunk])
        line.put(name + "_conv", dconv)

    send, keep = outer(owns[1], active, dresidual, final, dlogits)
    send, keep, dresidual = tie((send, keep, dresidual))
    line.begin("top", send, keep, orders[1])
    products("in0", 0)
    line.step("top", start=False)
    products("in1", 1)
    written = {}

    def write_top():
        mine, other = line.values["top"]
        *rest, written["losses"] = unpack_top(
            utts,
            owns[1],
            line.values["small"],
            line.after_last(mine),
            other,
            head_weight,
            gain_out[None],
            losses,
            weight_out.shape[1],
        )
        written["out"], written["head"], by_head, written["depth"] = rest
        line.put("by_head", by_head)

    def write_in(chunk, name):
        mine, other = line.values[name]
        before = (written["in"], line.values["by_in"]) if chunk else ()
        written["in"], by_in = unpack_inner(
            utts,
            owns[chunk],
            line.values["small"],
            line.after_last(mine),
            other,
            weight_in,
            gain_conv[None],
            chunk,
            before,
        )
        line.put("by_in", by_in)

    def sum_taps():
        names = ("in0_conv", "in1_conv")
        dconvs = line.after_last(tuple(line.values[name] for name in names))
        line.put("taps", tap_sums(lengths, gated, dconvs, taps, utterances))
        line.begin_small("small", line.values["taps"])

    kernels = {
        "taps": sum_taps,
        "write_top": write_top,
        "write0": functools.partial(write_in, 0, "in0"),
        "write1": functools.partial(write_in, 1, "in1"),
    }
    for name in ORDER:
        if name in kernels:
            kernels[name]()
        else:
            line.step(name)
    return (
        line.values["by_in"].reshape(model),
        written["in"],
        written["depth"],
        written["out"],
        line.values["by_head"].reshape(model),
        written["head"],
        written["losses"][:, 0, 0],
    )


def solution(mesh):
    members, others = mesh.devices.shape
    near, cores = 2, 2
    far = 2 * PLACES // (members * near)
    rest = others // (far * near * cores)
    split = jax.sharding.Mesh(
        mesh.devices.reshape(members, rest, far, near, cores),
        ("member", REST, FAR, "near", CORE),
    )
    dp = (REST, FAR, "near", CORE)
    in_specs = (
        P(dp + ("member",), None, None),
        P("member", dp, None, None),
        P(dp + ("member",)),
        P(),
        P(),
        P(),
        P(),
        P(),
        P(),
    )
    out_specs = (P(), P(), P(), P(), P(), P(), P(dp + ("member",)))
    return jax.shard_map(
        on_device, mesh=split, in_specs=in_specs, out_specs=out_specs, check_vma=False
    )
```

```python
import functools

import jax
import jax.numpy as jnp
from jax import lax
from jax.experimental import pallas as pl
from jax.experimental.pallas import tpu as pltpu
from jax.sharding import PartitionSpec as P

TEACHERS = 4
PLACES = 8
WIDE = 256
LANES = 128
TILE = 128
MARGIN = 16
CHUNKS = 2
VMEM = 56 << 20
ORDER = (
    "top", "in0", "in1", "taps", "top", "in0", "in1", "small", "in0", "top", "in1", "in0",
    "small", "top", "in1", "in0", "small", "top", "in0", "in1", "small", "top", "in1", "in0",
    "top", "small", "in1", "top", "write_top", "in0", "in1", "in0", "in1", "write_in",
)
SMEM_SPEC = pl.BlockSpec(memory_space=pltpu.SMEM)
F32 = jnp.float32
BF16 = jnp.bfloat16


def params():
    return pltpu.CompilerParams(vmem_limit_bytes=VMEM)


def cost(microseconds):
    return pl.CostEstimate(flops=int(microseconds * 1.15e9), bytes_accessed=1 << 20, transcendentals=0)


def dot(left, right, left_axis=1, right_axis=0):
    return lax.dot_general(
        left, right, (((left_axis,), (right_axis,)), ((), ())), preferred_element_type=F32
    )


def fixed(*shape):
    return pl.BlockSpec(shape, lambda i, *_: (0,) * len(shape))


FAR = "far"
REST = "rest"
CORE = "core"
ALL = ("member", REST, FAR, "near", CORE)
FIRST, SECOND = "first", "second"
SMALL_STEPS = ((CORE, 1), (FIRST, 1), (SECOND, 1), (FAR, 1), (FAR, 2))


def exchange(values, axis, bit=1):
    if axis not in (FIRST, SECOND):
        size = lax.axis_size(axis)
        return lax.ppermute(values, axis, [(i, i ^ bit) for i in range(size)])
    count = 1
    for name in ALL:
        count *= lax.axis_size(name)
    near, member = 2, count // 2
    pairs = [(i, i ^ (member if (i % 2 == 0) == (axis == FIRST) else near)) for i in range(count)]
    return lax.ppermute(values, ALL, pairs)


def add(own, other):
    return (own.astype(F32) + other.astype(F32)).astype(own.dtype)


def own_places():
    core, member, near = lax.axis_index(CORE), lax.axis_index("member"), lax.axis_index("near")
    low = lax.axis_index(FAR) & 1
    places = (member * 4 + near * 2 + low, near * 4 + member * 2 + low)
    own = jnp.where(core == 0, places[0], places[1])
    other = jnp.where(core == 0, places[1], places[0])
    return jnp.stack([core, own, other]).astype(jnp.int32)


def over_rest(values):
    return lax.psum(values, REST) if lax.axis_size(REST) > 1 else values


class Line:
    def __init__(self):
        self.values = {}
        self.pending = {}
        self.steps = {}
        self.last = None

    def after_last(self, value):
        if self.last is not None:
            value, self.values[self.last] = lax.optimization_barrier(
                (value, self.values[self.last])
            )
        return value

    def before_kernel(self, value):
        value = self.after_last(value)
        if self.last in self.steps and self.last not in self.pending:
            self.start(self.last)
        return value

    def put(self, name, value):
        self.values[name] = value
        self.last = name

    def begin(self, name, send, keep):
        self.values[name] = keep
        self.pending[name] = exchange(send, CORE)
        self.steps[name] = [
            ("add", CORE),
            ("halve", FIRST),
            ("halve", SECOND),
            ("halve", FAR),
            ("double", FAR),
            ("gather", FAR),
            ("gather", SECOND),
            ("gather", FIRST),
            ("done", CORE),
        ]

    def begin_small(self, name, value):
        self.values[name] = value
        self.steps[name] = [("sum", step) for step in SMALL_STEPS]
        self.start(name)

    def start(self, name):
        if not self.steps[name]:
            return
        kind, axis = self.steps[name][0]
        values = self.values[name]
        if kind == "halve":
            self.pending[name] = exchange(values[:, values.shape[1] // 2 :], axis)
        elif kind == "double":
            self.pending[name] = exchange(values, axis, 2)
        elif kind == "sum":
            self.pending[name] = exchange(values, *axis)
        else:
            self.pending[name] = exchange(values, axis)

    def step(self, name, start=True):
        kind, _ = self.steps[name].pop(0)
        got = self.after_last(self.pending.pop(name))
        own = self.values[name]
        if kind == "halve":
            own = own[:, : got.shape[1]]
        if kind == "gather":
            result = jnp.concatenate([own, got], axis=1)
        elif kind == "done":
            result = (own, got)
        else:
            result = add(own, got)
        if kind == "double" or (kind == "sum" and not self.steps[name]):
            result = over_rest(result)
        self.put(name, result)
        if start:
            self.start(name)


def write_pieces(own_ref, product, send_ref, keep_ref, group):
    rows = keep_ref.shape[-2]
    core = own_ref[0]

    def one(piece, carry):
        kept = pl.multiple_of((2 * (piece ^ own_ref[1]) + core) * rows, rows)
        sent = pl.multiple_of((2 * (piece ^ own_ref[2]) + 1 - core) * rows, rows)
        keep_ref[group, piece] = product[pl.ds(kept, rows), :].astype(BF16)
        send_ref[group, piece] = product[pl.ds(sent, rows), :].astype(BF16)
        return carry

    lax.fori_loop(0, keep_ref.shape[1], one, 0)


def teacher_kernel(member_ref, logits_ref, give_ref, keep_ref, *, own_count):
    step = pl.program_id(0)
    total = None
    for teacher in range(logits_ref.shape[0]):
        logits = logits_ref[teacher, 0].astype(F32)
        shifted = logits - jnp.max(logits, axis=-1, keepdims=True)
        logp = shifted - jnp.log(jnp.sum(jnp.exp(shifted), axis=-1, keepdims=True))
        total = logp if total is None else total + logp

    @pl.when(step < own_count)
    def _():
        give_ref[0] = total

    @pl.when(step >= own_count)
    def _():
        keep_ref[0] = total


def teacher_sums(member, logits, own_count):
    teachers, utterances, frames, symbols = logits.shape
    shape = jax.ShapeDtypeStruct((own_count, frames, symbols), F32)

    def source(i, member_ref):
        mine = member_ref[0] * own_count
        theirs = (1 - member_ref[0]) * own_count
        return (0, jnp.where(i < own_count, theirs + i, mine + i - own_count), 0, 0)

    return pl.pallas_call(
        functools.partial(teacher_kernel, own_count=own_count),
        out_shape=(shape, shape),
        grid_spec=pltpu.PrefetchScalarGridSpec(
            num_scalar_prefetch=1,
            grid=(2 * own_count,),
            in_specs=[pl.BlockSpec((teachers, 1, frames, symbols), source)],
            out_specs=(
                pl.BlockSpec(
                    (1, frames, symbols), lambda i, _: (jnp.minimum(i, own_count - 1), 0, 0)
                ),
                pl.BlockSpec(
                    (1, frames, symbols), lambda i, _: (jnp.maximum(i - own_count, 0), 0, 0)
                ),
            ),
        ),
        compiler_params=params(),
        cost_estimate=cost(4),
        name="teachers",
    )(member, logits)


def live_column(lengths_ref, utterance, frames):
    position = lax.broadcasted_iota(jnp.int32, (frames, 1), 0)
    return (position < lengths_ref[utterance]).astype(F32)


def clear_margins(pad_ref):
    frames = pad_ref.shape[2] - 2 * MARGIN
    zeros = jnp.zeros(pad_ref.shape[:2] + (MARGIN, LANES), F32)
    pad_ref[:, :, :MARGIN, :] = zeros
    pad_ref[:, :, MARGIN + frames :, :] = zeros


def shifted_views(pad_ref, lane, utterance, start, taps):
    first = MARGIN - taps // 2
    for phase in range(8):
        offsets = [offset for offset in range(first, first + taps) if offset % 8 == phase]
        if not offsets:
            continue
        low = offsets[0]
        span = offsets[-1] - low + TILE
        view = pad_ref[lane, utterance, start + low : start + low + span, :]
        for offset in offsets:
            yield offset - first, view[offset - low : offset - low + TILE]


def convolve(pad_ref, lane, utterance, start, depth_ref, flipped):
    taps = depth_ref.shape[0]
    columns = slice(lane * LANES, (lane + 1) * LANES)
    total = jnp.zeros((TILE, LANES), F32)
    for tap, view in shifted_views(pad_ref, lane, utterance, start, taps):
        row = taps - 1 - tap if flipped else tap
        total = total + view * depth_ref[row : row + 1, columns]
    return total


def forward_kernel(
    lengths_ref,
    features_ref,
    gain_ref,
    value_weight_ref,
    gate_weight_ref,
    depth_ref,
    out_weight_ref,
    turned_ref,
    gated_ref,
    gate_ref,
    slope_ref,
    active_ref,
    residual_ref,
    normed_ref,
    pad_ref,
):
    utterances = pad_ref.shape[1]
    frames = pad_ref.shape[2] - 2 * MARGIN

    @pl.when(pl.program_id(0) == 0)
    def _():
        values = features_ref[...].astype(F32)
        centred = values - jnp.mean(values, axis=-1, keepdims=True)
        spread = jnp.mean(centred * centred, axis=-1, keepdims=True)
        normed = centred * lax.rsqrt(spread + 1e-05) * gain_ref[...]
        normed_ref[...] = normed.astype(BF16)
        turned_ref[...] = normed.T.astype(BF16)
        residual_ref[...] = values
        clear_margins(pad_ref)

    for utterance in range(utterances):
        rows = slice(utterance * frames, (utterance + 1) * frames)
        normed = normed_ref[rows, :]
        gate = jax.nn.sigmoid(dot(normed, gate_weight_ref[...]))
        gated = dot(normed, value_weight_ref[...]) * gate
        gated = gated * live_column(lengths_ref, utterance, frames)
        gate_ref[rows, :] = gate
        gated_ref[rows, :] = gated
        for lane in range(WIDE // LANES):
            pad_ref[lane, utterance, MARGIN : MARGIN + frames, :] = gated[
                :, lane * LANES : (lane + 1) * LANES
            ]

    for lane in range(WIDE // LANES):
        columns = slice(lane * LANES, (lane + 1) * LANES)

        def one(utterance, carry, lane=lane, columns=columns):
            for start in range(0, frames, TILE):
                rows = pl.ds(pl.multiple_of(utterance * frames + start, TILE), TILE)
                convolved = convolve(pad_ref, lane, utterance, start, depth_ref, False)
                squash = jax.nn.sigmoid(convolved)
                active_ref[rows, columns] = (convolved * squash).astype(BF16)
                slope_ref[rows, columns] = squash * (1.0 + convolved * (1.0 - squash))
            return carry

        lax.fori_loop(0, utterances, one, 0)

    residual_ref[...] += dot(active_ref[...], out_weight_ref[...])


def forward(lengths, features, gain, weight_in, depth, weight_out, utterances):
    rows, model = features.shape
    frames = rows // utterances
    steps = model // WIDE
    column = pl.BlockSpec((rows, WIDE), lambda i: (0, i))
    wide = jax.ShapeDtypeStruct((rows, model), F32)
    narrow = jax.ShapeDtypeStruct((rows, model), BF16)
    return pl.pallas_call(
        forward_kernel,
        grid=(steps,),
        out_shape=(jax.ShapeDtypeStruct((model, rows), BF16), wide, wide, wide, narrow, wide),
        in_specs=[
            SMEM_SPEC,
            fixed(rows, model),
            fixed(1, model),
            pl.BlockSpec((model, WIDE), lambda i: (0, i)),
            pl.BlockSpec((model, WIDE), lambda i: (0, steps + i)),
            pl.BlockSpec((depth.shape[0], WIDE), lambda i: (0, i)),
            pl.BlockSpec((WIDE, model), lambda i: (i, 0)),
        ],
        out_specs=(fixed(model, rows), column, column, column, column, fixed(rows, model)),
        scratch_shapes=[
            pltpu.VMEM((rows, model), BF16),
            pltpu.VMEM((WIDE // LANES, utterances, frames + 2 * MARGIN, LANES), F32),
        ],
        compiler_params=params(),
        cost_estimate=cost(15),
        name="forward",
    )(lengths, features, gain, weight_in, weight_in, depth, weight_out)


def top_kernel(
    lengths_ref,
    residual_ref,
    gain_ref,
    head_ref,
    kept_ref,
    got_ref,
    loss_ref,
    final_ref,
    dlogits_ref,
    dresidual_ref,
):
    frames = residual_ref.shape[0]
    live = live_column(lengths_ref, pl.program_id(0), frames)
    values = residual_ref[...]
    centred = values - jnp.mean(values, axis=-1, keepdims=True)
    spread = jnp.mean(centred * centred, axis=-1, keepdims=True)
    inverse = lax.rsqrt(spread + 1e-05)
    unit = centred * inverse
    final = (unit * gain_ref[...]).astype(BF16)
    final_ref[...] = final

    def log_softmax(logits):
        shifted = logits - jnp.max(logits, axis=-1, keepdims=True)
        return shifted - jnp.log(jnp.sum(jnp.exp(shifted), axis=-1, keepdims=True))

    target = jnp.exp(log_softmax((kept_ref[0] + got_ref[0]) * (1.0 / TEACHERS)))
    logp = log_softmax(dot(final, head_ref[...]))
    cross = -jnp.sum(target * logp, axis=-1, keepdims=True)
    loss_ref[...] = jnp.broadcast_to(jnp.sum(cross * live, axis=0, keepdims=True), (1, 1, LANES))
    weight = jnp.sum(target, axis=-1, keepdims=True)
    dlogits = ((jnp.exp(logp) * weight - target) * live).astype(BF16)
    dlogits_ref[...] = dlogits
    dunit = dot(dlogits, head_ref[...], 1, 1) * gain_ref[...]
    average = jnp.mean(dunit, axis=-1, keepdims=True)
    along = jnp.mean(dunit * unit, axis=-1, keepdims=True)
    dresidual_ref[...] = (inverse * (dunit - average - unit * along)).astype(BF16)


def top(lengths, residual, gain, head, kept, got):
    rows, model = residual.shape
    utterances, frames, symbols = kept.shape
    per_row = pl.BlockSpec((frames, model), lambda i: (i, 0))
    sums = pl.BlockSpec((1, frames, symbols), lambda i: (i, 0, 0))
    return pl.pallas_call(
        top_kernel,
        grid=(utterances,),
        out_shape=(
            jax.ShapeDtypeStruct((utterances, 1, LANES), F32),
            jax.ShapeDtypeStruct((rows, model), BF16),
            jax.ShapeDtypeStruct((rows, symbols), BF16),
            jax.ShapeDtypeStruct((rows, model), BF16),
        ),
        in_specs=[SMEM_SPEC, per_row, fixed(1, model), fixed(model, symbols), sums, sums],
        out_specs=(
            pl.BlockSpec((1, 1, LANES), lambda i: (i, 0, 0)),
            per_row,
            pl.BlockSpec((frames, symbols), lambda i: (i, 0)),
            per_row,
        ),
        compiler_params=params(),
        cost_estimate=cost(5),
        name="top",
    )(lengths, residual, gain, head, kept, got)


def outer_kernel(
    own_ref, active_ref, dresidual_ref, final_ref, dlogits_ref, send_ref, keep_ref, product_ref
):
    width = dresidual_ref.shape[1]
    product_ref[:, :width] = dot(active_ref[...], dresidual_ref[...], 0, 0)
    product_ref[:, width:] = dot(final_ref[...], dlogits_ref[...], 0, 0)
    write_pieces(own_ref, product_ref, send_ref, keep_ref, 0)


def outer(own, active, dresidual, final, dlogits):
    rows, model = active.shape
    half_out = dresidual.shape[1] // 2
    half_head = dlogits.shape[1] // 2
    width = half_out + half_head
    piece = (PLACES, model // (2 * PLACES), width)
    shape = jax.ShapeDtypeStruct((2,) + piece, BF16)
    out = pl.BlockSpec((1,) + piece, lambda i: (i, 0, 0, 0))
    return pl.pallas_call(
        outer_kernel,
        grid=(2,),
        out_shape=(shape, shape),
        in_specs=[
            SMEM_SPEC,
            fixed(rows, model),
            pl.BlockSpec((rows, half_out), lambda i: (0, i)),
            fixed(rows, model),
            pl.BlockSpec((rows, half_head), lambda i: (0, i)),
        ],
        out_specs=(out, out),
        scratch_shapes=[pltpu.VMEM((model, width), F32)],
        compiler_params=params(),
        cost_estimate=cost(5),
        name="outer",
    )(own, active, dresidual, final, dlogits)


def inner_kernel(
    own_ref,
    lengths_ref,
    dresidual_ref,
    out_weight_ref,
    slope_ref,
    gated_ref,
    gate_ref,
    turned_ref,
    depth_ref,
    send_ref,
    keep_ref,
    dconv_ref,
    pad_ref,
    dvalue_ref,
    dgate_ref,
    product_ref,
):
    utterances = pad_ref.shape[1]
    frames = pad_ref.shape[2] - 2 * MARGIN

    @pl.when(pl.program_id(0) == 0)
    def _():
        clear_margins(pad_ref)

    for utterance in range(utterances):
        rows = slice(utterance * frames, (utterance + 1) * frames)
        dconv = dot(dresidual_ref[rows, :], out_weight_ref[...], 1, 1) * slope_ref[rows, :]
        dconv_ref[rows, :] = dconv
        for lane in range(WIDE // LANES):
            pad_ref[lane, utterance, MARGIN : MARGIN + frames, :] = dconv[
                :, lane * LANES : (lane + 1) * LANES
            ]

    for lane in range(WIDE // LANES):
        columns = slice(lane * LANES, (lane + 1) * LANES)

        def one(utterance, carry, lane=lane, columns=columns):
            for start in range(0, frames, TILE):
                rows = pl.ds(pl.multiple_of(utterance * frames + start, TILE), TILE)
                position = lax.broadcasted_iota(jnp.int32, (TILE, 1), 0) + start
                live = (position < lengths_ref[utterance]).astype(F32)
                dgated = convolve(pad_ref, lane, utterance, start, depth_ref, True) * live
                gate = gate_ref[rows, columns]
                dvalue_ref[rows, columns] = (dgated * gate).astype(BF16)
                dgate_ref[rows, columns] = (dgated * gated_ref[rows, columns] * (1.0 - gate)).astype(
                    BF16
                )
            return carry

        lax.fori_loop(0, utterances, one, 0)

    for group, source in ((0, dvalue_ref), (1, dgate_ref)):
        product_ref[...] = dot(turned_ref[...], source[...])
        write_pieces(own_ref, product_ref, send_ref, keep_ref, group)


def inner(own, lengths, dresidual, weight_out, slope, gated, gate, turned, depth, chunk, utterances):
    model, rows = turned.shape
    frames = rows // utterances
    steps = model // WIDE // CHUNKS
    first = chunk * steps
    column = pl.BlockSpec((rows, WIDE), lambda i: (0, first + i))
    piece = (2, PLACES, model // (2 * PLACES))
    shape = jax.ShapeDtypeStruct(piece + (steps * WIDE,), BF16)
    out = pl.BlockSpec(piece + (WIDE,), lambda i: (0, 0, 0, i))
    return pl.pallas_call(
        inner_kernel,
        grid=(steps,),
        out_shape=(shape, shape, jax.ShapeDtypeStruct((rows, steps * WIDE), F32)),
        in_specs=[
            SMEM_SPEC,
            SMEM_SPEC,
            fixed(rows, model),
            pl.BlockSpec((WIDE, model), lambda i: (first + i, 0)),
            column,
            column,
            column,
            fixed(model, rows),
            pl.BlockSpec((depth.shape[0], WIDE), lambda i: (0, first + i)),
        ],
        out_specs=(out, out, pl.BlockSpec((rows, WIDE), lambda i: (0, i))),
        scratch_shapes=[
            pltpu.VMEM((WIDE // LANES, utterances, frames + 2 * MARGIN, LANES), F32),
            pltpu.VMEM((rows, WIDE), BF16),
            pltpu.VMEM((rows, WIDE), BF16),
            pltpu.VMEM((model, WIDE), F32),
        ],
        compiler_params=params(),
        cost_estimate=cost(11),
        name="inner",
    )(own, lengths, dresidual, weight_out, slope, gated, gate, turned, depth)


def taps_kernel(lengths_ref, gated_ref, *refs):
    *dconv_refs, out_ref, pad_ref, sums_ref = refs
    utterances = pad_ref.shape[1]
    frames = pad_ref.shape[2] - 2 * MARGIN
    taps = out_ref.shape[0] - 1
    step = pl.program_id(0)
    per_chunk = pl.num_programs(0) // len(dconv_refs)
    valid = lengths_ref[0]
    for utterance in range(1, utterances):
        valid = valid + lengths_ref[utterance]

    @pl.when(step == 0)
    def _():
        clear_margins(pad_ref)

    for lane in range(WIDE // LANES):
        columns = slice(lane * LANES, (lane + 1) * LANES)
        for utterance in range(utterances):
            rows = slice(utterance * frames, (utterance + 1) * frames)
            pad_ref[lane, utterance, MARGIN : MARGIN + frames, :] = gated_ref[rows, columns]

    for chunk, dconv_ref in enumerate(dconv_refs):

        @pl.when(step // per_chunk == chunk)
        def _(dconv_ref=dconv_ref):
            for lane in range(WIDE // LANES):
                columns = slice(lane * LANES, (lane + 1) * LANES)
                sums_ref[...] = jnp.zeros_like(sums_ref)

                def one(utterance, carry, lane=lane, columns=columns):
                    for start in range(0, frames, TILE):
                        rows = pl.ds(pl.multiple_of(utterance * frames + start, TILE), TILE)
                        dconv = dconv_ref[rows, columns]
                        for tap, view in shifted_views(pad_ref, lane, utterance, start, taps):
                            sums_ref[tap] += jnp.sum(
                                (view * dconv).reshape(TILE // 8, 8, LANES), axis=0
                            )
                    return carry

                lax.fori_loop(0, utterances, one, 0)
                out_ref[:taps, columns] = jnp.sum(sums_ref[...], axis=1)

    out_ref[taps:, :] = jnp.zeros((1, WIDE), F32) + valid.astype(F32)


def tap_sums(lengths, gated, dconvs, taps, utterances):
    rows, model = gated.shape
    steps = model // WIDE
    per_chunk = steps // len(dconvs)

    def part(chunk):
        low = chunk * per_chunk
        return pl.BlockSpec((rows, WIDE), lambda i: (0, jnp.clip(i - low, 0, per_chunk - 1)))

    return pl.pallas_call(
        taps_kernel,
        grid=(steps,),
        out_shape=jax.ShapeDtypeStruct((taps + 1, model), F32),
        in_specs=[SMEM_SPEC, pl.BlockSpec((rows, WIDE), lambda i: (0, i))]
        + [part(chunk) for chunk in range(len(dconvs))],
        out_specs=pl.BlockSpec((taps + 1, WIDE), lambda i: (0, i)),
        scratch_shapes=[
            pltpu.VMEM((WIDE // LANES, utterances, rows // utterances + 2 * MARGIN, LANES), F32),
            pltpu.VMEM((taps, 8, LANES), F32),
        ],
        compiler_params=params(),
        cost_estimate=cost(9),
        name="taps",
    )(lengths, gated, *dconvs)


def gain_terms(weight, grad):
    terms = weight.astype(F32) * grad
    total = terms[:, :LANES]
    for first in range(LANES, terms.shape[1], LANES):
        total = total + terms[:, first : first + LANES]
    return total


def gain_row(terms):
    high = terms.astype(BF16)
    low = (terms - high.astype(F32)).astype(BF16)
    ones = jnp.ones((8, LANES), BF16)
    return (dot(ones, high, 1, 1) + dot(ones, low, 1, 1))[0:1, :]


def write_rows(own_ref, piece_refs, group, scale, targets):
    places, rows = piece_refs[0].shape[1:3]
    core = own_ref[0]
    for index in range(places):
        for whose, (side, source) in enumerate(zip((core, 1 - core), piece_refs)):
            piece = index ^ (own_ref[1 + whose] & (places - 1))
            here = pl.ds(pl.multiple_of(index * 2 * rows + side * rows, rows), rows)
            for target, there, first, width in targets:
                target[here, there : there + width] = (
                    source[group, piece, :, first : first + width].astype(F32) * scale
                )


def piece_spec(array, places, whose):
    return pl.BlockSpec(
        (2, places) + array.shape[2:], lambda i, own_ref: (0, i ^ (own_ref[1 + whose] // places), 0, 0)
    )


def unpack_top_kernel(
    utts,
    own_ref,
    small_ref,
    mine_ref,
    other_ref,
    head_ref,
    gain_ref,
    losses_ref,
    wout_ref,
    dhead_ref,
    dgain_ref,
    depth_ref,
    loss_ref,
):
    taps = depth_ref.shape[0]
    scale = utts / small_ref[taps:, 0:1]
    half_out = wout_ref.shape[1] // 2
    half_head = dhead_ref.shape[1] // 2
    for group in range(2):
        targets = (
            (wout_ref, group * half_out, 0, half_out),
            (dhead_ref, group * half_head, half_out, half_head),
        )
        write_rows(own_ref, (mine_ref, other_ref), group, scale, targets)
    dgain_ref[...] = gain_row(gain_terms(head_ref[...], dhead_ref[...])) / gain_ref[...]
    depth_ref[...] = small_ref[:taps, :] * scale
    loss_ref[...] = losses_ref[...] * scale[None]


def unpack_top(utts, own, small, mine, other, head, gain, losses, width_out):
    steps = 4
    model, symbols = head.shape
    rows = model // steps
    taps = small.shape[0] - 1
    places = PLACES // steps
    row = pl.BlockSpec((1, rows), lambda i, own_ref: (0, i))

    def block(width):
        return pl.BlockSpec((rows, width), lambda i, own_ref: (i, 0))

    return pl.pallas_call(
        functools.partial(unpack_top_kernel, utts),
        out_shape=(
            jax.ShapeDtypeStruct((model, width_out), F32),
            jax.ShapeDtypeStruct((model, symbols), F32),
            jax.ShapeDtypeStruct((1, model), F32),
            jax.ShapeDtypeStruct((taps, model), F32),
            jax.ShapeDtypeStruct(losses.shape, F32),
        ),
        grid_spec=pltpu.PrefetchScalarGridSpec(
            num_scalar_prefetch=1,
            grid=(steps,),
            in_specs=[
                fixed(*small.shape),
                piece_spec(mine, places, 0),
                piece_spec(other, places, 1),
                block(symbols),
                row,
                fixed(*losses.shape),
            ],
            out_specs=(
                block(width_out),
                block(symbols),
                row,
                fixed(taps, model),
                fixed(*losses.shape),
            ),
        ),
        compiler_params=params(),
        cost_estimate=cost(5),
        name="unpack_top",
    )(own, small, mine, other, head, gain, losses)


def unpack_inner_kernel(utts, own_ref, small_ref, weight_ref, gain_ref, *refs):
    *piece_refs, win_ref, dgain_ref = refs
    scale = utts / small_ref[small_ref.shape[0] - 1 :, 0:1]
    half = win_ref.shape[1] // 2
    for chunk in range(CHUNKS):
        pair = piece_refs[2 * chunk : 2 * chunk + 2]
        width = pair[0].shape[3]
        for group in range(2):
            targets = ((win_ref, group * half + chunk * width, 0, width),)
            write_rows(own_ref, pair, group, scale, targets)
    dgain_ref[...] = gain_row(gain_terms(weight_ref[...], win_ref[...])) / gain_ref[...]


def unpack_inner(utts, own, small, pieces, weight, gain):
    steps = 4
    model, width = weight.shape
    rows = model // steps
    places = PLACES // steps
    row = pl.BlockSpec((1, rows), lambda i, own_ref: (0, i))
    block = pl.BlockSpec((rows, width), lambda i, own_ref: (i, 0))
    return pl.pallas_call(
        functools.partial(unpack_inner_kernel, utts),
        out_shape=(
            jax.ShapeDtypeStruct((model, width), F32),
            jax.ShapeDtypeStruct((1, model), F32),
        ),
        grid_spec=pltpu.PrefetchScalarGridSpec(
            num_scalar_prefetch=1,
            grid=(steps,),
            in_specs=[fixed(*small.shape), block, row]
            + [piece_spec(array, places, index % 2) for index, array in enumerate(pieces)],
            out_specs=(block, row),
        ),
        compiler_params=params(),
        cost_estimate=cost(8),
        name="unpack_inner",
    )(own, small, weight, gain, *pieces)


def on_device(
    features,
    teacher_logits,
    lengths,
    gain_conv,
    weight_in,
    weight_depth,
    weight_out,
    gain_out,
    head_weight,
):
    count = 1
    for axis in ("member", "near", FAR, REST, CORE):
        count *= lax.axis_size(axis)
    member = lax.axis_index("member").astype(jnp.int32)[None]
    own = own_places()
    taps, model = weight_depth.shape
    utterances, frames, _ = features.shape
    utts = float(utterances * count)
    tie = lax.optimization_barrier

    give, kept = teacher_sums(member, teacher_logits, utterances)
    got = exchange(give, "member")
    flat = features.reshape(utterances * frames, model)
    turned, gated, gate, slope, active, residual = forward(
        lengths, flat, gain_conv[None], weight_in, weight_depth, weight_out, utterances
    )
    losses, final, dlogits, dresidual = top(
        lengths, residual, gain_out[None], head_weight, kept, got
    )

    line = Line()

    def products(name, chunk):
        nonlocal dresidual
        dresidual = line.before_kernel(dresidual)
        send, keep, dconv = inner(
            own,
            lengths,
            dresidual,
            weight_out,
            slope,
            gated,
            gate,
            turned,
            weight_depth,
            chunk,
            utterances,
        )
        line.begin(name, send, keep)
        line.put(name + "_conv", dconv)

    send, keep = outer(own, active, dresidual, final, dlogits)
    send, keep, dresidual = tie((send, keep, dresidual))
    line.begin("top", send, keep)
    products("in0", 0)
    line.step("top", start=False)
    products("in1", 1)
    written = {}

    def write_top():
        mine, other = line.values["top"]
        *rest, written["losses"] = unpack_top(
            utts,
            own,
            line.values["small"],
            line.after_last(mine),
            other,
            head_weight,
            gain_out[None],
            losses,
            weight_out.shape[1],
        )
        written["out"], written["head"], by_head, written["depth"] = rest
        line.put("by_head", by_head)

    def write_in():
        pieces = [array for name in ("in0", "in1") for array in line.values[name]]
        written["in"], by_in = unpack_inner(
            utts, own, line.values["small"], pieces, weight_in, gain_conv[None]
        )
        line.put("by_in", by_in)

    def sum_taps():
        names = ("in0_conv", "in1_conv")
        dconvs = line.after_last(tuple(line.values[name] for name in names))
        line.put("taps", tap_sums(lengths, gated, dconvs, taps, utterances))
        line.begin_small("small", line.values["taps"])

    kernels = {
        "taps": sum_taps,
        "write_top": write_top,
        "write_in": write_in,
    }
    for name in ORDER:
        if name in kernels:
            kernels[name]()
        else:
            line.step(name)
    return (
        line.values["by_in"].reshape(model),
        written["in"],
        written["depth"],
        written["out"],
        line.values["by_head"].reshape(model),
        written["head"],
        written["losses"][:, 0, 0],
    )


def solution(mesh):
    members, others = mesh.devices.shape
    near, cores = 2, 2
    far = 2 * PLACES // (members * near)
    rest = others // (far * near * cores)
    split = jax.sharding.Mesh(
        mesh.devices.reshape(members, rest, far, near, cores),
        ("member", REST, FAR, "near", CORE),
    )
    dp = (REST, FAR, "near", CORE)
    in_specs = (
        P(dp + ("member",), None, None),
        P("member", dp, None, None),
        P(dp + ("member",)),
        P(),
        P(),
        P(),
        P(),
        P(),
        P(),
    )
    out_specs = (P(), P(), P(), P(), P(), P(), P(dp + ("member",)))
    return jax.shard_map(
        on_device, mesh=split, in_specs=in_specs, out_specs=out_specs, check_vma=False
    )
```

```python
import functools

import jax
import jax.numpy as jnp
from jax import lax
from jax.experimental import pallas as pl
from jax.experimental.pallas import tpu as pltpu
from jax.sharding import PartitionSpec as P

TEACHERS = 4
PLACES = 8
WIDE = 256
LANES = 128
TILE = 128
MARGIN = 16
CHUNKS = 2
ORDER = (
    "top", "in0", "in1", "taps", "top", "small", "in0", "in1", "small", "top", "in0", "in1",
    "small", "top", "in0", "in1", "small", "top", "in0", "in1", "small", "top", "in0", "in1",
    "top", "in0", "in1", "top", "write_top", "in0", "in1", "in0", "in1", "write_in",
)
SMEM_SPEC = pl.BlockSpec(memory_space=pltpu.SMEM)
F32 = jnp.float32
BF16 = jnp.bfloat16


def params(mebibytes):
    return pltpu.CompilerParams(vmem_limit_bytes=mebibytes << 20)


def cost(microseconds):
    return pl.CostEstimate(flops=int(microseconds * 1.15e9), bytes_accessed=1 << 20, transcendentals=0)


def dot(left, right, left_axis=1, right_axis=0):
    return lax.dot_general(
        left, right, (((left_axis,), (right_axis,)), ((), ())), preferred_element_type=F32
    )


def fixed(*shape):
    return pl.BlockSpec(shape, lambda i, *_: (0,) * len(shape))


FAR = "far"
REST = "rest"
CORE = "core"
ALL = ("member", REST, FAR, "near", CORE)
STEPS = ("first", "second", "third", "fourth")


def exchange(values, step):
    if step in (CORE, "member"):
        return lax.ppermute(values, step, [(0, 1), (1, 0)])
    count = 1
    for name in ALL:
        count *= lax.axis_size(name)
    bits = (count // 2, 2, 4, 8)
    place = STEPS.index(step)
    return lax.ppermute(values, ALL, [(i, i ^ bits[place ^ (i % 2)]) for i in range(count)])


def add(own, other):
    return (own.astype(F32) + other.astype(F32)).astype(own.dtype)


def own_places():
    core, member, near = lax.axis_index(CORE), lax.axis_index("member"), lax.axis_index("near")
    far = lax.axis_index(FAR)
    places = (member * 4 + near * 2 + (far & 1), near * 4 + member * 2 + (far >> 1))
    own = jnp.where(core == 0, places[0], places[1])
    other = jnp.where(core == 0, places[1], places[0])
    return jnp.stack([core, own, other]).astype(jnp.int32)


def over_rest(values):
    return lax.psum(values, REST) if lax.axis_size(REST) > 1 else values


class Line:
    def __init__(self):
        self.values = {}
        self.pending = {}
        self.steps = {}
        self.last = None

    def after_last(self, value):
        if self.last is not None:
            value, self.values[self.last] = lax.optimization_barrier(
                (value, self.values[self.last])
            )
        return value

    def before_kernel(self, value):
        value = self.after_last(value)
        if self.last in self.steps and self.last not in self.pending:
            self.start(self.last)
        return value

    def put(self, name, value):
        self.values[name] = value
        self.last = name

    def begin(self, name, send, keep):
        self.values[name] = keep
        self.pending[name] = exchange(send, CORE)
        self.steps[name] = [
            ("add", CORE),
            ("halve", "first"),
            ("halve", "second"),
            ("halve", "third"),
            ("double", "fourth"),
            ("gather", "third"),
            ("gather", "second"),
            ("gather", "first"),
            ("done", CORE),
        ]

    def begin_small(self, name, value):
        self.values[name] = value
        self.steps[name] = [("sum", step) for step in STEPS + (CORE,)]
        self.start(name)

    def start(self, name):
        if not self.steps[name]:
            return
        kind, step = self.steps[name][0]
        values = self.values[name]
        if kind == "halve":
            values = values[:, values.shape[1] // 2 :]
        self.pending[name] = exchange(values, step)

    def step(self, name, start=True):
        kind, _ = self.steps[name].pop(0)
        got = self.after_last(self.pending.pop(name))
        own = self.values[name]
        if kind == "halve":
            own = own[:, : got.shape[1]]
        if kind == "gather":
            result = jnp.concatenate([own, got], axis=1)
        elif kind == "done":
            result = (own, got)
        else:
            result = add(own, got)
        if kind == "double" or (kind == "sum" and not self.steps[name]):
            result = over_rest(result)
        self.put(name, result)
        if start:
            self.start(name)


def write_pieces(own_ref, product, send_ref, keep_ref, group):
    rows = keep_ref.shape[-2]
    core = own_ref[0]

    def one(piece, carry):
        kept = pl.multiple_of((2 * (piece ^ own_ref[1]) + core) * rows, rows)
        sent = pl.multiple_of((2 * (piece ^ own_ref[2]) + 1 - core) * rows, rows)
        keep_ref[group, piece] = product[pl.ds(kept, rows), :].astype(BF16)
        send_ref[group, piece] = product[pl.ds(sent, rows), :].astype(BF16)
        return carry

    lax.fori_loop(0, keep_ref.shape[1], one, 0)


def teacher_kernel(member_ref, logits_ref, give_ref, keep_ref, *, own_count):
    step = pl.program_id(0)
    total = None
    for teacher in range(logits_ref.shape[0]):
        logits = logits_ref[teacher, 0].astype(F32)
        shifted = logits - jnp.max(logits, axis=-1, keepdims=True)
        logp = shifted - jnp.log(jnp.sum(jnp.exp(shifted), axis=-1, keepdims=True))
        total = logp if total is None else total + logp

    @pl.when(step < own_count)
    def _():
        give_ref[0] = total

    @pl.when(step >= own_count)
    def _():
        keep_ref[0] = total


def teacher_sums(member, logits, own_count):
    teachers, utterances, frames, symbols = logits.shape
    shape = jax.ShapeDtypeStruct((own_count, frames, symbols), F32)

    def source(i, member_ref):
        mine = member_ref[0] * own_count
        theirs = (1 - member_ref[0]) * own_count
        return (0, jnp.where(i < own_count, theirs + i, mine + i - own_count), 0, 0)

    return pl.pallas_call(
        functools.partial(teacher_kernel, own_count=own_count),
        out_shape=(shape, shape),
        grid_spec=pltpu.PrefetchScalarGridSpec(
            num_scalar_prefetch=1,
            grid=(2 * own_count,),
            in_specs=[pl.BlockSpec((teachers, 1, frames, symbols), source)],
            out_specs=(
                pl.BlockSpec(
                    (1, frames, symbols), lambda i, _: (jnp.minimum(i, own_count - 1), 0, 0)
                ),
                pl.BlockSpec(
                    (1, frames, symbols), lambda i, _: (jnp.maximum(i - own_count, 0), 0, 0)
                ),
            ),
        ),
        compiler_params=params(16),
        cost_estimate=cost(4),
        name="teachers",
    )(member, logits)


def live_column(lengths_ref, utterance, frames):
    position = lax.broadcasted_iota(jnp.int32, (frames, 1), 0)
    return (position < lengths_ref[utterance]).astype(F32)


def clear_margins(pad_ref):
    frames = pad_ref.shape[2] - 2 * MARGIN
    zeros = jnp.zeros(pad_ref.shape[:2] + (MARGIN, LANES), F32)
    pad_ref[:, :, :MARGIN, :] = zeros
    pad_ref[:, :, MARGIN + frames :, :] = zeros


def shifted_views(pad_ref, lane, utterance, start, taps):
    first = MARGIN - taps // 2
    for phase in range(8):
        offsets = [offset for offset in range(first, first + taps) if offset % 8 == phase]
        if not offsets:
            continue
        low = offsets[0]
        span = offsets[-1] - low + TILE
        view = pad_ref[lane, utterance, start + low : start + low + span, :]
        for offset in offsets:
            yield offset - first, view[offset - low : offset - low + TILE]


def convolve(pad_ref, lane, utterance, start, depth_ref, flipped):
    taps = depth_ref.shape[0]
    columns = slice(lane * LANES, (lane + 1) * LANES)
    total = jnp.zeros((TILE, LANES), F32)
    for tap, view in shifted_views(pad_ref, lane, utterance, start, taps):
        row = taps - 1 - tap if flipped else tap
        total = total + view * depth_ref[row : row + 1, columns]
    return total


def forward_kernel(
    lengths_ref,
    features_ref,
    gain_ref,
    value_weight_ref,
    gate_weight_ref,
    depth_ref,
    out_weight_ref,
    turned_ref,
    gated_ref,
    gate_ref,
    slope_ref,
    active_ref,
    residual_ref,
    normed_ref,
    pad_ref,
):
    utterances = pad_ref.shape[1]
    frames = pad_ref.shape[2] - 2 * MARGIN

    @pl.when(pl.program_id(0) == 0)
    def _():
        values = features_ref[...].astype(F32)
        centred = values - jnp.mean(values, axis=-1, keepdims=True)
        spread = jnp.mean(centred * centred, axis=-1, keepdims=True)
        normed = centred * lax.rsqrt(spread + 1e-05) * gain_ref[...]
        normed_ref[...] = normed.astype(BF16)
        turned_ref[...] = normed.T.astype(BF16)
        residual_ref[...] = values
        clear_margins(pad_ref)

    for utterance in range(utterances):
        rows = slice(utterance * frames, (utterance + 1) * frames)
        normed = normed_ref[rows, :]
        gate = jax.nn.sigmoid(dot(normed, gate_weight_ref[...]))
        gated = dot(normed, value_weight_ref[...]) * gate
        gated = gated * live_column(lengths_ref, utterance, frames)
        gate_ref[rows, :] = gate
        gated_ref[rows, :] = gated
        for lane in range(WIDE // LANES):
            pad_ref[lane, utterance, MARGIN : MARGIN + frames, :] = gated[
                :, lane * LANES : (lane + 1) * LANES
            ]

    for lane in range(WIDE // LANES):
        columns = slice(lane * LANES, (lane + 1) * LANES)

        def one(utterance, carry, lane=lane, columns=columns):
            for start in range(0, frames, TILE):
                rows = pl.ds(pl.multiple_of(utterance * frames + start, TILE), TILE)
                convolved = convolve(pad_ref, lane, utterance, start, depth_ref, False)
                squash = jax.nn.sigmoid(convolved)
                active_ref[rows, columns] = (convolved * squash).astype(BF16)
                slope_ref[rows, columns] = squash * (1.0 + convolved * (1.0 - squash))
            return carry

        lax.fori_loop(0, utterances, one, 0)

    residual_ref[...] += dot(active_ref[...], out_weight_ref[...])


def forward(lengths, features, gain, weight_in, depth, weight_out, utterances):
    rows, model = features.shape
    frames = rows // utterances
    steps = model // WIDE
    column = pl.BlockSpec((rows, WIDE), lambda i: (0, i))
    wide = jax.ShapeDtypeStruct((rows, model), F32)
    narrow = jax.ShapeDtypeStruct((rows, model), BF16)
    return pl.pallas_call(
        forward_kernel,
        grid=(steps,),
        out_shape=(jax.ShapeDtypeStruct((model, rows), BF16), wide, wide, wide, narrow, wide),
        in_specs=[
            SMEM_SPEC,
            fixed(rows, model),
            fixed(1, model),
            pl.BlockSpec((model, WIDE), lambda i: (0, i)),
            pl.BlockSpec((model, WIDE), lambda i: (0, steps + i)),
            pl.BlockSpec((depth.shape[0], WIDE), lambda i: (0, i)),
            pl.BlockSpec((WIDE, model), lambda i: (i, 0)),
        ],
        out_specs=(fixed(model, rows), column, column, column, column, fixed(rows, model)),
        scratch_shapes=[
            pltpu.VMEM((rows, model), BF16),
            pltpu.VMEM((WIDE // LANES, utterances, frames + 2 * MARGIN, LANES), F32),
        ],
        compiler_params=params(28),
        cost_estimate=cost(15),
        name="forward",
    )(lengths, features, gain, weight_in, weight_in, depth, weight_out)


def top_kernel(
    lengths_ref,
    residual_ref,
    gain_ref,
    head_ref,
    kept_ref,
    got_ref,
    loss_ref,
    final_ref,
    dlogits_ref,
    dresidual_ref,
):
    frames = residual_ref.shape[0]
    live = live_column(lengths_ref, pl.program_id(0), frames)
    values = residual_ref[...]
    centred = values - jnp.mean(values, axis=-1, keepdims=True)
    spread = jnp.mean(centred * centred, axis=-1, keepdims=True)
    inverse = lax.rsqrt(spread + 1e-05)
    unit = centred * inverse
    final = (unit * gain_ref[...]).astype(BF16)
    final_ref[...] = final

    def log_softmax(logits):
        shifted = logits - jnp.max(logits, axis=-1, keepdims=True)
        return shifted - jnp.log(jnp.sum(jnp.exp(shifted), axis=-1, keepdims=True))

    target = jnp.exp(log_softmax((kept_ref[0] + got_ref[0]) * (1.0 / TEACHERS)))
    logp = log_softmax(dot(final, head_ref[...]))
    cross = -jnp.sum(target * logp, axis=-1, keepdims=True)
    loss_ref[...] = jnp.broadcast_to(jnp.sum(cross * live, axis=0, keepdims=True), (1, 1, LANES))
    weight = jnp.sum(target, axis=-1, keepdims=True)
    dlogits = ((jnp.exp(logp) * weight - target) * live).astype(BF16)
    dlogits_ref[...] = dlogits
    dunit = dot(dlogits, head_ref[...], 1, 1) * gain_ref[...]
    average = jnp.mean(dunit, axis=-1, keepdims=True)
    along = jnp.mean(dunit * unit, axis=-1, keepdims=True)
    dresidual_ref[...] = (inverse * (dunit - average - unit * along)).astype(BF16)


def top(lengths, residual, gain, head, kept, got):
    rows, model = residual.shape
    utterances, frames, symbols = kept.shape
    per_row = pl.BlockSpec((frames, model), lambda i: (i, 0))
    sums = pl.BlockSpec((1, frames, symbols), lambda i: (i, 0, 0))
    return pl.pallas_call(
        top_kernel,
        grid=(utterances,),
        out_shape=(
            jax.ShapeDtypeStruct((utterances, 1, LANES), F32),
            jax.ShapeDtypeStruct((rows, model), BF16),
            jax.ShapeDtypeStruct((rows, symbols), BF16),
            jax.ShapeDtypeStruct((rows, model), BF16),
        ),
        in_specs=[SMEM_SPEC, per_row, fixed(1, model), fixed(model, symbols), sums, sums],
        out_specs=(
            pl.BlockSpec((1, 1, LANES), lambda i: (i, 0, 0)),
            per_row,
            pl.BlockSpec((frames, symbols), lambda i: (i, 0)),
            per_row,
        ),
        compiler_params=params(20),
        cost_estimate=cost(5),
        name="top",
    )(lengths, residual, gain, head, kept, got)


def outer_kernel(
    own_ref, active_ref, dresidual_ref, final_ref, dlogits_ref, send_ref, keep_ref, product_ref
):
    width = dresidual_ref.shape[1]
    product_ref[:, :width] = dot(active_ref[...], dresidual_ref[...], 0, 0)
    product_ref[:, width:] = dot(final_ref[...], dlogits_ref[...], 0, 0)
    write_pieces(own_ref, product_ref, send_ref, keep_ref, 0)


def outer(own, active, dresidual, final, dlogits):
    rows, model = active.shape
    half_out = dresidual.shape[1] // 2
    half_head = dlogits.shape[1] // 2
    width = half_out + half_head
    piece = (PLACES, model // (2 * PLACES), width)
    shape = jax.ShapeDtypeStruct((2,) + piece, BF16)
    out = pl.BlockSpec((1,) + piece, lambda i: (i, 0, 0, 0))
    return pl.pallas_call(
        outer_kernel,
        grid=(2,),
        out_shape=(shape, shape),
        in_specs=[
            SMEM_SPEC,
            fixed(rows, model),
            pl.BlockSpec((rows, half_out), lambda i: (0, i)),
            fixed(rows, model),
            pl.BlockSpec((rows, half_head), lambda i: (0, i)),
        ],
        out_specs=(out, out),
        scratch_shapes=[pltpu.VMEM((model, width), F32)],
        compiler_params=params(20),
        cost_estimate=cost(5),
        name="outer",
    )(own, active, dresidual, final, dlogits)


def inner_kernel(
    own_ref,
    lengths_ref,
    dresidual_ref,
    out_weight_ref,
    slope_ref,
    gated_ref,
    gate_ref,
    turned_ref,
    depth_ref,
    send_ref,
    keep_ref,
    dconv_ref,
    pad_ref,
    dvalue_ref,
    dgate_ref,
    product_ref,
):
    utterances = pad_ref.shape[1]
    frames = pad_ref.shape[2] - 2 * MARGIN

    @pl.when(pl.program_id(0) == 0)
    def _():
        clear_margins(pad_ref)

    for utterance in range(utterances):
        rows = slice(utterance * frames, (utterance + 1) * frames)
        dconv = dot(dresidual_ref[rows, :], out_weight_ref[...], 1, 1) * slope_ref[rows, :]
        dconv_ref[rows, :] = dconv
        for lane in range(WIDE // LANES):
            pad_ref[lane, utterance, MARGIN : MARGIN + frames, :] = dconv[
                :, lane * LANES : (lane + 1) * LANES
            ]

    for lane in range(WIDE // LANES):
        columns = slice(lane * LANES, (lane + 1) * LANES)

        def one(utterance, carry, lane=lane, columns=columns):
            for start in range(0, frames, TILE):
                rows = pl.ds(pl.multiple_of(utterance * frames + start, TILE), TILE)
                position = lax.broadcasted_iota(jnp.int32, (TILE, 1), 0) + start
                live = (position < lengths_ref[utterance]).astype(F32)
                dgated = convolve(pad_ref, lane, utterance, start, depth_ref, True) * live
                gate = gate_ref[rows, columns]
                dvalue_ref[rows, columns] = (dgated * gate).astype(BF16)
                dgate_ref[rows, columns] = (dgated * gated_ref[rows, columns] * (1.0 - gate)).astype(
                    BF16
                )
            return carry

        lax.fori_loop(0, utterances, one, 0)

    for group, source in ((0, dvalue_ref), (1, dgate_ref)):
        product_ref[...] = dot(turned_ref[...], source[...])
        write_pieces(own_ref, product_ref, send_ref, keep_ref, group)


def inner(own, lengths, dresidual, weight_out, slope, gated, gate, turned, depth, chunk, utterances):
    model, rows = turned.shape
    frames = rows // utterances
    steps = model // WIDE // CHUNKS
    first = chunk * steps
    column = pl.BlockSpec((rows, WIDE), lambda i: (0, first + i))
    piece = (2, PLACES, model // (2 * PLACES))
    shape = jax.ShapeDtypeStruct(piece + (steps * WIDE,), BF16)
    out = pl.BlockSpec(piece + (WIDE,), lambda i: (0, 0, 0, i))
    return pl.pallas_call(
        inner_kernel,
        grid=(steps,),
        out_shape=(shape, shape, jax.ShapeDtypeStruct((rows, steps * WIDE), F32)),
        in_specs=[
            SMEM_SPEC,
            SMEM_SPEC,
            fixed(rows, model),
            pl.BlockSpec((WIDE, model), lambda i: (first + i, 0)),
            column,
            column,
            column,
            fixed(model, rows),
            pl.BlockSpec((depth.shape[0], WIDE), lambda i: (0, first + i)),
        ],
        out_specs=(out, out, pl.BlockSpec((rows, WIDE), lambda i: (0, i))),
        scratch_shapes=[
            pltpu.VMEM((WIDE // LANES, utterances, frames + 2 * MARGIN, LANES), F32),
            pltpu.VMEM((rows, WIDE), BF16),
            pltpu.VMEM((rows, WIDE), BF16),
            pltpu.VMEM((model, WIDE), F32),
        ],
        compiler_params=params(24),
        cost_estimate=cost(11),
        name="inner",
    )(own, lengths, dresidual, weight_out, slope, gated, gate, turned, depth)


def taps_kernel(lengths_ref, gated_ref, *refs):
    *dconv_refs, out_ref, pad_ref, sums_ref = refs
    utterances = pad_ref.shape[1]
    frames = pad_ref.shape[2] - 2 * MARGIN
    taps = out_ref.shape[0] - 1
    step = pl.program_id(0)
    per_chunk = pl.num_programs(0) // len(dconv_refs)
    valid = lengths_ref[0]
    for utterance in range(1, utterances):
        valid = valid + lengths_ref[utterance]

    @pl.when(step == 0)
    def _():
        clear_margins(pad_ref)

    for lane in range(WIDE // LANES):
        columns = slice(lane * LANES, (lane + 1) * LANES)
        for utterance in range(utterances):
            rows = slice(utterance * frames, (utterance + 1) * frames)
            pad_ref[lane, utterance, MARGIN : MARGIN + frames, :] = gated_ref[rows, columns]

    for chunk, dconv_ref in enumerate(dconv_refs):

        @pl.when(step // per_chunk == chunk)
        def _(dconv_ref=dconv_ref):
            for lane in range(WIDE // LANES):
                columns = slice(lane * LANES, (lane + 1) * LANES)
                sums_ref[...] = jnp.zeros_like(sums_ref)

                def one(utterance, carry, lane=lane, columns=columns):
                    for start in range(0, frames, TILE):
                        rows = pl.ds(pl.multiple_of(utterance * frames + start, TILE), TILE)
                        dconv = dconv_ref[rows, columns]
                        for tap, view in shifted_views(pad_ref, lane, utterance, start, taps):
                            sums_ref[tap] += jnp.sum(
                                (view * dconv).reshape(TILE // 8, 8, LANES), axis=0
                            )
                    return carry

                lax.fori_loop(0, utterances, one, 0)
                out_ref[:taps, columns] = jnp.sum(sums_ref[...], axis=1)

    out_ref[taps:, :] = jnp.zeros((1, WIDE), F32) + valid.astype(F32)


def tap_sums(lengths, gated, dconvs, taps, utterances):
    rows, model = gated.shape
    steps = model // WIDE
    per_chunk = steps // len(dconvs)

    def part(chunk):
        low = chunk * per_chunk
        return pl.BlockSpec((rows, WIDE), lambda i: (0, jnp.clip(i - low, 0, per_chunk - 1)))

    return pl.pallas_call(
        taps_kernel,
        grid=(steps,),
        out_shape=jax.ShapeDtypeStruct((taps + 1, model), F32),
        in_specs=[SMEM_SPEC, pl.BlockSpec((rows, WIDE), lambda i: (0, i))]
        + [part(chunk) for chunk in range(len(dconvs))],
        out_specs=pl.BlockSpec((taps + 1, WIDE), lambda i: (0, i)),
        scratch_shapes=[
            pltpu.VMEM((WIDE // LANES, utterances, rows // utterances + 2 * MARGIN, LANES), F32),
            pltpu.VMEM((taps, 8, LANES), F32),
        ],
        compiler_params=params(16),
        cost_estimate=cost(9),
        name="taps",
    )(lengths, gated, *dconvs)


def gain_terms(weight, grad):
    terms = weight.astype(F32) * grad
    total = terms[:, :LANES]
    for first in range(LANES, terms.shape[1], LANES):
        total = total + terms[:, first : first + LANES]
    return total


def gain_row(terms):
    high = terms.astype(BF16)
    low = (terms - high.astype(F32)).astype(BF16)
    ones = jnp.ones((8, LANES), BF16)
    return (dot(ones, high, 1, 1) + dot(ones, low, 1, 1))[0:1, :]


def write_rows(own_ref, piece_refs, places, group, scale, targets):
    rows = piece_refs[0].shape[2]
    core = own_ref[0]
    first_place = pl.program_id(0) * places
    for index in range(places):
        for whose, (side, source) in enumerate(zip((core, 1 - core), piece_refs)):
            piece = (first_place + index) ^ own_ref[1 + whose]
            here = pl.ds(pl.multiple_of(index * 2 * rows + side * rows, rows), rows)
            for target, there, first, width in targets:
                target[here, there : there + width] = (
                    source[group, piece, :, first : first + width].astype(F32) * scale
                )


whole = pl.BlockSpec(memory_space=pltpu.VMEM)


def unpack_top_kernel(
    utts,
    own_ref,
    small_ref,
    mine_ref,
    other_ref,
    head_ref,
    gain_ref,
    losses_ref,
    wout_ref,
    dhead_ref,
    dgain_ref,
    depth_ref,
    loss_ref,
):
    taps = depth_ref.shape[0]
    scale = utts / small_ref[taps:, 0:1]
    half_out = wout_ref.shape[1] // 2
    half_head = dhead_ref.shape[1] // 2
    for group in range(2):
        targets = (
            (wout_ref, group * half_out, 0, half_out),
            (dhead_ref, group * half_head, half_out, half_head),
        )
        write_rows(own_ref, (mine_ref, other_ref), PLACES // 4, group, scale, targets)
    dgain_ref[...] = gain_row(gain_terms(head_ref[...], dhead_ref[...])) / gain_ref[...]
    depth_ref[...] = small_ref[:taps, :] * scale
    loss_ref[...] = losses_ref[...] * scale[None]


def unpack_top(utts, own, small, mine, other, head, gain, losses, width_out):
    steps = 4
    model, symbols = head.shape
    rows = model // steps
    taps = small.shape[0] - 1
    row = pl.BlockSpec((1, rows), lambda i, own_ref: (0, i))

    def block(width):
        return pl.BlockSpec((rows, width), lambda i, own_ref: (i, 0))

    return pl.pallas_call(
        functools.partial(unpack_top_kernel, utts),
        out_shape=(
            jax.ShapeDtypeStruct((model, width_out), F32),
            jax.ShapeDtypeStruct((model, symbols), F32),
            jax.ShapeDtypeStruct((1, model), F32),
            jax.ShapeDtypeStruct((taps, model), F32),
            jax.ShapeDtypeStruct(losses.shape, F32),
        ),
        grid_spec=pltpu.PrefetchScalarGridSpec(
            num_scalar_prefetch=1,
            grid=(steps,),
            in_specs=[
                fixed(*small.shape),
                whole,
                whole,
                block(symbols),
                row,
                fixed(*losses.shape),
            ],
            out_specs=(
                block(width_out),
                block(symbols),
                row,
                fixed(taps, model),
                fixed(*losses.shape),
            ),
        ),
        compiler_params=params(20),
        cost_estimate=cost(5),
        name="unpack_top",
    )(own, small, mine, other, head, gain, losses)


def unpack_inner_kernel(utts, own_ref, small_ref, weight_ref, gain_ref, *refs):
    *piece_refs, win_ref, dgain_ref = refs
    scale = utts / small_ref[small_ref.shape[0] - 1 :, 0:1]
    half = win_ref.shape[1] // 2
    for chunk in range(CHUNKS):
        pair = piece_refs[2 * chunk : 2 * chunk + 2]
        width = pair[0].shape[3]
        for group in range(2):
            targets = ((win_ref, group * half + chunk * width, 0, width),)
            write_rows(own_ref, pair, PLACES // 4, group, scale, targets)
    dgain_ref[...] = gain_row(gain_terms(weight_ref[...], win_ref[...])) / gain_ref[...]


def unpack_inner(utts, own, small, pieces, weight, gain):
    steps = 4
    model, width = weight.shape
    rows = model // steps
    row = pl.BlockSpec((1, rows), lambda i, own_ref: (0, i))
    block = pl.BlockSpec((rows, width), lambda i, own_ref: (i, 0))
    return pl.pallas_call(
        functools.partial(unpack_inner_kernel, utts),
        out_shape=(
            jax.ShapeDtypeStruct((model, width), F32),
            jax.ShapeDtypeStruct((1, model), F32),
        ),
        grid_spec=pltpu.PrefetchScalarGridSpec(
            num_scalar_prefetch=1,
            grid=(steps,),
            in_specs=[fixed(*small.shape), block, row]
            + [whole] * len(pieces),
            out_specs=(block, row),
        ),
        compiler_params=params(24),
        cost_estimate=cost(8),
        name="unpack_inner",
    )(own, small, weight, gain, *pieces)


def on_device(
    features,
    teacher_logits,
    lengths,
    gain_conv,
    weight_in,
    weight_depth,
    weight_out,
    gain_out,
    head_weight,
):
    count = 1
    for axis in ("member", "near", FAR, REST, CORE):
        count *= lax.axis_size(axis)
    member = lax.axis_index("member").astype(jnp.int32)[None]
    own = own_places()
    taps, model = weight_depth.shape
    utterances, frames, _ = features.shape
    utts = float(utterances * count)
    tie = lax.optimization_barrier

    give, kept = teacher_sums(member, teacher_logits, utterances)
    got = exchange(give, "member")
    flat = features.reshape(utterances * frames, model)
    turned, gated, gate, slope, active, residual = forward(
        lengths, flat, gain_conv[None], weight_in, weight_depth, weight_out, utterances
    )
    losses, final, dlogits, dresidual = top(
        lengths, residual, gain_out[None], head_weight, kept, got
    )

    line = Line()

    def products(name, chunk):
        nonlocal dresidual
        dresidual = line.before_kernel(dresidual)
        send, keep, dconv = inner(
            own,
            lengths,
            dresidual,
            weight_out,
            slope,
            gated,
            gate,
            turned,
            weight_depth,
            chunk,
            utterances,
        )
        line.begin(name, send, keep)
        line.put(name + "_conv", dconv)

    send, keep = outer(own, active, dresidual, final, dlogits)
    send, keep, dresidual = tie((send, keep, dresidual))
    line.begin("top", send, keep)
    products("in0", 0)
    line.step("top", start=False)
    products("in1", 1)
    written = {}

    def write_top():
        mine, other = line.values["top"]
        *rest, written["losses"] = unpack_top(
            utts,
            own,
            line.values["small"],
            line.after_last(mine),
            other,
            head_weight,
            gain_out[None],
            losses,
            weight_out.shape[1],
        )
        written["out"], written["head"], by_head, written["depth"] = rest
        line.put("by_head", by_head)

    def write_in():
        pieces = [array for name in ("in0", "in1") for array in line.values[name]]
        written["in"], by_in = unpack_inner(
            utts, own, line.values["small"], pieces, weight_in, gain_conv[None]
        )
        line.put("by_in", by_in)

    def sum_taps():
        names = ("in0_conv", "in1_conv")
        dconvs = line.after_last(tuple(line.values[name] for name in names))
        line.put("taps", tap_sums(lengths, gated, dconvs, taps, utterances))
        line.begin_small("small", line.values["taps"])

    kernels = {
        "taps": sum_taps,
        "write_top": write_top,
        "write_in": write_in,
    }
    for name in ORDER:
        if name in kernels:
            kernels[name]()
        else:
            line.step(name)
    return (
        line.values["by_in"].reshape(model),
        written["in"],
        written["depth"],
        written["out"],
        line.values["by_head"].reshape(model),
        written["head"],
        written["losses"][:, 0, 0],
    )


def solution(mesh):
    members, others = mesh.devices.shape
    near, cores = 2, 2
    far = 2 * PLACES // (members * near)
    rest = others // (far * near * cores)
    split = jax.sharding.Mesh(
        mesh.devices.reshape(members, rest, far, near, cores),
        ("member", REST, FAR, "near", CORE),
    )
    dp = (REST, FAR, "near", CORE)
    in_specs = (
        P(dp + ("member",), None, None),
        P("member", dp, None, None),
        P(dp + ("member",)),
        P(),
        P(),
        P(),
        P(),
        P(),
        P(),
    )
    out_specs = (P(), P(), P(), P(), P(), P(), P(dp + ("member",)))
    return jax.shard_map(
        on_device, mesh=split, in_specs=in_specs, out_specs=out_specs, check_vma=False
    )
```

```python
import functools

import jax
import jax.numpy as jnp
from jax import lax
from jax.experimental import pallas as pl
from jax.experimental.pallas import tpu as pltpu
from jax.sharding import PartitionSpec as P

TEACHERS = 4
PLACES = 8
WIDE = 256
LANES = 128
TILE = 128
MARGIN = 16
CHUNKS = 2
ORDER = (
    "top", "in0", "in1", "taps", "top", "in0", "in1", "small", "top", "in0", "in1", "small",
    "top", "in0", "in1", "small", "top", "in0", "in1", "small", "top", "in0", "in1", "small",
    "top", "in0", "in1", "top", "write_top", "in0", "in1", "in0", "in1", "write_in",
)
SMEM_SPEC = pl.BlockSpec(memory_space=pltpu.SMEM)
F32 = jnp.float32
BF16 = jnp.bfloat16


def params(mebibytes):
    return pltpu.CompilerParams(vmem_limit_bytes=mebibytes << 20)


def cost(microseconds):
    return pl.CostEstimate(flops=int(microseconds * 1.15e9), bytes_accessed=1 << 20, transcendentals=0)


def dot(left, right, left_axis=1, right_axis=0):
    return lax.dot_general(
        left, right, (((left_axis,), (right_axis,)), ((), ())), preferred_element_type=F32
    )


def fixed(*shape):
    return pl.BlockSpec(shape, lambda i, *_: (0,) * len(shape))


FAR = "far"
REST = "rest"
CORE = "core"
ALL = ("member", REST, FAR, "near", CORE)
STEPS = ("first", "second", "third", "fourth")


def exchange(values, step):
    if step in (CORE, "member"):
        return lax.ppermute(values, step, [(0, 1), (1, 0)])
    count = 1
    for name in ALL:
        count *= lax.axis_size(name)
    bits = (count // 2, 2, 4, 8)
    place = STEPS.index(step)
    return lax.ppermute(values, ALL, [(i, i ^ bits[place ^ (i % 2)]) for i in range(count)])


def add(own, other):
    return (own.astype(F32) + other.astype(F32)).astype(own.dtype)


def own_places():
    core, member, near = lax.axis_index(CORE), lax.axis_index("member"), lax.axis_index("near")
    far = lax.axis_index(FAR)
    places = (member * 4 + near * 2 + (far & 1), near * 4 + member * 2 + (far >> 1))
    own = jnp.where(core == 0, places[0], places[1])
    other = jnp.where(core == 0, places[1], places[0])
    return jnp.stack([core, own, other]).astype(jnp.int32)


def over_rest(values):
    return lax.psum(values, REST) if lax.axis_size(REST) > 1 else values


class Line:
    def __init__(self):
        self.values = {}
        self.pending = {}
        self.steps = {}
        self.last = None

    def after_last(self, value):
        if self.last is not None:
            value, self.values[self.last] = lax.optimization_barrier(
                (value, self.values[self.last])
            )
        return value

    def before_kernel(self, value):
        value = self.after_last(value)
        if self.last in self.steps and self.last not in self.pending:
            self.start(self.last)
        return value

    def put(self, name, value):
        self.values[name] = value
        self.last = name

    def begin(self, name, send, keep):
        self.values[name] = keep
        self.pending[name] = exchange(send, CORE)
        self.steps[name] = [
            ("add", CORE),
            ("halve", "first"),
            ("halve", "second"),
            ("halve", "third"),
            ("double", "fourth"),
            ("gather", "third"),
            ("gather", "second"),
            ("gather", "first"),
            ("done", CORE),
        ]

    def begin_small(self, name, value):
        self.values[name] = value
        self.steps[name] = [("sum", step) for step in STEPS + (CORE,)]
        self.start(name)

    def start(self, name):
        if not self.steps[name]:
            return
        kind, step = self.steps[name][0]
        values = self.values[name]
        if kind == "halve":
            values = values[:, values.shape[1] // 2 :]
        self.pending[name] = exchange(values, step)

    def step(self, name, start=True):
        kind, _ = self.steps[name].pop(0)
        got = self.after_last(self.pending.pop(name))
        own = self.values[name]
        if kind == "halve":
            own = own[:, : got.shape[1]]
        if kind == "gather":
            result = jnp.concatenate([own, got], axis=1)
        elif kind == "done":
            result = (own, got)
        else:
            result = add(own, got)
        if kind == "double" or (kind == "sum" and not self.steps[name]):
            result = over_rest(result)
        self.put(name, result)
        if start:
            self.start(name)


def write_pieces(own_ref, product, send_ref, keep_ref, group):
    rows = keep_ref.shape[-2]
    core = own_ref[0]

    def one(piece, carry):
        kept = pl.multiple_of((2 * (piece ^ own_ref[1]) + core) * rows, rows)
        sent = pl.multiple_of((2 * (piece ^ own_ref[2]) + 1 - core) * rows, rows)
        keep_ref[group, piece] = product[pl.ds(kept, rows), :].astype(BF16)
        send_ref[group, piece] = product[pl.ds(sent, rows), :].astype(BF16)
        return carry

    lax.fori_loop(0, keep_ref.shape[1], one, 0)


def teacher_kernel(member_ref, logits_ref, give_ref, keep_ref, *, own_count):
    step = pl.program_id(0)
    total = None
    for teacher in range(logits_ref.shape[0]):
        logits = logits_ref[teacher, 0].astype(F32)
        shifted = logits - jnp.max(logits, axis=-1, keepdims=True)
        logp = shifted - jnp.log(jnp.sum(jnp.exp(shifted), axis=-1, keepdims=True))
        total = logp if total is None else total + logp

    @pl.when(step < own_count)
    def _():
        give_ref[0] = total

    @pl.when(step >= own_count)
    def _():
        keep_ref[0] = total


def teacher_sums(member, logits, own_count):
    teachers, utterances, frames, symbols = logits.shape
    shape = jax.ShapeDtypeStruct((own_count, frames, symbols), F32)

    def source(i, member_ref):
        mine = member_ref[0] * own_count
        theirs = (1 - member_ref[0]) * own_count
        return (0, jnp.where(i < own_count, theirs + i, mine + i - own_count), 0, 0)

    return pl.pallas_call(
        functools.partial(teacher_kernel, own_count=own_count),
        out_shape=(shape, shape),
        grid_spec=pltpu.PrefetchScalarGridSpec(
            num_scalar_prefetch=1,
            grid=(2 * own_count,),
            in_specs=[pl.BlockSpec((teachers, 1, frames, symbols), source)],
            out_specs=(
                pl.BlockSpec(
                    (1, frames, symbols), lambda i, _: (jnp.minimum(i, own_count - 1), 0, 0)
                ),
                pl.BlockSpec(
                    (1, frames, symbols), lambda i, _: (jnp.maximum(i - own_count, 0), 0, 0)
                ),
            ),
        ),
        compiler_params=params(16),
        cost_estimate=cost(4),
        name="teachers",
    )(member, logits)


def live_column(lengths_ref, utterance, frames):
    position = lax.broadcasted_iota(jnp.int32, (frames, 1), 0)
    return (position < lengths_ref[utterance]).astype(F32)


def clear_margins(pad_ref):
    frames = pad_ref.shape[2] - 2 * MARGIN
    zeros = jnp.zeros(pad_ref.shape[:2] + (MARGIN, LANES), F32)
    pad_ref[:, :, :MARGIN, :] = zeros
    pad_ref[:, :, MARGIN + frames :, :] = zeros


def shifted_views(pad_ref, lane, utterance, start, taps):
    first = MARGIN - taps // 2
    for phase in range(8):
        offsets = [offset for offset in range(first, first + taps) if offset % 8 == phase]
        if not offsets:
            continue
        low = offsets[0]
        span = offsets[-1] - low + TILE
        view = pad_ref[lane, utterance, start + low : start + low + span, :]
        for offset in offsets:
            yield offset - first, view[offset - low : offset - low + TILE]


def convolve(pad_ref, lane, utterance, start, depth_ref, flipped):
    taps = depth_ref.shape[0]
    columns = slice(lane * LANES, (lane + 1) * LANES)
    total = jnp.zeros((TILE, LANES), F32)
    for tap, view in shifted_views(pad_ref, lane, utterance, start, taps):
        row = taps - 1 - tap if flipped else tap
        total = total + view * depth_ref[row : row + 1, columns]
    return total


def forward_kernel(
    lengths_ref,
    features_ref,
    gain_ref,
    value_weight_ref,
    gate_weight_ref,
    depth_ref,
    out_weight_ref,
    turned_ref,
    gated_ref,
    gate_ref,
    slope_ref,
    active_ref,
    residual_ref,
    normed_ref,
    pad_ref,
):
    utterances = pad_ref.shape[1]
    frames = pad_ref.shape[2] - 2 * MARGIN

    @pl.when(pl.program_id(0) == 0)
    def _():
        values = features_ref[...].astype(F32)
        centred = values - jnp.mean(values, axis=-1, keepdims=True)
        spread = jnp.mean(centred * centred, axis=-1, keepdims=True)
        normed = centred * lax.rsqrt(spread + 1e-05) * gain_ref[...]
        normed_ref[...] = normed.astype(BF16)
        turned_ref[...] = normed.T.astype(BF16)
        residual_ref[...] = values
        clear_margins(pad_ref)

    for utterance in range(utterances):
        rows = slice(utterance * frames, (utterance + 1) * frames)
        normed = normed_ref[rows, :]
        gate = jax.nn.sigmoid(dot(normed, gate_weight_ref[...]))
        gated = dot(normed, value_weight_ref[...]) * gate
        gated = gated * live_column(lengths_ref, utterance, frames)
        gate_ref[rows, :] = gate
        gated_ref[rows, :] = gated
        for lane in range(WIDE // LANES):
            pad_ref[lane, utterance, MARGIN : MARGIN + frames, :] = gated[
                :, lane * LANES : (lane + 1) * LANES
            ]

    for lane in range(WIDE // LANES):
        columns = slice(lane * LANES, (lane + 1) * LANES)

        def one(utterance, carry, lane=lane, columns=columns):
            for start in range(0, frames, TILE):
                rows = pl.ds(pl.multiple_of(utterance * frames + start, TILE), TILE)
                convolved = convolve(pad_ref, lane, utterance, start, depth_ref, False)
                squash = jax.nn.sigmoid(convolved)
                active_ref[rows, columns] = (convolved * squash).astype(BF16)
                slope_ref[rows, columns] = squash * (1.0 + convolved * (1.0 - squash))
            return carry

        lax.fori_loop(0, utterances, one, 0)

    residual_ref[...] += dot(active_ref[...], out_weight_ref[...])


def forward(lengths, features, gain, weight_in, depth, weight_out, utterances):
    rows, model = features.shape
    frames = rows // utterances
    steps = model // WIDE
    column = pl.BlockSpec((rows, WIDE), lambda i: (0, i))
    wide = jax.ShapeDtypeStruct((rows, model), F32)
    narrow = jax.ShapeDtypeStruct((rows, model), BF16)
    return pl.pallas_call(
        forward_kernel,
        grid=(steps,),
        out_shape=(jax.ShapeDtypeStruct((model, rows), BF16), wide, wide, wide, narrow, wide),
        in_specs=[
            SMEM_SPEC,
            fixed(rows, model),
            fixed(1, model),
            pl.BlockSpec((model, WIDE), lambda i: (0, i)),
            pl.BlockSpec((model, WIDE), lambda i: (0, steps + i)),
            pl.BlockSpec((depth.shape[0], WIDE), lambda i: (0, i)),
            pl.BlockSpec((WIDE, model), lambda i: (i, 0)),
        ],
        out_specs=(fixed(model, rows), column, column, column, column, fixed(rows, model)),
        scratch_shapes=[
            pltpu.VMEM((rows, model), BF16),
            pltpu.VMEM((WIDE // LANES, utterances, frames + 2 * MARGIN, LANES), F32),
        ],
        compiler_params=params(28),
        cost_estimate=cost(15),
        name="forward",
    )(lengths, features, gain, weight_in, weight_in, depth, weight_out)


def top_kernel(
    lengths_ref,
    residual_ref,
    gain_ref,
    head_ref,
    kept_ref,
    got_ref,
    loss_ref,
    final_ref,
    dlogits_ref,
    dresidual_ref,
):
    frames = residual_ref.shape[0]
    live = live_column(lengths_ref, pl.program_id(0), frames)
    values = residual_ref[...]
    centred = values - jnp.mean(values, axis=-1, keepdims=True)
    spread = jnp.mean(centred * centred, axis=-1, keepdims=True)
    inverse = lax.rsqrt(spread + 1e-05)
    unit = centred * inverse
    final = (unit * gain_ref[...]).astype(BF16)
    final_ref[...] = final

    def log_softmax(logits):
        shifted = logits - jnp.max(logits, axis=-1, keepdims=True)
        return shifted - jnp.log(jnp.sum(jnp.exp(shifted), axis=-1, keepdims=True))

    target = jnp.exp(log_softmax((kept_ref[0] + got_ref[0]) * (1.0 / TEACHERS)))
    logp = log_softmax(dot(final, head_ref[...]))
    cross = -jnp.sum(target * logp, axis=-1, keepdims=True)
    loss_ref[...] = jnp.broadcast_to(jnp.sum(cross * live, axis=0, keepdims=True), (1, 1, LANES))
    weight = jnp.sum(target, axis=-1, keepdims=True)
    dlogits = ((jnp.exp(logp) * weight - target) * live).astype(BF16)
    dlogits_ref[...] = dlogits
    dunit = dot(dlogits, head_ref[...], 1, 1) * gain_ref[...]
    average = jnp.mean(dunit, axis=-1, keepdims=True)
    along = jnp.mean(dunit * unit, axis=-1, keepdims=True)
    dresidual_ref[...] = (inverse * (dunit - average - unit * along)).astype(BF16)


def top(lengths, residual, gain, head, kept, got):
    rows, model = residual.shape
    utterances, frames, symbols = kept.shape
    per_row = pl.BlockSpec((frames, model), lambda i: (i, 0))
    sums = pl.BlockSpec((1, frames, symbols), lambda i: (i, 0, 0))
    return pl.pallas_call(
        top_kernel,
        grid=(utterances,),
        out_shape=(
            jax.ShapeDtypeStruct((utterances, 1, LANES), F32),
            jax.ShapeDtypeStruct((rows, model), BF16),
            jax.ShapeDtypeStruct((rows, symbols), BF16),
            jax.ShapeDtypeStruct((rows, model), BF16),
        ),
        in_specs=[SMEM_SPEC, per_row, fixed(1, model), fixed(model, symbols), sums, sums],
        out_specs=(
            pl.BlockSpec((1, 1, LANES), lambda i: (i, 0, 0)),
            per_row,
            pl.BlockSpec((frames, symbols), lambda i: (i, 0)),
            per_row,
        ),
        compiler_params=params(20),
        cost_estimate=cost(5),
        name="top",
    )(lengths, residual, gain, head, kept, got)


def outer_kernel(
    own_ref, active_ref, dresidual_ref, final_ref, dlogits_ref, send_ref, keep_ref, product_ref
):
    width = dresidual_ref.shape[1]
    product_ref[:, :width] = dot(active_ref[...], dresidual_ref[...], 0, 0)
    product_ref[:, width:] = dot(final_ref[...], dlogits_ref[...], 0, 0)
    write_pieces(own_ref, product_ref, send_ref, keep_ref, 0)


def outer(own, active, dresidual, final, dlogits):
    rows, model = active.shape
    half_out = dresidual.shape[1] // 2
    half_head = dlogits.shape[1] // 2
    width = half_out + half_head
    piece = (PLACES, model // (2 * PLACES), width)
    shape = jax.ShapeDtypeStruct((2,) + piece, BF16)
    out = pl.BlockSpec((1,) + piece, lambda i: (i, 0, 0, 0))
    return pl.pallas_call(
        outer_kernel,
        grid=(2,),
        out_shape=(shape, shape),
        in_specs=[
            SMEM_SPEC,
            fixed(rows, model),
            pl.BlockSpec((rows, half_out), lambda i: (0, i)),
            fixed(rows, model),
            pl.BlockSpec((rows, half_head), lambda i: (0, i)),
        ],
        out_specs=(out, out),
        scratch_shapes=[pltpu.VMEM((model, width), F32)],
        compiler_params=params(20),
        cost_estimate=cost(5),
        name="outer",
    )(own, active, dresidual, final, dlogits)


def inner_kernel(
    own_ref,
    lengths_ref,
    dresidual_ref,
    out_weight_ref,
    slope_ref,
    gated_ref,
    gate_ref,
    turned_ref,
    depth_ref,
    send_ref,
    keep_ref,
    dconv_ref,
    pad_ref,
    dvalue_ref,
    dgate_ref,
    product_ref,
):
    utterances = pad_ref.shape[1]
    frames = pad_ref.shape[2] - 2 * MARGIN

    @pl.when(pl.program_id(0) == 0)
    def _():
        clear_margins(pad_ref)

    for utterance in range(utterances):
        rows = slice(utterance * frames, (utterance + 1) * frames)
        dconv = dot(dresidual_ref[rows, :], out_weight_ref[...], 1, 1) * slope_ref[rows, :]
        dconv_ref[rows, :] = dconv
        for lane in range(WIDE // LANES):
            pad_ref[lane, utterance, MARGIN : MARGIN + frames, :] = dconv[
                :, lane * LANES : (lane + 1) * LANES
            ]

    for lane in range(WIDE // LANES):
        columns = slice(lane * LANES, (lane + 1) * LANES)

        def one(utterance, carry, lane=lane, columns=columns):
            for start in range(0, frames, TILE):
                rows = pl.ds(pl.multiple_of(utterance * frames + start, TILE), TILE)
                position = lax.broadcasted_iota(jnp.int32, (TILE, 1), 0) + start
                live = (position < lengths_ref[utterance]).astype(F32)
                dgated = convolve(pad_ref, lane, utterance, start, depth_ref, True) * live
                gate = gate_ref[rows, columns]
                dvalue_ref[rows, columns] = (dgated * gate).astype(BF16)
                dgate_ref[rows, columns] = (dgated * gated_ref[rows, columns] * (1.0 - gate)).astype(
                    BF16
                )
            return carry

        lax.fori_loop(0, utterances, one, 0)

    for group, source in ((0, dvalue_ref), (1, dgate_ref)):
        product_ref[...] = dot(turned_ref[...], source[...])
        write_pieces(own_ref, product_ref, send_ref, keep_ref, group)


def inner(own, lengths, dresidual, weight_out, slope, gated, gate, turned, depth, chunk, utterances):
    model, rows = turned.shape
    frames = rows // utterances
    steps = model // WIDE // CHUNKS
    first = chunk * steps
    column = pl.BlockSpec((rows, WIDE), lambda i: (0, first + i))
    piece = (2, PLACES, model // (2 * PLACES))
    shape = jax.ShapeDtypeStruct(piece + (steps * WIDE,), BF16)
    out = pl.BlockSpec(piece + (WIDE,), lambda i: (0, 0, 0, i))
    return pl.pallas_call(
        inner_kernel,
        grid=(steps,),
        out_shape=(shape, shape, jax.ShapeDtypeStruct((rows, steps * WIDE), F32)),
        in_specs=[
            SMEM_SPEC,
            SMEM_SPEC,
            fixed(rows, model),
            pl.BlockSpec((WIDE, model), lambda i: (first + i, 0)),
            column,
            column,
            column,
            fixed(model, rows),
            pl.BlockSpec((depth.shape[0], WIDE), lambda i: (0, first + i)),
        ],
        out_specs=(out, out, pl.BlockSpec((rows, WIDE), lambda i: (0, i))),
        scratch_shapes=[
            pltpu.VMEM((WIDE // LANES, utterances, frames + 2 * MARGIN, LANES), F32),
            pltpu.VMEM((rows, WIDE), BF16),
            pltpu.VMEM((rows, WIDE), BF16),
            pltpu.VMEM((model, WIDE), F32),
        ],
        compiler_params=params(24),
        cost_estimate=cost(11),
        name="inner",
    )(own, lengths, dresidual, weight_out, slope, gated, gate, turned, depth)


def taps_kernel(lengths_ref, gated_ref, *refs):
    *dconv_refs, out_ref, pad_ref, sums_ref = refs
    utterances = pad_ref.shape[1]
    frames = pad_ref.shape[2] - 2 * MARGIN
    taps = out_ref.shape[0] - 1
    step = pl.program_id(0)
    per_chunk = pl.num_programs(0) // len(dconv_refs)
    valid = lengths_ref[0]
    for utterance in range(1, utterances):
        valid = valid + lengths_ref[utterance]

    @pl.when(step == 0)
    def _():
        clear_margins(pad_ref)

    for lane in range(WIDE // LANES):
        columns = slice(lane * LANES, (lane + 1) * LANES)
        for utterance in range(utterances):
            rows = slice(utterance * frames, (utterance + 1) * frames)
            pad_ref[lane, utterance, MARGIN : MARGIN + frames, :] = gated_ref[rows, columns]

    for chunk, dconv_ref in enumerate(dconv_refs):

        @pl.when(step // per_chunk == chunk)
        def _(dconv_ref=dconv_ref):
            for lane in range(WIDE // LANES):
                columns = slice(lane * LANES, (lane + 1) * LANES)
                sums_ref[...] = jnp.zeros_like(sums_ref)

                def one(utterance, carry, lane=lane, columns=columns):
                    for start in range(0, frames, TILE):
                        rows = pl.ds(pl.multiple_of(utterance * frames + start, TILE), TILE)
                        dconv = dconv_ref[rows, columns]
                        for tap, view in shifted_views(pad_ref, lane, utterance, start, taps):
                            sums_ref[tap] += jnp.sum(
                                (view * dconv).reshape(TILE // 8, 8, LANES), axis=0
                            )
                    return carry

                lax.fori_loop(0, utterances, one, 0)
                out_ref[:taps, columns] = jnp.sum(sums_ref[...], axis=1)

    out_ref[taps:, :] = jnp.zeros((1, WIDE), F32) + valid.astype(F32)


def tap_sums(lengths, gated, dconvs, taps, utterances):
    rows, model = gated.shape
    steps = model // WIDE
    per_chunk = steps // len(dconvs)

    def part(chunk):
        low = chunk * per_chunk
        return pl.BlockSpec((rows, WIDE), lambda i: (0, jnp.clip(i - low, 0, per_chunk - 1)))

    return pl.pallas_call(
        taps_kernel,
        grid=(steps,),
        out_shape=jax.ShapeDtypeStruct((taps + 1, model), F32),
        in_specs=[SMEM_SPEC, pl.BlockSpec((rows, WIDE), lambda i: (0, i))]
        + [part(chunk) for chunk in range(len(dconvs))],
        out_specs=pl.BlockSpec((taps + 1, WIDE), lambda i: (0, i)),
        scratch_shapes=[
            pltpu.VMEM((WIDE // LANES, utterances, rows // utterances + 2 * MARGIN, LANES), F32),
            pltpu.VMEM((taps, 8, LANES), F32),
        ],
        compiler_params=params(16),
        cost_estimate=cost(9),
        name="taps",
    )(lengths, gated, *dconvs)


def gain_terms(weight, grad):
    terms = weight.astype(F32) * grad
    total = terms[:, :LANES]
    for first in range(LANES, terms.shape[1], LANES):
        total = total + terms[:, first : first + LANES]
    return total


def gain_row(terms):
    high = terms.astype(BF16)
    low = (terms - high.astype(F32)).astype(BF16)
    ones = jnp.ones((8, LANES), BF16)
    return (dot(ones, high, 1, 1) + dot(ones, low, 1, 1))[0:1, :]


def write_rows(own_ref, piece_refs, places, group, scale, targets):
    rows = piece_refs[0].shape[2]
    core = own_ref[0]
    first_place = pl.program_id(0) * places
    for index in range(places):
        for whose, (side, source) in enumerate(zip((core, 1 - core), piece_refs)):
            piece = (first_place + index) ^ own_ref[1 + whose]
            here = pl.ds(pl.multiple_of(index * 2 * rows + side * rows, rows), rows)
            for target, there, first, width in targets:
                target[here, there : there + width] = (
                    source[group, piece, :, first : first + width].astype(F32) * scale
                )


whole = pl.BlockSpec(memory_space=pltpu.VMEM)


def unpack_top_kernel(
    utts,
    own_ref,
    small_ref,
    mine_ref,
    other_ref,
    head_ref,
    gain_ref,
    losses_ref,
    wout_ref,
    dhead_ref,
    dgain_ref,
    depth_ref,
    loss_ref,
):
    taps = depth_ref.shape[0]
    scale = utts / small_ref[taps:, 0:1]
    half_out = wout_ref.shape[1] // 2
    half_head = dhead_ref.shape[1] // 2
    for group in range(2):
        targets = (
            (wout_ref, group * half_out, 0, half_out),
            (dhead_ref, group * half_head, half_out, half_head),
        )
        write_rows(own_ref, (mine_ref, other_ref), PLACES // 4, group, scale, targets)
    dgain_ref[...] = gain_row(gain_terms(head_ref[...], dhead_ref[...])) / gain_ref[...]
    depth_ref[...] = small_ref[:taps, :] * scale
    loss_ref[...] = losses_ref[...] * scale[None]


def unpack_top(utts, own, small, mine, other, head, gain, losses, width_out):
    steps = 4
    model, symbols = head.shape
    rows = model // steps
    taps = small.shape[0] - 1
    row = pl.BlockSpec((1, rows), lambda i, own_ref: (0, i))

    def block(width):
        return pl.BlockSpec((rows, width), lambda i, own_ref: (i, 0))

    return pl.pallas_call(
        functools.partial(unpack_top_kernel, utts),
        out_shape=(
            jax.ShapeDtypeStruct((model, width_out), F32),
            jax.ShapeDtypeStruct((model, symbols), F32),
            jax.ShapeDtypeStruct((1, model), F32),
            jax.ShapeDtypeStruct((taps, model), F32),
            jax.ShapeDtypeStruct(losses.shape, F32),
        ),
        grid_spec=pltpu.PrefetchScalarGridSpec(
            num_scalar_prefetch=1,
            grid=(steps,),
            in_specs=[
                fixed(*small.shape),
                whole,
                whole,
                block(symbols),
                row,
                fixed(*losses.shape),
            ],
            out_specs=(
                block(width_out),
                block(symbols),
                row,
                fixed(taps, model),
                fixed(*losses.shape),
            ),
        ),
        compiler_params=params(20),
        cost_estimate=cost(5),
        name="unpack_top",
    )(own, small, mine, other, head, gain, losses)


def unpack_inner_kernel(utts, own_ref, small_ref, weight_ref, gain_ref, *refs):
    *piece_refs, win_ref, dgain_ref = refs
    scale = utts / small_ref[small_ref.shape[0] - 1 :, 0:1]
    half = win_ref.shape[1] // 2
    for chunk in range(CHUNKS):
        pair = piece_refs[2 * chunk : 2 * chunk + 2]
        width = pair[0].shape[3]
        for group in range(2):
            targets = ((win_ref, group * half + chunk * width, 0, width),)
            write_rows(own_ref, pair, PLACES // 4, group, scale, targets)
    dgain_ref[...] = gain_row(gain_terms(weight_ref[...], win_ref[...])) / gain_ref[...]


def unpack_inner(utts, own, small, pieces, weight, gain):
    steps = 4
    model, width = weight.shape
    rows = model // steps
    row = pl.BlockSpec((1, rows), lambda i, own_ref: (0, i))
    block = pl.BlockSpec((rows, width), lambda i, own_ref: (i, 0))
    return pl.pallas_call(
        functools.partial(unpack_inner_kernel, utts),
        out_shape=(
            jax.ShapeDtypeStruct((model, width), F32),
            jax.ShapeDtypeStruct((1, model), F32),
        ),
        grid_spec=pltpu.PrefetchScalarGridSpec(
            num_scalar_prefetch=1,
            grid=(steps,),
            in_specs=[fixed(*small.shape), block, row]
            + [whole] * len(pieces),
            out_specs=(block, row),
        ),
        compiler_params=params(24),
        cost_estimate=cost(8),
        name="unpack_inner",
    )(own, small, weight, gain, *pieces)


def on_device(
    features,
    teacher_logits,
    lengths,
    gain_conv,
    weight_in,
    weight_depth,
    weight_out,
    gain_out,
    head_weight,
):
    count = 1
    for axis in ("member", "near", FAR, REST, CORE):
        count *= lax.axis_size(axis)
    member = lax.axis_index("member").astype(jnp.int32)[None]
    own = own_places()
    taps, model = weight_depth.shape
    utterances, frames, _ = features.shape
    utts = float(utterances * count)
    tie = lax.optimization_barrier

    own, member, teacher_logits = tie((own, member, teacher_logits))
    give, kept = teacher_sums(member, teacher_logits, utterances)
    got = exchange(give, "member")
    flat = features.reshape(utterances * frames, model)
    turned, gated, gate, slope, active, residual = forward(
        lengths, flat, gain_conv[None], weight_in, weight_depth, weight_out, utterances
    )
    losses, final, dlogits, dresidual = top(
        lengths, residual, gain_out[None], head_weight, kept, got
    )

    line = Line()

    def products(name, chunk):
        nonlocal dresidual
        dresidual = line.before_kernel(dresidual)
        send, keep, dconv = inner(
            own,
            lengths,
            dresidual,
            weight_out,
            slope,
            gated,
            gate,
            turned,
            weight_depth,
            chunk,
            utterances,
        )
        line.begin(name, send, keep)
        line.put(name + "_conv", dconv)

    send, keep = outer(own, active, dresidual, final, dlogits)
    send, keep, dresidual = tie((send, keep, dresidual))
    line.begin("top", send, keep)
    products("in0", 0)
    line.step("top", start=False)
    products("in1", 1)
    written = {}

    def write_top():
        mine, other = line.values["top"]
        *rest, written["losses"] = unpack_top(
            utts,
            own,
            line.values["small"],
            line.after_last(mine),
            other,
            head_weight,
            gain_out[None],
            losses,
            weight_out.shape[1],
        )
        written["out"], written["head"], by_head, written["depth"] = rest
        line.put("by_head", by_head)

    def write_in():
        pieces = [array for name in ("in0", "in1") for array in line.values[name]]
        written["in"], by_in = unpack_inner(
            utts, own, line.values["small"], pieces, weight_in, gain_conv[None]
        )
        line.put("by_in", by_in)

    def sum_taps():
        names = ("in0_conv", "in1_conv")
        dconvs = line.after_last(tuple(line.values[name] for name in names))
        line.put("taps", tap_sums(lengths, gated, dconvs, taps, utterances))
        line.begin_small("small", line.values["taps"])

    kernels = {
        "taps": sum_taps,
        "write_top": write_top,
        "write_in": write_in,
    }
    for name in ORDER:
        if name in kernels:
            kernels[name]()
        else:
            line.step(name)
    return (
        line.values["by_in"].reshape(model),
        written["in"],
        written["depth"],
        written["out"],
        line.values["by_head"].reshape(model),
        written["head"],
        written["losses"][:, 0, 0],
    )


def solution(mesh):
    members, others = mesh.devices.shape
    near, cores = 2, 2
    far = 2 * PLACES // (members * near)
    rest = others // (far * near * cores)
    split = jax.sharding.Mesh(
        mesh.devices.reshape(members, rest, far, near, cores),
        ("member", REST, FAR, "near", CORE),
    )
    dp = (REST, FAR, "near", CORE)
    in_specs = (
        P(dp + ("member",), None, None),
        P("member", dp, None, None),
        P(dp + ("member",)),
        P(),
        P(),
        P(),
        P(),
        P(),
        P(),
    )
    out_specs = (P(), P(), P(), P(), P(), P(), P(dp + ("member",)))
    return jax.shard_map(
        on_device, mesh=split, in_specs=in_specs, out_specs=out_specs, check_vma=False
    )
```

```python
import functools

import jax
import jax.numpy as jnp
from jax import lax
from jax.experimental import pallas as pl
from jax.experimental.pallas import tpu as pltpu
from jax.sharding import PartitionSpec as P

TEACHERS = 4
PLACES = 8
WIDE = 256
LANES = 128
TILE = 128
MARGIN = 16
CHUNKS = 2
ORDER = (
    "taps", "in", "top", "small", "top", "small", "in", "top", "small", "top", "in", "top",
    "small", "in", "top", "small", "in", "top", "in", "top", "write_top", "in", "in", "in",
    "write_in",
)
SMEM_SPEC = pl.BlockSpec(memory_space=pltpu.SMEM)
F32 = jnp.float32
BF16 = jnp.bfloat16


def params(mebibytes):
    return pltpu.CompilerParams(vmem_limit_bytes=mebibytes << 20)


def cost(microseconds):
    return pl.CostEstimate(flops=int(microseconds * 1.15e9), bytes_accessed=1 << 20, transcendentals=0)


def dot(left, right, left_axis=1, right_axis=0):
    return lax.dot_general(
        left, right, (((left_axis,), (right_axis,)), ((), ())), preferred_element_type=F32
    )


def fixed(*shape):
    return pl.BlockSpec(shape, lambda i, *_: (0,) * len(shape))


FAR = "far"
REST = "rest"
CORE = "core"
ALL = ("member", REST, FAR, "near", CORE)
STEPS = ("first", "second", "third", "fourth")


def exchange(values, step):
    if step in (CORE, "member"):
        return lax.ppermute(values, step, [(0, 1), (1, 0)])
    count = 1
    for name in ALL:
        count *= lax.axis_size(name)
    bits = (count // 2, 2, 4, 8)
    place = STEPS.index(step)
    return lax.ppermute(values, ALL, [(i, i ^ bits[place ^ (i % 2)]) for i in range(count)])


def add(own, other):
    return (own.astype(F32) + other.astype(F32)).astype(own.dtype)


def own_places():
    core, member, near = lax.axis_index(CORE), lax.axis_index("member"), lax.axis_index("near")
    far = lax.axis_index(FAR)
    places = (member * 4 + near * 2 + (far & 1), near * 4 + member * 2 + (far >> 1))
    own = jnp.where(core == 0, places[0], places[1])
    other = jnp.where(core == 0, places[1], places[0])
    return jnp.stack([core, own, other]).astype(jnp.int32)


def over_rest(values):
    return lax.psum(values, REST) if lax.axis_size(REST) > 1 else values


class Line:
    def __init__(self):
        self.values = {}
        self.pending = {}
        self.steps = {}
        self.last = None

    def after_last(self, value):
        if self.last is not None:
            value, self.values[self.last] = lax.optimization_barrier(
                (value, self.values[self.last])
            )
        return value

    def before_kernel(self, value):
        value = self.after_last(value)
        if self.last in self.steps and self.last not in self.pending:
            self.start(self.last)
        return value

    def put(self, name, value):
        self.values[name] = value
        self.last = name

    def begin(self, name, send, keep):
        self.values[name] = keep
        self.pending[name] = exchange(send, CORE)
        self.steps[name] = [
            ("add", CORE),
            ("halve", "first"),
            ("halve", "second"),
            ("halve", "third"),
            ("double", "fourth"),
            ("gather", "third"),
            ("gather", "second"),
            ("gather", "first"),
            ("done", CORE),
        ]

    def begin_small(self, name, value):
        self.values[name] = value
        self.steps[name] = [("sum", step) for step in STEPS + (CORE,)]
        self.start(name)

    def start(self, name):
        if not self.steps[name]:
            return
        kind, step = self.steps[name][0]
        values = self.values[name]
        if kind == "halve":
            values = values[:, values.shape[1] // 2 :]
        self.pending[name] = exchange(values, step)

    def step(self, name, start=True):
        kind, _ = self.steps[name].pop(0)
        got = self.after_last(self.pending.pop(name))
        own = self.values[name]
        if kind == "halve":
            own = own[:, : got.shape[1]]
        if kind == "gather":
            result = jnp.concatenate([own, got], axis=1)
        elif kind == "done":
            result = (own, got)
        else:
            result = add(own, got)
        if kind == "double" or (kind == "sum" and not self.steps[name]):
            result = over_rest(result)
        self.put(name, result)
        if start:
            self.start(name)


def write_pieces(own_ref, product, send_ref, keep_ref, group):
    rows = keep_ref.shape[-2]
    core = own_ref[0]

    def one(piece, carry):
        kept = pl.multiple_of((2 * (piece ^ own_ref[1]) + core) * rows, rows)
        sent = pl.multiple_of((2 * (piece ^ own_ref[2]) + 1 - core) * rows, rows)
        keep_ref[group, piece] = product[pl.ds(kept, rows), :].astype(BF16)
        send_ref[group, piece] = product[pl.ds(sent, rows), :].astype(BF16)
        return carry

    lax.fori_loop(0, keep_ref.shape[1], one, 0)


def teacher_kernel(member_ref, logits_ref, give_ref, keep_ref, *, own_count):
    step = pl.program_id(0)
    total = None
    for teacher in range(logits_ref.shape[0]):
        logits = logits_ref[teacher, 0].astype(F32)
        shifted = logits - jnp.max(logits, axis=-1, keepdims=True)
        logp = shifted - jnp.log(jnp.sum(jnp.exp(shifted), axis=-1, keepdims=True))
        total = logp if total is None else total + logp

    @pl.when(step < own_count)
    def _():
        give_ref[0] = total

    @pl.when(step >= own_count)
    def _():
        keep_ref[0] = total


def teacher_sums(member, logits, own_count):
    teachers, utterances, frames, symbols = logits.shape
    shape = jax.ShapeDtypeStruct((own_count, frames, symbols), F32)

    def source(i, member_ref):
        mine = member_ref[0] * own_count
        theirs = (1 - member_ref[0]) * own_count
        return (0, jnp.where(i < own_count, theirs + i, mine + i - own_count), 0, 0)

    return pl.pallas_call(
        functools.partial(teacher_kernel, own_count=own_count),
        out_shape=(shape, shape),
        grid_spec=pltpu.PrefetchScalarGridSpec(
            num_scalar_prefetch=1,
            grid=(2 * own_count,),
            in_specs=[pl.BlockSpec((teachers, 1, frames, symbols), source)],
            out_specs=(
                pl.BlockSpec(
                    (1, frames, symbols), lambda i, _: (jnp.minimum(i, own_count - 1), 0, 0)
                ),
                pl.BlockSpec(
                    (1, frames, symbols), lambda i, _: (jnp.maximum(i - own_count, 0), 0, 0)
                ),
            ),
        ),
        compiler_params=params(16),
        cost_estimate=cost(4),
        name="teachers",
    )(member, logits)


def live_column(lengths_ref, utterance, frames):
    position = lax.broadcasted_iota(jnp.int32, (frames, 1), 0)
    return (position < lengths_ref[utterance]).astype(F32)


def clear_margins(pad_ref):
    frames = pad_ref.shape[2] - 2 * MARGIN
    zeros = jnp.zeros(pad_ref.shape[:2] + (MARGIN, LANES), F32)
    pad_ref[:, :, :MARGIN, :] = zeros
    pad_ref[:, :, MARGIN + frames :, :] = zeros


def shifted_views(pad_ref, lane, utterance, start, taps):
    first = MARGIN - taps // 2
    for phase in range(8):
        offsets = [offset for offset in range(first, first + taps) if offset % 8 == phase]
        if not offsets:
            continue
        low = offsets[0]
        span = offsets[-1] - low + TILE
        view = pad_ref[lane, utterance, start + low : start + low + span, :]
        for offset in offsets:
            yield offset - first, view[offset - low : offset - low + TILE]


def convolve(pad_ref, lane, utterance, start, depth_ref, flipped):
    taps = depth_ref.shape[0]
    columns = slice(lane * LANES, (lane + 1) * LANES)
    total = jnp.zeros((TILE, LANES), F32)
    for tap, view in shifted_views(pad_ref, lane, utterance, start, taps):
        row = taps - 1 - tap if flipped else tap
        total = total + view * depth_ref[row : row + 1, columns]
    return total


def forward_kernel(
    lengths_ref,
    features_ref,
    gain_ref,
    value_weight_ref,
    gate_weight_ref,
    depth_ref,
    out_weight_ref,
    turned_ref,
    gated_ref,
    gate_ref,
    slope_ref,
    active_ref,
    residual_ref,
    normed_ref,
    pad_ref,
):
    utterances = pad_ref.shape[1]
    frames = pad_ref.shape[2] - 2 * MARGIN

    @pl.when(pl.program_id(0) == 0)
    def _():
        values = features_ref[...].astype(F32)
        centred = values - jnp.mean(values, axis=-1, keepdims=True)
        spread = jnp.mean(centred * centred, axis=-1, keepdims=True)
        normed = centred * lax.rsqrt(spread + 1e-05) * gain_ref[...]
        normed_ref[...] = normed.astype(BF16)
        turned_ref[...] = normed.T.astype(BF16)
        residual_ref[...] = values
        clear_margins(pad_ref)

    for utterance in range(utterances):
        rows = slice(utterance * frames, (utterance + 1) * frames)
        normed = normed_ref[rows, :]
        gate = jax.nn.sigmoid(dot(normed, gate_weight_ref[...]))
        gated = dot(normed, value_weight_ref[...]) * gate
        gated = gated * live_column(lengths_ref, utterance, frames)
        gate_ref[rows, :] = gate
        gated_ref[rows, :] = gated
        for lane in range(WIDE // LANES):
            pad_ref[lane, utterance, MARGIN : MARGIN + frames, :] = gated[
                :, lane * LANES : (lane + 1) * LANES
            ]

    for lane in range(WIDE // LANES):
        columns = slice(lane * LANES, (lane + 1) * LANES)

        def one(utterance, carry, lane=lane, columns=columns):
            for start in range(0, frames, TILE):
                rows = pl.ds(pl.multiple_of(utterance * frames + start, TILE), TILE)
                convolved = convolve(pad_ref, lane, utterance, start, depth_ref, False)
                squash = jax.nn.sigmoid(convolved)
                active_ref[rows, columns] = (convolved * squash).astype(BF16)
                slope_ref[rows, columns] = squash * (1.0 + convolved * (1.0 - squash))
            return carry

        lax.fori_loop(0, utterances, one, 0)

    residual_ref[...] += dot(active_ref[...], out_weight_ref[...])


def forward(lengths, features, gain, weight_in, depth, weight_out, utterances):
    rows, model = features.shape
    frames = rows // utterances
    steps = model // WIDE
    column = pl.BlockSpec((rows, WIDE), lambda i: (0, i))
    wide = jax.ShapeDtypeStruct((rows, model), F32)
    narrow = jax.ShapeDtypeStruct((rows, model), BF16)
    return pl.pallas_call(
        forward_kernel,
        grid=(steps,),
        out_shape=(jax.ShapeDtypeStruct((model, rows), BF16), wide, wide, wide, narrow, wide),
        in_specs=[
            SMEM_SPEC,
            fixed(rows, model),
            fixed(1, model),
            pl.BlockSpec((model, WIDE), lambda i: (0, i)),
            pl.BlockSpec((model, WIDE), lambda i: (0, steps + i)),
            pl.BlockSpec((depth.shape[0], WIDE), lambda i: (0, i)),
            pl.BlockSpec((WIDE, model), lambda i: (i, 0)),
        ],
        out_specs=(fixed(model, rows), column, column, column, column, fixed(rows, model)),
        scratch_shapes=[
            pltpu.VMEM((rows, model), BF16),
            pltpu.VMEM((WIDE // LANES, utterances, frames + 2 * MARGIN, LANES), F32),
        ],
        compiler_params=params(28),
        cost_estimate=cost(15),
        name="forward",
    )(lengths, features, gain, weight_in, weight_in, depth, weight_out)


def top_kernel(
    lengths_ref,
    residual_ref,
    gain_ref,
    head_ref,
    kept_ref,
    got_ref,
    loss_ref,
    final_ref,
    dlogits_ref,
    dresidual_ref,
):
    frames = residual_ref.shape[0]
    live = live_column(lengths_ref, pl.program_id(0), frames)
    values = residual_ref[...]
    centred = values - jnp.mean(values, axis=-1, keepdims=True)
    spread = jnp.mean(centred * centred, axis=-1, keepdims=True)
    inverse = lax.rsqrt(spread + 1e-05)
    unit = centred * inverse
    final = (unit * gain_ref[...]).astype(BF16)
    final_ref[...] = final

    def log_softmax(logits):
        shifted = logits - jnp.max(logits, axis=-1, keepdims=True)
        return shifted - jnp.log(jnp.sum(jnp.exp(shifted), axis=-1, keepdims=True))

    target = jnp.exp(log_softmax((kept_ref[0] + got_ref[0]) * (1.0 / TEACHERS)))
    logp = log_softmax(dot(final, head_ref[...]))
    cross = -jnp.sum(target * logp, axis=-1, keepdims=True)
    loss_ref[...] = jnp.broadcast_to(jnp.sum(cross * live, axis=0, keepdims=True), (1, 1, LANES))
    weight = jnp.sum(target, axis=-1, keepdims=True)
    dlogits = ((jnp.exp(logp) * weight - target) * live).astype(BF16)
    dlogits_ref[...] = dlogits
    dunit = dot(dlogits, head_ref[...], 1, 1) * gain_ref[...]
    average = jnp.mean(dunit, axis=-1, keepdims=True)
    along = jnp.mean(dunit * unit, axis=-1, keepdims=True)
    dresidual_ref[...] = (inverse * (dunit - average - unit * along)).astype(BF16)


def top(lengths, residual, gain, head, kept, got):
    rows, model = residual.shape
    utterances, frames, symbols = kept.shape
    per_row = pl.BlockSpec((frames, model), lambda i: (i, 0))
    sums = pl.BlockSpec((1, frames, symbols), lambda i: (i, 0, 0))
    return pl.pallas_call(
        top_kernel,
        grid=(utterances,),
        out_shape=(
            jax.ShapeDtypeStruct((utterances, 1, LANES), F32),
            jax.ShapeDtypeStruct((rows, model), BF16),
            jax.ShapeDtypeStruct((rows, symbols), BF16),
            jax.ShapeDtypeStruct((rows, model), BF16),
        ),
        in_specs=[SMEM_SPEC, per_row, fixed(1, model), fixed(model, symbols), sums, sums],
        out_specs=(
            pl.BlockSpec((1, 1, LANES), lambda i: (i, 0, 0)),
            per_row,
            pl.BlockSpec((frames, symbols), lambda i: (i, 0)),
            per_row,
        ),
        compiler_params=params(20),
        cost_estimate=cost(5),
        name="top",
    )(lengths, residual, gain, head, kept, got)


def outer_kernel(
    own_ref, active_ref, dresidual_ref, final_ref, dlogits_ref, send_ref, keep_ref, product_ref
):
    width = dresidual_ref.shape[1]
    product_ref[:, :width] = dot(active_ref[...], dresidual_ref[...], 0, 0)
    product_ref[:, width:] = dot(final_ref[...], dlogits_ref[...], 0, 0)
    write_pieces(own_ref, product_ref, send_ref, keep_ref, 0)


def outer(own, active, dresidual, final, dlogits):
    rows, model = active.shape
    half_out = dresidual.shape[1] // 2
    half_head = dlogits.shape[1] // 2
    width = half_out + half_head
    piece = (PLACES, model // (2 * PLACES), width)
    shape = jax.ShapeDtypeStruct((2,) + piece, BF16)
    out = pl.BlockSpec((1,) + piece, lambda i: (i, 0, 0, 0))
    return pl.pallas_call(
        outer_kernel,
        grid=(2,),
        out_shape=(shape, shape),
        in_specs=[
            SMEM_SPEC,
            fixed(rows, model),
            pl.BlockSpec((rows, half_out), lambda i: (0, i)),
            fixed(rows, model),
            pl.BlockSpec((rows, half_head), lambda i: (0, i)),
        ],
        out_specs=(out, out),
        scratch_shapes=[pltpu.VMEM((model, width), F32)],
        compiler_params=params(20),
        cost_estimate=cost(5),
        name="outer",
    )(own, active, dresidual, final, dlogits)


def inner_kernel(
    own_ref,
    lengths_ref,
    dresidual_ref,
    out_weight_ref,
    slope_ref,
    gated_ref,
    gate_ref,
    turned_ref,
    depth_ref,
    *refs,
):
    send_ref, keep_ref, dconv_ref, pad_ref, dvalue_ref, dgate_ref, product_ref = refs[-7:]
    utterances = pad_ref.shape[1]
    frames = pad_ref.shape[2] - 2 * MARGIN

    @pl.when(pl.program_id(0) == 0)
    def _():
        clear_margins(pad_ref)

    for utterance in range(utterances):
        rows = slice(utterance * frames, (utterance + 1) * frames)
        dconv = dot(dresidual_ref[rows, :], out_weight_ref[...], 1, 1) * slope_ref[rows, :]
        dconv_ref[rows, :] = dconv
        for lane in range(WIDE // LANES):
            pad_ref[lane, utterance, MARGIN : MARGIN + frames, :] = dconv[
                :, lane * LANES : (lane + 1) * LANES
            ]

    for lane in range(WIDE // LANES):
        columns = slice(lane * LANES, (lane + 1) * LANES)

        def one(utterance, carry, lane=lane, columns=columns):
            for start in range(0, frames, TILE):
                rows = pl.ds(pl.multiple_of(utterance * frames + start, TILE), TILE)
                position = lax.broadcasted_iota(jnp.int32, (TILE, 1), 0) + start
                live = (position < lengths_ref[utterance]).astype(F32)
                dgated = convolve(pad_ref, lane, utterance, start, depth_ref, True) * live
                gate = gate_ref[rows, columns]
                dvalue_ref[rows, columns] = (dgated * gate).astype(BF16)
                dgate_ref[rows, columns] = (dgated * gated_ref[rows, columns] * (1.0 - gate)).astype(
                    BF16
                )
            return carry

        lax.fori_loop(0, utterances, one, 0)

    for group, source in ((0, dvalue_ref), (1, dgate_ref)):
        product_ref[...] = dot(turned_ref[...], source[...])
        write_pieces(own_ref, product_ref, send_ref, keep_ref, group)


def inner(own, lengths, dresidual, weight_out, slope, gated, gate, turned, depth, chunk, utterances, before):
    model, rows = turned.shape
    frames = rows // utterances
    steps = model // WIDE // CHUNKS
    first = chunk * steps
    column = pl.BlockSpec((rows, WIDE), lambda i: (0, first + i))
    piece = (2, PLACES, model // (2 * PLACES))
    shape = jax.ShapeDtypeStruct(piece + (model,), BF16)
    out = pl.BlockSpec(piece + (WIDE,), lambda i: (0, 0, 0, first + i))
    return pl.pallas_call(
        inner_kernel,
        grid=(steps,),
        out_shape=(shape, shape, jax.ShapeDtypeStruct((rows, steps * WIDE), F32)),
        in_specs=[
            SMEM_SPEC,
            SMEM_SPEC,
            fixed(rows, model),
            pl.BlockSpec((WIDE, model), lambda i: (first + i, 0)),
            column,
            column,
            column,
            fixed(model, rows),
            pl.BlockSpec((depth.shape[0], WIDE), lambda i: (0, first + i)),
        ]
        + [pl.BlockSpec(memory_space=pl.ANY)] * len(before),
        out_specs=(out, out, pl.BlockSpec((rows, WIDE), lambda i: (0, i))),
        scratch_shapes=[
            pltpu.VMEM((WIDE // LANES, utterances, frames + 2 * MARGIN, LANES), F32),
            pltpu.VMEM((rows, WIDE), BF16),
            pltpu.VMEM((rows, WIDE), BF16),
            pltpu.VMEM((model, WIDE), F32),
        ],
        input_output_aliases={9: 0, 10: 1} if before else {},
        compiler_params=params(24),
        cost_estimate=cost(11),
        name="inner",
    )(own, lengths, dresidual, weight_out, slope, gated, gate, turned, depth, *before)


def taps_kernel(lengths_ref, gated_ref, *refs):
    *dconv_refs, out_ref, pad_ref, sums_ref = refs
    utterances = pad_ref.shape[1]
    frames = pad_ref.shape[2] - 2 * MARGIN
    taps = out_ref.shape[0] - 1
    step = pl.program_id(0)
    per_chunk = pl.num_programs(0) // len(dconv_refs)
    valid = lengths_ref[0]
    for utterance in range(1, utterances):
        valid = valid + lengths_ref[utterance]

    @pl.when(step == 0)
    def _():
        clear_margins(pad_ref)

    for lane in range(WIDE // LANES):
        columns = slice(lane * LANES, (lane + 1) * LANES)
        for utterance in range(utterances):
            rows = slice(utterance * frames, (utterance + 1) * frames)
            pad_ref[lane, utterance, MARGIN : MARGIN + frames, :] = gated_ref[rows, columns]

    for chunk, dconv_ref in enumerate(dconv_refs):

        @pl.when(step // per_chunk == chunk)
        def _(dconv_ref=dconv_ref):
            for lane in range(WIDE // LANES):
                columns = slice(lane * LANES, (lane + 1) * LANES)
                sums_ref[...] = jnp.zeros_like(sums_ref)

                def one(utterance, carry, lane=lane, columns=columns):
                    for start in range(0, frames, TILE):
                        rows = pl.ds(pl.multiple_of(utterance * frames + start, TILE), TILE)
                        dconv = dconv_ref[rows, columns]
                        for tap, view in shifted_views(pad_ref, lane, utterance, start, taps):
                            sums_ref[tap] += jnp.sum(
                                (view * dconv).reshape(TILE // 8, 8, LANES), axis=0
                            )
                    return carry

                lax.fori_loop(0, utterances, one, 0)
                out_ref[:taps, columns] = jnp.sum(sums_ref[...], axis=1)

    out_ref[taps:, :] = jnp.zeros((1, WIDE), F32) + valid.astype(F32)


def tap_sums(lengths, gated, dconvs, taps, utterances):
    rows, model = gated.shape
    steps = model // WIDE
    per_chunk = steps // len(dconvs)

    def part(chunk):
        low = chunk * per_chunk
        return pl.BlockSpec((rows, WIDE), lambda i: (0, jnp.clip(i - low, 0, per_chunk - 1)))

    return pl.pallas_call(
        taps_kernel,
        grid=(steps,),
        out_shape=jax.ShapeDtypeStruct((taps + 1, model), F32),
        in_specs=[SMEM_SPEC, pl.BlockSpec((rows, WIDE), lambda i: (0, i))]
        + [part(chunk) for chunk in range(len(dconvs))],
        out_specs=pl.BlockSpec((taps + 1, WIDE), lambda i: (0, i)),
        scratch_shapes=[
            pltpu.VMEM((WIDE // LANES, utterances, rows // utterances + 2 * MARGIN, LANES), F32),
            pltpu.VMEM((taps, 8, LANES), F32),
        ],
        compiler_params=params(16),
        cost_estimate=cost(9),
        name="taps",
    )(lengths, gated, *dconvs)


def gain_terms(weight, grad):
    terms = weight.astype(F32) * grad
    total = terms[:, :LANES]
    for first in range(LANES, terms.shape[1], LANES):
        total = total + terms[:, first : first + LANES]
    return total


def gain_row(terms):
    high = terms.astype(BF16)
    low = (terms - high.astype(F32)).astype(BF16)
    ones = jnp.ones((8, LANES), BF16)
    return (dot(ones, high, 1, 1) + dot(ones, low, 1, 1))[0:1, :]


def write_rows(own_ref, piece_refs, places, group, scale, targets):
    rows = piece_refs[0].shape[2]
    core = own_ref[0]
    first_place = pl.program_id(0) * places
    for index in range(places):
        for whose, (side, source) in enumerate(zip((core, 1 - core), piece_refs)):
            piece = (first_place + index) ^ own_ref[1 + whose]
            here = pl.ds(pl.multiple_of(index * 2 * rows + side * rows, rows), rows)
            for target, there, first, width in targets:
                target[here, there : there + width] = (
                    source[group, piece, :, first : first + width].astype(F32) * scale
                )


whole = pl.BlockSpec(memory_space=pltpu.VMEM)


def unpack_top_kernel(
    utts,
    own_ref,
    small_ref,
    mine_ref,
    other_ref,
    head_ref,
    gain_ref,
    losses_ref,
    wout_ref,
    dhead_ref,
    dgain_ref,
    depth_ref,
    loss_ref,
):
    taps = depth_ref.shape[0]
    scale = utts / small_ref[taps:, 0:1]
    half_out = wout_ref.shape[1] // 2
    half_head = dhead_ref.shape[1] // 2
    for group in range(2):
        targets = (
            (wout_ref, group * half_out, 0, half_out),
            (dhead_ref, group * half_head, half_out, half_head),
        )
        write_rows(own_ref, (mine_ref, other_ref), PLACES // 4, group, scale, targets)
    dgain_ref[...] = gain_row(gain_terms(head_ref[...], dhead_ref[...])) / gain_ref[...]
    depth_ref[...] = small_ref[:taps, :] * scale
    loss_ref[...] = losses_ref[...] * scale[None]


def unpack_top(utts, own, small, mine, other, head, gain, losses, width_out):
    steps = 4
    model, symbols = head.shape
    rows = model // steps
    taps = small.shape[0] - 1
    row = pl.BlockSpec((1, rows), lambda i, own_ref: (0, i))

    def block(width):
        return pl.BlockSpec((rows, width), lambda i, own_ref: (i, 0))

    return pl.pallas_call(
        functools.partial(unpack_top_kernel, utts),
        out_shape=(
            jax.ShapeDtypeStruct((model, width_out), F32),
            jax.ShapeDtypeStruct((model, symbols), F32),
            jax.ShapeDtypeStruct((1, model), F32),
            jax.ShapeDtypeStruct((taps, model), F32),
            jax.ShapeDtypeStruct(losses.shape, F32),
        ),
        grid_spec=pltpu.PrefetchScalarGridSpec(
            num_scalar_prefetch=1,
            grid=(steps,),
            in_specs=[
                fixed(*small.shape),
                whole,
                whole,
                block(symbols),
                row,
                fixed(*losses.shape),
            ],
            out_specs=(
                block(width_out),
                block(symbols),
                row,
                fixed(taps, model),
                fixed(*losses.shape),
            ),
        ),
        compiler_params=params(20),
        cost_estimate=cost(5),
        name="unpack_top",
    )(own, small, mine, other, head, gain, losses)


def unpack_inner_kernel(
    utts, own_ref, small_ref, weight_ref, gain_ref, mine_ref, other_ref, win_ref, dgain_ref
):
    scale = utts / small_ref[small_ref.shape[0] - 1 :, 0:1]
    half = win_ref.shape[1] // 2
    for group in range(2):
        targets = ((win_ref, group * half, 0, half),)
        write_rows(own_ref, (mine_ref, other_ref), PLACES // 4, group, scale, targets)
    dgain_ref[...] = gain_row(gain_terms(weight_ref[...], win_ref[...])) / gain_ref[...]


def unpack_inner(utts, own, small, mine, other, weight, gain):
    steps = 4
    model, width = weight.shape
    rows = model // steps
    row = pl.BlockSpec((1, rows), lambda i, own_ref: (0, i))
    block = pl.BlockSpec((rows, width), lambda i, own_ref: (i, 0))
    return pl.pallas_call(
        functools.partial(unpack_inner_kernel, utts),
        out_shape=(
            jax.ShapeDtypeStruct((model, width), F32),
            jax.ShapeDtypeStruct((1, model), F32),
        ),
        grid_spec=pltpu.PrefetchScalarGridSpec(
            num_scalar_prefetch=1,
            grid=(steps,),
            in_specs=[fixed(*small.shape), block, row, whole, whole],
            out_specs=(block, row),
        ),
        compiler_params=params(24),
        cost_estimate=cost(8),
        name="unpack_inner",
    )(own, small, weight, gain, mine, other)


def on_device(
    features,
    teacher_logits,
    lengths,
    gain_conv,
    weight_in,
    weight_depth,
    weight_out,
    gain_out,
    head_weight,
):
    count = 1
    for axis in ("member", "near", FAR, REST, CORE):
        count *= lax.axis_size(axis)
    member = lax.axis_index("member").astype(jnp.int32)[None]
    own = own_places()
    taps, model = weight_depth.shape
    utterances, frames, _ = features.shape
    utts = float(utterances * count)
    tie = lax.optimization_barrier

    own, member, teacher_logits = tie((own, member, teacher_logits))
    give, kept = teacher_sums(member, teacher_logits, utterances)
    got = exchange(give, "member")
    flat = features.reshape(utterances * frames, model)
    turned, gated, gate, slope, active, residual = forward(
        lengths, flat, gain_conv[None], weight_in, weight_depth, weight_out, utterances
    )
    losses, final, dlogits, dresidual = top(
        lengths, residual, gain_out[None], head_weight, kept, got
    )

    line = Line()

    def products(chunk, before):
        nonlocal dresidual
        dresidual = line.before_kernel(dresidual)
        send, keep, line.values["conv", chunk] = inner(
            own,
            lengths,
            dresidual,
            weight_out,
            slope,
            gated,
            gate,
            turned,
            weight_depth,
            chunk,
            utterances,
            before,
        )
        line.last = "conv", chunk
        return send, keep

    send, keep = outer(own, active, dresidual, final, dlogits)
    send, keep, dresidual = tie((send, keep, dresidual))
    line.begin("top", send, keep)
    pieces = products(0, ())
    line.step("top", start=False)
    line.begin("in", *products(1, pieces))
    written = {}

    def write_top():
        mine, other = line.values["top"]
        *rest, written["losses"] = unpack_top(
            utts,
            own,
            line.values["small"],
            line.after_last(mine),
            other,
            head_weight,
            gain_out[None],
            losses,
            weight_out.shape[1],
        )
        written["out"], written["head"], by_head, written["depth"] = rest
        line.put("by_head", by_head)

    def write_in():
        mine, other = line.values["in"]
        written["in"], by_in = unpack_inner(
            utts, own, line.values["small"], mine, other, weight_in, gain_conv[None]
        )
        line.put("by_in", by_in)

    def sum_taps():
        dconvs = line.after_last(tuple(line.values["conv", chunk] for chunk in range(CHUNKS)))
        line.put("taps", tap_sums(lengths, gated, dconvs, taps, utterances))
        line.begin_small("small", line.values["taps"])

    kernels = {
        "taps": sum_taps,
        "write_top": write_top,
        "write_in": write_in,
    }
    for name in ORDER:
        if name in kernels:
            kernels[name]()
        else:
            line.step(name)
    return (
        line.values["by_in"].reshape(model),
        written["in"],
        written["depth"],
        written["out"],
        line.values["by_head"].reshape(model),
        written["head"],
        written["losses"][:, 0, 0],
    )


def solution(mesh):
    members, others = mesh.devices.shape
    near, cores = 2, 2
    far = 2 * PLACES // (members * near)
    rest = others // (far * near * cores)
    split = jax.sharding.Mesh(
        mesh.devices.reshape(members, rest, far, near, cores),
        ("member", REST, FAR, "near", CORE),
    )
    dp = (REST, FAR, "near", CORE)
    in_specs = (
        P(dp + ("member",), None, None),
        P("member", dp, None, None),
        P(dp + ("member",)),
        P(),
        P(),
        P(),
        P(),
        P(),
        P(),
    )
    out_specs = (P(), P(), P(), P(), P(), P(), P(dp + ("member",)))
    return jax.shard_map(
        on_device, mesh=split, in_specs=in_specs, out_specs=out_specs, check_vma=False
    )
```

```python
import functools

import jax
import jax.numpy as jnp
from jax import lax
from jax.experimental import pallas as pl
from jax.experimental.pallas import tpu as pltpu
from jax.sharding import PartitionSpec as P

TEACHERS = 4
PLACES = 8
WIDE = 256
LANES = 128
TILE = 128
MARGIN = 16
CHUNKS = 2
FIRST_DIGIT = 32
DIGITS = 12
ORDER = (
    "top", "in0", "in1", "top", "in0", "in1", "top", "in0", "in1", "top", "in0", "in1", "top",
    "in0", "in1", "top", "in0", "in1", "top", "in0", "in1", "top", "write_top", "in0", "in1",
    "in0", "in1", "write_in",
)
SMEM_SPEC = pl.BlockSpec(memory_space=pltpu.SMEM)
F32 = jnp.float32
BF16 = jnp.bfloat16


def params(mebibytes):
    return pltpu.CompilerParams(vmem_limit_bytes=mebibytes << 20)


def cost(microseconds):
    return pl.CostEstimate(flops=int(microseconds * 1.15e9), bytes_accessed=1 << 20, transcendentals=0)


def dot(left, right, left_axis=1, right_axis=0):
    return lax.dot_general(
        left, right, (((left_axis,), (right_axis,)), ((), ())), preferred_element_type=F32
    )


def fixed(*shape):
    return pl.BlockSpec(shape, lambda i, *_: (0,) * len(shape))


FAR = "far"
REST = "rest"
CORE = "core"
ALL = ("member", REST, FAR, "near", CORE)
STEPS = ("first", "second", "third", "fourth")


def exchange(values, step):
    if step in (CORE, "member"):
        return lax.ppermute(values, step, [(0, 1), (1, 0)])
    count = 1
    for name in ALL:
        count *= lax.axis_size(name)
    bits = (count // 2, 2, 4, 8)
    place = STEPS.index(step)
    return lax.ppermute(values, ALL, [(i, i ^ bits[place ^ (i % 2)]) for i in range(count)])


def add(own, other):
    return (own.astype(F32) + other.astype(F32)).astype(own.dtype)


def own_places():
    core, member, near = lax.axis_index(CORE), lax.axis_index("member"), lax.axis_index("near")
    far = lax.axis_index(FAR)
    places = (member * 4 + near * 2 + (far & 1), near * 4 + member * 2 + (far >> 1))
    own = jnp.where(core == 0, places[0], places[1])
    other = jnp.where(core == 0, places[1], places[0])
    return jnp.stack([core, own, other]).astype(jnp.int32)


def over_rest(values):
    return lax.psum(values, REST) if lax.axis_size(REST) > 1 else values


class Line:
    def __init__(self):
        self.values = {}
        self.pending = {}
        self.steps = {}
        self.last = None

    def after_last(self, value):
        if self.last is not None:
            value, self.values[self.last] = lax.optimization_barrier(
                (value, self.values[self.last])
            )
        return value

    def before_kernel(self, value):
        value = self.after_last(value)
        if self.last in self.steps and self.last not in self.pending:
            self.start(self.last)
        return value

    def put(self, name, value):
        self.values[name] = value
        self.last = name

    def begin(self, name, send, keep):
        self.values[name] = keep
        self.pending[name] = exchange(send, CORE)
        self.steps[name] = [
            ("add", CORE),
            ("halve", "first"),
            ("halve", "second"),
            ("halve", "third"),
            ("double", "fourth"),
            ("gather", "third"),
            ("gather", "second"),
            ("gather", "first"),
            ("done", CORE),
        ]

    def start(self, name):
        if not self.steps[name]:
            return
        kind, step = self.steps[name][0]
        values = self.values[name]
        if kind == "halve":
            values = values[:, values.shape[1] // 2 :]
        self.pending[name] = exchange(values, step)

    def step(self, name, start=True):
        kind, _ = self.steps[name].pop(0)
        got = self.after_last(self.pending.pop(name))
        own = self.values[name]
        if kind == "halve":
            own = own[:, : got.shape[1]]
        if kind == "gather":
            result = jnp.concatenate([own, got], axis=1)
        elif kind == "done":
            result = (own, got)
        else:
            result = add(own, got)
        if kind == "double":
            result = over_rest(result)
        self.put(name, result)
        if start:
            self.start(name)


def write_pieces(own_ref, product, send_ref, keep_ref, group):
    rows = keep_ref.shape[-2]
    core = own_ref[0]

    def one(piece, carry):
        kept = pl.multiple_of((2 * (piece ^ own_ref[1]) + core) * rows, rows)
        sent = pl.multiple_of((2 * (piece ^ own_ref[2]) + 1 - core) * rows, rows)
        keep_ref[group, piece] = product[pl.ds(kept, rows), :].astype(BF16)
        send_ref[group, piece] = product[pl.ds(sent, rows), :].astype(BF16)
        return carry

    lax.fori_loop(0, keep_ref.shape[1], one, 0)


def teacher_kernel(member_ref, logits_ref, give_ref, keep_ref, *, own_count):
    step = pl.program_id(0)
    total = None
    for teacher in range(logits_ref.shape[0]):
        logits = logits_ref[teacher, 0].astype(F32)
        shifted = logits - jnp.max(logits, axis=-1, keepdims=True)
        logp = shifted - jnp.log(jnp.sum(jnp.exp(shifted), axis=-1, keepdims=True))
        total = logp if total is None else total + logp

    @pl.when(step < own_count)
    def _():
        give_ref[0] = total

    @pl.when(step >= own_count)
    def _():
        keep_ref[0] = total


def teacher_sums(member, logits, own_count):
    teachers, utterances, frames, symbols = logits.shape
    shape = jax.ShapeDtypeStruct((own_count, frames, symbols), F32)

    def source(i, member_ref):
        mine = member_ref[0] * own_count
        theirs = (1 - member_ref[0]) * own_count
        return (0, jnp.where(i < own_count, theirs + i, mine + i - own_count), 0, 0)

    return pl.pallas_call(
        functools.partial(teacher_kernel, own_count=own_count),
        out_shape=(shape, shape),
        grid_spec=pltpu.PrefetchScalarGridSpec(
            num_scalar_prefetch=1,
            grid=(2 * own_count,),
            in_specs=[pl.BlockSpec((teachers, 1, frames, symbols), source)],
            out_specs=(
                pl.BlockSpec(
                    (1, frames, symbols), lambda i, _: (jnp.minimum(i, own_count - 1), 0, 0)
                ),
                pl.BlockSpec(
                    (1, frames, symbols), lambda i, _: (jnp.maximum(i - own_count, 0), 0, 0)
                ),
            ),
        ),
        compiler_params=params(16),
        cost_estimate=cost(4),
        name="teachers",
    )(member, logits)


def live_column(lengths_ref, utterance, frames):
    position = lax.broadcasted_iota(jnp.int32, (frames, 1), 0)
    return (position < lengths_ref[utterance]).astype(F32)


def clear_margins(pad_ref):
    frames = pad_ref.shape[2] - 2 * MARGIN
    zeros = jnp.zeros(pad_ref.shape[:2] + (MARGIN, LANES), F32)
    pad_ref[:, :, :MARGIN, :] = zeros
    pad_ref[:, :, MARGIN + frames :, :] = zeros


def shifted_views(pad_ref, lane, utterance, start, taps):
    first = MARGIN - taps // 2
    for phase in range(8):
        offsets = [offset for offset in range(first, first + taps) if offset % 8 == phase]
        if not offsets:
            continue
        low = offsets[0]
        span = offsets[-1] - low + TILE
        view = pad_ref[lane, utterance, start + low : start + low + span, :]
        for offset in offsets:
            yield offset - first, view[offset - low : offset - low + TILE]


def convolve(pad_ref, lane, utterance, start, depth_ref, flipped):
    taps = depth_ref.shape[0]
    columns = slice(lane * LANES, (lane + 1) * LANES)
    total = jnp.zeros((TILE, LANES), F32)
    for tap, view in shifted_views(pad_ref, lane, utterance, start, taps):
        row = taps - 1 - tap if flipped else tap
        total = total + view * depth_ref[row : row + 1, columns]
    return total


def forward_kernel(
    lengths_ref,
    features_ref,
    gain_ref,
    value_weight_ref,
    gate_weight_ref,
    depth_ref,
    out_weight_ref,
    turned_ref,
    gated_ref,
    gate_ref,
    slope_ref,
    active_ref,
    residual_ref,
    normed_ref,
    pad_ref,
):
    utterances = pad_ref.shape[1]
    frames = pad_ref.shape[2] - 2 * MARGIN

    @pl.when(pl.program_id(0) == 0)
    def _():
        values = features_ref[...].astype(F32)
        centred = values - jnp.mean(values, axis=-1, keepdims=True)
        spread = jnp.mean(centred * centred, axis=-1, keepdims=True)
        normed = centred * lax.rsqrt(spread + 1e-05) * gain_ref[...]
        normed_ref[...] = normed.astype(BF16)
        turned_ref[...] = normed.T.astype(BF16)
        residual_ref[...] = values
        clear_margins(pad_ref)

    for utterance in range(utterances):
        rows = slice(utterance * frames, (utterance + 1) * frames)
        normed = normed_ref[rows, :]
        gate = jax.nn.sigmoid(dot(normed, gate_weight_ref[...]))
        gated = dot(normed, value_weight_ref[...]) * gate
        gated = gated * live_column(lengths_ref, utterance, frames)
        gate_ref[rows, :] = gate
        gated_ref[rows, :] = gated
        for lane in range(WIDE // LANES):
            pad_ref[lane, utterance, MARGIN : MARGIN + frames, :] = gated[
                :, lane * LANES : (lane + 1) * LANES
            ]

    for lane in range(WIDE // LANES):
        columns = slice(lane * LANES, (lane + 1) * LANES)

        def one(utterance, carry, lane=lane, columns=columns):
            for start in range(0, frames, TILE):
                rows = pl.ds(pl.multiple_of(utterance * frames + start, TILE), TILE)
                convolved = convolve(pad_ref, lane, utterance, start, depth_ref, False)
                squash = jax.nn.sigmoid(convolved)
                active_ref[rows, columns] = (convolved * squash).astype(BF16)
                slope_ref[rows, columns] = squash * (1.0 + convolved * (1.0 - squash))
            return carry

        lax.fori_loop(0, utterances, one, 0)

    residual_ref[...] += dot(active_ref[...], out_weight_ref[...])


def forward(lengths, features, gain, weight_in, depth, weight_out, utterances):
    rows, model = features.shape
    frames = rows // utterances
    steps = model // WIDE
    column = pl.BlockSpec((rows, WIDE), lambda i: (0, i))
    wide = jax.ShapeDtypeStruct((rows, model), F32)
    narrow = jax.ShapeDtypeStruct((rows, model), BF16)
    return pl.pallas_call(
        forward_kernel,
        grid=(steps,),
        out_shape=(jax.ShapeDtypeStruct((model, rows), BF16), wide, wide, wide, narrow, wide),
        in_specs=[
            SMEM_SPEC,
            fixed(rows, model),
            fixed(1, model),
            pl.BlockSpec((model, WIDE), lambda i: (0, i)),
            pl.BlockSpec((model, WIDE), lambda i: (0, steps + i)),
            pl.BlockSpec((depth.shape[0], WIDE), lambda i: (0, i)),
            pl.BlockSpec((WIDE, model), lambda i: (i, 0)),
        ],
        out_specs=(fixed(model, rows), column, column, column, column, fixed(rows, model)),
        scratch_shapes=[
            pltpu.VMEM((rows, model), BF16),
            pltpu.VMEM((WIDE // LANES, utterances, frames + 2 * MARGIN, LANES), F32),
        ],
        compiler_params=params(28),
        cost_estimate=cost(15),
        name="forward",
    )(lengths, features, gain, weight_in, weight_in, depth, weight_out)


def top_kernel(
    lengths_ref,
    residual_ref,
    gain_ref,
    head_ref,
    kept_ref,
    got_ref,
    loss_ref,
    final_ref,
    dlogits_ref,
    dresidual_ref,
):
    frames = residual_ref.shape[0]
    live = live_column(lengths_ref, pl.program_id(0), frames)
    values = residual_ref[...]
    centred = values - jnp.mean(values, axis=-1, keepdims=True)
    spread = jnp.mean(centred * centred, axis=-1, keepdims=True)
    inverse = lax.rsqrt(spread + 1e-05)
    unit = centred * inverse
    final = (unit * gain_ref[...]).astype(BF16)
    final_ref[...] = final

    def log_softmax(logits):
        shifted = logits - jnp.max(logits, axis=-1, keepdims=True)
        return shifted - jnp.log(jnp.sum(jnp.exp(shifted), axis=-1, keepdims=True))

    target = jnp.exp(log_softmax((kept_ref[0] + got_ref[0]) * (1.0 / TEACHERS)))
    logp = log_softmax(dot(final, head_ref[...]))
    cross = -jnp.sum(target * logp, axis=-1, keepdims=True)
    loss_ref[...] = jnp.broadcast_to(jnp.sum(cross * live, axis=0, keepdims=True), (1, 1, LANES))
    weight = jnp.sum(target, axis=-1, keepdims=True)
    dlogits = ((jnp.exp(logp) * weight - target) * live).astype(BF16)
    dlogits_ref[...] = dlogits
    dunit = dot(dlogits, head_ref[...], 1, 1) * gain_ref[...]
    average = jnp.mean(dunit, axis=-1, keepdims=True)
    along = jnp.mean(dunit * unit, axis=-1, keepdims=True)
    dresidual_ref[...] = (inverse * (dunit - average - unit * along)).astype(BF16)


def top(lengths, residual, gain, head, kept, got):
    rows, model = residual.shape
    utterances, frames, symbols = kept.shape
    per_row = pl.BlockSpec((frames, model), lambda i: (i, 0))
    sums = pl.BlockSpec((1, frames, symbols), lambda i: (i, 0, 0))
    return pl.pallas_call(
        top_kernel,
        grid=(utterances,),
        out_shape=(
            jax.ShapeDtypeStruct((utterances, 1, LANES), F32),
            jax.ShapeDtypeStruct((rows, model), BF16),
            jax.ShapeDtypeStruct((rows, symbols), BF16),
            jax.ShapeDtypeStruct((rows, model), BF16),
        ),
        in_specs=[SMEM_SPEC, per_row, fixed(1, model), fixed(model, symbols), sums, sums],
        out_specs=(
            pl.BlockSpec((1, 1, LANES), lambda i: (i, 0, 0)),
            per_row,
            pl.BlockSpec((frames, symbols), lambda i: (i, 0)),
            per_row,
        ),
        compiler_params=params(20),
        cost_estimate=cost(5),
        name="top",
    )(lengths, residual, gain, head, kept, got)


def outer_kernel(
    own_ref, active_ref, dresidual_ref, final_ref, dlogits_ref, taps_ref, send_ref, keep_ref, product_ref
):
    width = dresidual_ref.shape[1]
    product_ref[:, :width] = dot(active_ref[...], dresidual_ref[...], 0, 0)
    both = width + dlogits_ref.shape[1]
    product_ref[:, width:both] = dot(final_ref[...], dlogits_ref[...], 0, 0)
    product_ref[:, both:] = taps_ref[...]
    write_pieces(own_ref, product_ref, send_ref, keep_ref, 0)


def outer(own, active, dresidual, final, dlogits, turned_taps):
    rows, model = active.shape
    half_out = dresidual.shape[1] // 2
    half_head = dlogits.shape[1] // 2
    width = half_out + half_head + LANES
    piece = (PLACES, model // (2 * PLACES), width)
    shape = jax.ShapeDtypeStruct((2,) + piece, BF16)
    out = pl.BlockSpec((1,) + piece, lambda i: (i, 0, 0, 0))
    return pl.pallas_call(
        outer_kernel,
        grid=(2,),
        out_shape=(shape, shape),
        in_specs=[
            SMEM_SPEC,
            fixed(rows, model),
            pl.BlockSpec((rows, half_out), lambda i: (0, i)),
            fixed(rows, model),
            pl.BlockSpec((rows, half_head), lambda i: (0, i)),
            fixed(model, LANES),
        ],
        out_specs=(out, out),
        scratch_shapes=[pltpu.VMEM((model, width), F32)],
        compiler_params=params(20),
        cost_estimate=cost(5),
        name="outer",
    )(own, active, dresidual, final, dlogits, turned_taps)


def inner_kernel(
    own_ref,
    lengths_ref,
    dconv_ref,
    gated_ref,
    gate_ref,
    turned_ref,
    depth_ref,
    send_ref,
    keep_ref,
    pad_ref,
    dvalue_ref,
    dgate_ref,
    product_ref,
):
    utterances = pad_ref.shape[1]
    frames = pad_ref.shape[2] - 2 * MARGIN

    @pl.when(pl.program_id(0) == 0)
    def _():
        clear_margins(pad_ref)

    for utterance in range(utterances):
        rows = slice(utterance * frames, (utterance + 1) * frames)
        for lane in range(WIDE // LANES):
            pad_ref[lane, utterance, MARGIN : MARGIN + frames, :] = dconv_ref[
                rows, lane * LANES : (lane + 1) * LANES
            ]

    for lane in range(WIDE // LANES):
        columns = slice(lane * LANES, (lane + 1) * LANES)

        def one(utterance, carry, lane=lane, columns=columns):
            for start in range(0, frames, TILE):
                rows = pl.ds(pl.multiple_of(utterance * frames + start, TILE), TILE)
                position = lax.broadcasted_iota(jnp.int32, (TILE, 1), 0) + start
                live = (position < lengths_ref[utterance]).astype(F32)
                dgated = convolve(pad_ref, lane, utterance, start, depth_ref, True) * live
                gate = gate_ref[rows, columns]
                dvalue_ref[rows, columns] = (dgated * gate).astype(BF16)
                dgate_ref[rows, columns] = (dgated * gated_ref[rows, columns] * (1.0 - gate)).astype(
                    BF16
                )
            return carry

        lax.fori_loop(0, utterances, one, 0)

    for group, source in ((0, dvalue_ref), (1, dgate_ref)):
        product_ref[...] = dot(turned_ref[...], source[...])
        write_pieces(own_ref, product_ref, send_ref, keep_ref, group)


def inner(own, lengths, dconv, gated, gate, turned, depth, chunk, utterances):
    model, rows = turned.shape
    frames = rows // utterances
    steps = model // WIDE // CHUNKS
    first = chunk * steps
    column = pl.BlockSpec((rows, WIDE), lambda i: (0, first + i))
    piece = (2, PLACES, model // (2 * PLACES))
    shape = jax.ShapeDtypeStruct(piece + (steps * WIDE,), BF16)
    out = pl.BlockSpec(piece + (WIDE,), lambda i: (0, 0, 0, i))
    return pl.pallas_call(
        inner_kernel,
        grid=(steps,),
        out_shape=(shape, shape),
        in_specs=[
            SMEM_SPEC,
            SMEM_SPEC,
            column,
            column,
            column,
            fixed(model, rows),
            pl.BlockSpec((depth.shape[0], WIDE), lambda i: (0, first + i)),
        ],
        out_specs=(out, out),
        scratch_shapes=[
            pltpu.VMEM((WIDE // LANES, utterances, frames + 2 * MARGIN, LANES), F32),
            pltpu.VMEM((rows, WIDE), BF16),
            pltpu.VMEM((rows, WIDE), BF16),
            pltpu.VMEM((model, WIDE), F32),
        ],
        compiler_params=params(24),
        cost_estimate=cost(11),
        name="inner",
    )(own, lengths, dconv, gated, gate, turned, depth)


def taps_kernel(
    lengths_ref,
    dresidual_ref,
    out_weight_ref,
    slope_ref,
    gated_ref,
    dconv_ref,
    turned_ref,
    pad_ref,
    sums_ref,
    wide_ref,
):
    taps = sums_ref.shape[0]
    utterances = pad_ref.shape[1]
    frames = pad_ref.shape[2] - 2 * MARGIN
    valid = lengths_ref[0]
    for utterance in range(1, utterances):
        valid = valid + lengths_ref[utterance]

    @pl.when(pl.program_id(0) == 0)
    def _():
        clear_margins(pad_ref)
        wide_ref[...] = jnp.zeros_like(wide_ref)
        for digit in range(DIGITS):
            row = FIRST_DIGIT + digit
            wide_ref[row : row + 1, :] = jnp.zeros((1, WIDE), F32) + ((valid >> digit) & 1).astype(F32)

    for utterance in range(utterances):
        rows = slice(utterance * frames, (utterance + 1) * frames)
        dconv_ref[rows, :] = dot(dresidual_ref[rows, :], out_weight_ref[...], 1, 1) * slope_ref[rows, :]
        for lane in range(WIDE // LANES):
            pad_ref[lane, utterance, MARGIN : MARGIN + frames, :] = gated_ref[
                rows, lane * LANES : (lane + 1) * LANES
            ]

    for lane in range(WIDE // LANES):
        columns = slice(lane * LANES, (lane + 1) * LANES)
        sums_ref[...] = jnp.zeros_like(sums_ref)

        def one(utterance, carry, lane=lane, columns=columns):
            for start in range(0, frames, TILE):
                rows = pl.ds(pl.multiple_of(utterance * frames + start, TILE), TILE)
                dconv = dconv_ref[rows, columns]
                for tap, view in shifted_views(pad_ref, lane, utterance, start, taps):
                    sums_ref[tap] += jnp.sum((view * dconv).reshape(TILE // 8, 8, LANES), axis=0)
            return carry

        lax.fori_loop(0, utterances, one, 0)
        wide_ref[:taps, columns] = jnp.sum(sums_ref[...], axis=1)
    turned_ref[...] = wide_ref[...].T


def tap_sums(lengths, dresidual, weight_out, slope, gated, taps, utterances):
    rows, model = gated.shape
    column = pl.BlockSpec((rows, WIDE), lambda i: (0, i))
    return pl.pallas_call(
        taps_kernel,
        grid=(model // WIDE,),
        out_shape=(
            jax.ShapeDtypeStruct((rows, model), F32),
            jax.ShapeDtypeStruct((model, LANES), F32),
        ),
        in_specs=[
            SMEM_SPEC,
            fixed(rows, model),
            pl.BlockSpec((WIDE, model), lambda i: (i, 0)),
            column,
            column,
        ],
        out_specs=(column, pl.BlockSpec((WIDE, LANES), lambda i: (i, 0))),
        scratch_shapes=[
            pltpu.VMEM((WIDE // LANES, utterances, rows // utterances + 2 * MARGIN, LANES), F32),
            pltpu.VMEM((taps, 8, LANES), F32),
            pltpu.VMEM((LANES, WIDE), F32),
        ],
        compiler_params=params(20),
        cost_estimate=cost(8),
        name="taps",
    )(lengths, dresidual, weight_out, slope, gated)


def gain_terms(weight, grad):
    terms = weight.astype(F32) * grad
    total = terms[:, :LANES]
    for first in range(LANES, terms.shape[1], LANES):
        total = total + terms[:, first : first + LANES]
    return total


def gain_row(terms):
    high = terms.astype(BF16)
    low = (terms - high.astype(F32)).astype(BF16)
    ones = jnp.ones((8, LANES), BF16)
    return (dot(ones, high, 1, 1) + dot(ones, low, 1, 1))[0:1, :]


def write_rows(own_ref, piece_refs, places, group, scale, targets):
    rows = piece_refs[0].shape[2]
    core = own_ref[0]
    first_place = pl.program_id(0) * places
    for index in range(places):
        for whose, (side, source) in enumerate(zip((core, 1 - core), piece_refs)):
            piece = (first_place + index) ^ own_ref[1 + whose]
            here = pl.ds(pl.multiple_of(index * 2 * rows + side * rows, rows), rows)
            for target, there, first, width in targets:
                target[here, there : there + width] = (
                    source[group, piece, :, first : first + width].astype(F32) * scale
                )


whole = pl.BlockSpec(memory_space=pltpu.VMEM)


def unpack_top_kernel(
    utts,
    own_ref,
    mine_ref,
    other_ref,
    head_ref,
    gain_ref,
    losses_ref,
    wout_ref,
    dhead_ref,
    dgain_ref,
    depth_ref,
    loss_ref,
    scale_ref,
    turned_ref,
):
    half_out = wout_ref.shape[1] // 2
    half_head = dhead_ref.shape[1] // 2
    both = half_out + half_head
    digits = mine_ref[0, 0, 0:16, both:].astype(F32)[0:1, :]
    total = digits[:, FIRST_DIGIT : FIRST_DIGIT + 1]
    for digit in range(1, DIGITS):
        lane = FIRST_DIGIT + digit
        total = total + digits[:, lane : lane + 1] * float(1 << digit)
    scale = utts / total
    for group in range(2):
        targets = [
            (wout_ref, group * half_out, 0, half_out),
            (dhead_ref, group * half_head, half_out, half_head),
        ]
        if group == 0:
            targets.append((turned_ref, 0, both, LANES))
        write_rows(own_ref, (mine_ref, other_ref), PLACES // 4, group, scale, targets)
    dgain_ref[...] = gain_row(gain_terms(head_ref[...], dhead_ref[...])) / gain_ref[...]
    depth_ref[...] = turned_ref[...].T[: depth_ref.shape[0], :]
    loss_ref[...] = losses_ref[...] * scale[None]
    scale_ref[...] = jnp.broadcast_to(scale, scale_ref.shape)


def unpack_top(utts, own, mine, other, head, gain, losses, width_out, taps):
    steps = 4
    model, symbols = head.shape
    rows = model // steps
    row = pl.BlockSpec((1, rows), lambda i, own_ref: (0, i))

    def block(width):
        return pl.BlockSpec((rows, width), lambda i, own_ref: (i, 0))

    return pl.pallas_call(
        functools.partial(unpack_top_kernel, utts),
        out_shape=(
            jax.ShapeDtypeStruct((model, width_out), F32),
            jax.ShapeDtypeStruct((model, symbols), F32),
            jax.ShapeDtypeStruct((1, model), F32),
            jax.ShapeDtypeStruct((taps, model), F32),
            jax.ShapeDtypeStruct(losses.shape, F32),
            jax.ShapeDtypeStruct((8, LANES), F32),
        ),
        grid_spec=pltpu.PrefetchScalarGridSpec(
            num_scalar_prefetch=1,
            grid=(steps,),
            in_specs=[whole, whole, block(symbols), row, fixed(*losses.shape)],
            out_specs=(
                block(width_out),
                block(symbols),
                row,
                pl.BlockSpec((taps, rows), lambda i, own_ref: (0, i)),
                fixed(*losses.shape),
                fixed(8, LANES),
            ),
            scratch_shapes=[pltpu.VMEM((rows, LANES), F32)],
        ),
        compiler_params=params(20),
        cost_estimate=cost(4),
        name="unpack_top",
    )(own, mine, other, head, gain, losses)


def unpack_inner_kernel(own_ref, scale_ref, weight_ref, gain_ref, *refs):
    *piece_refs, win_ref, dgain_ref = refs
    scale = scale_ref[0:1, 0:1]
    half = win_ref.shape[1] // 2
    for chunk in range(CHUNKS):
        pair = piece_refs[2 * chunk : 2 * chunk + 2]
        width = pair[0].shape[3]
        for group in range(2):
            targets = ((win_ref, group * half + chunk * width, 0, width),)
            write_rows(own_ref, pair, PLACES // 4, group, scale, targets)
    dgain_ref[...] = gain_row(gain_terms(weight_ref[...], win_ref[...])) / gain_ref[...]


def unpack_inner(own, scale, pieces, weight, gain):
    steps = 4
    model, width = weight.shape
    rows = model // steps
    row = pl.BlockSpec((1, rows), lambda i, own_ref: (0, i))
    block = pl.BlockSpec((rows, width), lambda i, own_ref: (i, 0))
    return pl.pallas_call(
        unpack_inner_kernel,
        out_shape=(
            jax.ShapeDtypeStruct((model, width), F32),
            jax.ShapeDtypeStruct((1, model), F32),
        ),
        grid_spec=pltpu.PrefetchScalarGridSpec(
            num_scalar_prefetch=1,
            grid=(steps,),
            in_specs=[fixed(*scale.shape), block, row] + [whole] * len(pieces),
            out_specs=(block, row),
        ),
        compiler_params=params(24),
        cost_estimate=cost(8),
        name="unpack_inner",
    )(own, scale, weight, gain, *pieces)


def on_device(
    features,
    teacher_logits,
    lengths,
    gain_conv,
    weight_in,
    weight_depth,
    weight_out,
    gain_out,
    head_weight,
):
    count = 1
    for axis in ("member", "near", FAR, REST, CORE):
        count *= lax.axis_size(axis)
    member = lax.axis_index("member").astype(jnp.int32)[None]
    own = own_places()
    taps, model = weight_depth.shape
    utterances, frames, _ = features.shape
    utts = float(utterances * count)
    tie = lax.optimization_barrier

    own, member, teacher_logits = tie((own, member, teacher_logits))
    give, kept = teacher_sums(member, teacher_logits, utterances)
    got = exchange(give, "member")
    flat = features.reshape(utterances * frames, model)
    turned, gated, gate, slope, active, residual = forward(
        lengths, flat, gain_conv[None], weight_in, weight_depth, weight_out, utterances
    )
    losses, final, dlogits, dresidual = top(
        lengths, residual, gain_out[None], head_weight, kept, got
    )

    line = Line()

    def products(name, chunk):
        nonlocal dconv
        dconv = line.before_kernel(dconv)
        send, keep = inner(
            own, lengths, dconv, gated, gate, turned, weight_depth, chunk, utterances
        )
        line.begin(name, send, keep)
        line.last = name

    dconv, turned_taps = tap_sums(
        lengths, dresidual, weight_out, slope, gated, taps, utterances
    )
    send, keep = outer(own, active, dresidual, final, dlogits, turned_taps)
    send, keep, dconv = tie((send, keep, dconv))
    line.begin("top", send, keep)
    products("in0", 0)
    line.step("top", start=False)
    products("in1", 1)
    written = {}

    def write_top():
        mine, other = line.values["top"]
        written["out"], written["head"], by_head, *rest = unpack_top(
            utts,
            own,
            line.after_last(mine),
            other,
            head_weight,
            gain_out[None],
            losses,
            weight_out.shape[1],
            taps,
        )
        written["depth"], written["losses"], written["scale"] = rest
        line.put("by_head", by_head)

    def write_in():
        pieces = [array for name in ("in0", "in1") for array in line.values[name]]
        written["in"], by_in = unpack_inner(
            own, written["scale"], pieces, weight_in, gain_conv[None]
        )
        line.put("by_in", by_in)

    kernels = {"write_top": write_top, "write_in": write_in}
    for name in ORDER:
        if name in kernels:
            kernels[name]()
        else:
            line.step(name)
    return (
        line.values["by_in"].reshape(model),
        written["in"],
        written["depth"],
        written["out"],
        line.values["by_head"].reshape(model),
        written["head"],
        written["losses"][:, 0, 0],
    )


def solution(mesh):
    members, others = mesh.devices.shape
    near, cores = 2, 2
    far = 2 * PLACES // (members * near)
    rest = others // (far * near * cores)
    split = jax.sharding.Mesh(
        mesh.devices.reshape(members, rest, far, near, cores),
        ("member", REST, FAR, "near", CORE),
    )
    dp = (REST, FAR, "near", CORE)
    in_specs = (
        P(dp + ("member",), None, None),
        P("member", dp, None, None),
        P(dp + ("member",)),
        P(),
        P(),
        P(),
        P(),
        P(),
        P(),
    )
    out_specs = (P(), P(), P(), P(), P(), P(), P(dp + ("member",)))
    return jax.shard_map(
        on_device, mesh=split, in_specs=in_specs, out_specs=out_specs, check_vma=False
    )
```

```python
import functools

import jax
import jax.numpy as jnp
from jax import lax
from jax.experimental import pallas as pl
from jax.experimental.pallas import tpu as pltpu
from jax.sharding import PartitionSpec as P

TEACHERS = 4
PLACES = 8
WIDE = 256
LANES = 128
TILE = 128
MARGIN = 16
CHUNKS = 2
ORDER = (
    "top", "in0", "in1", "taps", "in0", "top", "in1", "small", "in0", "top", "in1", "in0",
    "top", "in1", "in0", "top", "in1", "in0", "top", "in1", "small", "in0", "top", "small",
    "in1", "in0", "top", "small", "in0", "in1", "small", "write_top", "in1", "write_in",
)
SMEM_SPEC = pl.BlockSpec(memory_space=pltpu.SMEM)
F32 = jnp.float32
BF16 = jnp.bfloat16


def params(mebibytes):
    return pltpu.CompilerParams(vmem_limit_bytes=mebibytes << 20)


def cost(microseconds):
    return pl.CostEstimate(flops=int(microseconds * 1.15e9), bytes_accessed=1 << 20, transcendentals=0)


def dot(left, right, left_axis=1, right_axis=0):
    return lax.dot_general(
        left, right, (((left_axis,), (right_axis,)), ((), ())), preferred_element_type=F32
    )


def fixed(*shape):
    return pl.BlockSpec(shape, lambda i, *_: (0,) * len(shape))


FAR = "far"
REST = "rest"
CORE = "core"
ALL = ("member", REST, FAR, "near", CORE)
STEPS = ("first", "second", "third", "fourth")


def exchange(values, step):
    if step in (CORE, "member"):
        return lax.ppermute(values, step, [(0, 1), (1, 0)])
    count = 1
    for name in ALL:
        count *= lax.axis_size(name)
    bits = (count // 2, 2, 4, 8)
    place = STEPS.index(step)
    return lax.ppermute(values, ALL, [(i, i ^ bits[place ^ (i % 2)]) for i in range(count)])


def add(own, other):
    return (own.astype(F32) + other.astype(F32)).astype(own.dtype)


def own_places():
    core, member, near = lax.axis_index(CORE), lax.axis_index("member"), lax.axis_index("near")
    far = lax.axis_index(FAR)
    places = (member * 4 + near * 2 + (far & 1), near * 4 + member * 2 + (far >> 1))
    own = jnp.where(core == 0, places[0], places[1])
    other = jnp.where(core == 0, places[1], places[0])
    return jnp.stack([core, own, other]).astype(jnp.int32)


def over_rest(values):
    return lax.psum(values, REST) if lax.axis_size(REST) > 1 else values


class Line:
    def __init__(self):
        self.values = {}
        self.pending = {}
        self.steps = {}
        self.last = None

    def after_last(self, value):
        if self.last is not None:
            value, self.values[self.last] = lax.optimization_barrier(
                (value, self.values[self.last])
            )
        return value

    def before_kernel(self, value):
        value = self.after_last(value)
        if self.last in self.steps and self.last not in self.pending:
            self.start(self.last)
        return value

    def put(self, name, value):
        self.values[name] = value
        self.last = name

    def begin(self, name, send, keep):
        self.values[name] = keep
        self.pending[name] = exchange(send, CORE)
        self.steps[name] = [
            ("add", CORE),
            ("halve", "first"),
            ("halve", "second"),
            ("halve", "third"),
            ("double", "fourth"),
            ("gather", "third"),
            ("gather", "second"),
            ("gather", "first"),
            ("done", CORE),
        ]

    def begin_small(self, name, value):
        self.values[name] = value
        self.steps[name] = [("sum", step) for step in STEPS + (CORE,)]
        self.start(name)

    def start(self, name):
        if not self.steps[name]:
            return
        kind, step = self.steps[name][0]
        values = self.values[name]
        if kind == "halve":
            values = values[:, values.shape[1] // 2 :]
        self.pending[name] = exchange(values, step)

    def step(self, name, start=True):
        kind, _ = self.steps[name].pop(0)
        got = self.after_last(self.pending.pop(name))
        own = self.values[name]
        if kind == "halve":
            own = own[:, : got.shape[1]]
        if kind == "gather":
            result = jnp.concatenate([own, got], axis=1)
        elif kind == "done":
            result = (own, got)
        else:
            result = add(own, got)
        if kind == "double" or (kind == "sum" and not self.steps[name]):
            result = over_rest(result)
        self.put(name, result)
        if start:
            self.start(name)


def write_pieces(own_ref, product, send_ref, keep_ref, group):
    rows = keep_ref.shape[-2]
    core = own_ref[0]

    def one(piece, carry):
        kept = pl.multiple_of((2 * (piece ^ own_ref[1]) + core) * rows, rows)
        sent = pl.multiple_of((2 * (piece ^ own_ref[2]) + 1 - core) * rows, rows)
        keep_ref[group, piece] = product[pl.ds(kept, rows), :].astype(BF16)
        send_ref[group, piece] = product[pl.ds(sent, rows), :].astype(BF16)
        return carry

    lax.fori_loop(0, keep_ref.shape[1], one, 0)


def teacher_kernel(member_ref, logits_ref, give_ref, keep_ref, *, own_count):
    step = pl.program_id(0)
    total = None
    for teacher in range(logits_ref.shape[0]):
        logits = logits_ref[teacher, 0].astype(F32)
        shifted = logits - jnp.max(logits, axis=-1, keepdims=True)
        logp = shifted - jnp.log(jnp.sum(jnp.exp(shifted), axis=-1, keepdims=True))
        total = logp if total is None else total + logp

    @pl.when(step < own_count)
    def _():
        give_ref[0] = total

    @pl.when(step >= own_count)
    def _():
        keep_ref[0] = total


def teacher_sums(member, logits, own_count):
    teachers, utterances, frames, symbols = logits.shape
    shape = jax.ShapeDtypeStruct((own_count, frames, symbols), F32)

    def source(i, member_ref):
        mine = member_ref[0] * own_count
        theirs = (1 - member_ref[0]) * own_count
        return (0, jnp.where(i < own_count, theirs + i, mine + i - own_count), 0, 0)

    return pl.pallas_call(
        functools.partial(teacher_kernel, own_count=own_count),
        out_shape=(shape, shape),
        grid_spec=pltpu.PrefetchScalarGridSpec(
            num_scalar_prefetch=1,
            grid=(2 * own_count,),
            in_specs=[pl.BlockSpec((teachers, 1, frames, symbols), source)],
            out_specs=(
                pl.BlockSpec(
                    (1, frames, symbols), lambda i, _: (jnp.minimum(i, own_count - 1), 0, 0)
                ),
                pl.BlockSpec(
                    (1, frames, symbols), lambda i, _: (jnp.maximum(i - own_count, 0), 0, 0)
                ),
            ),
        ),
        compiler_params=params(16),
        cost_estimate=cost(4),
        name="teachers",
    )(member, logits)


def live_column(lengths_ref, utterance, frames):
    position = lax.broadcasted_iota(jnp.int32, (frames, 1), 0)
    return (position < lengths_ref[utterance]).astype(F32)


def clear_margins(pad_ref):
    frames = pad_ref.shape[2] - 2 * MARGIN
    zeros = jnp.zeros(pad_ref.shape[:2] + (MARGIN, LANES), F32)
    pad_ref[:, :, :MARGIN, :] = zeros
    pad_ref[:, :, MARGIN + frames :, :] = zeros


def shifted_views(pad_ref, lane, utterance, start, taps):
    first = MARGIN - taps // 2
    for phase in range(8):
        offsets = [offset for offset in range(first, first + taps) if offset % 8 == phase]
        if not offsets:
            continue
        low = offsets[0]
        span = offsets[-1] - low + TILE
        view = pad_ref[lane, utterance, start + low : start + low + span, :]
        for offset in offsets:
            yield offset - first, view[offset - low : offset - low + TILE]


def convolve(pad_ref, lane, utterance, start, depth_ref, flipped):
    taps = depth_ref.shape[0]
    columns = slice(lane * LANES, (lane + 1) * LANES)
    total = jnp.zeros((TILE, LANES), F32)
    for tap, view in shifted_views(pad_ref, lane, utterance, start, taps):
        row = taps - 1 - tap if flipped else tap
        total = total + view * depth_ref[row : row + 1, columns]
    return total


def forward_kernel(
    lengths_ref,
    features_ref,
    gain_ref,
    value_weight_ref,
    gate_weight_ref,
    depth_ref,
    out_weight_ref,
    turned_ref,
    gated_ref,
    gate_ref,
    slope_ref,
    active_ref,
    residual_ref,
    normed_ref,
    pad_ref,
    kept_ref,
):
    utterances = pad_ref.shape[1]
    frames = pad_ref.shape[2] - 2 * MARGIN
    step = pl.program_id(0)

    @pl.when(step == 0)
    def _():
        values = features_ref[...].astype(F32)
        centred = values - jnp.mean(values, axis=-1, keepdims=True)
        spread = jnp.mean(centred * centred, axis=-1, keepdims=True)
        normed = centred * lax.rsqrt(spread + 1e-05) * gain_ref[...]
        normed_ref[...] = normed.astype(BF16)
        turned_ref[...] = normed.T.astype(BF16)
        clear_margins(pad_ref)

    gate = jax.nn.sigmoid(dot(normed_ref[...], gate_weight_ref[...]))
    gate_ref[...] = gate
    values = dot(normed_ref[...], value_weight_ref[...]) * gate
    for utterance in range(utterances):
        rows = slice(utterance * frames, (utterance + 1) * frames)
        gated = values[rows, :] * live_column(lengths_ref, utterance, frames)
        gated_ref[rows, :] = gated
        for lane in range(WIDE // LANES):
            pad_ref[lane, utterance, MARGIN : MARGIN + frames, :] = gated[
                :, lane * LANES : (lane + 1) * LANES
            ]

    for lane in range(WIDE // LANES):
        columns = slice(lane * LANES, (lane + 1) * LANES)

        def one(utterance, carry, lane=lane, columns=columns):
            for start in range(0, frames, TILE):
                rows = pl.ds(pl.multiple_of(utterance * frames + start, TILE), TILE)
                convolved = convolve(pad_ref, lane, utterance, start, depth_ref, False)
                squash = jax.nn.sigmoid(convolved)
                active = (convolved * squash).astype(BF16)
                active_ref[rows, columns] = active
                kept_ref[step, rows, columns] = active
                slope_ref[rows, columns] = squash * (1.0 + convolved * (1.0 - squash))
            return carry

        lax.fori_loop(0, utterances, one, 0)

    @pl.when(step == kept_ref.shape[0] - 1)
    def _():
        active = jnp.concatenate([kept_ref[part] for part in range(kept_ref.shape[0])], axis=1)
        residual_ref[...] = features_ref[...].astype(F32) + dot(active, out_weight_ref[...])


def forward(lengths, features, gain, weight_in, depth, weight_out, utterances):
    rows, model = features.shape
    frames = rows // utterances
    steps = model // WIDE
    column = pl.BlockSpec((rows, WIDE), lambda i: (0, i))
    wide = jax.ShapeDtypeStruct((rows, model), F32)
    narrow = jax.ShapeDtypeStruct((rows, model), BF16)
    return pl.pallas_call(
        forward_kernel,
        grid=(steps,),
        out_shape=(jax.ShapeDtypeStruct((model, rows), BF16), wide, wide, wide, narrow, wide),
        in_specs=[
            SMEM_SPEC,
            fixed(rows, model),
            fixed(1, model),
            pl.BlockSpec((model, WIDE), lambda i: (0, i)),
            pl.BlockSpec((model, WIDE), lambda i: (0, steps + i)),
            pl.BlockSpec((depth.shape[0], WIDE), lambda i: (0, i)),
            fixed(model, model),
        ],
        out_specs=(fixed(model, rows), column, column, column, column, fixed(rows, model)),
        scratch_shapes=[
            pltpu.VMEM((rows, model), BF16),
            pltpu.VMEM((WIDE // LANES, utterances, frames + 2 * MARGIN, LANES), F32),
            pltpu.VMEM((steps, rows, WIDE), BF16),
        ],
        compiler_params=params(32),
        cost_estimate=cost(15),
        name="forward",
    )(lengths, features, gain, weight_in, weight_in, depth, weight_out)


def top_kernel(
    lengths_ref,
    residual_ref,
    gain_ref,
    head_ref,
    kept_ref,
    got_ref,
    loss_ref,
    final_ref,
    dlogits_ref,
    dresidual_ref,
):
    frames = residual_ref.shape[0]
    live = live_column(lengths_ref, pl.program_id(0), frames)
    values = residual_ref[...]
    centred = values - jnp.mean(values, axis=-1, keepdims=True)
    spread = jnp.mean(centred * centred, axis=-1, keepdims=True)
    inverse = lax.rsqrt(spread + 1e-05)
    unit = centred * inverse
    final = (unit * gain_ref[...]).astype(BF16)
    final_ref[...] = final

    def log_softmax(logits):
        shifted = logits - jnp.max(logits, axis=-1, keepdims=True)
        return shifted - jnp.log(jnp.sum(jnp.exp(shifted), axis=-1, keepdims=True))

    target = jnp.exp(log_softmax((kept_ref[0] + got_ref[0]) * (1.0 / TEACHERS)))
    logp = log_softmax(dot(final, head_ref[...]))
    cross = -jnp.sum(target * logp, axis=-1, keepdims=True)
    loss_ref[...] = jnp.broadcast_to(jnp.sum(cross * live, axis=0, keepdims=True), (1, 1, LANES))
    weight = jnp.sum(target, axis=-1, keepdims=True)
    dlogits = ((jnp.exp(logp) * weight - target) * live).astype(BF16)
    dlogits_ref[...] = dlogits
    dunit = dot(dlogits, head_ref[...], 1, 1) * gain_ref[...]
    average = jnp.mean(dunit, axis=-1, keepdims=True)
    along = jnp.mean(dunit * unit, axis=-1, keepdims=True)
    dresidual_ref[...] = (inverse * (dunit - average - unit * along)).astype(BF16)


def top(lengths, residual, gain, head, kept, got):
    rows, model = residual.shape
    utterances, frames, symbols = kept.shape
    per_row = pl.BlockSpec((frames, model), lambda i: (i, 0))
    sums = pl.BlockSpec((1, frames, symbols), lambda i: (i, 0, 0))
    return pl.pallas_call(
        top_kernel,
        grid=(utterances,),
        out_shape=(
            jax.ShapeDtypeStruct((utterances, 1, LANES), F32),
            jax.ShapeDtypeStruct((rows, model), BF16),
            jax.ShapeDtypeStruct((rows, symbols), BF16),
            jax.ShapeDtypeStruct((rows, model), BF16),
        ),
        in_specs=[SMEM_SPEC, per_row, fixed(1, model), fixed(model, symbols), sums, sums],
        out_specs=(
            pl.BlockSpec((1, 1, LANES), lambda i: (i, 0, 0)),
            per_row,
            pl.BlockSpec((frames, symbols), lambda i: (i, 0)),
            per_row,
        ),
        compiler_params=params(20),
        cost_estimate=cost(5),
        name="top",
    )(lengths, residual, gain, head, kept, got)


def outer_kernel(
    own_ref, active_ref, dresidual_ref, final_ref, dlogits_ref, send_ref, keep_ref, product_ref
):
    width = dresidual_ref.shape[1]
    product_ref[:, :width] = dot(active_ref[...], dresidual_ref[...], 0, 0)
    product_ref[:, width:] = dot(final_ref[...], dlogits_ref[...], 0, 0)
    write_pieces(own_ref, product_ref, send_ref, keep_ref, 0)


def outer(own, active, dresidual, final, dlogits):
    rows, model = active.shape
    half_out = dresidual.shape[1] // 2
    half_head = dlogits.shape[1] // 2
    width = half_out + half_head
    piece = (PLACES, model // (2 * PLACES), width)
    shape = jax.ShapeDtypeStruct((2,) + piece, BF16)
    out = pl.BlockSpec((1,) + piece, lambda i: (i, 0, 0, 0))
    return pl.pallas_call(
        outer_kernel,
        grid=(2,),
        out_shape=(shape, shape),
        in_specs=[
            SMEM_SPEC,
            fixed(rows, model),
            pl.BlockSpec((rows, half_out), lambda i: (0, i)),
            fixed(rows, model),
            pl.BlockSpec((rows, half_head), lambda i: (0, i)),
        ],
        out_specs=(out, out),
        scratch_shapes=[pltpu.VMEM((model, width), F32)],
        compiler_params=params(20),
        cost_estimate=cost(5),
        name="outer",
    )(own, active, dresidual, final, dlogits)


def inner_kernel(
    own_ref,
    lengths_ref,
    dresidual_ref,
    out_weight_ref,
    slope_ref,
    gated_ref,
    gate_ref,
    turned_ref,
    depth_ref,
    send_ref,
    keep_ref,
    dconv_ref,
    pad_ref,
    dvalue_ref,
    dgate_ref,
    product_ref,
):
    utterances = pad_ref.shape[1]
    frames = pad_ref.shape[2] - 2 * MARGIN

    @pl.when(pl.program_id(0) == 0)
    def _():
        clear_margins(pad_ref)

    dconv = dot(dresidual_ref[...], out_weight_ref[...], 1, 1) * slope_ref[...]
    dconv_ref[...] = dconv
    for utterance in range(utterances):
        rows = slice(utterance * frames, (utterance + 1) * frames)
        for lane in range(WIDE // LANES):
            pad_ref[lane, utterance, MARGIN : MARGIN + frames, :] = dconv[
                rows, lane * LANES : (lane + 1) * LANES
            ]

    for lane in range(WIDE // LANES):
        columns = slice(lane * LANES, (lane + 1) * LANES)

        def one(utterance, carry, lane=lane, columns=columns):
            for start in range(0, frames, TILE):
                rows = pl.ds(pl.multiple_of(utterance * frames + start, TILE), TILE)
                position = lax.broadcasted_iota(jnp.int32, (TILE, 1), 0) + start
                live = (position < lengths_ref[utterance]).astype(F32)
                dgated = convolve(pad_ref, lane, utterance, start, depth_ref, True) * live
                gate = gate_ref[rows, columns]
                dvalue_ref[rows, columns] = (dgated * gate).astype(BF16)
                dgate_ref[rows, columns] = (dgated * gated_ref[rows, columns] * (1.0 - gate)).astype(
                    BF16
                )
            return carry

        lax.fori_loop(0, utterances, one, 0)

    for group, source in ((0, dvalue_ref), (1, dgate_ref)):
        product_ref[...] = dot(turned_ref[...], source[...])
        write_pieces(own_ref, product_ref, send_ref, keep_ref, group)


def inner(own, lengths, dresidual, weight_out, slope, gated, gate, turned, depth, chunk, utterances):
    model, rows = turned.shape
    frames = rows // utterances
    steps = model // WIDE // CHUNKS
    first = chunk * steps
    column = pl.BlockSpec((rows, WIDE), lambda i: (0, first + i))
    piece = (2, PLACES, model // (2 * PLACES))
    shape = jax.ShapeDtypeStruct(piece + (steps * WIDE,), BF16)
    out = pl.BlockSpec(piece + (WIDE,), lambda i: (0, 0, 0, i))
    return pl.pallas_call(
        inner_kernel,
        grid=(steps,),
        out_shape=(shape, shape, jax.ShapeDtypeStruct((rows, steps * WIDE), F32)),
        in_specs=[
            SMEM_SPEC,
            SMEM_SPEC,
            fixed(rows, model),
            pl.BlockSpec((WIDE, model), lambda i: (first + i, 0)),
            column,
            column,
            column,
            fixed(model, rows),
            pl.BlockSpec((depth.shape[0], WIDE), lambda i: (0, first + i)),
        ],
        out_specs=(out, out, pl.BlockSpec((rows, WIDE), lambda i: (0, i))),
        scratch_shapes=[
            pltpu.VMEM((WIDE // LANES, utterances, frames + 2 * MARGIN, LANES), F32),
            pltpu.VMEM((rows, WIDE), BF16),
            pltpu.VMEM((rows, WIDE), BF16),
            pltpu.VMEM((model, WIDE), F32),
        ],
        compiler_params=params(24),
        cost_estimate=cost(11),
        name="inner",
    )(own, lengths, dresidual, weight_out, slope, gated, gate, turned, depth)


def taps_kernel(lengths_ref, gated_ref, *refs):
    *dconv_refs, out_ref, pad_ref, sums_ref = refs
    utterances = pad_ref.shape[1]
    frames = pad_ref.shape[2] - 2 * MARGIN
    taps = out_ref.shape[0] - 1
    step = pl.program_id(0)
    per_chunk = pl.num_programs(0) // len(dconv_refs)
    valid = lengths_ref[0]
    for utterance in range(1, utterances):
        valid = valid + lengths_ref[utterance]

    @pl.when(step == 0)
    def _():
        clear_margins(pad_ref)

    for lane in range(WIDE // LANES):
        columns = slice(lane * LANES, (lane + 1) * LANES)
        for utterance in range(utterances):
            rows = slice(utterance * frames, (utterance + 1) * frames)
            pad_ref[lane, utterance, MARGIN : MARGIN + frames, :] = gated_ref[rows, columns]

    for chunk, dconv_ref in enumerate(dconv_refs):

        @pl.when(step // per_chunk == chunk)
        def _(dconv_ref=dconv_ref):
            for lane in range(WIDE // LANES):
                columns = slice(lane * LANES, (lane + 1) * LANES)
                sums_ref[...] = jnp.zeros_like(sums_ref)

                def one(utterance, carry, lane=lane, columns=columns):
                    for start in range(0, frames, TILE):
                        rows = pl.ds(pl.multiple_of(utterance * frames + start, TILE), TILE)
                        dconv = dconv_ref[rows, columns]
                        for tap, view in shifted_views(pad_ref, lane, utterance, start, taps):
                            sums_ref[tap] += jnp.sum(
                                (view * dconv).reshape(TILE // 8, 8, LANES), axis=0
                            )
                    return carry

                lax.fori_loop(0, utterances, one, 0)
                out_ref[:taps, columns] = jnp.sum(sums_ref[...], axis=1)

    out_ref[taps:, :] = jnp.zeros((1, WIDE), F32) + valid.astype(F32)


def tap_sums(lengths, gated, dconvs, taps, utterances):
    rows, model = gated.shape
    steps = model // WIDE
    per_chunk = steps // len(dconvs)

    def part(chunk):
        low = chunk * per_chunk
        return pl.BlockSpec((rows, WIDE), lambda i: (0, jnp.clip(i - low, 0, per_chunk - 1)))

    return pl.pallas_call(
        taps_kernel,
        grid=(steps,),
        out_shape=jax.ShapeDtypeStruct((taps + 1, model), F32),
        in_specs=[SMEM_SPEC, pl.BlockSpec((rows, WIDE), lambda i: (0, i))]
        + [part(chunk) for chunk in range(len(dconvs))],
        out_specs=pl.BlockSpec((taps + 1, WIDE), lambda i: (0, i)),
        scratch_shapes=[
            pltpu.VMEM((WIDE // LANES, utterances, rows // utterances + 2 * MARGIN, LANES), F32),
            pltpu.VMEM((taps, 8, LANES), F32),
        ],
        compiler_params=params(16),
        cost_estimate=cost(9),
        name="taps",
    )(lengths, gated, *dconvs)


def gain_terms(weight, grad):
    terms = weight.astype(F32) * grad
    total = terms[:, :LANES]
    for first in range(LANES, terms.shape[1], LANES):
        total = total + terms[:, first : first + LANES]
    return total


def gain_row(terms):
    high = terms.astype(BF16)
    low = (terms - high.astype(F32)).astype(BF16)
    ones = jnp.ones((8, LANES), BF16)
    return (dot(ones, high, 1, 1) + dot(ones, low, 1, 1))[0:1, :]


def write_rows(own_ref, piece_refs, places, group, scale, targets):
    rows = piece_refs[0].shape[2]
    core = own_ref[0]
    first_place = pl.program_id(0) * places
    for index in range(places):
        for whose, (side, source) in enumerate(zip((core, 1 - core), piece_refs)):
            piece = (first_place + index) ^ own_ref[1 + whose]
            here = pl.ds(pl.multiple_of(index * 2 * rows + side * rows, rows), rows)
            for target, there, first, width in targets:
                target[here, there : there + width] = (
                    source[group, piece, :, first : first + width].astype(F32) * scale
                )


whole = pl.BlockSpec(memory_space=pltpu.VMEM)


def unpack_top_kernel(
    utts,
    own_ref,
    small_ref,
    mine_ref,
    other_ref,
    head_ref,
    gain_ref,
    losses_ref,
    wout_ref,
    dhead_ref,
    dgain_ref,
    depth_ref,
    loss_ref,
):
    taps = depth_ref.shape[0]
    scale = utts / small_ref[taps:, 0:1]
    half_out = wout_ref.shape[1] // 2
    half_head = dhead_ref.shape[1] // 2
    for group in range(2):
        targets = (
            (wout_ref, group * half_out, 0, half_out),
            (dhead_ref, group * half_head, half_out, half_head),
        )
        write_rows(own_ref, (mine_ref, other_ref), PLACES // 4, group, scale, targets)
    dgain_ref[...] = gain_row(gain_terms(head_ref[...], dhead_ref[...])) / gain_ref[...]
    depth_ref[...] = small_ref[:taps, :] * scale
    loss_ref[...] = losses_ref[...] * scale[None]


def unpack_top(utts, own, small, mine, other, head, gain, losses, width_out):
    steps = 4
    model, symbols = head.shape
    rows = model // steps
    taps = small.shape[0] - 1
    row = pl.BlockSpec((1, rows), lambda i, own_ref: (0, i))

    def block(width):
        return pl.BlockSpec((rows, width), lambda i, own_ref: (i, 0))

    return pl.pallas_call(
        functools.partial(unpack_top_kernel, utts),
        out_shape=(
            jax.ShapeDtypeStruct((model, width_out), F32),
            jax.ShapeDtypeStruct((model, symbols), F32),
            jax.ShapeDtypeStruct((1, model), F32),
            jax.ShapeDtypeStruct((taps, model), F32),
            jax.ShapeDtypeStruct(losses.shape, F32),
        ),
        grid_spec=pltpu.PrefetchScalarGridSpec(
            num_scalar_prefetch=1,
            grid=(steps,),
            in_specs=[
                fixed(*small.shape),
                whole,
                whole,
                block(symbols),
                row,
                fixed(*losses.shape),
            ],
            out_specs=(
                block(width_out),
                block(symbols),
                row,
                fixed(taps, model),
                fixed(*losses.shape),
            ),
        ),
        compiler_params=params(20),
        cost_estimate=cost(5),
        name="unpack_top",
    )(own, small, mine, other, head, gain, losses)


def unpack_inner_kernel(utts, own_ref, small_ref, weight_ref, gain_ref, *refs):
    *piece_refs, win_ref, dgain_ref = refs
    scale = utts / small_ref[small_ref.shape[0] - 1 :, 0:1]
    half = win_ref.shape[1] // 2
    for chunk in range(CHUNKS):
        pair = piece_refs[2 * chunk : 2 * chunk + 2]
        width = pair[0].shape[3]
        for group in range(2):
            targets = ((win_ref, group * half + chunk * width, 0, width),)
            write_rows(own_ref, pair, PLACES // 4, group, scale, targets)
    dgain_ref[...] = gain_row(gain_terms(weight_ref[...], win_ref[...])) / gain_ref[...]


def unpack_inner(utts, own, small, pieces, weight, gain):
    steps = 4
    model, width = weight.shape
    rows = model // steps
    row = pl.BlockSpec((1, rows), lambda i, own_ref: (0, i))
    block = pl.BlockSpec((rows, width), lambda i, own_ref: (i, 0))
    return pl.pallas_call(
        functools.partial(unpack_inner_kernel, utts),
        out_shape=(
            jax.ShapeDtypeStruct((model, width), F32),
            jax.ShapeDtypeStruct((1, model), F32),
        ),
        grid_spec=pltpu.PrefetchScalarGridSpec(
            num_scalar_prefetch=1,
            grid=(steps,),
            in_specs=[fixed(*small.shape), block, row]
            + [whole] * len(pieces),
            out_specs=(block, row),
        ),
        compiler_params=params(24),
        cost_estimate=cost(8),
        name="unpack_inner",
    )(own, small, weight, gain, *pieces)


def on_device(
    features,
    teacher_logits,
    lengths,
    gain_conv,
    weight_in,
    weight_depth,
    weight_out,
    gain_out,
    head_weight,
):
    count = 1
    for axis in ("member", "near", FAR, REST, CORE):
        count *= lax.axis_size(axis)
    member = lax.axis_index("member").astype(jnp.int32)[None]
    own = own_places()
    taps, model = weight_depth.shape
    utterances, frames, _ = features.shape
    utts = float(utterances * count)
    tie = lax.optimization_barrier

    own, member, teacher_logits = tie((own, member, teacher_logits))
    give, kept = teacher_sums(member, teacher_logits, utterances)
    got = exchange(give, "member")
    flat = features.reshape(utterances * frames, model)
    turned, gated, gate, slope, active, residual = forward(
        lengths, flat, gain_conv[None], weight_in, weight_depth, weight_out, utterances
    )
    losses, final, dlogits, dresidual = top(
        lengths, residual, gain_out[None], head_weight, kept, got
    )

    line = Line()

    def products(name, chunk):
        nonlocal dresidual
        dresidual = line.before_kernel(dresidual)
        send, keep, dconv = inner(
            own,
            lengths,
            dresidual,
            weight_out,
            slope,
            gated,
            gate,
            turned,
            weight_depth,
            chunk,
            utterances,
        )
        line.begin(name, send, keep)
        line.put(name + "_conv", dconv)

    send, keep = outer(own, active, dresidual, final, dlogits)
    send, keep, dresidual = tie((send, keep, dresidual))
    line.begin("top", send, keep)
    products("in0", 0)
    line.step("top", start=False)
    products("in1", 1)
    written = {}

    def write_top():
        mine, other = line.values["top"]
        *rest, written["losses"] = unpack_top(
            utts,
            own,
            line.values["small"],
            line.after_last(mine),
            other,
            head_weight,
            gain_out[None],
            losses,
            weight_out.shape[1],
        )
        written["out"], written["head"], by_head, written["depth"] = rest
        line.put("by_head", by_head)

    def write_in():
        pieces = [array for name in ("in0", "in1") for array in line.values[name]]
        written["in"], by_in = unpack_inner(
            utts, own, line.values["small"], pieces, weight_in, gain_conv[None]
        )
        line.put("by_in", by_in)

    def sum_taps():
        names = ("in0_conv", "in1_conv")
        dconvs = line.after_last(tuple(line.values[name] for name in names))
        line.put("taps", tap_sums(lengths, gated, dconvs, taps, utterances))
        line.begin_small("small", line.values["taps"])

    kernels = {
        "taps": sum_taps,
        "write_top": write_top,
        "write_in": write_in,
    }
    for name in ORDER:
        if name in kernels:
            kernels[name]()
        else:
            line.step(name)
    return (
        line.values["by_in"].reshape(model),
        written["in"],
        written["depth"],
        written["out"],
        line.values["by_head"].reshape(model),
        written["head"],
        written["losses"][:, 0, 0],
    )


def solution(mesh):
    members, others = mesh.devices.shape
    near, cores = 2, 2
    far = 2 * PLACES // (members * near)
    rest = others // (far * near * cores)
    split = jax.sharding.Mesh(
        mesh.devices.reshape(members, rest, far, near, cores),
        ("member", REST, FAR, "near", CORE),
    )
    dp = (REST, FAR, "near", CORE)
    in_specs = (
        P(dp + ("member",), None, None),
        P("member", dp, None, None),
        P(dp + ("member",)),
        P(),
        P(),
        P(),
        P(),
        P(),
        P(),
    )
    out_specs = (P(), P(), P(), P(), P(), P(), P(dp + ("member",)))
    return jax.shard_map(
        on_device, mesh=split, in_specs=in_specs, out_specs=out_specs, check_vma=False
    )
```

```python
import functools

import jax
import jax.numpy as jnp
from jax import lax
from jax.experimental import pallas as pl
from jax.experimental.pallas import tpu as pltpu
from jax.sharding import PartitionSpec as P

TEACHERS = 4
PLACES = 8
WIDE = 256
LANES = 128
TILE = 128
MARGIN = 16
CHUNKS = 2
ORDER = (
    "top", "in0", "in1", "taps", "in0", "top", "in1", "small", "in0", "top", "in1", "in0",
    "top", "in1", "in0", "top", "in1", "small", "in0", "top", "in1", "small", "in0", "top",
    "in1", "small", "in0", "top", "small", "in0", "in1", "write_top", "in1", "write_in",
)
SMEM_SPEC = pl.BlockSpec(memory_space=pltpu.SMEM)
F32 = jnp.float32
BF16 = jnp.bfloat16


def params(mebibytes):
    return pltpu.CompilerParams(vmem_limit_bytes=mebibytes << 20)


def cost(microseconds):
    return pl.CostEstimate(flops=int(microseconds * 1.15e9), bytes_accessed=1 << 20, transcendentals=0)


def dot(left, right, left_axis=1, right_axis=0):
    return lax.dot_general(
        left, right, (((left_axis,), (right_axis,)), ((), ())), preferred_element_type=F32
    )


def fixed(*shape):
    return pl.BlockSpec(shape, lambda i, *_: (0,) * len(shape))


FAR = "far"
REST = "rest"
CORE = "core"
ALL = ("member", REST, FAR, "near", CORE)
STEPS = ("first", "second", "third", "fourth")


def exchange(values, step):
    if step in (CORE, "member"):
        return lax.ppermute(values, step, [(0, 1), (1, 0)])
    count = 1
    for name in ALL:
        count *= lax.axis_size(name)
    bits = (count // 2, 2, 4, 8)
    place = STEPS.index(step)
    return lax.ppermute(values, ALL, [(i, i ^ bits[place ^ (i % 2)]) for i in range(count)])


def add(own, other):
    return (own.astype(F32) + other.astype(F32)).astype(own.dtype)


def own_places():
    core, member, near = lax.axis_index(CORE), lax.axis_index("member"), lax.axis_index("near")
    far = lax.axis_index(FAR)
    places = (member * 4 + near * 2 + (far & 1), near * 4 + member * 2 + (far >> 1))
    own = jnp.where(core == 0, places[0], places[1])
    other = jnp.where(core == 0, places[1], places[0])
    return jnp.stack([core, own, other]).astype(jnp.int32)


def over_rest(values):
    return lax.psum(values, REST) if lax.axis_size(REST) > 1 else values


class Line:
    def __init__(self):
        self.values = {}
        self.pending = {}
        self.steps = {}
        self.last = None

    def after_last(self, value):
        if self.last is not None:
            value, self.values[self.last] = lax.optimization_barrier(
                (value, self.values[self.last])
            )
        return value

    def before_kernel(self, value):
        value = self.after_last(value)
        if self.last in self.steps and self.last not in self.pending:
            self.start(self.last)
        return value

    def put(self, name, value):
        self.values[name] = value
        self.last = name

    def begin(self, name, send, keep):
        self.values[name] = keep
        self.pending[name] = exchange(send, CORE)
        self.steps[name] = [
            ("add", CORE),
            ("halve", "first"),
            ("halve", "second"),
            ("halve", "third"),
            ("double", "fourth"),
            ("gather", "third"),
            ("gather", "second"),
            ("gather", "first"),
            ("done", CORE),
        ]

    def begin_small(self, name, value):
        self.values[name] = value
        self.steps[name] = [("sum", step) for step in STEPS + (CORE,)]
        self.start(name)

    def start(self, name):
        if not self.steps[name]:
            return
        kind, step = self.steps[name][0]
        values = self.values[name]
        if kind == "halve":
            values = values[:, values.shape[1] // 2 :]
        self.pending[name] = exchange(values, step)

    def step(self, name, start=True):
        kind, _ = self.steps[name].pop(0)
        got = self.after_last(self.pending.pop(name))
        own = self.values[name]
        if kind == "halve":
            own = own[:, : got.shape[1]]
        if kind == "gather":
            result = jnp.concatenate([own, got], axis=1)
        elif kind == "done":
            result = (own, got)
        else:
            result = add(own, got)
        if kind == "double" or (kind == "sum" and not self.steps[name]):
            result = over_rest(result)
        self.put(name, result)
        if start:
            self.start(name)


def write_pieces(own_ref, product, send_ref, keep_ref, group):
    rows = keep_ref.shape[-2]
    core = own_ref[0]

    def one(piece, carry):
        kept = pl.multiple_of((2 * (piece ^ own_ref[1]) + core) * rows, rows)
        sent = pl.multiple_of((2 * (piece ^ own_ref[2]) + 1 - core) * rows, rows)
        keep_ref[group, piece] = product[pl.ds(kept, rows), :].astype(BF16)
        send_ref[group, piece] = product[pl.ds(sent, rows), :].astype(BF16)
        return carry

    lax.fori_loop(0, keep_ref.shape[1], one, 0)


def teacher_kernel(member_ref, logits_ref, give_ref, keep_ref, *, own_count):
    step = pl.program_id(0)
    total = None
    for teacher in range(logits_ref.shape[0]):
        logits = logits_ref[teacher, 0].astype(F32)
        shifted = logits - jnp.max(logits, axis=-1, keepdims=True)
        logp = shifted - jnp.log(jnp.sum(jnp.exp(shifted), axis=-1, keepdims=True))
        total = logp if total is None else total + logp

    @pl.when(step < own_count)
    def _():
        give_ref[0] = total

    @pl.when(step >= own_count)
    def _():
        keep_ref[0] = total


def teacher_sums(member, logits, own_count):
    teachers, utterances, frames, symbols = logits.shape
    shape = jax.ShapeDtypeStruct((own_count, frames, symbols), F32)

    def source(i, member_ref):
        mine = member_ref[0] * own_count
        theirs = (1 - member_ref[0]) * own_count
        return (0, jnp.where(i < own_count, theirs + i, mine + i - own_count), 0, 0)

    return pl.pallas_call(
        functools.partial(teacher_kernel, own_count=own_count),
        out_shape=(shape, shape),
        grid_spec=pltpu.PrefetchScalarGridSpec(
            num_scalar_prefetch=1,
            grid=(2 * own_count,),
            in_specs=[pl.BlockSpec((teachers, 1, frames, symbols), source)],
            out_specs=(
                pl.BlockSpec(
                    (1, frames, symbols), lambda i, _: (jnp.minimum(i, own_count - 1), 0, 0)
                ),
                pl.BlockSpec(
                    (1, frames, symbols), lambda i, _: (jnp.maximum(i - own_count, 0), 0, 0)
                ),
            ),
        ),
        compiler_params=params(16),
        cost_estimate=cost(4),
        name="teachers",
    )(member, logits)


def live_column(lengths_ref, utterance, frames):
    position = lax.broadcasted_iota(jnp.int32, (frames, 1), 0)
    return (position < lengths_ref[utterance]).astype(F32)


def clear_margins(pad_ref):
    frames = pad_ref.shape[2] - 2 * MARGIN
    zeros = jnp.zeros(pad_ref.shape[:2] + (MARGIN, LANES), F32)
    pad_ref[:, :, :MARGIN, :] = zeros
    pad_ref[:, :, MARGIN + frames :, :] = zeros


def shifted_views(pad_ref, lane, utterance, start, taps):
    first = MARGIN - taps // 2
    for phase in range(8):
        offsets = [offset for offset in range(first, first + taps) if offset % 8 == phase]
        if not offsets:
            continue
        low = offsets[0]
        span = offsets[-1] - low + TILE
        view = pad_ref[lane, utterance, start + low : start + low + span, :]
        for offset in offsets:
            yield offset - first, view[offset - low : offset - low + TILE]


def convolve(pad_ref, lane, utterance, start, depth_ref, flipped):
    taps = depth_ref.shape[0]
    columns = slice(lane * LANES, (lane + 1) * LANES)
    total = jnp.zeros((TILE, LANES), F32)
    for tap, view in shifted_views(pad_ref, lane, utterance, start, taps):
        row = taps - 1 - tap if flipped else tap
        total = total + view * depth_ref[row : row + 1, columns]
    return total


def forward_kernel(
    lengths_ref,
    features_ref,
    gain_ref,
    value_weight_ref,
    gate_weight_ref,
    depth_ref,
    out_weight_ref,
    turned_ref,
    gated_ref,
    gate_ref,
    slope_ref,
    active_ref,
    residual_ref,
    normed_ref,
    pad_ref,
    kept_ref,
):
    utterances = pad_ref.shape[1]
    frames = pad_ref.shape[2] - 2 * MARGIN
    step = pl.program_id(0)

    @pl.when(step == 0)
    def _():
        values = features_ref[...].astype(F32)
        centred = values - jnp.mean(values, axis=-1, keepdims=True)
        spread = jnp.mean(centred * centred, axis=-1, keepdims=True)
        normed = centred * lax.rsqrt(spread + 1e-05) * gain_ref[...]
        normed_ref[...] = normed.astype(BF16)
        turned_ref[...] = normed.T.astype(BF16)
        clear_margins(pad_ref)

    gate = jax.nn.sigmoid(dot(normed_ref[...], gate_weight_ref[...]))
    gate_ref[...] = gate
    values = dot(normed_ref[...], value_weight_ref[...]) * gate
    for utterance in range(utterances):
        rows = slice(utterance * frames, (utterance + 1) * frames)
        gated = values[rows, :] * live_column(lengths_ref, utterance, frames)
        gated_ref[rows, :] = gated
        for lane in range(WIDE // LANES):
            pad_ref[lane, utterance, MARGIN : MARGIN + frames, :] = gated[
                :, lane * LANES : (lane + 1) * LANES
            ]

    for lane in range(WIDE // LANES):
        columns = slice(lane * LANES, (lane + 1) * LANES)

        def one(utterance, carry, lane=lane, columns=columns):
            for start in range(0, frames, TILE):
                rows = pl.ds(pl.multiple_of(utterance * frames + start, TILE), TILE)
                convolved = convolve(pad_ref, lane, utterance, start, depth_ref, False)
                squash = jax.nn.sigmoid(convolved)
                active = (convolved * squash).astype(BF16)
                active_ref[rows, columns] = active
                kept_ref[step, rows, columns] = active
                slope_ref[rows, columns] = squash * (1.0 + convolved * (1.0 - squash))
            return carry

        lax.fori_loop(0, utterances, one, 0)

    @pl.when(step == kept_ref.shape[0] - 1)
    def _():
        active = jnp.concatenate([kept_ref[part] for part in range(kept_ref.shape[0])], axis=1)
        residual_ref[...] = features_ref[...].astype(F32) + dot(active, out_weight_ref[...])


def forward(lengths, features, gain, weight_in, depth, weight_out, utterances):
    rows, model = features.shape
    frames = rows // utterances
    steps = model // WIDE
    column = pl.BlockSpec((rows, WIDE), lambda i: (0, i))
    wide = jax.ShapeDtypeStruct((rows, model), F32)
    narrow = jax.ShapeDtypeStruct((rows, model), BF16)
    return pl.pallas_call(
        forward_kernel,
        grid=(steps,),
        out_shape=(jax.ShapeDtypeStruct((model, rows), BF16), wide, wide, wide, narrow, wide),
        in_specs=[
            SMEM_SPEC,
            fixed(rows, model),
            fixed(1, model),
            pl.BlockSpec((model, WIDE), lambda i: (0, i)),
            pl.BlockSpec((model, WIDE), lambda i: (0, steps + i)),
            pl.BlockSpec((depth.shape[0], WIDE), lambda i: (0, i)),
            fixed(model, model),
        ],
        out_specs=(fixed(model, rows), column, column, column, column, fixed(rows, model)),
        scratch_shapes=[
            pltpu.VMEM((rows, model), BF16),
            pltpu.VMEM((WIDE // LANES, utterances, frames + 2 * MARGIN, LANES), F32),
            pltpu.VMEM((steps, rows, WIDE), BF16),
        ],
        compiler_params=params(32),
        cost_estimate=cost(15),
        name="forward",
    )(lengths, features, gain, weight_in, weight_in, depth, weight_out)


def top_kernel(
    lengths_ref,
    residual_ref,
    gain_ref,
    head_ref,
    kept_ref,
    got_ref,
    loss_ref,
    final_ref,
    dlogits_ref,
    dresidual_ref,
):
    frames = residual_ref.shape[0]
    live = live_column(lengths_ref, pl.program_id(0), frames)
    values = residual_ref[...]
    centred = values - jnp.mean(values, axis=-1, keepdims=True)
    spread = jnp.mean(centred * centred, axis=-1, keepdims=True)
    inverse = lax.rsqrt(spread + 1e-05)
    unit = centred * inverse
    final = (unit * gain_ref[...]).astype(BF16)
    final_ref[...] = final

    def log_softmax(logits):
        shifted = logits - jnp.max(logits, axis=-1, keepdims=True)
        return shifted - jnp.log(jnp.sum(jnp.exp(shifted), axis=-1, keepdims=True))

    target = jnp.exp(log_softmax((kept_ref[0] + got_ref[0]) * (1.0 / TEACHERS)))
    logp = log_softmax(dot(final, head_ref[...]))
    cross = -jnp.sum(target * logp, axis=-1, keepdims=True)
    loss_ref[...] = jnp.broadcast_to(jnp.sum(cross * live, axis=0, keepdims=True), (1, 1, LANES))
    weight = jnp.sum(target, axis=-1, keepdims=True)
    dlogits = ((jnp.exp(logp) * weight - target) * live).astype(BF16)
    dlogits_ref[...] = dlogits
    dunit = dot(dlogits, head_ref[...], 1, 1) * gain_ref[...]
    average = jnp.mean(dunit, axis=-1, keepdims=True)
    along = jnp.mean(dunit * unit, axis=-1, keepdims=True)
    dresidual_ref[...] = (inverse * (dunit - average - unit * along)).astype(BF16)


def top(lengths, residual, gain, head, kept, got):
    rows, model = residual.shape
    utterances, frames, symbols = kept.shape
    per_row = pl.BlockSpec((frames, model), lambda i: (i, 0))
    sums = pl.BlockSpec((1, frames, symbols), lambda i: (i, 0, 0))
    return pl.pallas_call(
        top_kernel,
        grid=(utterances,),
        out_shape=(
            jax.ShapeDtypeStruct((utterances, 1, LANES), F32),
            jax.ShapeDtypeStruct((rows, model), BF16),
            jax.ShapeDtypeStruct((rows, symbols), BF16),
            jax.ShapeDtypeStruct((rows, model), BF16),
        ),
        in_specs=[SMEM_SPEC, per_row, fixed(1, model), fixed(model, symbols), sums, sums],
        out_specs=(
            pl.BlockSpec((1, 1, LANES), lambda i: (i, 0, 0)),
            per_row,
            pl.BlockSpec((frames, symbols), lambda i: (i, 0)),
            per_row,
        ),
        compiler_params=params(20),
        cost_estimate=cost(5),
        name="top",
    )(lengths, residual, gain, head, kept, got)


def outer_kernel(
    own_ref, active_ref, dresidual_ref, final_ref, dlogits_ref, send_ref, keep_ref, product_ref
):
    width = dresidual_ref.shape[1]
    product_ref[:, :width] = dot(active_ref[...], dresidual_ref[...], 0, 0)
    product_ref[:, width:] = dot(final_ref[...], dlogits_ref[...], 0, 0)
    write_pieces(own_ref, product_ref, send_ref, keep_ref, 0)


def outer(own, active, dresidual, final, dlogits):
    rows, model = active.shape
    half_out = dresidual.shape[1] // 2
    half_head = dlogits.shape[1] // 2
    width = half_out + half_head
    piece = (PLACES, model // (2 * PLACES), width)
    shape = jax.ShapeDtypeStruct((2,) + piece, BF16)
    out = pl.BlockSpec((1,) + piece, lambda i: (i, 0, 0, 0))
    return pl.pallas_call(
        outer_kernel,
        grid=(2,),
        out_shape=(shape, shape),
        in_specs=[
            SMEM_SPEC,
            fixed(rows, model),
            pl.BlockSpec((rows, half_out), lambda i: (0, i)),
            fixed(rows, model),
            pl.BlockSpec((rows, half_head), lambda i: (0, i)),
        ],
        out_specs=(out, out),
        scratch_shapes=[pltpu.VMEM((model, width), F32)],
        compiler_params=params(20),
        cost_estimate=cost(5),
        name="outer",
    )(own, active, dresidual, final, dlogits)


def inner_kernel(
    own_ref,
    lengths_ref,
    dresidual_ref,
    out_weight_ref,
    slope_ref,
    gated_ref,
    gate_ref,
    turned_ref,
    depth_ref,
    send_ref,
    keep_ref,
    dconv_ref,
    pad_ref,
    dvalue_ref,
    dgate_ref,
    product_ref,
):
    utterances = pad_ref.shape[1]
    frames = pad_ref.shape[2] - 2 * MARGIN

    @pl.when(pl.program_id(0) == 0)
    def _():
        clear_margins(pad_ref)

    dconv = dot(dresidual_ref[...], out_weight_ref[...], 1, 1) * slope_ref[...]
    dconv_ref[...] = dconv
    for utterance in range(utterances):
        rows = slice(utterance * frames, (utterance + 1) * frames)
        for lane in range(WIDE // LANES):
            pad_ref[lane, utterance, MARGIN : MARGIN + frames, :] = dconv[
                rows, lane * LANES : (lane + 1) * LANES
            ]

    for lane in range(WIDE // LANES):
        columns = slice(lane * LANES, (lane + 1) * LANES)

        def one(utterance, carry, lane=lane, columns=columns):
            for start in range(0, frames, TILE):
                rows = pl.ds(pl.multiple_of(utterance * frames + start, TILE), TILE)
                position = lax.broadcasted_iota(jnp.int32, (TILE, 1), 0) + start
                live = (position < lengths_ref[utterance]).astype(F32)
                dgated = convolve(pad_ref, lane, utterance, start, depth_ref, True) * live
                gate = gate_ref[rows, columns]
                dvalue_ref[rows, columns] = (dgated * gate).astype(BF16)
                dgate_ref[rows, columns] = (dgated * gated_ref[rows, columns] * (1.0 - gate)).astype(
                    BF16
                )
            return carry

        lax.fori_loop(0, utterances, one, 0)

    for group, source in ((0, dvalue_ref), (1, dgate_ref)):
        product_ref[...] = dot(turned_ref[...], source[...])
        write_pieces(own_ref, product_ref, send_ref, keep_ref, group)


def inner(own, lengths, dresidual, weight_out, slope, gated, gate, turned, depth, chunk, utterances):
    model, rows = turned.shape
    frames = rows // utterances
    steps = model // WIDE // CHUNKS
    first = chunk * steps
    column = pl.BlockSpec((rows, WIDE), lambda i: (0, first + i))
    piece = (2, PLACES, model // (2 * PLACES))
    shape = jax.ShapeDtypeStruct(piece + (steps * WIDE,), BF16)
    out = pl.BlockSpec(piece + (WIDE,), lambda i: (0, 0, 0, i))
    return pl.pallas_call(
        inner_kernel,
        grid=(steps,),
        out_shape=(shape, shape, jax.ShapeDtypeStruct((rows, steps * WIDE), F32)),
        in_specs=[
            SMEM_SPEC,
            SMEM_SPEC,
            fixed(rows, model),
            pl.BlockSpec((WIDE, model), lambda i: (first + i, 0)),
            column,
            column,
            column,
            fixed(model, rows),
            pl.BlockSpec((depth.shape[0], WIDE), lambda i: (0, first + i)),
        ],
        out_specs=(out, out, pl.BlockSpec((rows, WIDE), lambda i: (0, i))),
        scratch_shapes=[
            pltpu.VMEM((WIDE // LANES, utterances, frames + 2 * MARGIN, LANES), F32),
            pltpu.VMEM((rows, WIDE), BF16),
            pltpu.VMEM((rows, WIDE), BF16),
            pltpu.VMEM((model, WIDE), F32),
        ],
        compiler_params=params(24),
        cost_estimate=cost(11),
        name="inner",
    )(own, lengths, dresidual, weight_out, slope, gated, gate, turned, depth)


def taps_kernel(lengths_ref, gated_ref, *refs):
    *dconv_refs, out_ref, pad_ref, sums_ref = refs
    utterances = pad_ref.shape[1]
    frames = pad_ref.shape[2] - 2 * MARGIN
    taps = out_ref.shape[0] - 1
    step = pl.program_id(0)
    per_chunk = pl.num_programs(0) // len(dconv_refs)
    valid = lengths_ref[0]
    for utterance in range(1, utterances):
        valid = valid + lengths_ref[utterance]

    @pl.when(step == 0)
    def _():
        clear_margins(pad_ref)

    for lane in range(WIDE // LANES):
        columns = slice(lane * LANES, (lane + 1) * LANES)
        for utterance in range(utterances):
            rows = slice(utterance * frames, (utterance + 1) * frames)
            pad_ref[lane, utterance, MARGIN : MARGIN + frames, :] = gated_ref[rows, columns]

    for chunk, dconv_ref in enumerate(dconv_refs):

        @pl.when(step // per_chunk == chunk)
        def _(dconv_ref=dconv_ref):
            for lane in range(WIDE // LANES):
                columns = slice(lane * LANES, (lane + 1) * LANES)
                sums_ref[...] = jnp.zeros_like(sums_ref)

                def one(utterance, carry, lane=lane, columns=columns):
                    for start in range(0, frames, TILE):
                        rows = pl.ds(pl.multiple_of(utterance * frames + start, TILE), TILE)
                        dconv = dconv_ref[rows, columns]
                        for tap, view in shifted_views(pad_ref, lane, utterance, start, taps):
                            sums_ref[tap] += jnp.sum(
                                (view * dconv).reshape(TILE // 8, 8, LANES), axis=0
                            )
                    return carry

                lax.fori_loop(0, utterances, one, 0)
                out_ref[:taps, columns] = jnp.sum(sums_ref[...], axis=1)

    out_ref[taps:, :] = jnp.zeros((1, WIDE), F32) + valid.astype(F32)


def tap_sums(lengths, gated, dconvs, taps, utterances):
    rows, model = gated.shape
    steps = model // WIDE
    per_chunk = steps // len(dconvs)

    def part(chunk):
        low = chunk * per_chunk
        return pl.BlockSpec((rows, WIDE), lambda i: (0, jnp.clip(i - low, 0, per_chunk - 1)))

    return pl.pallas_call(
        taps_kernel,
        grid=(steps,),
        out_shape=jax.ShapeDtypeStruct((taps + 1, model), F32),
        in_specs=[SMEM_SPEC, pl.BlockSpec((rows, WIDE), lambda i: (0, i))]
        + [part(chunk) for chunk in range(len(dconvs))],
        out_specs=pl.BlockSpec((taps + 1, WIDE), lambda i: (0, i)),
        scratch_shapes=[
            pltpu.VMEM((WIDE // LANES, utterances, rows // utterances + 2 * MARGIN, LANES), F32),
            pltpu.VMEM((taps, 8, LANES), F32),
        ],
        compiler_params=params(16),
        cost_estimate=cost(9),
        name="taps",
    )(lengths, gated, *dconvs)


def gain_terms(weight, grad):
    terms = weight.astype(F32) * grad
    total = terms[:, :LANES]
    for first in range(LANES, terms.shape[1], LANES):
        total = total + terms[:, first : first + LANES]
    return total


def gain_row(terms):
    high = terms.astype(BF16)
    low = (terms - high.astype(F32)).astype(BF16)
    ones = jnp.ones((8, LANES), BF16)
    return (dot(ones, high, 1, 1) + dot(ones, low, 1, 1))[0:1, :]


def write_rows(own_ref, piece_refs, places, group, scale, targets):
    rows = piece_refs[0].shape[2]
    core = own_ref[0]
    first_place = pl.program_id(0) * places
    for index in range(places):
        for whose, (side, source) in enumerate(zip((core, 1 - core), piece_refs)):
            piece = (first_place + index) ^ own_ref[1 + whose]
            here = pl.ds(pl.multiple_of(index * 2 * rows + side * rows, rows), rows)
            for target, there, first, width in targets:
                target[here, there : there + width] = (
                    source[group, piece, :, first : first + width].astype(F32) * scale
                )


whole = pl.BlockSpec(memory_space=pltpu.VMEM)


def unpack_top_kernel(
    utts,
    own_ref,
    small_ref,
    mine_ref,
    other_ref,
    head_ref,
    gain_ref,
    losses_ref,
    wout_ref,
    dhead_ref,
    dgain_ref,
    depth_ref,
    loss_ref,
):
    taps = depth_ref.shape[0]
    scale = utts / small_ref[taps:, 0:1]
    half_out = wout_ref.shape[1] // 2
    half_head = dhead_ref.shape[1] // 2
    for group in range(2):
        targets = (
            (wout_ref, group * half_out, 0, half_out),
            (dhead_ref, group * half_head, half_out, half_head),
        )
        write_rows(own_ref, (mine_ref, other_ref), PLACES // 4, group, scale, targets)
    dgain_ref[...] = gain_row(gain_terms(head_ref[...], dhead_ref[...])) / gain_ref[...]
    depth_ref[...] = small_ref[:taps, :] * scale
    loss_ref[...] = losses_ref[...] * scale[None]


def unpack_top(utts, own, small, mine, other, head, gain, losses, width_out):
    steps = 4
    model, symbols = head.shape
    rows = model // steps
    taps = small.shape[0] - 1
    row = pl.BlockSpec((1, rows), lambda i, own_ref: (0, i))

    def block(width):
        return pl.BlockSpec((rows, width), lambda i, own_ref: (i, 0))

    return pl.pallas_call(
        functools.partial(unpack_top_kernel, utts),
        out_shape=(
            jax.ShapeDtypeStruct((model, width_out), F32),
            jax.ShapeDtypeStruct((model, symbols), F32),
            jax.ShapeDtypeStruct((1, model), F32),
            jax.ShapeDtypeStruct((taps, model), F32),
            jax.ShapeDtypeStruct(losses.shape, F32),
        ),
        grid_spec=pltpu.PrefetchScalarGridSpec(
            num_scalar_prefetch=1,
            grid=(steps,),
            in_specs=[
                fixed(*small.shape),
                whole,
                whole,
                block(symbols),
                row,
                fixed(*losses.shape),
            ],
            out_specs=(
                block(width_out),
                block(symbols),
                row,
                fixed(taps, model),
                fixed(*losses.shape),
            ),
        ),
        compiler_params=params(20),
        cost_estimate=cost(5),
        name="unpack_top",
    )(own, small, mine, other, head, gain, losses)


def unpack_inner_kernel(utts, own_ref, small_ref, weight_ref, gain_ref, *refs):
    *piece_refs, win_ref, dgain_ref = refs
    scale = utts / small_ref[small_ref.shape[0] - 1 :, 0:1]
    half = win_ref.shape[1] // 2
    for chunk in range(CHUNKS):
        pair = piece_refs[2 * chunk : 2 * chunk + 2]
        width = pair[0].shape[3]
        for group in range(2):
            targets = ((win_ref, group * half + chunk * width, 0, width),)
            write_rows(own_ref, pair, PLACES // 4, group, scale, targets)
    dgain_ref[...] = gain_row(gain_terms(weight_ref[...], win_ref[...])) / gain_ref[...]


def unpack_inner(utts, own, small, pieces, weight, gain):
    steps = 4
    model, width = weight.shape
    rows = model // steps
    row = pl.BlockSpec((1, rows), lambda i, own_ref: (0, i))
    block = pl.BlockSpec((rows, width), lambda i, own_ref: (i, 0))
    return pl.pallas_call(
        functools.partial(unpack_inner_kernel, utts),
        out_shape=(
            jax.ShapeDtypeStruct((model, width), F32),
            jax.ShapeDtypeStruct((1, model), F32),
        ),
        grid_spec=pltpu.PrefetchScalarGridSpec(
            num_scalar_prefetch=1,
            grid=(steps,),
            in_specs=[fixed(*small.shape), block, row]
            + [whole] * len(pieces),
            out_specs=(block, row),
        ),
        compiler_params=params(24),
        cost_estimate=cost(8),
        name="unpack_inner",
    )(own, small, weight, gain, *pieces)


def on_device(
    features,
    teacher_logits,
    lengths,
    gain_conv,
    weight_in,
    weight_depth,
    weight_out,
    gain_out,
    head_weight,
):
    count = 1
    for axis in ("member", "near", FAR, REST, CORE):
        count *= lax.axis_size(axis)
    member = lax.axis_index("member").astype(jnp.int32)[None]
    own = own_places()
    taps, model = weight_depth.shape
    utterances, frames, _ = features.shape
    utts = float(utterances * count)
    tie = lax.optimization_barrier

    own, member, teacher_logits = tie((own, member, teacher_logits))
    give, kept = teacher_sums(member, teacher_logits, utterances)
    got = exchange(give, "member")
    flat = features.reshape(utterances * frames, model)
    turned, gated, gate, slope, active, residual = forward(
        lengths, flat, gain_conv[None], weight_in, weight_depth, weight_out, utterances
    )
    losses, final, dlogits, dresidual = top(
        lengths, residual, gain_out[None], head_weight, kept, got
    )

    line = Line()

    def products(name, chunk):
        nonlocal dresidual
        dresidual = line.before_kernel(dresidual)
        send, keep, dconv = inner(
            own,
            lengths,
            dresidual,
            weight_out,
            slope,
            gated,
            gate,
            turned,
            weight_depth,
            chunk,
            utterances,
        )
        line.begin(name, send, keep)
        line.put(name + "_conv", dconv)

    send, keep = outer(own, active, dresidual, final, dlogits)
    send, keep, dresidual = tie((send, keep, dresidual))
    line.begin("top", send, keep)
    products("in0", 0)
    line.step("top", start=False)
    products("in1", 1)
    written = {}

    def write_top():
        mine, other = line.values["top"]
        *rest, written["losses"] = unpack_top(
            utts,
            own,
            line.values["small"],
            line.after_last(mine),
            other,
            head_weight,
            gain_out[None],
            losses,
            weight_out.shape[1],
        )
        written["out"], written["head"], by_head, written["depth"] = rest
        line.put("by_head", by_head)

    def write_in():
        pieces = [array for name in ("in0", "in1") for array in line.values[name]]
        written["in"], by_in = unpack_inner(
            utts, own, line.values["small"], pieces, weight_in, gain_conv[None]
        )
        line.put("by_in", by_in)

    def sum_taps():
        names = ("in0_conv", "in1_conv")
        dconvs = line.after_last(tuple(line.values[name] for name in names))
        line.put("taps", tap_sums(lengths, gated, dconvs, taps, utterances))
        line.begin_small("small", line.values["taps"])

    kernels = {
        "taps": sum_taps,
        "write_top": write_top,
        "write_in": write_in,
    }
    for name in ORDER:
        if name in kernels:
            kernels[name]()
        else:
            line.step(name)
    return (
        line.values["by_in"].reshape(model),
        written["in"],
        written["depth"],
        written["out"],
        line.values["by_head"].reshape(model),
        written["head"],
        written["losses"][:, 0, 0],
    )


def solution(mesh):
    members, others = mesh.devices.shape
    near, cores = 2, 2
    far = 2 * PLACES // (members * near)
    rest = others // (far * near * cores)
    split = jax.sharding.Mesh(
        mesh.devices.reshape(members, rest, far, near, cores),
        ("member", REST, FAR, "near", CORE),
    )
    dp = (REST, FAR, "near", CORE)
    in_specs = (
        P(dp + ("member",), None, None),
        P("member", dp, None, None),
        P(dp + ("member",)),
        P(),
        P(),
        P(),
        P(),
        P(),
        P(),
    )
    out_specs = (P(), P(), P(), P(), P(), P(), P(dp + ("member",)))
    return jax.shard_map(
        on_device, mesh=split, in_specs=in_specs, out_specs=out_specs, check_vma=False
    )
```

```python
import functools

import jax
import jax.numpy as jnp
from jax import lax
from jax.experimental import pallas as pl
from jax.experimental.pallas import tpu as pltpu
from jax.sharding import PartitionSpec as P

TEACHERS = 4
PLACES = 8
WIDE = 256
LANES = 128
TILE = 128
MARGIN = 16
CHUNKS = 2
ORDER = (
    "top", "in0", "in1", "taps", "in0", "top", "in1", "small", "in0", "top", "in1", "in0",
    "top", "in1", "in0", "top", "in1", "small", "in0", "top", "in1", "small", "in0", "top",
    "in1", "small", "in0", "top", "small", "in0", "write_top", "in1", "in1", "write_in",
)
SMEM_SPEC = pl.BlockSpec(memory_space=pltpu.SMEM)
F32 = jnp.float32
BF16 = jnp.bfloat16


def params(mebibytes):
    return pltpu.CompilerParams(vmem_limit_bytes=mebibytes << 20)


def cost(microseconds):
    return pl.CostEstimate(flops=int(microseconds * 1.15e9), bytes_accessed=1 << 20, transcendentals=0)


def dot(left, right, left_axis=1, right_axis=0):
    return lax.dot_general(
        left, right, (((left_axis,), (right_axis,)), ((), ())), preferred_element_type=F32
    )


def fixed(*shape):
    return pl.BlockSpec(shape, lambda i, *_: (0,) * len(shape))


FAR = "far"
REST = "rest"
CORE = "core"
ALL = ("member", REST, FAR, "near", CORE)
STEPS = ("first", "second", "third", "fourth")


def exchange(values, step):
    if step in (CORE, "member"):
        return lax.ppermute(values, step, [(0, 1), (1, 0)])
    count = 1
    for name in ALL:
        count *= lax.axis_size(name)
    bits = (count // 2, 2, 4, 8)
    place = STEPS.index(step)
    return lax.ppermute(values, ALL, [(i, i ^ bits[place ^ (i % 2)]) for i in range(count)])


def add(own, other):
    return (own.astype(F32) + other.astype(F32)).astype(own.dtype)


def own_places():
    core, member, near = lax.axis_index(CORE), lax.axis_index("member"), lax.axis_index("near")
    far = lax.axis_index(FAR)
    places = (member * 4 + near * 2 + (far & 1), near * 4 + member * 2 + (far >> 1))
    own = jnp.where(core == 0, places[0], places[1])
    other = jnp.where(core == 0, places[1], places[0])
    return jnp.stack([core, own, other]).astype(jnp.int32)


def over_rest(values):
    return lax.psum(values, REST) if lax.axis_size(REST) > 1 else values


class Line:
    def __init__(self):
        self.values = {}
        self.pending = {}
        self.steps = {}
        self.last = None

    def after_last(self, value):
        if self.last is not None:
            value, self.values[self.last] = lax.optimization_barrier(
                (value, self.values[self.last])
            )
        return value

    def before_kernel(self, value):
        value = self.after_last(value)
        if self.last in self.steps and self.last not in self.pending:
            self.start(self.last)
        return value

    def put(self, name, value):
        self.values[name] = value
        self.last = name

    def begin(self, name, send, keep):
        self.values[name] = keep
        self.pending[name] = exchange(send, CORE)
        self.steps[name] = [
            ("add", CORE),
            ("halve", "first"),
            ("halve", "second"),
            ("halve", "third"),
            ("double", "fourth"),
            ("gather", "third"),
            ("gather", "second"),
            ("gather", "first"),
            ("done", CORE),
        ]

    def begin_small(self, name, value):
        self.values[name] = value
        self.steps[name] = [("sum", step) for step in STEPS + (CORE,)]
        self.start(name)

    def start(self, name):
        if not self.steps[name]:
            return
        kind, step = self.steps[name][0]
        values = self.values[name]
        if kind == "halve":
            values = values[:, values.shape[1] // 2 :]
        self.pending[name] = exchange(values, step)

    def step(self, name, start=True):
        kind, _ = self.steps[name].pop(0)
        got = self.after_last(self.pending.pop(name))
        own = self.values[name]
        if kind == "halve":
            own = own[:, : got.shape[1]]
        if kind == "gather":
            result = jnp.concatenate([own, got], axis=1)
        elif kind == "done":
            result = (own, got)
        else:
            result = add(own, got)
        if kind == "double" or (kind == "sum" and not self.steps[name]):
            result = over_rest(result)
        self.put(name, result)
        if start:
            self.start(name)


def write_pieces(own_ref, product, send_ref, keep_ref, group):
    rows = keep_ref.shape[-2]
    core = own_ref[0]

    def one(piece, carry):
        kept = pl.multiple_of((2 * (piece ^ own_ref[1]) + core) * rows, rows)
        sent = pl.multiple_of((2 * (piece ^ own_ref[2]) + 1 - core) * rows, rows)
        keep_ref[group, piece] = product[pl.ds(kept, rows), :].astype(BF16)
        send_ref[group, piece] = product[pl.ds(sent, rows), :].astype(BF16)
        return carry

    lax.fori_loop(0, keep_ref.shape[1], one, 0)


def teacher_kernel(member_ref, logits_ref, give_ref, keep_ref, *, own_count):
    step = pl.program_id(0)
    total = None
    for teacher in range(logits_ref.shape[0]):
        logits = logits_ref[teacher, 0].astype(F32)
        shifted = logits - jnp.max(logits, axis=-1, keepdims=True)
        logp = shifted - jnp.log(jnp.sum(jnp.exp(shifted), axis=-1, keepdims=True))
        total = logp if total is None else total + logp

    @pl.when(step < own_count)
    def _():
        give_ref[0] = total

    @pl.when(step >= own_count)
    def _():
        keep_ref[0] = total


def teacher_sums(member, logits, own_count):
    teachers, utterances, frames, symbols = logits.shape
    shape = jax.ShapeDtypeStruct((own_count, frames, symbols), F32)

    def source(i, member_ref):
        mine = member_ref[0] * own_count
        theirs = (1 - member_ref[0]) * own_count
        return (0, jnp.where(i < own_count, theirs + i, mine + i - own_count), 0, 0)

    return pl.pallas_call(
        functools.partial(teacher_kernel, own_count=own_count),
        out_shape=(shape, shape),
        grid_spec=pltpu.PrefetchScalarGridSpec(
            num_scalar_prefetch=1,
            grid=(2 * own_count,),
            in_specs=[pl.BlockSpec((teachers, 1, frames, symbols), source)],
            out_specs=(
                pl.BlockSpec(
                    (1, frames, symbols), lambda i, _: (jnp.minimum(i, own_count - 1), 0, 0)
                ),
                pl.BlockSpec(
                    (1, frames, symbols), lambda i, _: (jnp.maximum(i - own_count, 0), 0, 0)
                ),
            ),
        ),
        compiler_params=params(16),
        cost_estimate=cost(4),
        name="teachers",
    )(member, logits)


def live_column(lengths_ref, utterance, frames):
    position = lax.broadcasted_iota(jnp.int32, (frames, 1), 0)
    return (position < lengths_ref[utterance]).astype(F32)


def clear_margins(pad_ref):
    frames = pad_ref.shape[2] - 2 * MARGIN
    zeros = jnp.zeros(pad_ref.shape[:2] + (MARGIN, LANES), F32)
    pad_ref[:, :, :MARGIN, :] = zeros
    pad_ref[:, :, MARGIN + frames :, :] = zeros


def shifted_views(pad_ref, lane, utterance, start, taps):
    first = MARGIN - taps // 2
    for phase in range(8):
        offsets = [offset for offset in range(first, first + taps) if offset % 8 == phase]
        if not offsets:
            continue
        low = offsets[0]
        span = offsets[-1] - low + TILE
        view = pad_ref[lane, utterance, start + low : start + low + span, :]
        for offset in offsets:
            yield offset - first, view[offset - low : offset - low + TILE]


def convolve(pad_ref, lane, utterance, start, depth_ref, flipped):
    taps = depth_ref.shape[0]
    columns = slice(lane * LANES, (lane + 1) * LANES)
    total = jnp.zeros((TILE, LANES), F32)
    for tap, view in shifted_views(pad_ref, lane, utterance, start, taps):
        row = taps - 1 - tap if flipped else tap
        total = total + view * depth_ref[row : row + 1, columns]
    return total


def forward_kernel(
    lengths_ref,
    features_ref,
    gain_ref,
    value_weight_ref,
    gate_weight_ref,
    depth_ref,
    out_weight_ref,
    turned_ref,
    gated_ref,
    gate_ref,
    slope_ref,
    active_ref,
    residual_ref,
    normed_ref,
    pad_ref,
    kept_ref,
):
    utterances = pad_ref.shape[1]
    frames = pad_ref.shape[2] - 2 * MARGIN
    step = pl.program_id(0)

    @pl.when(step == 0)
    def _():
        values = features_ref[...].astype(F32)
        centred = values - jnp.mean(values, axis=-1, keepdims=True)
        spread = jnp.mean(centred * centred, axis=-1, keepdims=True)
        normed = centred * lax.rsqrt(spread + 1e-05) * gain_ref[...]
        normed_ref[...] = normed.astype(BF16)
        turned_ref[...] = normed.T.astype(BF16)
        clear_margins(pad_ref)

    gate = jax.nn.sigmoid(dot(normed_ref[...], gate_weight_ref[...]))
    gate_ref[...] = gate
    values = dot(normed_ref[...], value_weight_ref[...]) * gate
    for utterance in range(utterances):
        rows = slice(utterance * frames, (utterance + 1) * frames)
        gated = values[rows, :] * live_column(lengths_ref, utterance, frames)
        gated_ref[rows, :] = gated
        for lane in range(WIDE // LANES):
            pad_ref[lane, utterance, MARGIN : MARGIN + frames, :] = gated[
                :, lane * LANES : (lane + 1) * LANES
            ]

    for lane in range(WIDE // LANES):
        columns = slice(lane * LANES, (lane + 1) * LANES)

        def one(utterance, carry, lane=lane, columns=columns):
            for start in range(0, frames, TILE):
                rows = pl.ds(pl.multiple_of(utterance * frames + start, TILE), TILE)
                convolved = convolve(pad_ref, lane, utterance, start, depth_ref, False)
                squash = jax.nn.sigmoid(convolved)
                active = (convolved * squash).astype(BF16)
                active_ref[rows, columns] = active
                kept_ref[step, rows, columns] = active
                slope_ref[rows, columns] = squash * (1.0 + convolved * (1.0 - squash))
            return carry

        lax.fori_loop(0, utterances, one, 0)

    @pl.when(step == kept_ref.shape[0] - 1)
    def _():
        active = jnp.concatenate([kept_ref[part] for part in range(kept_ref.shape[0])], axis=1)
        residual_ref[...] = features_ref[...].astype(F32) + dot(active, out_weight_ref[...])


def forward(lengths, features, gain, weight_in, depth, weight_out, utterances):
    rows, model = features.shape
    frames = rows // utterances
    steps = model // WIDE
    column = pl.BlockSpec((rows, WIDE), lambda i: (0, i))
    wide = jax.ShapeDtypeStruct((rows, model), F32)
    narrow = jax.ShapeDtypeStruct((rows, model), BF16)
    return pl.pallas_call(
        forward_kernel,
        grid=(steps,),
        out_shape=(jax.ShapeDtypeStruct((model, rows), BF16), wide, wide, wide, narrow, wide),
        in_specs=[
            SMEM_SPEC,
            fixed(rows, model),
            fixed(1, model),
            pl.BlockSpec((model, WIDE), lambda i: (0, i)),
            pl.BlockSpec((model, WIDE), lambda i: (0, steps + i)),
            pl.BlockSpec((depth.shape[0], WIDE), lambda i: (0, i)),
            fixed(model, model),
        ],
        out_specs=(fixed(model, rows), column, column, column, column, fixed(rows, model)),
        scratch_shapes=[
            pltpu.VMEM((rows, model), BF16),
            pltpu.VMEM((WIDE // LANES, utterances, frames + 2 * MARGIN, LANES), F32),
            pltpu.VMEM((steps, rows, WIDE), BF16),
        ],
        compiler_params=params(32),
        cost_estimate=cost(15),
        name="forward",
    )(lengths, features, gain, weight_in, weight_in, depth, weight_out)


def top_kernel(
    lengths_ref,
    residual_ref,
    gain_ref,
    head_ref,
    kept_ref,
    got_ref,
    loss_ref,
    final_ref,
    dlogits_ref,
    dresidual_ref,
):
    frames = residual_ref.shape[0]
    live = live_column(lengths_ref, pl.program_id(0), frames)
    values = residual_ref[...]
    centred = values - jnp.mean(values, axis=-1, keepdims=True)
    spread = jnp.mean(centred * centred, axis=-1, keepdims=True)
    inverse = lax.rsqrt(spread + 1e-05)
    unit = centred * inverse
    final = (unit * gain_ref[...]).astype(BF16)
    final_ref[...] = final

    def log_softmax(logits):
        shifted = logits - jnp.max(logits, axis=-1, keepdims=True)
        return shifted - jnp.log(jnp.sum(jnp.exp(shifted), axis=-1, keepdims=True))

    target = jnp.exp(log_softmax((kept_ref[0] + got_ref[0]) * (1.0 / TEACHERS)))
    logp = log_softmax(dot(final, head_ref[...]))
    cross = -jnp.sum(target * logp, axis=-1, keepdims=True)
    loss_ref[...] = jnp.broadcast_to(jnp.sum(cross * live, axis=0, keepdims=True), (1, 1, LANES))
    weight = jnp.sum(target, axis=-1, keepdims=True)
    dlogits = ((jnp.exp(logp) * weight - target) * live).astype(BF16)
    dlogits_ref[...] = dlogits
    dunit = dot(dlogits, head_ref[...], 1, 1) * gain_ref[...]
    average = jnp.mean(dunit, axis=-1, keepdims=True)
    along = jnp.mean(dunit * unit, axis=-1, keepdims=True)
    dresidual_ref[...] = (inverse * (dunit - average - unit * along)).astype(BF16)


def top(lengths, residual, gain, head, kept, got):
    rows, model = residual.shape
    utterances, frames, symbols = kept.shape
    per_row = pl.BlockSpec((frames, model), lambda i: (i, 0))
    sums = pl.BlockSpec((1, frames, symbols), lambda i: (i, 0, 0))
    return pl.pallas_call(
        top_kernel,
        grid=(utterances,),
        out_shape=(
            jax.ShapeDtypeStruct((utterances, 1, LANES), F32),
            jax.ShapeDtypeStruct((rows, model), BF16),
            jax.ShapeDtypeStruct((rows, symbols), BF16),
            jax.ShapeDtypeStruct((rows, model), BF16),
        ),
        in_specs=[SMEM_SPEC, per_row, fixed(1, model), fixed(model, symbols), sums, sums],
        out_specs=(
            pl.BlockSpec((1, 1, LANES), lambda i: (i, 0, 0)),
            per_row,
            pl.BlockSpec((frames, symbols), lambda i: (i, 0)),
            per_row,
        ),
        compiler_params=params(20),
        cost_estimate=cost(5),
        name="top",
    )(lengths, residual, gain, head, kept, got)


def outer_kernel(
    own_ref, active_ref, dresidual_ref, final_ref, dlogits_ref, send_ref, keep_ref, product_ref
):
    width = dresidual_ref.shape[1]
    product_ref[:, :width] = dot(active_ref[...], dresidual_ref[...], 0, 0)
    product_ref[:, width:] = dot(final_ref[...], dlogits_ref[...], 0, 0)
    write_pieces(own_ref, product_ref, send_ref, keep_ref, 0)


def outer(own, active, dresidual, final, dlogits):
    rows, model = active.shape
    half_out = dresidual.shape[1] // 2
    half_head = dlogits.shape[1] // 2
    width = half_out + half_head
    piece = (PLACES, model // (2 * PLACES), width)
    shape = jax.ShapeDtypeStruct((2,) + piece, BF16)
    out = pl.BlockSpec((1,) + piece, lambda i: (i, 0, 0, 0))
    return pl.pallas_call(
        outer_kernel,
        grid=(2,),
        out_shape=(shape, shape),
        in_specs=[
            SMEM_SPEC,
            fixed(rows, model),
            pl.BlockSpec((rows, half_out), lambda i: (0, i)),
            fixed(rows, model),
            pl.BlockSpec((rows, half_head), lambda i: (0, i)),
        ],
        out_specs=(out, out),
        scratch_shapes=[pltpu.VMEM((model, width), F32)],
        compiler_params=params(20),
        cost_estimate=cost(5),
        name="outer",
    )(own, active, dresidual, final, dlogits)


def inner_kernel(
    own_ref,
    lengths_ref,
    dresidual_ref,
    out_weight_ref,
    slope_ref,
    gated_ref,
    gate_ref,
    turned_ref,
    depth_ref,
    send_ref,
    keep_ref,
    dconv_ref,
    pad_ref,
    dvalue_ref,
    dgate_ref,
    product_ref,
):
    utterances = pad_ref.shape[1]
    frames = pad_ref.shape[2] - 2 * MARGIN

    @pl.when(pl.program_id(0) == 0)
    def _():
        clear_margins(pad_ref)

    dconv = dot(dresidual_ref[...], out_weight_ref[...], 1, 1) * slope_ref[...]
    dconv_ref[...] = dconv
    for utterance in range(utterances):
        rows = slice(utterance * frames, (utterance + 1) * frames)
        for lane in range(WIDE // LANES):
            pad_ref[lane, utterance, MARGIN : MARGIN + frames, :] = dconv[
                rows, lane * LANES : (lane + 1) * LANES
            ]

    for lane in range(WIDE // LANES):
        columns = slice(lane * LANES, (lane + 1) * LANES)

        def one(utterance, carry, lane=lane, columns=columns):
            for start in range(0, frames, TILE):
                rows = pl.ds(pl.multiple_of(utterance * frames + start, TILE), TILE)
                position = lax.broadcasted_iota(jnp.int32, (TILE, 1), 0) + start
                live = (position < lengths_ref[utterance]).astype(F32)
                dgated = convolve(pad_ref, lane, utterance, start, depth_ref, True) * live
                gate = gate_ref[rows, columns]
                dvalue_ref[rows, columns] = (dgated * gate).astype(BF16)
                dgate_ref[rows, columns] = (dgated * gated_ref[rows, columns] * (1.0 - gate)).astype(
                    BF16
                )
            return carry

        lax.fori_loop(0, utterances, one, 0)

    for group, source in ((0, dvalue_ref), (1, dgate_ref)):
        product_ref[...] = dot(turned_ref[...], source[...])
        write_pieces(own_ref, product_ref, send_ref, keep_ref, group)


def inner(own, lengths, dresidual, weight_out, slope, gated, gate, turned, depth, chunk, utterances):
    model, rows = turned.shape
    frames = rows // utterances
    steps = model // WIDE // CHUNKS
    first = chunk * steps
    column = pl.BlockSpec((rows, WIDE), lambda i: (0, first + i))
    piece = (2, PLACES, model // (2 * PLACES))
    shape = jax.ShapeDtypeStruct(piece + (steps * WIDE,), BF16)
    out = pl.BlockSpec(piece + (WIDE,), lambda i: (0, 0, 0, i))
    return pl.pallas_call(
        inner_kernel,
        grid=(steps,),
        out_shape=(shape, shape, jax.ShapeDtypeStruct((rows, steps * WIDE), F32)),
        in_specs=[
            SMEM_SPEC,
            SMEM_SPEC,
            fixed(rows, model),
            pl.BlockSpec((WIDE, model), lambda i: (first + i, 0)),
            column,
            column,
            column,
            fixed(model, rows),
            pl.BlockSpec((depth.shape[0], WIDE), lambda i: (0, first + i)),
        ],
        out_specs=(out, out, pl.BlockSpec((rows, WIDE), lambda i: (0, i))),
        scratch_shapes=[
            pltpu.VMEM((WIDE // LANES, utterances, frames + 2 * MARGIN, LANES), F32),
            pltpu.VMEM((rows, WIDE), BF16),
            pltpu.VMEM((rows, WIDE), BF16),
            pltpu.VMEM((model, WIDE), F32),
        ],
        compiler_params=params(24),
        cost_estimate=cost(11),
        name="inner",
    )(own, lengths, dresidual, weight_out, slope, gated, gate, turned, depth)


def taps_kernel(lengths_ref, gated_ref, *refs):
    *dconv_refs, out_ref, pad_ref, sums_ref = refs
    utterances = pad_ref.shape[1]
    frames = pad_ref.shape[2] - 2 * MARGIN
    taps = out_ref.shape[0] - 1
    step = pl.program_id(0)
    per_chunk = pl.num_programs(0) // len(dconv_refs)
    valid = lengths_ref[0]
    for utterance in range(1, utterances):
        valid = valid + lengths_ref[utterance]

    @pl.when(step == 0)
    def _():
        clear_margins(pad_ref)

    for lane in range(WIDE // LANES):
        columns = slice(lane * LANES, (lane + 1) * LANES)
        for utterance in range(utterances):
            rows = slice(utterance * frames, (utterance + 1) * frames)
            pad_ref[lane, utterance, MARGIN : MARGIN + frames, :] = gated_ref[rows, columns]

    for chunk, dconv_ref in enumerate(dconv_refs):

        @pl.when(step // per_chunk == chunk)
        def _(dconv_ref=dconv_ref):
            for lane in range(WIDE // LANES):
                columns = slice(lane * LANES, (lane + 1) * LANES)
                sums_ref[...] = jnp.zeros_like(sums_ref)

                def one(utterance, carry, lane=lane, columns=columns):
                    for start in range(0, frames, TILE):
                        rows = pl.ds(pl.multiple_of(utterance * frames + start, TILE), TILE)
                        dconv = dconv_ref[rows, columns]
                        for tap, view in shifted_views(pad_ref, lane, utterance, start, taps):
                            sums_ref[tap] += jnp.sum(
                                (view * dconv).reshape(TILE // 8, 8, LANES), axis=0
                            )
                    return carry

                lax.fori_loop(0, utterances, one, 0)
                out_ref[:taps, columns] = jnp.sum(sums_ref[...], axis=1)

    out_ref[taps:, :] = jnp.zeros((1, WIDE), F32) + valid.astype(F32)


def tap_sums(lengths, gated, dconvs, taps, utterances):
    rows, model = gated.shape
    steps = model // WIDE
    per_chunk = steps // len(dconvs)

    def part(chunk):
        low = chunk * per_chunk
        return pl.BlockSpec((rows, WIDE), lambda i: (0, jnp.clip(i - low, 0, per_chunk - 1)))

    return pl.pallas_call(
        taps_kernel,
        grid=(steps,),
        out_shape=jax.ShapeDtypeStruct((taps + 1, model), F32),
        in_specs=[SMEM_SPEC, pl.BlockSpec((rows, WIDE), lambda i: (0, i))]
        + [part(chunk) for chunk in range(len(dconvs))],
        out_specs=pl.BlockSpec((taps + 1, WIDE), lambda i: (0, i)),
        scratch_shapes=[
            pltpu.VMEM((WIDE // LANES, utterances, rows // utterances + 2 * MARGIN, LANES), F32),
            pltpu.VMEM((taps, 8, LANES), F32),
        ],
        compiler_params=params(16),
        cost_estimate=cost(9),
        name="taps",
    )(lengths, gated, *dconvs)


def gain_terms(weight, grad):
    terms = weight.astype(F32) * grad
    total = terms[:, :LANES]
    for first in range(LANES, terms.shape[1], LANES):
        total = total + terms[:, first : first + LANES]
    return total


def gain_row(terms):
    high = terms.astype(BF16)
    low = (terms - high.astype(F32)).astype(BF16)
    ones = jnp.ones((8, LANES), BF16)
    return (dot(ones, high, 1, 1) + dot(ones, low, 1, 1))[0:1, :]


def write_rows(own_ref, piece_refs, places, group, scale, targets):
    rows = piece_refs[0].shape[2]
    core = own_ref[0]
    first_place = pl.program_id(0) * places
    for index in range(places):
        for whose, (side, source) in enumerate(zip((core, 1 - core), piece_refs)):
            piece = (first_place + index) ^ own_ref[1 + whose]
            here = pl.ds(pl.multiple_of(index * 2 * rows + side * rows, rows), rows)
            for target, there, first, width in targets:
                target[here, there : there + width] = (
                    source[group, piece, :, first : first + width].astype(F32) * scale
                )


whole = pl.BlockSpec(memory_space=pltpu.VMEM)


def unpack_top_kernel(
    utts,
    own_ref,
    small_ref,
    mine_ref,
    other_ref,
    head_ref,
    gain_ref,
    losses_ref,
    wout_ref,
    dhead_ref,
    dgain_ref,
    depth_ref,
    loss_ref,
):
    taps = depth_ref.shape[0]
    scale = utts / small_ref[taps:, 0:1]
    half_out = wout_ref.shape[1] // 2
    half_head = dhead_ref.shape[1] // 2
    for group in range(2):
        targets = (
            (wout_ref, group * half_out, 0, half_out),
            (dhead_ref, group * half_head, half_out, half_head),
        )
        write_rows(own_ref, (mine_ref, other_ref), PLACES // 4, group, scale, targets)
    dgain_ref[...] = gain_row(gain_terms(head_ref[...], dhead_ref[...])) / gain_ref[...]
    depth_ref[...] = small_ref[:taps, :] * scale
    loss_ref[...] = losses_ref[...] * scale[None]


def unpack_top(utts, own, small, mine, other, head, gain, losses, width_out):
    steps = 4
    model, symbols = head.shape
    rows = model // steps
    taps = small.shape[0] - 1
    row = pl.BlockSpec((1, rows), lambda i, own_ref: (0, i))

    def block(width):
        return pl.BlockSpec((rows, width), lambda i, own_ref: (i, 0))

    return pl.pallas_call(
        functools.partial(unpack_top_kernel, utts),
        out_shape=(
            jax.ShapeDtypeStruct((model, width_out), F32),
            jax.ShapeDtypeStruct((model, symbols), F32),
            jax.ShapeDtypeStruct((1, model), F32),
            jax.ShapeDtypeStruct((taps, model), F32),
            jax.ShapeDtypeStruct(losses.shape, F32),
        ),
        grid_spec=pltpu.PrefetchScalarGridSpec(
            num_scalar_prefetch=1,
            grid=(steps,),
            in_specs=[
                fixed(*small.shape),
                whole,
                whole,
                block(symbols),
                row,
                fixed(*losses.shape),
            ],
            out_specs=(
                block(width_out),
                block(symbols),
                row,
                fixed(taps, model),
                fixed(*losses.shape),
            ),
        ),
        compiler_params=params(20),
        cost_estimate=cost(5),
        name="unpack_top",
    )(own, small, mine, other, head, gain, losses)


def unpack_inner_kernel(utts, own_ref, small_ref, weight_ref, gain_ref, *refs):
    *piece_refs, win_ref, dgain_ref = refs
    scale = utts / small_ref[small_ref.shape[0] - 1 :, 0:1]
    half = win_ref.shape[1] // 2
    for chunk in range(CHUNKS):
        pair = piece_refs[2 * chunk : 2 * chunk + 2]
        width = pair[0].shape[3]
        for group in range(2):
            targets = ((win_ref, group * half + chunk * width, 0, width),)
            write_rows(own_ref, pair, PLACES // 4, group, scale, targets)
    dgain_ref[...] = gain_row(gain_terms(weight_ref[...], win_ref[...])) / gain_ref[...]


def unpack_inner(utts, own, small, pieces, weight, gain):
    steps = 4
    model, width = weight.shape
    rows = model // steps
    row = pl.BlockSpec((1, rows), lambda i, own_ref: (0, i))
    block = pl.BlockSpec((rows, width), lambda i, own_ref: (i, 0))
    return pl.pallas_call(
        functools.partial(unpack_inner_kernel, utts),
        out_shape=(
            jax.ShapeDtypeStruct((model, width), F32),
            jax.ShapeDtypeStruct((1, model), F32),
        ),
        grid_spec=pltpu.PrefetchScalarGridSpec(
            num_scalar_prefetch=1,
            grid=(steps,),
            in_specs=[fixed(*small.shape), block, row]
            + [whole] * len(pieces),
            out_specs=(block, row),
        ),
        compiler_params=params(24),
        cost_estimate=cost(8),
        name="unpack_inner",
    )(own, small, weight, gain, *pieces)


def on_device(
    features,
    teacher_logits,
    lengths,
    gain_conv,
    weight_in,
    weight_depth,
    weight_out,
    gain_out,
    head_weight,
):
    count = 1
    for axis in ("member", "near", FAR, REST, CORE):
        count *= lax.axis_size(axis)
    member = lax.axis_index("member").astype(jnp.int32)[None]
    own = own_places()
    taps, model = weight_depth.shape
    utterances, frames, _ = features.shape
    utts = float(utterances * count)
    tie = lax.optimization_barrier

    own, member, teacher_logits = tie((own, member, teacher_logits))
    give, kept = teacher_sums(member, teacher_logits, utterances)
    got = exchange(give, "member")
    flat = features.reshape(utterances * frames, model)
    turned, gated, gate, slope, active, residual = forward(
        lengths, flat, gain_conv[None], weight_in, weight_depth, weight_out, utterances
    )
    losses, final, dlogits, dresidual = top(
        lengths, residual, gain_out[None], head_weight, kept, got
    )

    line = Line()

    def products(name, chunk):
        nonlocal dresidual
        dresidual = line.before_kernel(dresidual)
        send, keep, dconv = inner(
            own,
            lengths,
            dresidual,
            weight_out,
            slope,
            gated,
            gate,
            turned,
            weight_depth,
            chunk,
            utterances,
        )
        line.begin(name, send, keep)
        line.put(name + "_conv", dconv)

    send, keep = outer(own, active, dresidual, final, dlogits)
    send, keep, dresidual = tie((send, keep, dresidual))
    line.begin("top", send, keep)
    products("in0", 0)
    line.step("top", start=False)
    products("in1", 1)
    written = {}

    def write_top():
        mine, other = line.values["top"]
        *rest, written["losses"] = unpack_top(
            utts,
            own,
            line.values["small"],
            line.after_last(mine),
            other,
            head_weight,
            gain_out[None],
            losses,
            weight_out.shape[1],
        )
        written["out"], written["head"], by_head, written["depth"] = rest
        line.put("by_head", by_head)

    def write_in():
        pieces = [array for name in ("in0", "in1") for array in line.values[name]]
        written["in"], by_in = unpack_inner(
            utts, own, line.values["small"], pieces, weight_in, gain_conv[None]
        )
        line.put("by_in", by_in)

    def sum_taps():
        names = ("in0_conv", "in1_conv")
        dconvs = line.after_last(tuple(line.values[name] for name in names))
        line.put("taps", tap_sums(lengths, gated, dconvs, taps, utterances))
        line.begin_small("small", line.values["taps"])

    kernels = {
        "taps": sum_taps,
        "write_top": write_top,
        "write_in": write_in,
    }
    for name in ORDER:
        if name in kernels:
            kernels[name]()
        else:
            line.step(name)
    return (
        line.values["by_in"].reshape(model),
        written["in"],
        written["depth"],
        written["out"],
        line.values["by_head"].reshape(model),
        written["head"],
        written["losses"][:, 0, 0],
    )


def solution(mesh):
    members, others = mesh.devices.shape
    near, cores = 2, 2
    far = 2 * PLACES // (members * near)
    rest = others // (far * near * cores)
    split = jax.sharding.Mesh(
        mesh.devices.reshape(members, rest, far, near, cores),
        ("member", REST, FAR, "near", CORE),
    )
    dp = (REST, FAR, "near", CORE)
    in_specs = (
        P(dp + ("member",), None, None),
        P("member", dp, None, None),
        P(dp + ("member",)),
        P(),
        P(),
        P(),
        P(),
        P(),
        P(),
    )
    out_specs = (P(), P(), P(), P(), P(), P(), P(dp + ("member",)))
    return jax.shard_map(
        on_device, mesh=split, in_specs=in_specs, out_specs=out_specs, check_vma=False
    )
```
